32 devices in a mesh: dp: 8 (over y, x, core), mp: 4 (over z).
Axes of the slice: x: 2, y: 2, z: 4, core: 2. Of those that a mesh axis runs over, the one named last changes fastest.
Arguments:
- hidden: bfloat16 [8192, 2048], P('dp', 'mp'), may hold values from -6 to 6
- teacher: bfloat16 [8192, 2048], P('dp', 'mp'), may hold values from -6 to 6
- lengths: int32 [8], replicated, may hold values from 256 to 1024, as said below
- feature_params: bfloat16 [2048, 18], P(('dp', 'mp')), may hold values from -10 to 3, as said below
- decay_down: bfloat16 [2048, 96], P(('dp', 'mp')), may hold values from -0.125 to 0.125
- rate_down: bfloat16 [2048, 96], P(('dp', 'mp')), may hold values from -0.125 to 0.125
- gate_down: bfloat16 [2048, 256], P(('dp', 'mp')), may hold values from -0.125 to 0.125
- decay_up: bfloat16 [96, 2048], P('dp', 'mp'), may hold values from -0.625 to 0.625
- rate_up: bfloat16 [96, 2048], P('dp', 'mp'), may hold values from -0.625 to 0.625
- gate_up: bfloat16 [256, 2048], P('dp', 'mp'), may hold values from -0.375 to 0.375
- receptance: bfloat16 [2048, 2048], P('dp', 'mp'), may hold values from -0.125 to 0.125
- key_proj: bfloat16 [2048, 2048], P('dp', 'mp'), may hold values from -0.125 to 0.125
- value_proj: bfloat16 [2048, 2048], P('dp', 'mp'), may hold values from -0.125 to 0.125
- output_proj: bfloat16 [2048, 2048], P('mp', 'dp'), may hold values from -0.1875 to 0.1875
- ffn_key: bfloat16 [2048, 8192], P('dp', 'mp'), may hold values from -0.125 to 0.125
- ffn_value: bfloat16 [8192, 2048], P('mp', 'dp'), may hold values from -0.0625 to 0.0625
Outputs:
- out_state: bfloat16 [8192, 2048], P('dp', 'mp')
- grad_hidden: float32 [8192, 2048], P('dp', 'mp')
- grad_params: float32 [2048, 18], P(('dp', 'mp'))
- grad_decay_down: float32 [2048, 96], P(('dp', 'mp'))
- grad_rate_down: float32 [2048, 96], P(('dp', 'mp'))
- grad_gate_down: float32 [2048, 256], P(('dp', 'mp'))
- grad_decay_up: float32 [96, 2048], P('dp', 'mp')
- grad_rate_up: float32 [96, 2048], P('dp', 'mp')
- grad_gate_up: float32 [256, 2048], P('dp', 'mp')
- grad_receptance: float32 [2048, 2048], P('dp', 'mp')
- grad_key_proj: float32 [2048, 2048], P('dp', 'mp')
- grad_value_proj: float32 [2048, 2048], P('dp', 'mp')
- grad_output_proj: float32 [2048, 2048], P('mp', 'dp')
- grad_ffn_key: float32 [2048, 8192], P('dp', 'mp')
- grad_ffn_value: float32 [8192, 2048], P('mp', 'dp')
The draws below stay inside these ranges and needn't reach their ends.
Inputs may be any that keep to these rules, and one draw needn't show every extreme that they name: `lengths`: each sequence's valid tokens fill its first slots; one sequence holds 1024 valid tokens and one holds 256. `feature_params`: the columns are in the order that the steps list.
All inputs are finite; a program needn't handle non-finite values.
Results may differ from the reference program's by a relative error of at most 0.015.
Values may be sent and summed in bfloat16 or wider, within the bound.
A program may use at most 576 MiB of HBM per device.

```python
import math
import jax
import jax.numpy as jnp
from jax import lax

MODEL_BREADTH = 2048
SUBSPACE_SIZE = 64
FF = 8192
LW = 96
LA = 96
LG = 256
SEQ_LEN = 1024
MIN_LEN = 256
SUBSPACE_COUNT = 32
SEQS = 8
TOKENS = 8192


def draw_lengths(key, part):
    drawn = jax.random.randint(jax.random.fold_in(key, 1), (SEQS,), MIN_LEN, SEQ_LEN + 1)
    longest = jax.random.randint(jax.random.fold_in(key, 2), (), 0, SEQS)
    offset_pick = jax.random.randint(jax.random.fold_in(key, 3), (), 0, max(SEQS - 1, 1))
    shortest = (longest + 1 + offset_pick) % SEQS
    drawn = drawn.at[shortest].set(MIN_LEN)
    return drawn.at[longest].set(SEQ_LEN).astype(jnp.int32)


def draw_feature_params(key, part):

    def evenly(column, low_end, high_end):
        return jax.random.uniform(jax.random.fold_in(key, column), (MODEL_BREADTH,), jnp.float32, low_end, high_end)

    def spread(column, width_scale):
        return width_scale * jnp.clip(jax.random.normal(jax.random.fold_in(key, column), (MODEL_BREADTH,), jnp.float32), -3.0, 3.0)
    head_bias = jax.random.uniform(jax.random.fold_in(key, 40), (SUBSPACE_COUNT,), jnp.float32, -7.0, -1.0)
    gain_range = (0.6, 1.4)
    decay_bias = jnp.repeat(head_bias, SUBSPACE_SIZE) + spread(41, 0.5)
    columns_out = [evenly(0, gain_range[0], gain_range[1]), spread(1, 0.3)]
    columns_out += [evenly(column, 0.0, 1.0) for column in range(2, 8)]
    columns_out += [decay_bias, spread(9, 1.0), evenly(10, 0.5, 1.5), evenly(11, 0.5, 1.5), spread(12, 0.5), evenly(13, gain_range[0], gain_range[1]), spread(14, 0.3), evenly(15, gain_range[0], gain_range[1]), spread(16, 0.3), evenly(17, 0.0, 1.0)]
    return jnp.stack(columns_out, axis=1).astype(jnp.bfloat16)


def levels(key, shape, shards, least, high):
    def one(position, parts):
        heights = jax.random.uniform(jax.random.fold_in(jax.random.fold_in(key, 6), position), (parts,), jnp.float32, least / len(shards), high / len(shards))
        return jnp.repeat(jnp.exp(heights), shape[position] // parts).reshape((-1,) + (1,) * (len(shape) - position - 1))

    factor_of = one(*shards[0])
    for cut in shards[1:]:
        factor_of = factor_of * one(*cut)
    return factor_of


def noise(key, extent, scale, bound, pieces=(), held_as=jnp.bfloat16):
    loudness = levels(key, extent, pieces, -0.22, 0.18) if pieces else 1.0
    values = jax.random.normal(key, extent, jnp.float32) * scale * loudness
    return jnp.minimum(jnp.maximum(values, -bound), bound).astype(held_as)


def setup_inputs(seed: int = 0) -> dict:
    streams_of = jax.random.split(jax.random.key(seed), 17)
    hidden = noise(streams_of[0], (TOKENS, MODEL_BREADTH), 1.0, 6.0, ((0, 8), (1, 4)))
    teacher = noise(streams_of[1], (TOKENS, MODEL_BREADTH), 1.0, 6.0, ((0, 8), (1, 4)))
    lengths = draw_lengths(jax.random.fold_in(streams_of[16], 71), 0)
    feature_params = draw_feature_params(jax.random.fold_in(streams_of[16], 71), 0)
    decay_down = noise(streams_of[4], (MODEL_BREADTH, LW), MODEL_BREADTH ** -0.5, 0.125, ((0, 32),))
    rate_down = noise(streams_of[5], (MODEL_BREADTH, LA), MODEL_BREADTH ** -0.5, 0.125, ((0, 32),))
    gate_down = noise(streams_of[6], (MODEL_BREADTH, LG), MODEL_BREADTH ** -0.5, 0.125, ((0, 32),))
    decay_up = noise(streams_of[7], (LW, MODEL_BREADTH), LW ** -0.5, 0.625, ((0, 8), (1, 4)))
    rate_up = noise(streams_of[8], (LA, MODEL_BREADTH), LA ** -0.5, 0.625, ((0, 8), (1, 4)))
    gate_up = noise(streams_of[9], (LG, MODEL_BREADTH), LG ** -0.5, 0.375, ((0, 8), (1, 4)))
    receptance = noise(streams_of[10], (MODEL_BREADTH, MODEL_BREADTH), MODEL_BREADTH ** -0.5, 0.125, ((0, 8), (1, 4)))
    key_proj = noise(streams_of[11], (MODEL_BREADTH, MODEL_BREADTH), MODEL_BREADTH ** -0.5, 0.125, ((0, 8), (1, 4)))
    value_proj = noise(streams_of[12], (MODEL_BREADTH, MODEL_BREADTH), MODEL_BREADTH ** -0.5, 0.125, ((0, 8), (1, 4)))
    output_proj = noise(streams_of[13], (MODEL_BREADTH, MODEL_BREADTH), (MODEL_BREADTH // 2) ** -0.5, 0.1875, ((0, 4), (1, 8)))
    ffn_key = noise(streams_of[14], (MODEL_BREADTH, FF), MODEL_BREADTH ** -0.5, 0.125, ((0, 8), (1, 4)))
    ffn_value = noise(streams_of[15], (FF, MODEL_BREADTH), FF ** -0.5, 0.0625, ((0, 4), (1, 8)))
    return {"hidden": hidden, "teacher": teacher, "lengths": lengths, "feature_params": feature_params, "decay_down": decay_down, "rate_down": rate_down, "gate_down": gate_down, "decay_up": decay_up, "rate_up": rate_up, "gate_up": gate_up, "receptance": receptance, "key_proj": key_proj, "value_proj": value_proj, "output_proj": output_proj, "ffn_key": ffn_key, "ffn_value": ffn_value}


@jax.custom_vjp
def narrow_latent(v):
    return lax.optimization_barrier(v.astype(jnp.bfloat16)).astype(jnp.float32)

@jax.custom_vjp
def low_back(v):
    return v

def low_keep(v):
    return (narrow_latent(v), None)

def low_pass(kept, grad):
    return (grad,)

def back_keep(v):
    return (v, None)

def back_low(kept, grad):
    return (narrow_latent(grad),)
narrow_latent.defvjp(low_keep, low_pass)
low_back.defvjp(back_keep, back_low)
hi_prec = lax.Precision.HIGHEST
norm_eps = 1e-05
group_eps = 0.00064

def matmul(left_op, right_op):
    return jnp.dot(left_op, right_op, preferred_element_type=jnp.float32, precision=hi_prec)

def layer_norm(values, scale_in, offset):
    centre = lax.optimization_barrier(jnp.mean(values, axis=-1, keepdims=True))
    centred = values - centre
    spread = lax.optimization_barrier(jnp.mean(centred * centred, axis=-1, keepdims=True))
    return centred * lax.rsqrt(spread + norm_eps) * scale_in + offset

def shifted(values):
    grid_view = values.reshape(values.shape[0] // SEQ_LEN, SEQ_LEN, values.shape[1])
    earlier = jnp.concatenate([jnp.zeros_like(grid_view[:, :1]), grid_view[:, :-1]], axis=1)
    return earlier.reshape(values.shape)

def token_step(state, members):
    acceptance_matrix, decay_rate, remove_dir, write_dir, value_rows, key_rows = members
    removed = jnp.einsum('ghij,ghj->ghi', state, remove_dir, precision=hi_prec)
    state = state * decay_rate[:, :, None, :] + removed[..., None] * write_dir[:, :, None, :] + value_rows[..., None] * key_rows[:, :, None, :]
    return (state, jnp.einsum('ghij,ghj->ghi', state, acceptance_matrix, precision=hi_prec))

def run_block(state, members):
    return lax.scan(token_step, state, members)

def recurrence(members, seq_count):
    block_len = math.gcd(SEQ_LEN, 64)

    def arrange(values):
        shaped = values.reshape(seq_count, SEQ_LEN, SUBSPACE_COUNT, SUBSPACE_SIZE).transpose(1, 0, 2, 3)
        return shaped.reshape(SEQ_LEN // block_len, block_len, seq_count, SUBSPACE_COUNT, SUBSPACE_SIZE)
    arranged = tuple((arrange(member) for member in members))
    start_state = jnp.zeros((seq_count, SUBSPACE_COUNT, SUBSPACE_SIZE, SUBSPACE_SIZE), jnp.float32)
    final_state, outputs = lax.scan(jax.checkpoint(run_block), start_state, arranged)
    outputs = outputs.reshape(SEQ_LEN, seq_count, SUBSPACE_COUNT, SUBSPACE_SIZE).transpose(1, 0, 2, 3)
    return outputs.reshape(seq_count * SEQ_LEN, MODEL_BREADTH)

def layer_loss(hidden, teacher, valid, loss_scale, weights):
    feature_params, decay_down, rate_down, gate_down, decay_up, rate_up, gate_up, receptance, key_proj, value_proj, output_proj, ffn_key, ffn_value = weights
    shard_positions = hidden.shape[0]
    seq_count = shard_positions // SEQ_LEN
    standardized_source = layer_norm(hidden, feature_params[:, 0], feature_params[:, 1])
    shift_diff = shifted(standardized_source) - standardized_source
    mix_r, mix_w, mix_k, mix_v, mix_a, mix_g = tuple((narrow_latent(standardized_source + shift_diff * feature_params[:, column]) for column in range(2, 8)))
    acceptance_matrix = low_back(matmul(mix_r, receptance))
    keys_in = low_back(matmul(mix_k, key_proj))
    payload_source = low_back(matmul(mix_v, value_proj))
    decay_hid = narrow_latent(jnp.tanh(low_back(matmul(mix_w, decay_down))))
    decay_in = low_back(matmul(decay_hid, decay_up))
    rate_hid = narrow_latent(low_back(matmul(mix_a, rate_down)))
    rate_in = low_back(matmul(rate_hid, rate_up))
    gate_hid = narrow_latent(jax.nn.sigmoid(low_back(matmul(mix_g, gate_down))))
    sigmoid_source = low_back(matmul(gate_hid, gate_up))
    log_decay = -jnp.exp(-jax.nn.softplus(-(decay_in + feature_params[:, 8])) - 0.5)
    learn_rate = jax.nn.sigmoid(rate_in + feature_params[:, 9])
    scaled_keys = (keys_in * feature_params[:, 10]).reshape(shard_positions, SUBSPACE_COUNT, SUBSPACE_SIZE)
    unit_keys = scaled_keys * lax.rsqrt(lax.optimization_barrier(jnp.sum(scaled_keys * scaled_keys, axis=-1, keepdims=True)) + 1e-06)
    unit_keys = unit_keys.reshape(shard_positions, MODEL_BREADTH)
    lagged_lookups = keys_in * (1.0 + (learn_rate - 1.0) * feature_params[:, 11])
    live = valid[:, None] > 0.5
    decay_rate = jnp.where(live, jnp.exp(log_decay), 1.0)
    unit_keys = jnp.where(live, unit_keys, 0.0)
    lagged_lookups = jnp.where(live, lagged_lookups, 0.0)
    state_out = recurrence((acceptance_matrix, decay_rate, -unit_keys, unit_keys * learn_rate, payload_source, lagged_lookups), seq_count)
    grouped = state_out.reshape(shard_positions, SUBSPACE_COUNT, SUBSPACE_SIZE)
    centre = lax.optimization_barrier(jnp.mean(grouped, axis=-1, keepdims=True))
    centred = grouped - centre
    spread = lax.optimization_barrier(jnp.mean(centred * centred, axis=-1, keepdims=True))
    rescaled_subspaces = (centred * lax.rsqrt(spread + group_eps)).reshape(shard_positions, MODEL_BREADTH) * feature_params[:, 13] + feature_params[:, 14]
    current_reward = lax.optimization_barrier(jnp.sum((acceptance_matrix * lagged_lookups * feature_params[:, 12]).reshape(shard_positions, SUBSPACE_COUNT, SUBSPACE_SIZE), axis=-1, keepdims=True))
    current_reward = (current_reward * payload_source.reshape(shard_positions, SUBSPACE_COUNT, SUBSPACE_SIZE)).reshape(shard_positions, MODEL_BREADTH)
    masked_result = narrow_latent((rescaled_subspaces + current_reward) * sigmoid_source)
    residual = hidden + low_back(matmul(masked_result, output_proj))
    normed_two = layer_norm(residual, feature_params[:, 15], feature_params[:, 16])
    mix_c = narrow_latent(normed_two + (shifted(normed_two) - normed_two) * feature_params[:, 17])
    active = jax.nn.relu(low_back(matmul(mix_c, ffn_key)))
    squared = narrow_latent(active * active)
    result = residual + low_back(matmul(squared, ffn_value))
    error = (result - teacher) * valid[:, None]
    return (0.5 * loss_scale * jnp.sum(error * error), result)

def reference(hidden, teacher, lengths, feature_params, decay_down, rate_down, gate_down, decay_up, rate_up, gate_up, receptance, key_proj, value_proj, output_proj, ffn_key, ffn_value):
    weights = tuple((member.astype(jnp.float32) for member in (feature_params, decay_down, rate_down, gate_down, decay_up, rate_up, gate_up, receptance, key_proj, value_proj, output_proj, ffn_key, ffn_value)))
    loss_scale = TOKENS / jnp.sum(lengths).astype(jnp.float32)
    places = jnp.arange(SEQ_LEN, dtype=jnp.int32)
    valid = (places[None, :] < lengths[:, None]).astype(jnp.float32)
    group_size = math.gcd(SEQS, 4)
    rounds = SEQS // group_size
    group_rows = group_size * SEQ_LEN
    hidden_groups = hidden.astype(jnp.float32).reshape(rounds, group_rows, MODEL_BREADTH)
    teacher_groups = teacher.astype(jnp.float32).reshape(rounds, group_rows, MODEL_BREADTH)
    valid_groups = valid.reshape(rounds, group_rows)
    step_fn = jax.checkpoint(layer_loss)

    def total(hidden_all, weight_all):

        def one_group(carry, members):
            loss_part, result = step_fn(members[0], members[1], members[2], loss_scale, weight_all)
            return (carry + loss_part, result)
        loss_sum, results = lax.scan(one_group, jnp.zeros((), jnp.float32), (hidden_all, teacher_groups, valid_groups))
        return (loss_sum, results)
    loss_sum, back_fn, results = jax.vjp(total, hidden_groups, weights, has_aux=True)
    grad_groups, grad_weights = back_fn(jnp.ones((), jnp.float32))
    return (results.reshape(TOKENS, MODEL_BREADTH).astype(jnp.bfloat16), grad_groups.reshape(TOKENS, MODEL_BREADTH), grad_weights[0], grad_weights[1], grad_weights[2], grad_weights[3], grad_weights[4], grad_weights[5], grad_weights[6], grad_weights[7], grad_weights[8], grad_weights[9], grad_weights[10], grad_weights[11], grad_weights[12])
```

```python
from functools import partial
import math

import jax
import jax.numpy as jnp
from jax import lax
from jax.experimental import pallas as pl
from jax.experimental.pallas import tpu as pltpu
from jax.sharding import PartitionSpec as P

norm_eps = 1e-05
SUBSPACE_SIZE = 64
SEQ_LEN = 1024
group_eps = 0.00064
CHUNK = 64
PAIR = 2 * SUBSPACE_SIZE
CHUNKS_FWD = 2
CHUNKS_BWD = 2
DECAY_SCALE = math.exp(-0.5)


def dot_nn(left_op, right_op):
    return lax.dot_general(left_op, right_op, (((1,), (0,)), ((), ())), preferred_element_type=jnp.float32)


def dot_nt(left_op, right_op):
    return lax.dot_general(left_op, right_op, (((1,), (1,)), ((), ())), preferred_element_type=jnp.float32)


def dot_tn(left_op, right_op):
    return lax.dot_general(left_op, right_op, (((0,), (0,)), ((), ())), preferred_element_type=jnp.float32)


def low(values):
    return values.astype(jnp.bfloat16)


def split_dot(ones_op, values):
    top = low(values)
    rest = values - top.astype(jnp.float32)
    mid = low(rest)
    tail = low(rest - mid.astype(jnp.float32))
    return dot_nn(ones_op, top) + dot_nn(ones_op, mid) + dot_nn(ones_op, tail)


def halves(values):
    top = low(values)
    return top, low(values - top.astype(jnp.float32))


def iota(shape, axis):
    return lax.broadcasted_iota(jnp.int32, shape, axis)


def head_masks():
    lane = iota((CHUNK, PAIR), 1)
    return lane < SUBSPACE_SIZE


def stack_heads(values):
    first = iota(values.shape, 1) < SUBSPACE_SIZE
    zero = jnp.zeros_like(values)
    return jnp.concatenate(
        [jnp.where(first, values, zero), jnp.where(first, zero, values)], axis=0
    )


def fold_heads(values):
    first = iota((CHUNK, PAIR), 1) < SUBSPACE_SIZE
    return jnp.where(first, values[:CHUNK], values[CHUNK:])


def head_ones():
    return (
        iota((PAIR, PAIR), 0) // SUBSPACE_SIZE == iota((PAIR, PAIR), 1) // SUBSPACE_SIZE
    )


def head_sum(values, ones_op):
    top = low(values)
    rest = low(values - top.astype(jnp.float32))
    return dot_nn(top, ones_op) + dot_nn(rest, ones_op)


def lower_inverses(lower_parts):
    row = iota((CHUNK, PAIR), 0)
    col = iota((CHUNK, PAIR), 1) % CHUNK
    eye = jnp.where(row == col, 1.0, 0.0)

    def times(lefts, rights):
        return [
            dot_nn(low(left_op), stack_heads(low(right_op)))
            for left_op, right_op in zip(lefts, rights)
        ]

    def plus(*lists):
        return [sum(members[1:], members[0]) for members in zip(*lists)]

    near = row // 8 == col // 8
    base = [jnp.where(near, part, 0.0) for part in lower_parts]
    square = times(base, base)
    cube = times(base, square)
    fourth = times(square, square)
    accum = [eye + first + second + third for first, second, third in zip(base, square, cube)]
    accum = plus(accum, times(accum, fourth))
    width = 8
    while width < CHUNK:
        level = (row // (2 * width) == col // (2 * width)) & (row // width != col // width)
        off = [jnp.where(level, part, 0.0) for part in lower_parts]
        accum = plus(accum, times(times(accum, off), accum))
        width *= 2
    return accum


def prepare(r, k, dw, da, cols, live, tri_op, ones_op):
    sw = jax.nn.sigmoid(dw + cols[0:1])
    full_log = -DECAY_SCALE * sw
    log_decay = jnp.where(live, full_log, 0.0)
    rate = jax.nn.sigmoid(da + cols[1:2])
    scaled = k * cols[2:3]
    inv = lax.rsqrt(head_sum(scaled * scaled, ones_op) + 1e-06)
    unit = scaled * inv
    unit_live = jnp.where(live, unit, 0.0)
    lag_scale = 1.0 + (rate - 1.0) * cols[3:4]
    lagged = jnp.where(live, k * lag_scale, 0.0)
    running = split_dot(tri_op, log_decay)
    grown = jnp.exp(running)
    before = jnp.exp(running - log_decay)
    shrunk = jnp.exp(-running)
    last = running[CHUNK - 1 : CHUNK]
    til_end = jnp.exp(last - running)
    write = unit_live * rate
    return dict(
        sw=sw,
        full_log=full_log,
        rate=rate,
        inv=inv,
        unit=unit,
        unit_live=unit_live,
        lag_scale=lag_scale,
        lagged=lagged,
        grown=grown,
        before=before,
        shrunk=shrunk,
        til_end=til_end,
        final=jnp.exp(last),
        read_wide=r * grown,
        write_wide=write * shrunk,
        key_wide=lagged * shrunk,
        read_hat=low(r * grown),
        remove_hat=low(-unit_live * before),
        write_hat=low(write * shrunk),
        key_hat=low(lagged * shrunk),
        write_end=low(write * til_end),
        key_end=low(lagged * til_end),
    )


def tri_masks():
    row = iota((CHUNK, PAIR), 0)
    col = iota((CHUNK, PAIR), 1) % CHUNK
    return row > col, row >= col


def mixer_forward(
    steps_per_seq,
    length_ref,
    r_ref,
    k_ref,
    v_ref,
    dw_ref,
    da_ref,
    gate_ref,
    cols_ref,
    z_ref,
    y_ref,
    t_ref,
    u_ref,
    s_ref,
    lk_ref,
    reads_ref,
    state,
):
    step = pl.program_id(0)
    within_seq = lax.rem(step, steps_per_seq)
    length = length_ref[step // steps_per_seq]

    @pl.when(within_seq == 0)
    def _():
        state[...] = jnp.zeros_like(state)

    rows_each = r_ref.shape[0]
    chunks = rows_each // CHUNK
    pairs = r_ref.shape[1] // PAIR
    ones_mask = head_ones()
    ones_op = jnp.where(ones_mask, 1.0, 0.0).astype(jnp.bfloat16)
    tri_op = jnp.where(iota((CHUNK, CHUNK), 0) >= iota((CHUNK, CHUNK), 1), 1.0, 0.0).astype(jnp.bfloat16)
    strict, within = tri_masks()
    within_two = jnp.concatenate([within, within], axis=1)
    units = [(chunk, pair) for chunk in range(chunks) for pair in range(pairs)]

    def place_of(unit):
        chunk, pair = unit
        return slice(chunk * CHUNK, (chunk + 1) * CHUNK), slice(pair * PAIR, (pair + 1) * PAIR)

    prepared, scored, lower_parts = [], [], []
    for unit in units:
        rows, lanes = place_of(unit)
        live = within_seq * rows_each + unit[0] * CHUNK + iota((CHUNK, PAIR), 0) < length
        got = prepare(
            r_ref[rows, lanes],
            k_ref[rows, lanes],
            dw_ref[rows, lanes],
            da_ref[rows, lanes],
            cols_ref[:, lanes],
            live,
            tri_op,
            ones_op,
        )
        prepared.append(got)
    for unit, got in zip(units, prepared):
        got["both"] = jnp.concatenate([got["remove_hat"], got["read_hat"]], axis=0)
        past = jnp.concatenate([stack_heads(got["write_hat"]), stack_heads(got["key_hat"])], axis=0)
        scores = dot_nt(got["both"], past)
        past_rest = jnp.concatenate(
            [stack_heads(halves(got["write_wide"])[1]), stack_heads(halves(got["key_wide"])[1])], axis=0
        )
        got["read_rest"] = halves(got["read_wide"])[1]
        fine = scores[CHUNK:] + (dot_nt(got["read_rest"], past) + dot_nt(got["read_hat"], past_rest))
        lower_parts.append(jnp.where(strict, scores[:CHUNK, :PAIR], 0.0))
        lower_key = low(jnp.where(strict, scores[:CHUNK, PAIR:], 0.0))
        reads = low(jnp.where(within_two, fine, 0.0))
        scored.append((lower_key, reads))
    solves = [low(part) for part in lower_inverses(lower_parts)]
    for unit, solve in zip(units, solves):
        t_ref[place_of(unit)] = solve
    for chunk in range(chunks):
        group = [index for index, unit in enumerate(units) if unit[0] == chunk]
        lows = [low(v_ref[place_of(units[index])]) for index in group]
        stacks = [stack_heads(values) for values in lows]
        olds = [state[units[index][1]] for index in group]
        old_parts = [halves(old) for old in olds]
        from_state = [dot_nt(prepared[index]["both"], old[0]) for index, old in zip(group, old_parts)]
        read_state = [
            part[CHUNK:]
            + (dot_nt(prepared[index]["read_rest"], old[0]) + dot_nt(prepared[index]["read_hat"], old[1]))
            for index, part, old in zip(group, from_state, old_parts)
        ]
        right = [
            low(part[:CHUNK] + dot_nn(scored[index][0], stack))
            for index, part, stack in zip(group, from_state, stacks)
        ]
        removed = [low(dot_nn(solves[index], stack_heads(part))) for index, part in zip(group, right)]
        for slot, index in enumerate(group):
            pair = units[index][1]
            got = prepared[index]
            ends = jnp.concatenate([got["write_end"], got["key_end"]], axis=0)
            adds = dot_tn(jnp.concatenate([removed[slot], lows[slot]], axis=0), ends)
            state[pair] = olds[slot] * got["final"] + jnp.where(ones_mask, adds, 0.0)
            u_ref[place_of(units[index])] = removed[slot]
            rows, lanes = place_of(units[index])
            lk_ref[rows, lanes], reads_ref[rows, slice(2 * lanes.start, 2 * lanes.stop)] = scored[index]
            s_ref[chunk, pair] = olds[slot]
        outs = [
            read_state[slot]
            + dot_nn(scored[index][1], jnp.concatenate([stack_heads(removed[slot]), stacks[slot]], axis=0))
            for slot, index in enumerate(group)
        ]
        centred = [y - head_sum(y, ones_op) * (1.0 / SUBSPACE_SIZE) for y in outs]
        spread = [head_sum(part * part, ones_op) * (1.0 / SUBSPACE_SIZE) for part in centred]
        for slot, index in enumerate(group):
            rows, lanes = place_of(units[index])
            cols = cols_ref[:, lanes]
            normed = centred[slot] * lax.rsqrt(spread[slot] + group_eps)
            bonus = head_sum(r_ref[rows, lanes] * prepared[index]["lagged"] * cols[4:5], ones_op)
            mixed = normed * cols[5:6] + cols[6:7] + bonus * v_ref[rows, lanes]
            y_ref[rows, lanes] = outs[slot]
            z_ref[rows, lanes] = low(mixed * gate_ref[rows, lanes])


def mixer_backward(
    steps_per_seq,
    length_ref,
    r_ref,
    k_ref,
    v_ref,
    dw_ref,
    da_ref,
    gate_ref,
    cols_ref,
    y_ref,
    t_ref,
    u_ref,
    s_ref,
    lk_ref,
    reads_ref,
    dz_ref,
    dr_ref,
    dk_ref,
    dv_ref,
    ddw_ref,
    dda_ref,
    dgate_ref,
    dcols_ref,
    dstate,
):
    step = pl.num_programs(0) - 1 - pl.program_id(0)
    within_seq = lax.rem(step, steps_per_seq)
    length = length_ref[step // steps_per_seq]

    @pl.when(within_seq == steps_per_seq - 1)
    def _():
        dstate[...] = jnp.zeros_like(dstate)

    @pl.when(pl.program_id(0) == 0)
    def _():
        dcols_ref[...] = jnp.zeros_like(dcols_ref)

    rows_each = r_ref.shape[0]
    chunks = rows_each // CHUNK
    pairs = r_ref.shape[1] // PAIR
    ones_mask = head_ones()
    ones_op = jnp.where(ones_mask, 1.0, 0.0).astype(jnp.bfloat16)
    row = iota((CHUNK, CHUNK), 0)
    col = iota((CHUNK, CHUNK), 1)
    tri_op = jnp.where(row >= col, 1.0, 0.0).astype(jnp.bfloat16)
    suffix_op = jnp.where(row <= col, 1.0, 0.0).astype(jnp.bfloat16)
    prefix_op = jnp.where(row > col, 1.0, 0.0).astype(jnp.bfloat16)
    sums_op = jnp.concatenate([suffix_op, prefix_op], axis=1)
    strict, within = tri_masks()

    def add_col(index, lanes, values):
        part = values[0:8]
        for start in range(8, CHUNK, 8):
            part = part + values[start : start + 8]
        dcols_ref[index, :, lanes] += part

    strict_two = jnp.concatenate([strict, strict], axis=1)
    within_two = jnp.concatenate([within, within], axis=1)
    all_masks = jnp.concatenate([strict_two, within_two], axis=0)
    units = [(chunk, pair) for chunk in reversed(range(chunks)) for pair in range(pairs)]
    mean_of = 1.0 / SUBSPACE_SIZE
    known = []
    for chunk, pair in units:
        rows = slice(chunk * CHUNK, (chunk + 1) * CHUNK)
        lanes = slice(pair * PAIR, (pair + 1) * PAIR)
        live = within_seq * rows_each + chunk * CHUNK + iota((CHUNK, PAIR), 0) < length
        cols = cols_ref[:, lanes]
        got = prepare(
            r_ref[rows, lanes],
            k_ref[rows, lanes],
            dw_ref[rows, lanes],
            da_ref[rows, lanes],
            cols,
            live,
            tri_op,
            ones_op,
        )
        got.update(rows=rows, lanes=lanes, live=live, cols=cols, pair=pair, chunk=chunk)
        known.append(got)
    for got in known:
        y = y_ref[got["rows"], got["lanes"]]
        got["centred"] = y - head_sum(y, ones_op) * mean_of
    for got in known:
        spread = head_sum(got["centred"] * got["centred"], ones_op) * mean_of
        got["inv_y"] = lax.rsqrt(spread + group_eps)
    for got in known:
        rows, lanes, cols = got["rows"], got["lanes"], got["cols"]
        r, v, dz = r_ref[rows, lanes], v_ref[rows, lanes], dz_ref[rows, lanes]
        normed = got["centred"] * got["inv_y"]
        got["bonus"] = head_sum(r * got["lagged"] * cols[4:5], ones_op)
        mixed = normed * cols[5:6] + cols[6:7] + got["bonus"] * v
        dgate_ref[rows, lanes] = low(dz * mixed)
        dmix = dz * gate_ref[rows, lanes]
        add_col(5, lanes, dmix * normed)
        add_col(6, lanes, dmix)
        dnormed = dmix * cols[5:6]
        got["dbonus"] = head_sum(dmix * v, ones_op)
        mean_grad = head_sum(dnormed, ones_op) * mean_of
        mean_prod = head_sum(dnormed * normed, ones_op) * mean_of
        got["dy_low"], got["dy_rest"] = halves(got["inv_y"] * (dnormed - mean_grad - normed * mean_prod))
        got["dv"] = got["bonus"] * dmix
    for got in known:
        rows, lanes = got["rows"], got["lanes"]
        got["both"] = jnp.concatenate([got["remove_hat"], got["read_hat"]], axis=0)
        got["past"] = jnp.concatenate(
            [stack_heads(got["write_hat"]), stack_heads(got["key_hat"])], axis=0
        )
        got["lower_key"] = lk_ref[rows, lanes]
        reads = reads_ref[rows, slice(2 * lanes.start, 2 * lanes.stop)]
        got["from_y"] = dot_tn(reads, got["dy_low"])
        v_low = low(v_ref[rows, lanes])
        removed = u_ref[rows, lanes]
        got["sent"] = jnp.concatenate([removed, v_low], axis=0)
        got["stacks"] = jnp.concatenate([stack_heads(removed), stack_heads(v_low)], axis=0)
    for chunk in reversed(range(chunks)):
        group = [got for got in known if got["chunk"] == chunk]
        for got in group:
            got["later"] = dstate[got["pair"]]
            got["later_low"], got["later_rest"] = halves(got["later"])
            ends = jnp.concatenate([got["write_end"], got["key_end"]], axis=0)
            got["from_later"] = dot_nt(ends, got["later_low"])
        for got in group:
            dremoved = low(got["from_later"][:CHUNK] + fold_heads(got["from_y"][:PAIR]))
            got["dright"] = low(fold_heads(dot_tn(t_ref[got["rows"], got["lanes"]], dremoved)))
        for got in group:
            got["douts"] = jnp.concatenate([got["dright"], got["dy_low"]], axis=0)
            adds = dot_tn(got["douts"], got["both"]) + dot_tn(got["dy_rest"], got["read_hat"])
            adds = jnp.where(ones_mask, adds, 0.0)
            dstate[got["pair"]] = got["later"] * got["final"] + adds
    for got in known:
        dv = got["dv"] + got["from_later"][CHUNK:] + fold_heads(got["from_y"][PAIR:])
        dv = dv + fold_heads(dot_tn(got["lower_key"], got["dright"]))
        dv_ref[got["rows"], got["lanes"]] = low(dv)
        dscores = dot_nt(got["douts"], got["stacks"])
        fine = dscores[CHUNK:] + dot_nt(got["dy_rest"], got["stacks"])
        dscores = low(jnp.where(all_masks, jnp.concatenate([dscores[:CHUNK], fine], axis=0), 0.0))
        old_wide = s_ref[got["chunk"], got["pair"]]
        old_low, old_rest = halves(old_wide)
        from_old = dot_nn(got["douts"], old_low)
        fine = from_old[CHUNK:] + (dot_nn(got["dy_rest"], old_low) + dot_nn(got["dy_low"], old_rest))
        got["dboth"] = jnp.concatenate([from_old[:CHUNK], fine], axis=0) + dot_nn(dscores, got["past"])
        dpast = dot_tn(dscores, got["both"])
        got["dwrite_hat"] = fold_heads(dpast[:PAIR])
        got["dkey_hat"] = fold_heads(dpast[PAIR:])
        got["dends"] = dot_nn(got["sent"], got["later_low"]) + dot_nn(got["sent"], got["later_rest"])
        got["dfinal"] = jnp.sum(got["later"] * old_wide, axis=0, keepdims=True)
    for got in known:
        rows, lanes, cols, live = got["rows"], got["lanes"], got["cols"], got["live"]

        def wide(name):
            return got[name].astype(jnp.float32)

        r, k = r_ref[rows, lanes], k_ref[rows, lanes]
        dwrite_hat, dkey_hat = got["dwrite_hat"], got["dkey_hat"]
        dwrite_end, dkey_end = got["dends"][:CHUNK], got["dends"][CHUNK:]
        dremove_hat, dread_hat = got["dboth"][:CHUNK], got["dboth"][CHUNK:]
        dbonus, lagged = got["dbonus"], got["lagged"]
        bonus_lag = dbonus * lagged
        add_col(4, lanes, bonus_lag * r)
        dr_ref[rows, lanes] = low(bonus_lag * cols[4:5] + dread_hat * got["grown"])
        minus = wide("remove_hat") * dremove_hat
        plus = wide("read_hat") * dread_hat + minus
        plus = plus - wide("write_hat") * dwrite_hat - wide("key_hat") * dkey_hat
        ending = wide("write_end") * dwrite_end + wide("key_end") * dkey_end
        sums = split_dot(sums_op, jnp.concatenate([plus, ending], axis=0))
        dlog = sums - minus + got["final"] * got["dfinal"]
        ddw = jnp.where(live, dlog * got["full_log"] * (1.0 - got["sw"]), 0.0)
        add_col(0, lanes, ddw)
        ddw_ref[rows, lanes] = low(ddw)
        dwrite = dwrite_hat * got["shrunk"] + dwrite_end * got["til_end"]
        dlag = dbonus * r * cols[4:5] + dkey_hat * got["shrunk"] + dkey_end * got["til_end"]
        dlag = jnp.where(live, dlag, 0.0)
        rate = got["rate"]
        dunit = jnp.where(live, dwrite * rate - dremove_hat * got["before"], 0.0)
        lag_k = dlag * k
        drate = dwrite * got["unit_live"] + lag_k * cols[3:4]
        add_col(3, lanes, lag_k * (rate - 1.0))
        dscaled = got["inv"] * (dunit - got["unit"] * head_sum(dunit * got["unit"], ones_op))
        add_col(2, lanes, dscaled * k)
        dk_ref[rows, lanes] = low(dlag * got["lag_scale"] + dscaled * cols[2:3])
        dda = drate * rate * (1.0 - rate)
        add_col(1, lanes, dda)
        dda_ref[rows, lanes] = low(dda)


def run_mixer_forward(lengths, r, k, v, dw, da, gate, cols):
    positions, part_width = r.shape
    rows_each = CHUNKS_FWD * CHUNK
    steps = positions // rows_each
    steps_per_seq = SEQ_LEN // rows_each
    pairs = part_width // PAIR
    wide = pl.BlockSpec((rows_each, part_width), lambda i: (i, 0))
    shape = jax.ShapeDtypeStruct
    return pl.pallas_call(
        partial(mixer_forward, steps_per_seq),
        grid=(steps,),
        in_specs=[pl.BlockSpec(memory_space=pltpu.SMEM)]
        + [wide] * 6
        + [pl.BlockSpec((8, part_width), lambda i: (0, 0))],
        out_specs=[wide] * 4
        + [
            pl.BlockSpec((CHUNKS_FWD, pairs, PAIR, PAIR), lambda i: (i, 0, 0, 0)),
            wide,
            pl.BlockSpec((rows_each, 2 * part_width), lambda i: (i, 0)),
        ],
        out_shape=[
            shape((positions, part_width), jnp.bfloat16),
            shape((positions, part_width), jnp.float32),
            shape((positions, part_width), jnp.bfloat16),
            shape((positions, part_width), jnp.bfloat16),
            shape((positions // CHUNK, pairs, PAIR, PAIR), jnp.float32),
            shape((positions, part_width), jnp.bfloat16),
            shape((positions, 2 * part_width), jnp.bfloat16),
        ],
        scratch_shapes=[pltpu.VMEM((pairs, PAIR, PAIR), jnp.float32)],
        compiler_params=pltpu.CompilerParams(
            dimension_semantics=("arbitrary",), vmem_limit_bytes=40 * 1024 * 1024
        ),
        name="mixer_forward",
    )(lengths, r, k, v, dw, da, gate, cols)


def run_mixer_backward(lengths, r, k, v, dw, da, gate, cols, y, t, u, s, lk, reads, dz):
    positions, part_width = r.shape
    rows_each = CHUNKS_BWD * CHUNK
    steps = positions // rows_each
    steps_per_seq = SEQ_LEN // rows_each
    pairs = part_width // PAIR
    wide = pl.BlockSpec((rows_each, part_width), lambda i: (steps - 1 - i, 0))
    shape = jax.ShapeDtypeStruct
    return pl.pallas_call(
        partial(mixer_backward, steps_per_seq),
        grid=(steps,),
        in_specs=[pl.BlockSpec(memory_space=pltpu.SMEM)]
        + [wide] * 6
        + [pl.BlockSpec((8, part_width), lambda i: (0, 0))]
        + [wide] * 3
        + [
            pl.BlockSpec((CHUNKS_BWD, pairs, PAIR, PAIR), lambda i: (steps - 1 - i, 0, 0, 0)),
            wide,
            pl.BlockSpec((rows_each, 2 * part_width), lambda i: (steps - 1 - i, 0)),
            wide,
        ],
        out_specs=[wide] * 6 + [pl.BlockSpec((8, 8, part_width), lambda i: (0, 0, 0))],
        out_shape=[shape((positions, part_width), jnp.bfloat16)] * 6
        + [shape((8, 8, part_width), jnp.float32)],
        scratch_shapes=[pltpu.VMEM((pairs, PAIR, PAIR), jnp.float32)],
        compiler_params=pltpu.CompilerParams(
            dimension_semantics=("arbitrary",), vmem_limit_bytes=40 * 1024 * 1024
        ),
        name="mixer_backward",
    )(lengths, r, k, v, dw, da, gate, cols, y, t, u, s, lk, reads, dz)


LINE = "mp"
END_LAG = 4
MID_LAG = 2


def link_cost(elements):
    return elements * 2 * 2 * 40


def line_barrier(size):
    me = lax.axis_index(LINE)
    barrier = pltpu.get_barrier_semaphore()

    @pl.when(me > 0)
    def _():
        pl.semaphore_signal(barrier, inc=1, device_id={LINE: me - 1}, device_id_type=pl.DeviceIdType.MESH)

    @pl.when(me < size - 1)
    def _():
        pl.semaphore_signal(barrier, inc=1, device_id={LINE: me + 1}, device_id_type=pl.DeviceIdType.MESH)

    ends = jnp.where((me == 0) | (me == size - 1), 1, 2)
    pl.semaphore_wait(barrier, ends)


class Flow:
    def __init__(self, size, side):
        self.size = size
        self.side = side
        self.me = lax.axis_index(LINE)
        self.step = 1 - 2 * side
        self.target = self.me + self.step
        source = self.me - self.step
        self.has_source = (source >= 0) & (source < size)
        self.has_target = (self.target >= 0) & (self.target < size)

    def copy(self, source, place, send_sem, recv_sem):
        return pltpu.make_async_remote_copy(
            src_ref=source,
            dst_ref=place,
            send_sem=send_sem,
            recv_sem=recv_sem,
            device_id={LINE: self.target},
            device_id_type=pl.DeviceIdType.MESH,
        )


def two_flows(size):
    me = lax.axis_index(LINE)
    near = jnp.where(me < size // 2, 0, 1)
    return Flow(size, near), Flow(size, 1 - near)


def line_sum_kernel(size, chunk_rows, x_ref, out_ref, got, sent, send_sem, recv_sem):
    line_barrier(size)
    me = lax.axis_index(LINE)
    flows = two_flows(size)
    chunks = x_ref.shape[0] // chunk_rows

    def copy_of(flow, chunk, source):
        rows = pl.ds(pl.multiple_of(chunk * chunk_rows, chunk_rows), chunk_rows)
        return flow.copy(
            source.at[rows], got.at[flow.side, rows], send_sem.at[flow.side, chunk], recv_sem.at[flow.side, chunk]
        )

    def pass_on(flow, chunk):
        rows = pl.ds(pl.multiple_of(chunk * chunk_rows, chunk_rows), chunk_rows)

        @pl.when(flow.has_source)
        def _():
            copy_of(flow, chunk, x_ref).wait_recv()

        @pl.when(flow.has_source & flow.has_target)
        def _():
            total = got[flow.side, rows].astype(jnp.float32) + x_ref[rows].astype(jnp.float32)
            sent[flow.side, rows] = total.astype(sent.dtype)
            copy_of(flow, chunk, sent.at[flow.side]).start()

        @pl.when(jnp.logical_not(flow.has_source))
        def _():
            copy_of(flow, chunk, x_ref).start()

    is_end = (me == 0) | (me == size - 1)
    lag = jnp.where(is_end, END_LAG, MID_LAG)

    def step(turn, carry):
        @pl.when(turn < chunks)
        def _():
            pass_on(flows[0], turn)

        chunk = turn - lag

        @pl.when((chunk >= 0) & (chunk < chunks))
        def _():
            pass_on(flows[1], chunk)
            rows = pl.ds(pl.multiple_of(chunk * chunk_rows, chunk_rows), chunk_rows)

            @pl.when(is_end)
            def _():
                other = got[flows[1].side, rows].astype(jnp.float32)
                out_ref[rows] = (other + x_ref[rows].astype(jnp.float32)).astype(out_ref.dtype)

            @pl.when(jnp.logical_not(is_end))
            def _():
                other = got[0, rows].astype(jnp.float32) + got[1, rows].astype(jnp.float32)
                out_ref[rows] = (other + x_ref[rows].astype(jnp.float32)).astype(out_ref.dtype)

        return carry

    lax.fori_loop(0, chunks + END_LAG, step, 0)

    def drain(chunk, carry):
        for flow in flows:

            @pl.when(flow.has_target)
            def _():
                copy_of(flow, chunk, x_ref).wait_send()

        return carry

    lax.fori_loop(0, chunks, drain, 0)


def line_sum(x, size, collective_id, chunk_rows=64):
    rows, cols = x.shape
    chunks = rows // chunk_rows
    return pl.pallas_call(
        partial(line_sum_kernel, size, chunk_rows),
        out_shape=jax.ShapeDtypeStruct(x.shape, x.dtype),
        in_specs=[pl.BlockSpec(memory_space=pltpu.VMEM)],
        out_specs=pl.BlockSpec(memory_space=pltpu.VMEM),
        scratch_shapes=[
            pltpu.VMEM((2, rows, cols), x.dtype),
            pltpu.VMEM((2, rows, cols), x.dtype),
            pltpu.SemaphoreType.DMA((2, chunks)),
            pltpu.SemaphoreType.DMA((2, chunks)),
        ],
        compiler_params=pltpu.CompilerParams(
            collective_id=collective_id, has_side_effects=True, vmem_limit_bytes=48 * 1024 * 1024
        ),
        cost_estimate=pl.CostEstimate(flops=0, bytes_accessed=link_cost(rows * cols), transcendentals=0),
        name="line_sum",
    )(x)


def line_gather_kernel(size, chunk_rows, x_ref, out_ref, send_sem, recv_sem):
    line_barrier(size)
    me = lax.axis_index(LINE)
    flows = two_flows(size)
    width = x_ref.shape[1]
    chunks = x_ref.shape[0] // chunk_rows

    def place(block, chunk):
        rows = pl.ds(pl.multiple_of(chunk * chunk_rows, chunk_rows), chunk_rows)
        return out_ref.at[rows, pl.ds(pl.multiple_of(block * width, width), width)]

    def copy_of(flow, block, chunk):
        return flow.copy(
            place(block, chunk), place(block, chunk), send_sem.at[flow.side, block, chunk], recv_sem.at[flow.side, block, chunk]
        )

    def step(chunk, carry):
        rows = pl.ds(pl.multiple_of(chunk * chunk_rows, chunk_rows), chunk_rows)
        out_ref[rows, pl.ds(pl.multiple_of(me * width, width), width)] = x_ref[rows]
        for flow in flows:

            @pl.when(flow.has_target)
            def _():
                copy_of(flow, me, chunk).start()

        return carry

    lax.fori_loop(0, chunks, step, 0)
    for hop in range(1, size):

        def forward(chunk, carry):
            for flow in flows:
                block = me - hop * flow.step
                exists = (block >= 0) & (block < size)

                @pl.when(exists)
                def _():
                    copy_of(flow, block, chunk).wait_recv()

                @pl.when(exists & flow.has_target)
                def _():
                    copy_of(flow, block, chunk).start()

            return carry

        lax.fori_loop(0, chunks, forward, 0)
    for hop in range(size):

        def drain(chunk, carry):
            for flow in flows:
                block = me - hop * flow.step
                exists = (block >= 0) & (block < size)

                @pl.when(exists & flow.has_target)
                def _():
                    copy_of(flow, block, chunk).wait_send()

            return carry

        lax.fori_loop(0, chunks, drain, 0)


def line_gather(x, size, collective_id, chunk_rows=256):
    rows, cols = x.shape
    chunks = rows // chunk_rows
    return pl.pallas_call(
        partial(line_gather_kernel, size, chunk_rows),
        out_shape=jax.ShapeDtypeStruct((rows, size * cols), x.dtype),
        in_specs=[pl.BlockSpec(memory_space=pltpu.VMEM)],
        out_specs=pl.BlockSpec(memory_space=pltpu.VMEM),
        scratch_shapes=[
            pltpu.SemaphoreType.DMA((2, size, chunks)),
            pltpu.SemaphoreType.DMA((2, size, chunks)),
        ],
        compiler_params=pltpu.CompilerParams(
            collective_id=collective_id, has_side_effects=True, vmem_limit_bytes=48 * 1024 * 1024
        ),
        cost_estimate=pl.CostEstimate(flops=0, bytes_accessed=link_cost(3 * rows * cols), transcendentals=0),
        name="line_gather",
    )(x)


def line_scatter_kernel(size, chunk_rows, x_ref, out_ref, got, sent, send_sem, recv_sem):
    line_barrier(size)
    me = lax.axis_index(LINE)
    flows = two_flows(size)
    width = out_ref.shape[1]
    chunks = x_ref.shape[0] // chunk_rows

    def rows_of(chunk):
        return pl.ds(pl.multiple_of(chunk * chunk_rows, chunk_rows), chunk_rows)

    def cols_of(block):
        return pl.ds(pl.multiple_of(block * width, width), width)

    def copy_of(flow, block, chunk, source):
        return flow.copy(
            source,
            got.at[flow.side, rows_of(chunk), cols_of(block)],
            send_sem.at[flow.side, block, chunk],
            recv_sem.at[flow.side, block, chunk],
        )

    def own(block, chunk):
        return x_ref[rows_of(chunk), cols_of(block)].astype(jnp.float32)

    for hop in range(size - 1):

        def forward(chunk, carry):
            for flow in flows:
                block = jnp.where(flow.side == 0, size - 1 - hop, hop)
                ahead = (block - me) * flow.step > 0

                @pl.when(ahead & flow.has_source)
                def _():
                    source = x_ref.at[rows_of(chunk), cols_of(block)]
                    copy_of(flow, block, chunk, source).wait_recv()
                    total = got[flow.side, rows_of(chunk), cols_of(block)].astype(jnp.float32) + own(block, chunk)
                    sent[flow.side, rows_of(chunk), cols_of(block)] = total.astype(sent.dtype)
                    copy_of(flow, block, chunk, sent.at[flow.side, rows_of(chunk), cols_of(block)]).start()

                @pl.when(ahead & jnp.logical_not(flow.has_source))
                def _():
                    copy_of(flow, block, chunk, x_ref.at[rows_of(chunk), cols_of(block)]).start()

            return carry

        lax.fori_loop(0, chunks, forward, 0)

    def finish(chunk, carry):
        rows = rows_of(chunk)
        for flow in flows:

            @pl.when(flow.has_source)
            def _():
                copy_of(flow, me, chunk, x_ref.at[rows, cols_of(me)]).wait_recv()

        @pl.when(me == 0)
        def _():
            out_ref[rows] = (got[1, rows, cols_of(me)].astype(jnp.float32) + own(me, chunk)).astype(out_ref.dtype)

        @pl.when(me == size - 1)
        def _():
            out_ref[rows] = (got[0, rows, cols_of(me)].astype(jnp.float32) + own(me, chunk)).astype(out_ref.dtype)

        @pl.when((me > 0) & (me < size - 1))
        def _():
            other = got[0, rows, cols_of(me)].astype(jnp.float32) + got[1, rows, cols_of(me)].astype(jnp.float32)
            out_ref[rows] = (other + own(me, chunk)).astype(out_ref.dtype)

        return carry

    lax.fori_loop(0, chunks, finish, 0)
    for hop in range(size - 1):

        def drain(chunk, carry):
            for flow in flows:
                block = jnp.where(flow.side == 0, size - 1 - hop, hop)
                ahead = (block - me) * flow.step > 0

                @pl.when(ahead)
                def _():
                    copy_of(flow, block, chunk, x_ref.at[rows_of(chunk), cols_of(block)]).wait_send()

            return carry

        lax.fori_loop(0, chunks, drain, 0)


def line_scatter(x, size, collective_id, out_dtype=jnp.float32, chunk_rows=256):
    rows, cols = x.shape
    chunks = rows // chunk_rows
    return pl.pallas_call(
        partial(line_scatter_kernel, size, chunk_rows),
        out_shape=jax.ShapeDtypeStruct((rows, cols // size), out_dtype),
        in_specs=[pl.BlockSpec(memory_space=pltpu.VMEM)],
        out_specs=pl.BlockSpec(memory_space=pltpu.VMEM),
        scratch_shapes=[
            pltpu.VMEM((2, rows, cols), x.dtype),
            pltpu.VMEM((2, rows, cols), x.dtype),
            pltpu.SemaphoreType.DMA((2, size, chunks)),
            pltpu.SemaphoreType.DMA((2, size, chunks)),
        ],
        compiler_params=pltpu.CompilerParams(
            collective_id=collective_id, has_side_effects=True, vmem_limit_bytes=48 * 1024 * 1024
        ),
        cost_estimate=pl.CostEstimate(flops=0, bytes_accessed=link_cost(3 * rows * cols // size), transcendentals=0),
        name="line_scatter",
    )(x)


def matmul(left_op, right_op):
    return jnp.dot(left_op, right_op, preferred_element_type=jnp.float32)


def contract_rows(left_op, right_op):
    return jnp.einsum("tk,tn->kn", left_op, right_op, preferred_element_type=jnp.float32)


def against(grad_op, weight_op):
    return jnp.einsum("tn,kn->tk", grad_op, weight_op, preferred_element_type=jnp.float32)


def layer_norm(values, scale_in, offset):
    centre = jnp.mean(values, axis=-1, keepdims=True)
    centred = values - centre
    spread = jnp.mean(centred * centred, axis=-1, keepdims=True)
    return centred * lax.rsqrt(spread + norm_eps) * scale_in + offset


def shifted(values):
    grid_view = values.reshape(values.shape[0] // SEQ_LEN, SEQ_LEN, values.shape[1])
    earlier = jnp.concatenate([jnp.zeros_like(grid_view[:, :1]), grid_view[:, :-1]], axis=1)
    return earlier.reshape(values.shape)


def section_in(hidden, scale_in, offset, mix_rates):
    standardized_source = layer_norm(hidden, scale_in, offset)
    shift_diff = shifted(standardized_source) - standardized_source
    return tuple((standardized_source + shift_diff * mix_rates[:, column] for column in range(6)))


def section_out(residual, scale_in, offset, mix_rate):
    standardized_source = layer_norm(residual, scale_in, offset)
    return standardized_source + (shifted(standardized_source) - standardized_source) * mix_rate


def body(
    hidden,
    teacher,
    lengths,
    feature_params,
    decay_down,
    rate_down,
    gate_down,
    decay_up,
    rate_up,
    gate_up,
    receptance,
    key_proj,
    value_proj,
    output_proj,
    ffn_key,
    ffn_value,
):
    position_count, part_width = hidden.shape
    seq_dev = position_count // SEQ_LEN
    mp_index = lax.axis_index("mp")
    col_start = mp_index * part_width
    quarter = position_count // lax.axis_size("mp")
    row_start = mp_index * quarter
    own_lengths = lax.dynamic_slice_in_dim(lengths, lax.axis_index("dp") * seq_dev, seq_dev)
    places = jnp.arange(SEQ_LEN, dtype=jnp.int32)
    valid = (places[None, :] < own_lengths[:, None]).astype(jnp.float32).reshape(position_count)
    loss_scale = position_count * lax.axis_size("dp") / jnp.sum(lengths).astype(jnp.float32)
    line_size = lax.axis_size("mp")
    whole = line_gather(hidden, line_size, 1).astype(jnp.float32)
    low_rank = (decay_down.shape[1], rate_down.shape[1], gate_down.shape[1])
    narrow = jnp.concatenate([decay_down, rate_down, gate_down, feature_params], axis=1)
    narrow = jnp.pad(narrow, ((0, 0), (0, -narrow.shape[1] % 128)))
    narrow_w = lax.all_gather(narrow, "mp", axis=0, tiled=True)
    narrow_w = lax.all_gather(narrow_w, "dp", axis=0, tiled=True)
    decay_down_w = narrow_w[:, : low_rank[0]]
    rate_down_w = narrow_w[:, low_rank[0] : low_rank[0] + low_rank[1]]
    gate_down_w = narrow_w[:, low_rank[0] + low_rank[1] : sum(low_rank)]
    params_low = narrow_w[:, sum(low_rank) : sum(low_rank) + feature_params.shape[1]]
    three = lax.all_gather(
        jnp.concatenate([receptance, key_proj, value_proj], axis=1), "dp", axis=0, tiled=True
    )
    recept_w = three[:, :part_width]
    key_w = three[:, part_width : 2 * part_width]
    value_w = three[:, 2 * part_width :]
    up_rows = (decay_up.shape[0], rate_up.shape[0], gate_up.shape[0])
    ups = lax.all_gather(jnp.concatenate([decay_up, rate_up, gate_up], axis=0), "dp", axis=0)
    decay_up_w = ups[:, : up_rows[0]].reshape(-1, part_width)
    rate_up_w = ups[:, up_rows[0] : up_rows[0] + up_rows[1]].reshape(-1, part_width)
    gate_up_w = ups[:, up_rows[0] + up_rows[1] :].reshape(-1, part_width)
    output_w = lax.all_gather(output_proj, "dp", axis=1, tiled=True)
    ffn_key_w = lax.all_gather(ffn_key, "dp", axis=0, tiled=True)
    ffn_value_w = lax.all_gather(ffn_value, "dp", axis=1, tiled=True)
    params = params_low.astype(jnp.float32)
    model_width = whole.shape[1]
    mixed, back_in = jax.vjp(section_in, whole, params[:, 0], params[:, 1], params[:, 2:8])
    mix_r, mix_w, mix_k, mix_v, mix_a, mix_g = tuple(
        (member.astype(jnp.bfloat16) for member in mixed)
    )
    acceptance_matrix = matmul(mix_r, recept_w)
    keys_in = matmul(mix_k, key_w)
    payload_source = matmul(mix_v, value_w)
    decay_hid = jnp.tanh(matmul(mix_w, decay_down_w))
    decay_low = decay_hid.astype(jnp.bfloat16)
    rate_low = matmul(mix_a, rate_down_w).astype(jnp.bfloat16)
    gate_hid = jax.nn.sigmoid(matmul(mix_g, gate_down_w))
    gate_low = gate_hid.astype(jnp.bfloat16)
    decay_in = matmul(decay_low, decay_up_w)
    rate_in = matmul(rate_low, rate_up_w)
    sigmoid_source = matmul(gate_low, gate_up_w)
    columns = lax.dynamic_slice_in_dim(params, col_start, part_width, 0)[:, 8:15].T
    columns = jnp.pad(columns, ((0, 1), (0, 0)))
    mixer_args = (
        own_lengths,
        acceptance_matrix,
        keys_in,
        payload_source,
        decay_in,
        rate_in,
        sigmoid_source,
        columns,
    )
    gated_low, *kept = run_mixer_forward(*mixer_args)
    residual = whole + line_sum(matmul(gated_low, output_w).astype(jnp.bfloat16), line_size, 2).astype(
        jnp.float32
    )
    ffn_in, back_out = jax.vjp(section_out, residual, params[:, 15], params[:, 16], params[:, 17])
    ffn_low = ffn_in.astype(jnp.bfloat16)
    pre_act = matmul(ffn_low, ffn_key_w)
    active = jnp.maximum(pre_act, 0.0)
    squared = (active * active).astype(jnp.bfloat16)
    ffn_part = line_scatter(matmul(squared, ffn_value_w).astype(jnp.bfloat16), line_size, 3)
    result = lax.dynamic_slice_in_dim(residual, col_start, part_width, 1) + ffn_part
    grad_result = loss_scale * valid[:, None] * (result - teacher.astype(jnp.float32))
    grad_low = line_gather(grad_result.astype(jnp.bfloat16), line_size, 4)
    grad_ffn_value = contract_rows(squared, grad_low).astype(jnp.bfloat16)
    grad_low, grad_ffn_value = lax.optimization_barrier((grad_low, grad_ffn_value))
    grad_ffn_value = lax.psum_scatter(grad_ffn_value, "dp", scatter_dimension=1, tiled=True)
    grad_squared = against(grad_low, ffn_value_w)
    grad_pre = (grad_squared * 2.0 * active).astype(jnp.bfloat16)
    grad_ffn_key = contract_rows(ffn_low, grad_pre).astype(jnp.bfloat16)
    grad_pre, grad_ffn_key = lax.optimization_barrier((grad_pre, grad_ffn_key))
    grad_ffn_key = lax.psum_scatter(grad_ffn_key, "dp", scatter_dimension=0, tiled=True)
    d_resid_part, d_scale_two, d_offset_two, d_mix_two = back_out(against(grad_pre, ffn_key_w))
    d_residual = grad_low.astype(jnp.float32) + line_sum(
        d_resid_part.astype(jnp.bfloat16), line_size, 5
    ).astype(jnp.float32)
    d_low = d_residual.astype(jnp.bfloat16)
    grad_output_proj = contract_rows(gated_low, d_low).astype(jnp.bfloat16)
    d_low, grad_output_proj = lax.optimization_barrier((d_low, grad_output_proj))
    grad_output_proj = lax.psum_scatter(grad_output_proj, "dp", scatter_dimension=1, tiled=True)
    d_gated = against(d_low, output_w)
    d_gated, grad_ffn_value = lax.optimization_barrier((d_gated, grad_ffn_value))
    d_recept, d_keys, d_values, d_decay, d_rate, d_gate, d_columns = run_mixer_backward(
        *mixer_args, *kept, d_gated
    )
    d_columns = jnp.sum(d_columns, axis=1)[:7].T
    grad_three = jnp.concatenate(
        [
            contract_rows(mix_r, d_recept).astype(jnp.bfloat16),
            contract_rows(mix_k, d_keys).astype(jnp.bfloat16),
            contract_rows(mix_v, d_values).astype(jnp.bfloat16),
        ],
        axis=1,
    )
    d_recept, d_keys, d_values, grad_three = lax.optimization_barrier(
        (d_recept, d_keys, d_values, grad_three)
    )
    grad_three = lax.psum_scatter(grad_three, "dp", scatter_dimension=0, tiled=True)
    grad_decay_up = contract_rows(decay_low, d_decay)
    grad_rate_up = contract_rows(rate_low, d_rate)
    grad_gate_up = contract_rows(gate_low, d_gate)
    d_inner = jnp.concatenate(
        [against(d_decay, decay_up_w), against(d_rate, rate_up_w), against(d_gate, gate_up_w)], axis=1
    ).astype(jnp.bfloat16)
    d_inner = jnp.pad(d_inner, ((0, 0), (0, -d_inner.shape[1] % 128)))
    d_inner = line_sum(d_inner, line_size, 6)
    d_inner, grad_ffn_key = lax.optimization_barrier((d_inner, grad_ffn_key))
    d_inner = d_inner.astype(jnp.float32)
    d_decay_hid = d_inner[:, : low_rank[0]]
    d_rate_hid = d_inner[:, low_rank[0] : low_rank[0] + low_rank[1]]
    d_gate_hid = d_inner[:, low_rank[0] + low_rank[1] : sum(low_rank)]
    d_decay_pre = (d_decay_hid * (1.0 - decay_hid * decay_hid)).astype(jnp.bfloat16)
    d_rate_pre = d_rate_hid.astype(jnp.bfloat16)
    d_gate_pre = (d_gate_hid * gate_hid * (1.0 - gate_hid)).astype(jnp.bfloat16)

    def own_rows(values):
        return lax.dynamic_slice_in_dim(values, row_start, quarter, 0)

    def place_rows(values):
        return lax.dynamic_update_slice_in_dim(
            jnp.zeros((position_count, values.shape[1]), jnp.float32), values, row_start, 0
        )

    groups = lax.axis_size("dp")
    row_block = decay_down.shape[0]

    def own_features(values):
        split = values.reshape(position_count, groups, lax.axis_size("mp"), row_block)
        taken = lax.dynamic_index_in_dim(split, mp_index, 2, keepdims=False)
        return taken.reshape(position_count, groups * row_block)

    grad_downs = jnp.concatenate(
        [
            contract_rows(own_features(mix_w), d_decay_pre),
            contract_rows(own_features(mix_a), d_rate_pre),
            contract_rows(own_features(mix_g), d_gate_pre),
        ],
        axis=1,
    )
    cotangents = (
        against(d_recept, recept_w),
        place_rows(against(own_rows(d_decay_pre), decay_down_w)),
        against(d_keys, key_w),
        against(d_values, value_w),
        place_rows(against(own_rows(d_rate_pre), rate_down_w)),
        place_rows(against(own_rows(d_gate_pre), gate_down_w)),
    )
    d_in_part, d_scale_one, d_offset_one, d_mix_one = back_in(cotangents)
    d_in_part, grad_output_proj = lax.optimization_barrier((d_in_part.astype(jnp.bfloat16), grad_output_proj))
    grad_hidden = lax.dynamic_slice_in_dim(d_residual, col_start, part_width, 1) + line_scatter(
        d_in_part, line_size, 7
    )
    core_grads = lax.dynamic_update_slice_in_dim(
        jnp.zeros((model_width, 7), jnp.float32), d_columns, col_start, 0
    )
    grad_params = jnp.concatenate(
        [
            d_scale_one[:, None],
            d_offset_one[:, None],
            d_mix_one,
            core_grads,
            d_scale_two[:, None],
            d_offset_two[:, None],
            d_mix_two[:, None],
        ],
        axis=1,
    )
    param_parts = grad_params.reshape(groups, lax.axis_size("mp"), row_block, grad_params.shape[1])
    param_parts = lax.psum_scatter(
        param_parts.transpose(1, 0, 2, 3), "mp", scatter_dimension=0, tiled=True
    ).reshape(model_width // lax.axis_size("mp"), grad_params.shape[1])
    narrow_grads = lax.psum_scatter(
        jnp.concatenate([grad_downs, param_parts], axis=1), "dp", scatter_dimension=0, tiled=True
    )
    up_grads = jnp.concatenate(
        [member.reshape(groups, -1, part_width) for member in (grad_decay_up, grad_rate_up, grad_gate_up)],
        axis=1,
    ).astype(jnp.bfloat16)
    up_grads = lax.psum_scatter(up_grads, "dp", scatter_dimension=0, tiled=True)
    up_grads = up_grads.reshape(-1, part_width).astype(jnp.float32)
    first, second = low_rank[0], low_rank[0] + low_rank[1]
    return (
        result.astype(jnp.bfloat16),
        grad_hidden,
        narrow_grads[:, sum(low_rank) :],
        narrow_grads[:, :first],
        narrow_grads[:, first:second],
        narrow_grads[:, second : sum(low_rank)],
        up_grads[: up_rows[0]],
        up_grads[up_rows[0] : up_rows[0] + up_rows[1]],
        up_grads[up_rows[0] + up_rows[1] :],
        grad_three[:, :part_width].astype(jnp.float32),
        grad_three[:, part_width : 2 * part_width].astype(jnp.float32),
        grad_three[:, 2 * part_width :].astype(jnp.float32),
        grad_output_proj.astype(jnp.float32),
        grad_ffn_key.astype(jnp.float32),
        grad_ffn_value.astype(jnp.float32),
    )


def solution(mesh):
    in_specs = (
        P("dp", "mp"),
        P("dp", "mp"),
        P(),
        P(("dp", "mp"), None),
        P(("dp", "mp"), None),
        P(("dp", "mp"), None),
        P(("dp", "mp"), None),
        P("dp", "mp"),
        P("dp", "mp"),
        P("dp", "mp"),
        P("dp", "mp"),
        P("dp", "mp"),
        P("dp", "mp"),
        P("mp", "dp"),
        P("dp", "mp"),
        P("mp", "dp"),
    )
    out_specs = (
        P("dp", "mp"),
        P("dp", "mp"),
        P(("dp", "mp"), None),
        P(("dp", "mp"), None),
        P(("dp", "mp"), None),
        P(("dp", "mp"), None),
        P("dp", "mp"),
        P("dp", "mp"),
        P("dp", "mp"),
        P("dp", "mp"),
        P("dp", "mp"),
        P("dp", "mp"),
        P("mp", "dp"),
        P("dp", "mp"),
        P("mp", "dp"),
    )
    return jax.shard_map(body, mesh=mesh, in_specs=in_specs, out_specs=out_specs, check_vma=False)
```

```python
from functools import partial
import math
from types import SimpleNamespace

import jax
import jax.numpy as jnp
from jax import lax
from jax.experimental import pallas as pl
from jax.experimental.pallas import tpu as pltpu
from jax.sharding import PartitionSpec as P

norm_eps = 1e-05
SUBSPACE_SIZE = 64
SEQ_LEN = 1024
group_eps = 0.00064
CHUNK = 64
PAIR = 2 * SUBSPACE_SIZE
CHUNKS_FWD = 2
CHUNKS_BWD = 2
DECAY_SCALE = math.exp(-0.5)


def dot_nn(left_op, right_op):
    return lax.dot_general(left_op, right_op, (((1,), (0,)), ((), ())), preferred_element_type=jnp.float32)


def dot_nt(left_op, right_op):
    return lax.dot_general(left_op, right_op, (((1,), (1,)), ((), ())), preferred_element_type=jnp.float32)


def dot_tn(left_op, right_op):
    return lax.dot_general(left_op, right_op, (((0,), (0,)), ((), ())), preferred_element_type=jnp.float32)


def low(values):
    return values.astype(jnp.bfloat16)


def split_dot(ones_op, values):
    top = low(values)
    rest = values - top.astype(jnp.float32)
    mid = low(rest)
    tail = low(rest - mid.astype(jnp.float32))
    return dot_nn(ones_op, top) + dot_nn(ones_op, mid) + dot_nn(ones_op, tail)


def halves(values):
    top = low(values)
    return top, low(values - top.astype(jnp.float32))


def iota(shape, axis):
    return lax.broadcasted_iota(jnp.int32, shape, axis)


def head_masks():
    lane = iota((CHUNK, PAIR), 1)
    return lane < SUBSPACE_SIZE


def stack_heads(values):
    first = iota(values.shape, 1) < SUBSPACE_SIZE
    zero = jnp.zeros_like(values)
    return jnp.concatenate(
        [jnp.where(first, values, zero), jnp.where(first, zero, values)], axis=0
    )


def fold_heads(values):
    first = iota((CHUNK, PAIR), 1) < SUBSPACE_SIZE
    return jnp.where(first, values[:CHUNK], values[CHUNK:])


def head_ones():
    return (
        iota((PAIR, PAIR), 0) // SUBSPACE_SIZE == iota((PAIR, PAIR), 1) // SUBSPACE_SIZE
    )


def head_sum(values, ones_op):
    top = low(values)
    rest = low(values - top.astype(jnp.float32))
    return dot_nn(top, ones_op) + dot_nn(rest, ones_op)


def lower_inverses(lower_parts):
    row = iota((CHUNK, PAIR), 0)
    col = iota((CHUNK, PAIR), 1) % CHUNK
    eye = jnp.where(row == col, 1.0, 0.0)

    def times(lefts, rights):
        return [
            dot_nn(low(left_op), stack_heads(low(right_op)))
            for left_op, right_op in zip(lefts, rights)
        ]

    def plus(*lists):
        return [sum(members[1:], members[0]) for members in zip(*lists)]

    near = row // 8 == col // 8
    base = [jnp.where(near, part, 0.0) for part in lower_parts]
    square = times(base, base)
    cube = times(base, square)
    fourth = times(square, square)
    accum = [eye + first + second + third for first, second, third in zip(base, square, cube)]
    accum = plus(accum, times(accum, fourth))
    width = 8
    while width < CHUNK:
        level = (row // (2 * width) == col // (2 * width)) & (row // width != col // width)
        off = [jnp.where(level, part, 0.0) for part in lower_parts]
        accum = plus(accum, times(times(accum, off), accum))
        width *= 2
    return accum


def prepare(r, k, dw, da, cols, live, tri_op, ones_op):
    sw = jax.nn.sigmoid(dw + cols[0:1])
    full_log = -DECAY_SCALE * sw
    log_decay = jnp.where(live, full_log, 0.0)
    rate = jax.nn.sigmoid(da + cols[1:2])
    scaled = k * cols[2:3]
    inv = lax.rsqrt(head_sum(scaled * scaled, ones_op) + 1e-06)
    unit = scaled * inv
    unit_live = jnp.where(live, unit, 0.0)
    lag_scale = 1.0 + (rate - 1.0) * cols[3:4]
    lagged = jnp.where(live, k * lag_scale, 0.0)
    running = split_dot(tri_op, log_decay)
    grown = jnp.exp(running)
    before = jnp.exp(running - log_decay)
    shrunk = jnp.exp(-running)
    last = running[CHUNK - 1 : CHUNK]
    til_end = jnp.exp(last - running)
    write = unit_live * rate
    return SimpleNamespace(
        sw=sw,
        full_log=full_log,
        rate=rate,
        inv=inv,
        unit=unit,
        unit_live=unit_live,
        lag_scale=lag_scale,
        lagged=lagged,
        grown=grown,
        before=before,
        shrunk=shrunk,
        til_end=til_end,
        final=jnp.exp(last),
        read_wide=r * grown,
        write_wide=write * shrunk,
        key_wide=lagged * shrunk,
        read_hat=low(r * grown),
        remove_hat=low(-unit_live * before),
        write_hat=low(write * shrunk),
        key_hat=low(lagged * shrunk),
        write_end=low(write * til_end),
        key_end=low(lagged * til_end),
    )


def tri_masks():
    row = iota((CHUNK, PAIR), 0)
    col = iota((CHUNK, PAIR), 1) % CHUNK
    return row > col, row >= col


def mixer_forward(
    steps_per_seq,
    length_ref,
    r_ref,
    k_ref,
    v_ref,
    dw_ref,
    da_ref,
    gate_ref,
    cols_ref,
    z_ref,
    y_ref,
    t_ref,
    u_ref,
    s_ref,
    lk_ref,
    reads_ref,
    state,
):
    step = pl.program_id(0)
    within_seq = lax.rem(step, steps_per_seq)
    length = length_ref[step // steps_per_seq]

    @pl.when(within_seq == 0)
    def _():
        state[...] = jnp.zeros_like(state)

    rows_each = r_ref.shape[0]
    chunks = rows_each // CHUNK
    pairs = r_ref.shape[1] // PAIR
    ones_mask = head_ones()
    ones_op = jnp.where(ones_mask, 1.0, 0.0).astype(jnp.bfloat16)
    tri_op = jnp.where(iota((CHUNK, CHUNK), 0) >= iota((CHUNK, CHUNK), 1), 1.0, 0.0).astype(jnp.bfloat16)
    strict, within = tri_masks()
    within_two = jnp.concatenate([within, within], axis=1)
    units = [(chunk, pair) for chunk in range(chunks) for pair in range(pairs)]

    def place_of(unit):
        chunk, pair = unit
        return slice(chunk * CHUNK, (chunk + 1) * CHUNK), slice(pair * PAIR, (pair + 1) * PAIR)

    prepared, scored, lower_parts = [], [], []
    for unit in units:
        rows, lanes = place_of(unit)
        live = within_seq * rows_each + unit[0] * CHUNK + iota((CHUNK, PAIR), 0) < length
        got = prepare(
            r_ref[rows, lanes],
            k_ref[rows, lanes],
            dw_ref[rows, lanes],
            da_ref[rows, lanes],
            cols_ref[:, lanes],
            live,
            tri_op,
            ones_op,
        )
        prepared.append(got)
    for unit, got in zip(units, prepared):
        got.both = jnp.concatenate([got.remove_hat, got.read_hat], axis=0)
        past = jnp.concatenate([stack_heads(got.write_hat), stack_heads(got.key_hat)], axis=0)
        scores = dot_nt(got.both, past)
        past_rest = jnp.concatenate(
            [stack_heads(halves(got.write_wide)[1]), stack_heads(halves(got.key_wide)[1])], axis=0
        )
        got.read_rest = halves(got.read_wide)[1]
        fine = scores[CHUNK:] + (dot_nt(got.read_rest, past) + dot_nt(got.read_hat, past_rest))
        lower_parts.append(jnp.where(strict, scores[:CHUNK, :PAIR], 0.0))
        lower_key = low(jnp.where(strict, scores[:CHUNK, PAIR:], 0.0))
        reads = low(jnp.where(within_two, fine, 0.0))
        scored.append((lower_key, reads))
    solves = [low(part) for part in lower_inverses(lower_parts)]
    for unit, solve in zip(units, solves):
        t_ref[place_of(unit)] = solve
    for chunk in range(chunks):
        group = [index for index, unit in enumerate(units) if unit[0] == chunk]
        lows = [low(v_ref[place_of(units[index])]) for index in group]
        stacks = [stack_heads(values) for values in lows]
        olds = [state[units[index][1]] for index in group]
        old_parts = [halves(old) for old in olds]
        from_state = [dot_nt(prepared[index].both, old[0]) for index, old in zip(group, old_parts)]
        read_state = [
            part[CHUNK:]
            + (dot_nt(prepared[index].read_rest, old[0]) + dot_nt(prepared[index].read_hat, old[1]))
            for index, part, old in zip(group, from_state, old_parts)
        ]
        right = [
            low(part[:CHUNK] + dot_nn(scored[index][0], stack))
            for index, part, stack in zip(group, from_state, stacks)
        ]
        removed = [low(dot_nn(solves[index], stack_heads(part))) for index, part in zip(group, right)]
        for slot, index in enumerate(group):
            pair = units[index][1]
            got = prepared[index]
            ends = jnp.concatenate([got.write_end, got.key_end], axis=0)
            adds = dot_tn(jnp.concatenate([removed[slot], lows[slot]], axis=0), ends)
            state[pair] = olds[slot] * got.final + jnp.where(ones_mask, adds, 0.0)
            u_ref[place_of(units[index])] = removed[slot]
            rows, lanes = place_of(units[index])
            lk_ref[rows, lanes], reads_ref[rows, slice(2 * lanes.start, 2 * lanes.stop)] = scored[index]
            s_ref[chunk, pair] = olds[slot]
        outs = [
            read_state[slot]
            + dot_nn(scored[index][1], jnp.concatenate([stack_heads(removed[slot]), stacks[slot]], axis=0))
            for slot, index in enumerate(group)
        ]
        centred = [y - head_sum(y, ones_op) * (1.0 / SUBSPACE_SIZE) for y in outs]
        spread = [head_sum(part * part, ones_op) * (1.0 / SUBSPACE_SIZE) for part in centred]
        for slot, index in enumerate(group):
            rows, lanes = place_of(units[index])
            cols = cols_ref[:, lanes]
            normed = centred[slot] * lax.rsqrt(spread[slot] + group_eps)
            bonus = head_sum(r_ref[rows, lanes] * prepared[index].lagged * cols[4:5], ones_op)
            mixed = normed * cols[5:6] + cols[6:7] + bonus * v_ref[rows, lanes]
            y_ref[rows, lanes] = outs[slot]
            z_ref[rows, lanes] = low(mixed * gate_ref[rows, lanes])


def mixer_backward(
    steps_per_seq,
    length_ref,
    r_ref,
    k_ref,
    v_ref,
    dw_ref,
    da_ref,
    gate_ref,
    cols_ref,
    y_ref,
    t_ref,
    u_ref,
    s_ref,
    lk_ref,
    reads_ref,
    dz_ref,
    dr_ref,
    dk_ref,
    dv_ref,
    ddw_ref,
    dda_ref,
    dgate_ref,
    dcols_ref,
    dstate,
):
    step = pl.num_programs(0) - 1 - pl.program_id(0)
    within_seq = lax.rem(step, steps_per_seq)
    length = length_ref[step // steps_per_seq]

    @pl.when(within_seq == steps_per_seq - 1)
    def _():
        dstate[...] = jnp.zeros_like(dstate)

    @pl.when(pl.program_id(0) == 0)
    def _():
        dcols_ref[...] = jnp.zeros_like(dcols_ref)

    rows_each = r_ref.shape[0]
    chunks = rows_each // CHUNK
    pairs = r_ref.shape[1] // PAIR
    ones_mask = head_ones()
    ones_op = jnp.where(ones_mask, 1.0, 0.0).astype(jnp.bfloat16)
    row = iota((CHUNK, CHUNK), 0)
    col = iota((CHUNK, CHUNK), 1)
    tri_op = jnp.where(row >= col, 1.0, 0.0).astype(jnp.bfloat16)
    suffix_op = jnp.where(row <= col, 1.0, 0.0).astype(jnp.bfloat16)
    prefix_op = jnp.where(row > col, 1.0, 0.0).astype(jnp.bfloat16)
    sums_op = jnp.concatenate([suffix_op, prefix_op], axis=1)
    strict, within = tri_masks()

    def add_col(index, lanes, values):
        part = values[0:8]
        for start in range(8, CHUNK, 8):
            part = part + values[start : start + 8]
        dcols_ref[index, :, lanes] += part

    strict_two = jnp.concatenate([strict, strict], axis=1)
    within_two = jnp.concatenate([within, within], axis=1)
    all_masks = jnp.concatenate([strict_two, within_two], axis=0)
    units = [(chunk, pair) for chunk in reversed(range(chunks)) for pair in range(pairs)]
    mean_of = 1.0 / SUBSPACE_SIZE
    known = []
    for chunk, pair in units:
        rows = slice(chunk * CHUNK, (chunk + 1) * CHUNK)
        lanes = slice(pair * PAIR, (pair + 1) * PAIR)
        live = within_seq * rows_each + chunk * CHUNK + iota((CHUNK, PAIR), 0) < length
        cols = cols_ref[:, lanes]
        got = prepare(
            r_ref[rows, lanes],
            k_ref[rows, lanes],
            dw_ref[rows, lanes],
            da_ref[rows, lanes],
            cols,
            live,
            tri_op,
            ones_op,
        )
        got.rows, got.lanes, got.live, got.cols = rows, lanes, live, cols
        got.pair, got.chunk = pair, chunk
        known.append(got)
    for got in known:
        y = y_ref[got.rows, got.lanes]
        got.centred = y - head_sum(y, ones_op) * mean_of
    for got in known:
        spread = head_sum(got.centred * got.centred, ones_op) * mean_of
        got.inv_y = lax.rsqrt(spread + group_eps)
    for got in known:
        rows, lanes, cols = got.rows, got.lanes, got.cols
        r, v, dz = r_ref[rows, lanes], v_ref[rows, lanes], dz_ref[rows, lanes]
        normed = got.centred * got.inv_y
        got.bonus = head_sum(r * got.lagged * cols[4:5], ones_op)
        mixed = normed * cols[5:6] + cols[6:7] + got.bonus * v
        dgate_ref[rows, lanes] = low(dz * mixed)
        dmix = dz * gate_ref[rows, lanes]
        add_col(5, lanes, dmix * normed)
        add_col(6, lanes, dmix)
        dnormed = dmix * cols[5:6]
        got.dbonus = head_sum(dmix * v, ones_op)
        mean_grad = head_sum(dnormed, ones_op) * mean_of
        mean_prod = head_sum(dnormed * normed, ones_op) * mean_of
        got.dy_low, got.dy_rest = halves(got.inv_y * (dnormed - mean_grad - normed * mean_prod))
        got.dv = got.bonus * dmix
    for got in known:
        rows, lanes = got.rows, got.lanes
        got.both = jnp.concatenate([got.remove_hat, got.read_hat], axis=0)
        got.past = jnp.concatenate(
            [stack_heads(got.write_hat), stack_heads(got.key_hat)], axis=0
        )
        got.lower_key = lk_ref[rows, lanes]
        reads = reads_ref[rows, slice(2 * lanes.start, 2 * lanes.stop)]
        got.from_y = dot_tn(reads, got.dy_low)
        v_low = low(v_ref[rows, lanes])
        removed = u_ref[rows, lanes]
        got.sent = jnp.concatenate([removed, v_low], axis=0)
        got.stacks = jnp.concatenate([stack_heads(removed), stack_heads(v_low)], axis=0)
    for chunk in reversed(range(chunks)):
        group = [got for got in known if got.chunk == chunk]
        for got in group:
            got.later = dstate[got.pair]
            got.later_low, got.later_rest = halves(got.later)
            ends = jnp.concatenate([got.write_end, got.key_end], axis=0)
            got.from_later = dot_nt(ends, got.later_low)
        for got in group:
            dremoved = low(got.from_later[:CHUNK] + fold_heads(got.from_y[:PAIR]))
            got.dright = low(fold_heads(dot_tn(t_ref[got.rows, got.lanes], dremoved)))
        for got in group:
            got.douts = jnp.concatenate([got.dright, got.dy_low], axis=0)
            adds = dot_tn(got.douts, got.both) + dot_tn(got.dy_rest, got.read_hat)
            adds = jnp.where(ones_mask, adds, 0.0)
            dstate[got.pair] = got.later * got.final + adds
    for got in known:
        dv = got.dv + got.from_later[CHUNK:] + fold_heads(got.from_y[PAIR:])
        dv = dv + fold_heads(dot_tn(got.lower_key, got.dright))
        dv_ref[got.rows, got.lanes] = low(dv)
        dscores = dot_nt(got.douts, got.stacks)
        fine = dscores[CHUNK:] + dot_nt(got.dy_rest, got.stacks)
        dscores = low(jnp.where(all_masks, jnp.concatenate([dscores[:CHUNK], fine], axis=0), 0.0))
        old_wide = s_ref[got.chunk, got.pair]
        old_low, old_rest = halves(old_wide)
        from_old = dot_nn(got.douts, old_low)
        fine = from_old[CHUNK:] + (dot_nn(got.dy_rest, old_low) + dot_nn(got.dy_low, old_rest))
        got.dboth = jnp.concatenate([from_old[:CHUNK], fine], axis=0) + dot_nn(dscores, got.past)
        dpast = dot_tn(dscores, got.both)
        got.dwrite_hat = fold_heads(dpast[:PAIR])
        got.dkey_hat = fold_heads(dpast[PAIR:])
        got.dends = dot_nn(got.sent, got.later_low) + dot_nn(got.sent, got.later_rest)
        got.dfinal = jnp.sum(got.later * old_wide, axis=0, keepdims=True)
    for got in known:
        rows, lanes, cols, live = got.rows, got.lanes, got.cols, got.live

        def wide(values):
            return values.astype(jnp.float32)

        r, k = r_ref[rows, lanes], k_ref[rows, lanes]
        dwrite_hat, dkey_hat = got.dwrite_hat, got.dkey_hat
        dwrite_end, dkey_end = got.dends[:CHUNK], got.dends[CHUNK:]
        dremove_hat, dread_hat = got.dboth[:CHUNK], got.dboth[CHUNK:]
        dbonus, lagged = got.dbonus, got.lagged
        bonus_lag = dbonus * lagged
        add_col(4, lanes, bonus_lag * r)
        dr_ref[rows, lanes] = low(bonus_lag * cols[4:5] + dread_hat * got.grown)
        minus = wide(got.remove_hat) * dremove_hat
        plus = wide(got.read_hat) * dread_hat + minus
        plus = plus - wide(got.write_hat) * dwrite_hat - wide(got.key_hat) * dkey_hat
        ending = wide(got.write_end) * dwrite_end + wide(got.key_end) * dkey_end
        sums = split_dot(sums_op, jnp.concatenate([plus, ending], axis=0))
        dlog = sums - minus + got.final * got.dfinal
        ddw = jnp.where(live, dlog * got.full_log * (1.0 - got.sw), 0.0)
        add_col(0, lanes, ddw)
        ddw_ref[rows, lanes] = low(ddw)
        dwrite = dwrite_hat * got.shrunk + dwrite_end * got.til_end
        dlag = dbonus * r * cols[4:5] + dkey_hat * got.shrunk + dkey_end * got.til_end
        dlag = jnp.where(live, dlag, 0.0)
        rate = got.rate
        dunit = jnp.where(live, dwrite * rate - dremove_hat * got.before, 0.0)
        lag_k = dlag * k
        drate = dwrite * got.unit_live + lag_k * cols[3:4]
        add_col(3, lanes, lag_k * (rate - 1.0))
        dscaled = got.inv * (dunit - got.unit * head_sum(dunit * got.unit, ones_op))
        add_col(2, lanes, dscaled * k)
        dk_ref[rows, lanes] = low(dlag * got.lag_scale + dscaled * cols[2:3])
        dda = drate * rate * (1.0 - rate)
        add_col(1, lanes, dda)
        dda_ref[rows, lanes] = low(dda)


def run_mixer_forward(lengths, r, k, v, dw, da, gate, cols):
    positions, part_width = r.shape
    rows_each = CHUNKS_FWD * CHUNK
    steps = positions // rows_each
    steps_per_seq = SEQ_LEN // rows_each
    pairs = part_width // PAIR
    wide = pl.BlockSpec((rows_each, part_width), lambda i: (i, 0))
    shape = jax.ShapeDtypeStruct
    return pl.pallas_call(
        partial(mixer_forward, steps_per_seq),
        grid=(steps,),
        in_specs=[pl.BlockSpec(memory_space=pltpu.SMEM)]
        + [wide] * 6
        + [pl.BlockSpec((8, part_width), lambda i: (0, 0))],
        out_specs=[wide] * 4
        + [
            pl.BlockSpec((CHUNKS_FWD, pairs, PAIR, PAIR), lambda i: (i, 0, 0, 0)),
            wide,
            pl.BlockSpec((rows_each, 2 * part_width), lambda i: (i, 0)),
        ],
        out_shape=[
            shape((positions, part_width), jnp.bfloat16),
            shape((positions, part_width), jnp.float32),
            shape((positions, part_width), jnp.bfloat16),
            shape((positions, part_width), jnp.bfloat16),
            shape((positions // CHUNK, pairs, PAIR, PAIR), jnp.float32),
            shape((positions, part_width), jnp.bfloat16),
            shape((positions, 2 * part_width), jnp.bfloat16),
        ],
        scratch_shapes=[pltpu.VMEM((pairs, PAIR, PAIR), jnp.float32)],
        compiler_params=pltpu.CompilerParams(
            dimension_semantics=("arbitrary",), vmem_limit_bytes=40 * 1024 * 1024
        ),
        name="mixer_forward",
    )(lengths, r, k, v, dw, da, gate, cols)


def run_mixer_backward(lengths, r, k, v, dw, da, gate, cols, y, t, u, s, lk, reads, dz):
    positions, part_width = r.shape
    rows_each = CHUNKS_BWD * CHUNK
    steps = positions // rows_each
    steps_per_seq = SEQ_LEN // rows_each
    pairs = part_width // PAIR
    wide = pl.BlockSpec((rows_each, part_width), lambda i: (steps - 1 - i, 0))
    shape = jax.ShapeDtypeStruct
    return pl.pallas_call(
        partial(mixer_backward, steps_per_seq),
        grid=(steps,),
        in_specs=[pl.BlockSpec(memory_space=pltpu.SMEM)]
        + [wide] * 6
        + [pl.BlockSpec((8, part_width), lambda i: (0, 0))]
        + [wide] * 3
        + [
            pl.BlockSpec((CHUNKS_BWD, pairs, PAIR, PAIR), lambda i: (steps - 1 - i, 0, 0, 0)),
            wide,
            pl.BlockSpec((rows_each, 2 * part_width), lambda i: (steps - 1 - i, 0)),
            wide,
        ],
        out_specs=[wide] * 6 + [pl.BlockSpec((8, 8, part_width), lambda i: (0, 0, 0))],
        out_shape=[shape((positions, part_width), jnp.bfloat16)] * 6
        + [shape((8, 8, part_width), jnp.float32)],
        scratch_shapes=[pltpu.VMEM((pairs, PAIR, PAIR), jnp.float32)],
        compiler_params=pltpu.CompilerParams(
            dimension_semantics=("arbitrary",), vmem_limit_bytes=40 * 1024 * 1024
        ),
        name="mixer_backward",
    )(lengths, r, k, v, dw, da, gate, cols, y, t, u, s, lk, reads, dz)


LINE = "mp"
END_LAG = 4
MID_LAG = 2


def link_cost(elements):
    return elements * 2 * 2 * 40


def line_barrier(size):
    me = lax.axis_index(LINE)
    barrier = pltpu.get_barrier_semaphore()

    @pl.when(me > 0)
    def _():
        pl.semaphore_signal(barrier, inc=1, device_id={LINE: me - 1}, device_id_type=pl.DeviceIdType.MESH)

    @pl.when(me < size - 1)
    def _():
        pl.semaphore_signal(barrier, inc=1, device_id={LINE: me + 1}, device_id_type=pl.DeviceIdType.MESH)

    ends = jnp.where((me == 0) | (me == size - 1), 1, 2)
    pl.semaphore_wait(barrier, ends)


class Flow:
    def __init__(self, size, side):
        self.size = size
        self.side = side
        self.me = lax.axis_index(LINE)
        self.step = 1 - 2 * side
        self.target = self.me + self.step
        source = self.me - self.step
        self.has_source = (source >= 0) & (source < size)
        self.has_target = (self.target >= 0) & (self.target < size)

    def copy(self, source, place, send_sem, recv_sem):
        return pltpu.make_async_remote_copy(
            src_ref=source,
            dst_ref=place,
            send_sem=send_sem,
            recv_sem=recv_sem,
            device_id={LINE: self.target},
            device_id_type=pl.DeviceIdType.MESH,
        )


def two_flows(size):
    me = lax.axis_index(LINE)
    near = jnp.where(me < size // 2, 0, 1)
    return Flow(size, near), Flow(size, 1 - near)


def line_sum_kernel(size, chunk_rows, x_ref, out_ref, got, sent, send_sem, recv_sem):
    line_barrier(size)
    me = lax.axis_index(LINE)
    flows = two_flows(size)
    chunks = x_ref.shape[0] // chunk_rows

    def copy_of(flow, chunk, source):
        rows = pl.ds(pl.multiple_of(chunk * chunk_rows, chunk_rows), chunk_rows)
        return flow.copy(
            source.at[rows], got.at[flow.side, rows], send_sem.at[flow.side, chunk], recv_sem.at[flow.side, chunk]
        )

    def pass_on(flow, chunk):
        rows = pl.ds(pl.multiple_of(chunk * chunk_rows, chunk_rows), chunk_rows)

        @pl.when(flow.has_source)
        def _():
            copy_of(flow, chunk, x_ref).wait_recv()

        @pl.when(flow.has_source & flow.has_target)
        def _():
            total = got[flow.side, rows].astype(jnp.float32) + x_ref[rows].astype(jnp.float32)
            sent[flow.side, rows] = total.astype(sent.dtype)
            copy_of(flow, chunk, sent.at[flow.side]).start()

        @pl.when(jnp.logical_not(flow.has_source))
        def _():
            copy_of(flow, chunk, x_ref).start()

    is_end = (me == 0) | (me == size - 1)
    lag = jnp.where(is_end, END_LAG, MID_LAG)

    def step(turn, carry):
        @pl.when(turn < chunks)
        def _():
            pass_on(flows[0], turn)

        chunk = turn - lag

        @pl.when((chunk >= 0) & (chunk < chunks))
        def _():
            pass_on(flows[1], chunk)
            rows = pl.ds(pl.multiple_of(chunk * chunk_rows, chunk_rows), chunk_rows)

            @pl.when(is_end)
            def _():
                other = got[flows[1].side, rows].astype(jnp.float32)
                out_ref[rows] = (other + x_ref[rows].astype(jnp.float32)).astype(out_ref.dtype)

            @pl.when(jnp.logical_not(is_end))
            def _():
                other = got[0, rows].astype(jnp.float32) + got[1, rows].astype(jnp.float32)
                out_ref[rows] = (other + x_ref[rows].astype(jnp.float32)).astype(out_ref.dtype)

        return carry

    lax.fori_loop(0, chunks + END_LAG, step, 0)

    def drain(chunk, carry):
        for flow in flows:

            @pl.when(flow.has_target)
            def _():
                copy_of(flow, chunk, x_ref).wait_send()

        return carry

    lax.fori_loop(0, chunks, drain, 0)


def line_sum(x, size, collective_id, chunk_rows=64):
    rows, cols = x.shape
    chunks = rows // chunk_rows
    return pl.pallas_call(
        partial(line_sum_kernel, size, chunk_rows),
        out_shape=jax.ShapeDtypeStruct(x.shape, x.dtype),
        in_specs=[pl.BlockSpec(memory_space=pltpu.VMEM)],
        out_specs=pl.BlockSpec(memory_space=pltpu.VMEM),
        scratch_shapes=[
            pltpu.VMEM((2, rows, cols), x.dtype),
            pltpu.VMEM((2, rows, cols), x.dtype),
            pltpu.SemaphoreType.DMA((2, chunks)),
            pltpu.SemaphoreType.DMA((2, chunks)),
        ],
        compiler_params=pltpu.CompilerParams(
            collective_id=collective_id, has_side_effects=True, vmem_limit_bytes=48 * 1024 * 1024
        ),
        cost_estimate=pl.CostEstimate(flops=0, bytes_accessed=link_cost(rows * cols), transcendentals=0),
        name="line_sum",
    )(x)


def line_gather_kernel(size, chunk_rows, x_ref, out_ref, send_sem, recv_sem):
    line_barrier(size)
    me = lax.axis_index(LINE)
    flows = two_flows(size)
    width = x_ref.shape[1]
    chunks = x_ref.shape[0] // chunk_rows

    def place(block, chunk):
        rows = pl.ds(pl.multiple_of(chunk * chunk_rows, chunk_rows), chunk_rows)
        return out_ref.at[rows, pl.ds(pl.multiple_of(block * width, width), width)]

    def copy_of(flow, block, chunk):
        return flow.copy(
            place(block, chunk), place(block, chunk), send_sem.at[flow.side, block, chunk], recv_sem.at[flow.side, block, chunk]
        )

    def step(chunk, carry):
        rows = pl.ds(pl.multiple_of(chunk * chunk_rows, chunk_rows), chunk_rows)
        out_ref[rows, pl.ds(pl.multiple_of(me * width, width), width)] = x_ref[rows]
        for flow in flows:

            @pl.when(flow.has_target)
            def _():
                copy_of(flow, me, chunk).start()

        return carry

    lax.fori_loop(0, chunks, step, 0)
    for hop in range(1, size):

        def forward(chunk, carry):
            for flow in flows:
                block = me - hop * flow.step
                exists = (block >= 0) & (block < size)

                @pl.when(exists)
                def _():
                    copy_of(flow, block, chunk).wait_recv()

                @pl.when(exists & flow.has_target)
                def _():
                    copy_of(flow, block, chunk).start()

            return carry

        lax.fori_loop(0, chunks, forward, 0)
    for hop in range(size):

        def drain(chunk, carry):
            for flow in flows:
                block = me - hop * flow.step
                exists = (block >= 0) & (block < size)

                @pl.when(exists & flow.has_target)
                def _():
                    copy_of(flow, block, chunk).wait_send()

            return carry

        lax.fori_loop(0, chunks, drain, 0)


def line_gather(x, size, collective_id, chunk_rows=256):
    rows, cols = x.shape
    chunks = rows // chunk_rows
    return pl.pallas_call(
        partial(line_gather_kernel, size, chunk_rows),
        out_shape=jax.ShapeDtypeStruct((rows, size * cols), x.dtype),
        in_specs=[pl.BlockSpec(memory_space=pltpu.VMEM)],
        out_specs=pl.BlockSpec(memory_space=pltpu.VMEM),
        scratch_shapes=[
            pltpu.SemaphoreType.DMA((2, size, chunks)),
            pltpu.SemaphoreType.DMA((2, size, chunks)),
        ],
        compiler_params=pltpu.CompilerParams(
            collective_id=collective_id, has_side_effects=True, vmem_limit_bytes=48 * 1024 * 1024
        ),
        cost_estimate=pl.CostEstimate(flops=0, bytes_accessed=link_cost(3 * rows * cols), transcendentals=0),
        name="line_gather",
    )(x)


def line_scatter_kernel(size, chunk_rows, x_ref, out_ref, got, sent, send_sem, recv_sem):
    line_barrier(size)
    me = lax.axis_index(LINE)
    flows = two_flows(size)
    width = out_ref.shape[1]
    chunks = x_ref.shape[0] // chunk_rows

    def rows_of(chunk):
        return pl.ds(pl.multiple_of(chunk * chunk_rows, chunk_rows), chunk_rows)

    def cols_of(block):
        return pl.ds(pl.multiple_of(block * width, width), width)

    def copy_of(flow, block, chunk, source):
        return flow.copy(
            source,
            got.at[flow.side, rows_of(chunk), cols_of(block)],
            send_sem.at[flow.side, block, chunk],
            recv_sem.at[flow.side, block, chunk],
        )

    def own(block, chunk):
        return x_ref[rows_of(chunk), cols_of(block)].astype(jnp.float32)

    for hop in range(size - 1):

        def forward(chunk, carry):
            for flow in flows:
                block = jnp.where(flow.side == 0, size - 1 - hop, hop)
                ahead = (block - me) * flow.step > 0

                @pl.when(ahead & flow.has_source)
                def _():
                    source = x_ref.at[rows_of(chunk), cols_of(block)]
                    copy_of(flow, block, chunk, source).wait_recv()
                    total = got[flow.side, rows_of(chunk), cols_of(block)].astype(jnp.float32) + own(block, chunk)
                    sent[flow.side, rows_of(chunk), cols_of(block)] = total.astype(sent.dtype)
                    copy_of(flow, block, chunk, sent.at[flow.side, rows_of(chunk), cols_of(block)]).start()

                @pl.when(ahead & jnp.logical_not(flow.has_source))
                def _():
                    copy_of(flow, block, chunk, x_ref.at[rows_of(chunk), cols_of(block)]).start()

            return carry

        lax.fori_loop(0, chunks, forward, 0)

    def finish(chunk, carry):
        rows = rows_of(chunk)
        for flow in flows:

            @pl.when(flow.has_source)
            def _():
                copy_of(flow, me, chunk, x_ref.at[rows, cols_of(me)]).wait_recv()

        @pl.when(me == 0)
        def _():
            out_ref[rows] = (got[1, rows, cols_of(me)].astype(jnp.float32) + own(me, chunk)).astype(out_ref.dtype)

        @pl.when(me == size - 1)
        def _():
            out_ref[rows] = (got[0, rows, cols_of(me)].astype(jnp.float32) + own(me, chunk)).astype(out_ref.dtype)

        @pl.when((me > 0) & (me < size - 1))
        def _():
            other = got[0, rows, cols_of(me)].astype(jnp.float32) + got[1, rows, cols_of(me)].astype(jnp.float32)
            out_ref[rows] = (other + own(me, chunk)).astype(out_ref.dtype)

        return carry

    lax.fori_loop(0, chunks, finish, 0)
    for hop in range(size - 1):

        def drain(chunk, carry):
            for flow in flows:
                block = jnp.where(flow.side == 0, size - 1 - hop, hop)
                ahead = (block - me) * flow.step > 0

                @pl.when(ahead)
                def _():
                    copy_of(flow, block, chunk, x_ref.at[rows_of(chunk), cols_of(block)]).wait_send()

            return carry

        lax.fori_loop(0, chunks, drain, 0)


def line_scatter(x, size, collective_id, out_dtype=jnp.float32, chunk_rows=256):
    rows, cols = x.shape
    chunks = rows // chunk_rows
    return pl.pallas_call(
        partial(line_scatter_kernel, size, chunk_rows),
        out_shape=jax.ShapeDtypeStruct((rows, cols // size), out_dtype),
        in_specs=[pl.BlockSpec(memory_space=pltpu.VMEM)],
        out_specs=pl.BlockSpec(memory_space=pltpu.VMEM),
        scratch_shapes=[
            pltpu.VMEM((2, rows, cols), x.dtype),
            pltpu.VMEM((2, rows, cols), x.dtype),
            pltpu.SemaphoreType.DMA((2, size, chunks)),
            pltpu.SemaphoreType.DMA((2, size, chunks)),
        ],
        compiler_params=pltpu.CompilerParams(
            collective_id=collective_id, has_side_effects=True, vmem_limit_bytes=48 * 1024 * 1024
        ),
        cost_estimate=pl.CostEstimate(flops=0, bytes_accessed=link_cost(3 * rows * cols // size), transcendentals=0),
        name="line_scatter",
    )(x)


def input_backward_kernel(
    seq_len, splits, whole_ref, dr_ref, dk_ref, dv_ref, dl_ref, three_ref, down_ref, params_ref, din_ref, gparams_ref, gdown_ref, carry, kept
):
    step = pl.program_id(0)
    tile = pl.num_programs(0) - 1 - step
    rows_each = dr_ref.shape[0]
    part = dr_ref.shape[1]
    width = whole_ref.shape[1]
    start = tile * rows_each
    at_start = lax.rem(start, seq_len) == 0
    at_end = lax.rem(start + rows_each, seq_len) == 0

    @pl.when(step == 0)
    def _():
        gparams_ref[...] = jnp.zeros_like(gparams_ref)
        gdown_ref[...] = jnp.zeros_like(gdown_ref)

    @pl.when(at_end)
    def _():
        carry[...] = jnp.zeros_like(carry)

    edge = 16
    rows = pl.ds(pl.multiple_of(start, rows_each), rows_each)
    edge_rows = pl.ds(pl.multiple_of(jnp.maximum(start - edge, 0), edge), edge)
    inverse_width = 1.0 / width

    def moments(place):
        values = whole_ref[place, :].astype(jnp.float32)
        centre = jnp.sum(values, axis=1, keepdims=True) * inverse_width
        values = values - centre
        spread = jnp.sum(values * values, axis=1, keepdims=True) * inverse_width
        return centre, lax.rsqrt(spread + norm_eps)

    centre, inv = moments(rows)
    edge_centre, edge_inv = moments(edge_rows)
    block_cols = 256
    row_index = iota((rows_each, block_cols), 0)
    dl = dl_ref[...]
    lane = iota(dl.shape, 1)
    zero = jnp.zeros_like(dl)
    first, second = splits
    dls = (
        jnp.where(lane < first, dl, zero),
        jnp.where((lane >= first) & (lane < second), dl, zero),
        jnp.where(lane >= second, dl, zero),
    )
    down_row = iota((dl.shape[1], block_cols), 0)
    sum_grad = jnp.zeros((rows_each, 1), jnp.float32)
    sum_prod = jnp.zeros((rows_each, 1), jnp.float32)

    def add_param(index, cols, values):
        total = values[0:8]
        for place in range(8, rows_each, 8):
            total = total + values[place : place + 8]
        gparams_ref[index, :, cols] += total

    for block in range(width // block_cols):
        cols = slice(block * block_cols, (block + 1) * block_cols)
        gain, bias = params_ref[0:1, cols], params_ref[1:2, cols]
        unit = (whole_ref[rows, cols].astype(jnp.float32) - centre) * inv
        normed = unit * gain + bias
        edge_unit = (whole_ref[edge_rows, cols].astype(jnp.float32) - edge_centre) * edge_inv
        edge_normed = (edge_unit * gain + bias)[edge - 1 : edge]
        edge_normed = jnp.where(at_start, 0.0, edge_normed)
        before = jnp.where(row_index == 0, edge_normed, pltpu.roll(normed, 1, 0))
        shift = before - normed
        down = down_ref[cols, :]
        weights = three_ref[cols, :]
        grads = (
            dot_nt(dr_ref[...], weights[:, :part]),
            dot_nt(dls[0], down),
            dot_nt(dk_ref[...], weights[:, part : 2 * part]),
            dot_nt(dv_ref[...], weights[:, 2 * part :]),
            dot_nt(dls[1], down),
            dot_nt(dls[2], down),
        )
        total = grads[0]
        for grad in grads[1:]:
            total = total + grad
        mixed = None
        for index, grad in enumerate(grads):
            rate = params_ref[2 + index : 3 + index, cols]
            mixed = grad * rate if mixed is None else mixed + grad * rate
            add_param(2 + index, cols, grad * shift)
        after = jnp.where(row_index == rows_each - 1, carry[0:1, cols], pltpu.roll(mixed, rows_each - 1, 0))
        carry[0:1, cols] = mixed[0:1]
        dnormed = total - mixed + after
        add_param(0, cols, dnormed * unit)
        add_param(1, cols, dnormed)
        dunit = dnormed * gain
        kept[:, cols] = dunit
        sum_grad = sum_grad + jnp.sum(dunit, axis=1, keepdims=True)
        sum_prod = sum_prod + jnp.sum(dunit * unit, axis=1, keepdims=True)
        outs = [
            dot_tn(dl, low(normed + shift * params_ref[index : index + 1, cols])) for index in (3, 6, 7)
        ]
        gdown_ref[:, cols] += jnp.where(
            down_row < first, outs[0], jnp.where(down_row < second, outs[1], outs[2])
        )
    sum_grad = sum_grad * inverse_width
    sum_prod = sum_prod * inverse_width
    for block in range(width // block_cols):
        cols = slice(block * block_cols, (block + 1) * block_cols)
        unit = (whole_ref[rows, cols].astype(jnp.float32) - centre) * inv
        din_ref[:, cols] = low(inv * (kept[:, cols] - sum_grad - unit * sum_prod))


def input_backward(whole, dr, dk, dv, dl, splits, three, down, params):
    positions, width = whole.shape
    part = dr.shape[1]
    rows_each = 256
    steps = positions // rows_each
    tile = lambda cols: pl.BlockSpec((rows_each, cols), lambda i: (steps - 1 - i, 0))
    full = pl.BlockSpec(memory_space=pltpu.VMEM)
    shape = jax.ShapeDtypeStruct
    return pl.pallas_call(
        partial(input_backward_kernel, SEQ_LEN, splits),
        grid=(steps,),
        in_specs=[full, tile(part), tile(part), tile(part), tile(dl.shape[1]), full, full, full],
        out_specs=[
            tile(width),
            pl.BlockSpec((8, 8, width), lambda i: (0, 0, 0)),
            pl.BlockSpec((dl.shape[1], width), lambda i: (0, 0)),
        ],
        out_shape=[
            shape((positions, width), jnp.bfloat16),
            shape((8, 8, width), jnp.float32),
            shape((dl.shape[1], width), jnp.float32),
        ],
        scratch_shapes=[pltpu.VMEM((8, width), jnp.float32), pltpu.VMEM((rows_each, width), jnp.float32)],
        compiler_params=pltpu.CompilerParams(
            dimension_semantics=("arbitrary",), vmem_limit_bytes=48 * 1024 * 1024
        ),
        name="input_backward",
    )(whole, dr, dk, dv, dl, three, down, params)


def weight_grads_kernel(left_refs, right_refs, out_ref):
    part = right_refs[0].shape[1]
    for index, (left_ref, right_ref) in enumerate(zip(left_refs, right_refs)):
        out_ref[:, index * part : (index + 1) * part] = low(dot_tn(left_ref[...], right_ref[...]))


def weight_grads(lefts, rights):
    positions, width = lefts[0].shape
    part = rights[0].shape[1]
    count = len(lefts)
    block = 512

    def kernel(*refs):
        weight_grads_kernel(refs[:count], refs[count : 2 * count], refs[2 * count])

    return pl.pallas_call(
        kernel,
        grid=(width // block,),
        in_specs=[pl.BlockSpec((positions, block), lambda i: (0, i))] * count
        + [pl.BlockSpec((positions, part), lambda i: (0, 0))] * count,
        out_specs=pl.BlockSpec((block, count * part), lambda i: (i, 0)),
        out_shape=jax.ShapeDtypeStruct((width, count * part), jnp.bfloat16),
        compiler_params=pltpu.CompilerParams(
            dimension_semantics=("arbitrary",), vmem_limit_bytes=40 * 1024 * 1024
        ),
        name="weight_grads",
    )(*lefts, *rights)


def matmul(left_op, right_op):
    return jnp.dot(left_op, right_op, preferred_element_type=jnp.float32)


def contract_rows(left_op, right_op):
    return jnp.einsum("tk,tn->kn", left_op, right_op, preferred_element_type=jnp.float32)


def against(grad_op, weight_op):
    return jnp.einsum("tn,kn->tk", grad_op, weight_op, preferred_element_type=jnp.float32)


def layer_norm(values, scale_in, offset):
    centre = jnp.mean(values, axis=-1, keepdims=True)
    centred = values - centre
    spread = jnp.mean(centred * centred, axis=-1, keepdims=True)
    return centred * lax.rsqrt(spread + norm_eps) * scale_in + offset


def shifted(values):
    grid_view = values.reshape(values.shape[0] // SEQ_LEN, SEQ_LEN, values.shape[1])
    earlier = jnp.concatenate([jnp.zeros_like(grid_view[:, :1]), grid_view[:, :-1]], axis=1)
    return earlier.reshape(values.shape)


def section_in(hidden, scale_in, offset, mix_rates):
    standardized_source = layer_norm(hidden, scale_in, offset)
    shift_diff = shifted(standardized_source) - standardized_source
    return tuple((standardized_source + shift_diff * mix_rates[:, column] for column in range(6)))


def section_out(residual, scale_in, offset, mix_rate):
    standardized_source = layer_norm(residual, scale_in, offset)
    return standardized_source + (shifted(standardized_source) - standardized_source) * mix_rate


def body(
    hidden,
    teacher,
    lengths,
    feature_params,
    decay_down,
    rate_down,
    gate_down,
    decay_up,
    rate_up,
    gate_up,
    receptance,
    key_proj,
    value_proj,
    output_proj,
    ffn_key,
    ffn_value,
):
    position_count, part_width = hidden.shape
    seq_dev = position_count // SEQ_LEN
    mp_index = lax.axis_index("mp")
    col_start = mp_index * part_width
    groups = lax.axis_size("dp")
    own_lengths = lax.dynamic_slice_in_dim(lengths, lax.axis_index("dp") * seq_dev, seq_dev)
    places = jnp.arange(SEQ_LEN, dtype=jnp.int32)
    valid = (places[None, :] < own_lengths[:, None]).astype(jnp.float32).reshape(position_count)
    loss_scale = position_count * lax.axis_size("dp") / jnp.sum(lengths).astype(jnp.float32)
    line_size = lax.axis_size("mp")
    whole_low = line_gather(hidden, line_size, 1)
    whole = whole_low.astype(jnp.float32)
    low_rank = (decay_down.shape[1], rate_down.shape[1], gate_down.shape[1])
    narrow = jnp.concatenate([decay_down, rate_down, gate_down, feature_params], axis=1)
    narrow = jnp.pad(narrow, ((0, 0), (0, -narrow.shape[1] % 128)))
    narrow_w = lax.all_gather(narrow, "mp", axis=0, tiled=True)
    narrow_w = lax.all_gather(narrow_w, "dp", axis=0, tiled=True)
    decay_down_w = narrow_w[:, : low_rank[0]]
    rate_down_w = narrow_w[:, low_rank[0] : low_rank[0] + low_rank[1]]
    gate_down_w = narrow_w[:, low_rank[0] + low_rank[1] : sum(low_rank)]
    params_low = narrow_w[:, sum(low_rank) : sum(low_rank) + feature_params.shape[1]]
    three = lax.all_gather(
        jnp.concatenate([receptance, key_proj, value_proj], axis=1), "dp", axis=0, tiled=True
    )
    recept_w = three[:, :part_width]
    key_w = three[:, part_width : 2 * part_width]
    value_w = three[:, 2 * part_width :]
    up_rows = (decay_up.shape[0], rate_up.shape[0], gate_up.shape[0])
    ups = lax.all_gather(jnp.concatenate([decay_up, rate_up, gate_up], axis=0), "dp", axis=0)
    decay_up_w = ups[:, : up_rows[0]].reshape(-1, part_width)
    rate_up_w = ups[:, up_rows[0] : up_rows[0] + up_rows[1]].reshape(-1, part_width)
    gate_up_w = ups[:, up_rows[0] + up_rows[1] :].reshape(-1, part_width)
    output_w = lax.all_gather(output_proj, "dp", axis=1, tiled=True)
    ffn_key_w = lax.all_gather(ffn_key, "dp", axis=0, tiled=True)
    ffn_value_w = lax.all_gather(ffn_value, "dp", axis=1, tiled=True)
    params = params_low.astype(jnp.float32)
    model_width = whole.shape[1]
    mixed = section_in(whole, params[:, 0], params[:, 1], params[:, 2:8])
    mix_r, mix_w, mix_k, mix_v, mix_a, mix_g = tuple(
        (member.astype(jnp.bfloat16) for member in mixed)
    )
    acceptance_matrix = matmul(mix_r, recept_w)
    keys_in = matmul(mix_k, key_w)
    payload_source = matmul(mix_v, value_w)
    decay_hid = jnp.tanh(matmul(mix_w, decay_down_w))
    decay_low = decay_hid.astype(jnp.bfloat16)
    rate_low = matmul(mix_a, rate_down_w).astype(jnp.bfloat16)
    gate_hid = jax.nn.sigmoid(matmul(mix_g, gate_down_w))
    gate_low = gate_hid.astype(jnp.bfloat16)
    decay_in = matmul(decay_low, decay_up_w)
    rate_in = matmul(rate_low, rate_up_w)
    sigmoid_source = matmul(gate_low, gate_up_w)
    columns = lax.dynamic_slice_in_dim(params, col_start, part_width, 0)[:, 8:15].T
    columns = jnp.pad(columns, ((0, 1), (0, 0)))
    mixer_args = (
        own_lengths,
        acceptance_matrix,
        keys_in,
        payload_source,
        decay_in,
        rate_in,
        sigmoid_source,
        columns,
    )
    gated_low, *kept = run_mixer_forward(*mixer_args)
    residual = whole + line_sum(matmul(gated_low, output_w).astype(jnp.bfloat16), line_size, 2).astype(
        jnp.float32
    )
    ffn_in, back_out = jax.vjp(section_out, residual, params[:, 15], params[:, 16], params[:, 17])
    ffn_low = ffn_in.astype(jnp.bfloat16)
    pre_act = matmul(ffn_low, ffn_key_w)
    active = jnp.maximum(pre_act, 0.0)
    squared = (active * active).astype(jnp.bfloat16)
    ffn_part = line_scatter(matmul(squared, ffn_value_w).astype(jnp.bfloat16), line_size, 3)
    result = lax.dynamic_slice_in_dim(residual, col_start, part_width, 1) + ffn_part
    grad_result = loss_scale * valid[:, None] * (result - teacher.astype(jnp.float32))
    grad_low = line_gather(grad_result.astype(jnp.bfloat16), line_size, 4)
    grad_ffn_value = contract_rows(squared, grad_low).astype(jnp.bfloat16)
    grad_low, grad_ffn_value = lax.optimization_barrier((grad_low, grad_ffn_value))
    grad_ffn_value = lax.psum_scatter(grad_ffn_value, "dp", scatter_dimension=1, tiled=True)
    grad_squared = against(grad_low, ffn_value_w)
    grad_pre = (grad_squared * 2.0 * active).astype(jnp.bfloat16)
    grad_ffn_key = contract_rows(ffn_low, grad_pre).astype(jnp.bfloat16)
    grad_pre, grad_ffn_key = lax.optimization_barrier((grad_pre, grad_ffn_key))
    grad_ffn_key = lax.psum_scatter(grad_ffn_key, "dp", scatter_dimension=0, tiled=True)
    d_resid_part, d_scale_two, d_offset_two, d_mix_two = back_out(against(grad_pre, ffn_key_w))
    d_residual = grad_low.astype(jnp.float32) + line_sum(
        d_resid_part.astype(jnp.bfloat16), line_size, 5
    ).astype(jnp.float32)
    d_low = d_residual.astype(jnp.bfloat16)
    grad_output_proj = contract_rows(gated_low, d_low).astype(jnp.bfloat16)
    d_low, grad_output_proj = lax.optimization_barrier((d_low, grad_output_proj))
    grad_output_proj = lax.psum_scatter(grad_output_proj, "dp", scatter_dimension=1, tiled=True)
    d_gated = against(d_low, output_w)
    d_gated, grad_ffn_value = lax.optimization_barrier((d_gated, grad_ffn_value))
    d_recept, d_keys, d_values, d_decay, d_rate, d_gate, d_columns = run_mixer_backward(
        *mixer_args, *kept, d_gated
    )
    d_columns = jnp.sum(d_columns, axis=1)[:7]
    grad_three = weight_grads((mix_r, mix_k, mix_v), (d_recept, d_keys, d_values))
    d_decay, d_rate, d_gate, grad_three = lax.optimization_barrier((d_decay, d_rate, d_gate, grad_three))
    grad_three = lax.psum_scatter(grad_three, "dp", scatter_dimension=0, tiled=True)
    shares = [rank // line_size for rank in low_rank]
    starts = (0, shares[0], shares[0] + shares[1])
    own_rank = sum(shares) + -sum(shares) % 128

    def spread_rows(weight, share, start):
        grouped = weight.reshape(line_size, share, part_width)
        grouped = jnp.pad(grouped, ((0, 0), (start, own_rank - start - share), (0, 0)))
        return grouped.reshape(line_size * own_rank, part_width)

    def own_columns(values, share):
        return lax.dynamic_slice_in_dim(values, mp_index * share, share, 1)

    def own_group(members):
        taken = jnp.concatenate(
            [own_columns(member, share) for member, share in zip(members, shares)], axis=1
        )
        return jnp.pad(taken, ((0, 0), (0, own_rank - sum(shares))))

    d_inner = (
        against(d_decay, spread_rows(decay_up_w, shares[0], starts[0]))
        + against(d_rate, spread_rows(rate_up_w, shares[1], starts[1]))
        + against(d_gate, spread_rows(gate_up_w, shares[2], starts[2]))
    ).astype(jnp.bfloat16)
    d_own = line_scatter(d_inner, line_size, 6)
    d_own, grad_ffn_key, grad_output_proj = lax.optimization_barrier(
        (d_own, grad_ffn_key, grad_output_proj)
    )
    slope = own_group(
        (
            1.0 - decay_hid * decay_hid,
            jnp.ones((position_count, low_rank[1]), jnp.float32),
            gate_hid * (1.0 - gate_hid),
        )
    )
    d_own_pre = (d_own * slope).astype(jnp.bfloat16)
    down_own = own_group((decay_down_w, rate_down_w, gate_down_w))
    params_rows = jnp.pad(params.T, ((0, -params.shape[1] % 8), (0, 0)))
    d_in_part, d_params_in, d_down = input_backward(
        whole_low, d_recept, d_keys, d_values, d_own_pre, starts[1:], three, down_own, params_rows
    )
    up_grads = jnp.concatenate(
        [
            contract_rows(low_part, grad).reshape(groups, -1, part_width)
            for low_part, grad in ((decay_low, d_decay), (rate_low, d_rate), (gate_low, d_gate))
        ],
        axis=1,
    ).astype(jnp.bfloat16)
    d_in_part, grad_three, up_grads = lax.optimization_barrier((d_in_part, grad_three, up_grads))
    up_grads = lax.psum_scatter(up_grads, "dp", scatter_dimension=0, tiled=True)
    up_grads = up_grads.reshape(-1, part_width).astype(jnp.float32)
    core_grads = lax.dynamic_update_slice_in_dim(
        jnp.zeros((7, model_width), jnp.float32), d_columns, col_start, 1
    )
    param_rows = jnp.concatenate(
        [
            jnp.sum(d_params_in, axis=1),
            core_grads,
            d_scale_two[None],
            d_offset_two[None],
            d_mix_two[None],
        ],
        axis=0,
    )
    param_count = param_rows.shape[0]
    narrow_grads = jnp.pad(
        jnp.concatenate([d_down, param_rows], axis=0), ((0, -(own_rank + param_count) % 8), (0, 0))
    )
    d_in_part, narrow_grads = lax.optimization_barrier((d_in_part, narrow_grads))
    narrow_grads = lax.psum_scatter(narrow_grads, "dp", scatter_dimension=1, tiled=True)
    grad_hidden = lax.dynamic_slice_in_dim(d_residual, col_start, part_width, 1) + line_scatter(
        d_in_part, line_size, 7
    )
    row_block = decay_down.shape[0]
    narrow_grads = lax.all_gather(narrow_grads, "mp", axis=0)
    narrow_grads = lax.dynamic_slice_in_dim(narrow_grads, mp_index * row_block, row_block, 2)

    def down_grad(start, share):
        return narrow_grads[:, start : start + share].reshape(line_size * share, row_block).T

    grad_params = jnp.sum(narrow_grads[:, own_rank : own_rank + param_count], axis=0).T
    return (
        result.astype(jnp.bfloat16),
        grad_hidden,
        grad_params,
        down_grad(starts[0], shares[0]),
        down_grad(starts[1], shares[1]),
        down_grad(starts[2], shares[2]),
        up_grads[: up_rows[0]],
        up_grads[up_rows[0] : up_rows[0] + up_rows[1]],
        up_grads[up_rows[0] + up_rows[1] :],
        grad_three[:, :part_width].astype(jnp.float32),
        grad_three[:, part_width : 2 * part_width].astype(jnp.float32),
        grad_three[:, 2 * part_width :].astype(jnp.float32),
        grad_output_proj.astype(jnp.float32),
        grad_ffn_key.astype(jnp.float32),
        grad_ffn_value.astype(jnp.float32),
    )


def solution(mesh):
    in_specs = (
        P("dp", "mp"),
        P("dp", "mp"),
        P(),
        P(("dp", "mp"), None),
        P(("dp", "mp"), None),
        P(("dp", "mp"), None),
        P(("dp", "mp"), None),
        P("dp", "mp"),
        P("dp", "mp"),
        P("dp", "mp"),
        P("dp", "mp"),
        P("dp", "mp"),
        P("dp", "mp"),
        P("mp", "dp"),
        P("dp", "mp"),
        P("mp", "dp"),
    )
    out_specs = (
        P("dp", "mp"),
        P("dp", "mp"),
        P(("dp", "mp"), None),
        P(("dp", "mp"), None),
        P(("dp", "mp"), None),
        P(("dp", "mp"), None),
        P("dp", "mp"),
        P("dp", "mp"),
        P("dp", "mp"),
        P("dp", "mp"),
        P("dp", "mp"),
        P("dp", "mp"),
        P("mp", "dp"),
        P("dp", "mp"),
        P("mp", "dp"),
    )
    return jax.shard_map(body, mesh=mesh, in_specs=in_specs, out_specs=out_specs, check_vma=False)
```

```python
from functools import partial
import math
from types import SimpleNamespace

import jax
import jax.numpy as jnp
from jax import lax
from jax.experimental import pallas as pl
from jax.experimental.pallas import tpu as pltpu
from jax.sharding import PartitionSpec as P

norm_eps = 1e-05
SUBSPACE_SIZE = 64
SEQ_LEN = 1024
group_eps = 0.00064
CHUNK = 64
PAIR = 2 * SUBSPACE_SIZE
CHUNKS_FWD = 2
CHUNKS_BWD = 2
DECAY_SCALE = math.exp(-0.5)


def dot_nn(left_op, right_op):
    return lax.dot_general(left_op, right_op, (((1,), (0,)), ((), ())), preferred_element_type=jnp.float32)


def dot_nt(left_op, right_op):
    return lax.dot_general(left_op, right_op, (((1,), (1,)), ((), ())), preferred_element_type=jnp.float32)


def dot_tn(left_op, right_op):
    return lax.dot_general(left_op, right_op, (((0,), (0,)), ((), ())), preferred_element_type=jnp.float32)


def low(values):
    return values.astype(jnp.bfloat16)


def split_dot(ones_op, values):
    top = low(values)
    rest = values - top.astype(jnp.float32)
    mid = low(rest)
    tail = low(rest - mid.astype(jnp.float32))
    return dot_nn(ones_op, top) + dot_nn(ones_op, mid) + dot_nn(ones_op, tail)


def halves(values):
    top = low(values)
    return top, low(values - top.astype(jnp.float32))


def iota(shape, axis):
    return lax.broadcasted_iota(jnp.int32, shape, axis)


def head_masks():
    lane = iota((CHUNK, PAIR), 1)
    return lane < SUBSPACE_SIZE


def stack_heads(values):
    first = iota(values.shape, 1) < SUBSPACE_SIZE
    zero = jnp.zeros_like(values)
    return jnp.concatenate(
        [jnp.where(first, values, zero), jnp.where(first, zero, values)], axis=0
    )


def fold_heads(values):
    first = iota((CHUNK, PAIR), 1) < SUBSPACE_SIZE
    return jnp.where(first, values[:CHUNK], values[CHUNK:])


def head_ones():
    return (
        iota((PAIR, PAIR), 0) // SUBSPACE_SIZE == iota((PAIR, PAIR), 1) // SUBSPACE_SIZE
    )


def head_sum(values, ones_op):
    top = low(values)
    rest = low(values - top.astype(jnp.float32))
    return dot_nn(top, ones_op) + dot_nn(rest, ones_op)


def lower_inverses(lower_parts):
    row = iota((CHUNK, PAIR), 0)
    col = iota((CHUNK, PAIR), 1) % CHUNK
    eye = jnp.where(row == col, 1.0, 0.0)

    def times(lefts, rights):
        return [
            dot_nn(low(left_op), stack_heads(low(right_op)))
            for left_op, right_op in zip(lefts, rights)
        ]

    def plus(*lists):
        return [sum(members[1:], members[0]) for members in zip(*lists)]

    near = row // 8 == col // 8
    base = [jnp.where(near, part, 0.0) for part in lower_parts]
    square = times(base, base)
    cube = times(base, square)
    fourth = times(square, square)
    accum = [eye + first + second + third for first, second, third in zip(base, square, cube)]
    accum = plus(accum, times(accum, fourth))
    width = 8
    while width < CHUNK:
        level = (row // (2 * width) == col // (2 * width)) & (row // width != col // width)
        off = [jnp.where(level, part, 0.0) for part in lower_parts]
        accum = plus(accum, times(times(accum, off), accum))
        width *= 2
    return accum


def prepare(r, k, dw, da, cols, live, tri_op, ones_op):
    sw = jax.nn.sigmoid(dw + cols[0:1])
    full_log = -DECAY_SCALE * sw
    log_decay = jnp.where(live, full_log, 0.0)
    rate = jax.nn.sigmoid(da + cols[1:2])
    scaled = k * cols[2:3]
    inv = lax.rsqrt(head_sum(scaled * scaled, ones_op) + 1e-06)
    unit = scaled * inv
    unit_live = jnp.where(live, unit, 0.0)
    lag_scale = 1.0 + (rate - 1.0) * cols[3:4]
    lagged = jnp.where(live, k * lag_scale, 0.0)
    running = split_dot(tri_op, log_decay)
    grown = jnp.exp(running)
    before = jnp.exp(running - log_decay)
    shrunk = jnp.exp(-running)
    last = running[CHUNK - 1 : CHUNK]
    til_end = jnp.exp(last - running)
    write = unit_live * rate
    return SimpleNamespace(
        sw=sw,
        full_log=full_log,
        rate=rate,
        inv=inv,
        unit=unit,
        unit_live=unit_live,
        lag_scale=lag_scale,
        lagged=lagged,
        grown=grown,
        before=before,
        shrunk=shrunk,
        til_end=til_end,
        final=jnp.exp(last),
        read_wide=r * grown,
        write_wide=write * shrunk,
        key_wide=lagged * shrunk,
        read_hat=low(r * grown),
        remove_hat=low(-unit_live * before),
        write_hat=low(write * shrunk),
        key_hat=low(lagged * shrunk),
        write_end=low(write * til_end),
        key_end=low(lagged * til_end),
    )


def tri_masks():
    row = iota((CHUNK, PAIR), 0)
    col = iota((CHUNK, PAIR), 1) % CHUNK
    return row > col, row >= col


def mixer_forward(
    steps_per_seq,
    length_ref,
    r_ref,
    k_ref,
    v_ref,
    dw_ref,
    da_ref,
    gate_ref,
    cols_ref,
    z_ref,
    y_ref,
    t_ref,
    u_ref,
    s_ref,
    lk_ref,
    reads_ref,
    state,
):
    step = pl.program_id(0)
    within_seq = lax.rem(step, steps_per_seq)
    length = length_ref[step // steps_per_seq]

    @pl.when(within_seq == 0)
    def _():
        state[...] = jnp.zeros_like(state)

    rows_each = r_ref.shape[0]
    chunks = rows_each // CHUNK
    pairs = r_ref.shape[1] // PAIR
    ones_mask = head_ones()
    ones_op = jnp.where(ones_mask, 1.0, 0.0).astype(jnp.bfloat16)
    tri_op = jnp.where(iota((CHUNK, CHUNK), 0) >= iota((CHUNK, CHUNK), 1), 1.0, 0.0).astype(jnp.bfloat16)
    strict, within = tri_masks()
    within_two = jnp.concatenate([within, within], axis=1)
    units = [(chunk, pair) for chunk in range(chunks) for pair in range(pairs)]

    def place_of(unit):
        chunk, pair = unit
        return slice(chunk * CHUNK, (chunk + 1) * CHUNK), slice(pair * PAIR, (pair + 1) * PAIR)

    prepared, scored, lower_parts = [], [], []
    for unit in units:
        rows, lanes = place_of(unit)
        live = within_seq * rows_each + unit[0] * CHUNK + iota((CHUNK, PAIR), 0) < length
        got = prepare(
            r_ref[rows, lanes],
            k_ref[rows, lanes],
            dw_ref[rows, lanes],
            da_ref[rows, lanes],
            cols_ref[:, lanes],
            live,
            tri_op,
            ones_op,
        )
        prepared.append(got)
    for unit, got in zip(units, prepared):
        got.both = jnp.concatenate([got.remove_hat, got.read_hat], axis=0)
        past = jnp.concatenate([stack_heads(got.write_hat), stack_heads(got.key_hat)], axis=0)
        scores = dot_nt(got.both, past)
        past_rest = jnp.concatenate(
            [stack_heads(halves(got.write_wide)[1]), stack_heads(halves(got.key_wide)[1])], axis=0
        )
        got.read_rest = halves(got.read_wide)[1]
        fine = scores[CHUNK:] + (dot_nt(got.read_rest, past) + dot_nt(got.read_hat, past_rest))
        lower_parts.append(jnp.where(strict, scores[:CHUNK, :PAIR], 0.0))
        lower_key = low(jnp.where(strict, scores[:CHUNK, PAIR:], 0.0))
        reads = low(jnp.where(within_two, fine, 0.0))
        scored.append((lower_key, reads))
    solves = [low(part) for part in lower_inverses(lower_parts)]
    for unit, solve in zip(units, solves):
        t_ref[place_of(unit)] = solve
    for chunk in range(chunks):
        group = [index for index, unit in enumerate(units) if unit[0] == chunk]
        lows = [low(v_ref[place_of(units[index])]) for index in group]
        stacks = [stack_heads(values) for values in lows]
        olds = [state[units[index][1]] for index in group]
        old_parts = [halves(old) for old in olds]
        from_state = [dot_nt(prepared[index].both, old[0]) for index, old in zip(group, old_parts)]
        read_state = [
            part[CHUNK:]
            + (dot_nt(prepared[index].read_rest, old[0]) + dot_nt(prepared[index].read_hat, old[1]))
            for index, part, old in zip(group, from_state, old_parts)
        ]
        right = [
            low(part[:CHUNK] + dot_nn(scored[index][0], stack))
            for index, part, stack in zip(group, from_state, stacks)
        ]
        removed = [low(dot_nn(solves[index], stack_heads(part))) for index, part in zip(group, right)]
        for slot, index in enumerate(group):
            pair = units[index][1]
            got = prepared[index]
            ends = jnp.concatenate([got.write_end, got.key_end], axis=0)
            adds = dot_tn(jnp.concatenate([removed[slot], lows[slot]], axis=0), ends)
            state[pair] = olds[slot] * got.final + jnp.where(ones_mask, adds, 0.0)
            u_ref[place_of(units[index])] = removed[slot]
            rows, lanes = place_of(units[index])
            lk_ref[rows, lanes], reads_ref[rows, slice(2 * lanes.start, 2 * lanes.stop)] = scored[index]
            s_ref[chunk, pair] = olds[slot]
        outs = [
            read_state[slot]
            + dot_nn(scored[index][1], jnp.concatenate([stack_heads(removed[slot]), stacks[slot]], axis=0))
            for slot, index in enumerate(group)
        ]
        centred = [y - head_sum(y, ones_op) * (1.0 / SUBSPACE_SIZE) for y in outs]
        spread = [head_sum(part * part, ones_op) * (1.0 / SUBSPACE_SIZE) for part in centred]
        for slot, index in enumerate(group):
            rows, lanes = place_of(units[index])
            cols = cols_ref[:, lanes]
            normed = centred[slot] * lax.rsqrt(spread[slot] + group_eps)
            bonus = head_sum(r_ref[rows, lanes] * prepared[index].lagged * cols[4:5], ones_op)
            mixed = normed * cols[5:6] + cols[6:7] + bonus * v_ref[rows, lanes]
            y_ref[rows, lanes] = outs[slot]
            z_ref[rows, lanes] = low(mixed * gate_ref[rows, lanes])


def mixer_backward(
    steps_per_seq,
    length_ref,
    r_ref,
    k_ref,
    v_ref,
    dw_ref,
    da_ref,
    gate_ref,
    cols_ref,
    y_ref,
    t_ref,
    u_ref,
    s_ref,
    lk_ref,
    reads_ref,
    dz_ref,
    dr_ref,
    dk_ref,
    dv_ref,
    ddw_ref,
    dda_ref,
    dgate_ref,
    dcols_ref,
    dstate,
):
    step = pl.num_programs(0) - 1 - pl.program_id(0)
    within_seq = lax.rem(step, steps_per_seq)
    length = length_ref[step // steps_per_seq]

    @pl.when(within_seq == steps_per_seq - 1)
    def _():
        dstate[...] = jnp.zeros_like(dstate)

    @pl.when(pl.program_id(0) == 0)
    def _():
        dcols_ref[...] = jnp.zeros_like(dcols_ref)

    rows_each = r_ref.shape[0]
    chunks = rows_each // CHUNK
    pairs = r_ref.shape[1] // PAIR
    ones_mask = head_ones()
    ones_op = jnp.where(ones_mask, 1.0, 0.0).astype(jnp.bfloat16)
    row = iota((CHUNK, CHUNK), 0)
    col = iota((CHUNK, CHUNK), 1)
    tri_op = jnp.where(row >= col, 1.0, 0.0).astype(jnp.bfloat16)
    suffix_op = jnp.where(row <= col, 1.0, 0.0).astype(jnp.bfloat16)
    prefix_op = jnp.where(row > col, 1.0, 0.0).astype(jnp.bfloat16)
    sums_op = jnp.concatenate([suffix_op, prefix_op], axis=1)
    strict, within = tri_masks()

    def add_col(index, lanes, values):
        part = values[0:8]
        for start in range(8, CHUNK, 8):
            part = part + values[start : start + 8]
        dcols_ref[index, :, lanes] += part

    strict_two = jnp.concatenate([strict, strict], axis=1)
    within_two = jnp.concatenate([within, within], axis=1)
    all_masks = jnp.concatenate([strict_two, within_two], axis=0)
    units = [(chunk, pair) for chunk in reversed(range(chunks)) for pair in range(pairs)]
    mean_of = 1.0 / SUBSPACE_SIZE
    known = []
    for chunk, pair in units:
        rows = slice(chunk * CHUNK, (chunk + 1) * CHUNK)
        lanes = slice(pair * PAIR, (pair + 1) * PAIR)
        live = within_seq * rows_each + chunk * CHUNK + iota((CHUNK, PAIR), 0) < length
        cols = cols_ref[:, lanes]
        got = prepare(
            r_ref[rows, lanes],
            k_ref[rows, lanes],
            dw_ref[rows, lanes],
            da_ref[rows, lanes],
            cols,
            live,
            tri_op,
            ones_op,
        )
        got.rows, got.lanes, got.live, got.cols = rows, lanes, live, cols
        got.pair, got.chunk = pair, chunk
        known.append(got)
    for got in known:
        y = y_ref[got.rows, got.lanes]
        got.centred = y - head_sum(y, ones_op) * mean_of
    for got in known:
        spread = head_sum(got.centred * got.centred, ones_op) * mean_of
        got.inv_y = lax.rsqrt(spread + group_eps)
    for got in known:
        rows, lanes, cols = got.rows, got.lanes, got.cols
        r, v, dz = r_ref[rows, lanes], v_ref[rows, lanes], dz_ref[rows, lanes]
        normed = got.centred * got.inv_y
        got.bonus = head_sum(r * got.lagged * cols[4:5], ones_op)
        mixed = normed * cols[5:6] + cols[6:7] + got.bonus * v
        dgate_ref[rows, lanes] = low(dz * mixed)
        dmix = dz * gate_ref[rows, lanes]
        add_col(5, lanes, dmix * normed)
        add_col(6, lanes, dmix)
        dnormed = dmix * cols[5:6]
        got.dbonus = head_sum(dmix * v, ones_op)
        mean_grad = head_sum(dnormed, ones_op) * mean_of
        mean_prod = head_sum(dnormed * normed, ones_op) * mean_of
        got.dy_low, got.dy_rest = halves(got.inv_y * (dnormed - mean_grad - normed * mean_prod))
        got.dv = got.bonus * dmix
    for got in known:
        rows, lanes = got.rows, got.lanes
        got.both = jnp.concatenate([got.remove_hat, got.read_hat], axis=0)
        got.past = jnp.concatenate(
            [stack_heads(got.write_hat), stack_heads(got.key_hat)], axis=0
        )
        got.lower_key = lk_ref[rows, lanes]
        reads = reads_ref[rows, slice(2 * lanes.start, 2 * lanes.stop)]
        got.from_y = dot_tn(reads, got.dy_low)
        v_low = low(v_ref[rows, lanes])
        removed = u_ref[rows, lanes]
        got.sent = jnp.concatenate([removed, v_low], axis=0)
        got.stacks = jnp.concatenate([stack_heads(removed), stack_heads(v_low)], axis=0)
    for chunk in reversed(range(chunks)):
        group = [got for got in known if got.chunk == chunk]
        for got in group:
            got.later = dstate[got.pair]
            got.later_low, got.later_rest = halves(got.later)
            ends = jnp.concatenate([got.write_end, got.key_end], axis=0)
            got.from_later = dot_nt(ends, got.later_low)
        for got in group:
            dremoved = low(got.from_later[:CHUNK] + fold_heads(got.from_y[:PAIR]))
            got.dright = low(fold_heads(dot_tn(t_ref[got.rows, got.lanes], dremoved)))
        for got in group:
            got.douts = jnp.concatenate([got.dright, got.dy_low], axis=0)
            adds = dot_tn(got.douts, got.both) + dot_tn(got.dy_rest, got.read_hat)
            adds = jnp.where(ones_mask, adds, 0.0)
            dstate[got.pair] = got.later * got.final + adds
    for got in known:
        dv = got.dv + got.from_later[CHUNK:] + fold_heads(got.from_y[PAIR:])
        dv = dv + fold_heads(dot_tn(got.lower_key, got.dright))
        dv_ref[got.rows, got.lanes] = low(dv)
        dscores = dot_nt(got.douts, got.stacks)
        fine = dscores[CHUNK:] + dot_nt(got.dy_rest, got.stacks)
        dscores = low(jnp.where(all_masks, jnp.concatenate([dscores[:CHUNK], fine], axis=0), 0.0))
        old_wide = s_ref[got.chunk, got.pair]
        old_low, old_rest = halves(old_wide)
        from_old = dot_nn(got.douts, old_low)
        fine = from_old[CHUNK:] + (dot_nn(got.dy_rest, old_low) + dot_nn(got.dy_low, old_rest))
        got.dboth = jnp.concatenate([from_old[:CHUNK], fine], axis=0) + dot_nn(dscores, got.past)
        dpast = dot_tn(dscores, got.both)
        got.dwrite_hat = fold_heads(dpast[:PAIR])
        got.dkey_hat = fold_heads(dpast[PAIR:])
        got.dends = dot_nn(got.sent, got.later_low) + dot_nn(got.sent, got.later_rest)
        got.dfinal = jnp.sum(got.later * old_wide, axis=0, keepdims=True)
    for got in known:
        rows, lanes, cols, live = got.rows, got.lanes, got.cols, got.live

        def wide(values):
            return values.astype(jnp.float32)

        r, k = r_ref[rows, lanes], k_ref[rows, lanes]
        dwrite_hat, dkey_hat = got.dwrite_hat, got.dkey_hat
        dwrite_end, dkey_end = got.dends[:CHUNK], got.dends[CHUNK:]
        dremove_hat, dread_hat = got.dboth[:CHUNK], got.dboth[CHUNK:]
        dbonus, lagged = got.dbonus, got.lagged
        bonus_lag = dbonus * lagged
        add_col(4, lanes, bonus_lag * r)
        dr_ref[rows, lanes] = low(bonus_lag * cols[4:5] + dread_hat * got.grown)
        minus = wide(got.remove_hat) * dremove_hat
        plus = wide(got.read_hat) * dread_hat + minus
        plus = plus - wide(got.write_hat) * dwrite_hat - wide(got.key_hat) * dkey_hat
        ending = wide(got.write_end) * dwrite_end + wide(got.key_end) * dkey_end
        sums = split_dot(sums_op, jnp.concatenate([plus, ending], axis=0))
        dlog = sums - minus + got.final * got.dfinal
        ddw = jnp.where(live, dlog * got.full_log * (1.0 - got.sw), 0.0)
        add_col(0, lanes, ddw)
        ddw_ref[rows, lanes] = low(ddw)
        dwrite = dwrite_hat * got.shrunk + dwrite_end * got.til_end
        dlag = dbonus * r * cols[4:5] + dkey_hat * got.shrunk + dkey_end * got.til_end
        dlag = jnp.where(live, dlag, 0.0)
        rate = got.rate
        dunit = jnp.where(live, dwrite * rate - dremove_hat * got.before, 0.0)
        lag_k = dlag * k
        drate = dwrite * got.unit_live + lag_k * cols[3:4]
        add_col(3, lanes, lag_k * (rate - 1.0))
        dscaled = got.inv * (dunit - got.unit * head_sum(dunit * got.unit, ones_op))
        add_col(2, lanes, dscaled * k)
        dk_ref[rows, lanes] = low(dlag * got.lag_scale + dscaled * cols[2:3])
        dda = drate * rate * (1.0 - rate)
        add_col(1, lanes, dda)
        dda_ref[rows, lanes] = low(dda)


def run_mixer_forward(lengths, r, k, v, dw, da, gate, cols):
    positions, part_width = r.shape
    rows_each = CHUNKS_FWD * CHUNK
    steps = positions // rows_each
    steps_per_seq = SEQ_LEN // rows_each
    pairs = part_width // PAIR
    wide = pl.BlockSpec((rows_each, part_width), lambda i: (i, 0))
    shape = jax.ShapeDtypeStruct
    return pl.pallas_call(
        partial(mixer_forward, steps_per_seq),
        grid=(steps,),
        in_specs=[pl.BlockSpec(memory_space=pltpu.SMEM)]
        + [wide] * 6
        + [pl.BlockSpec((8, part_width), lambda i: (0, 0))],
        out_specs=[wide] * 4
        + [
            pl.BlockSpec((CHUNKS_FWD, pairs, PAIR, PAIR), lambda i: (i, 0, 0, 0)),
            wide,
            pl.BlockSpec((rows_each, 2 * part_width), lambda i: (i, 0)),
        ],
        out_shape=[
            shape((positions, part_width), jnp.bfloat16),
            shape((positions, part_width), jnp.float32),
            shape((positions, part_width), jnp.bfloat16),
            shape((positions, part_width), jnp.bfloat16),
            shape((positions // CHUNK, pairs, PAIR, PAIR), jnp.float32),
            shape((positions, part_width), jnp.bfloat16),
            shape((positions, 2 * part_width), jnp.bfloat16),
        ],
        scratch_shapes=[pltpu.VMEM((pairs, PAIR, PAIR), jnp.float32)],
        compiler_params=pltpu.CompilerParams(
            dimension_semantics=("arbitrary",), vmem_limit_bytes=40 * 1024 * 1024
        ),
        name="mixer_forward",
    )(lengths, r, k, v, dw, da, gate, cols)


def run_mixer_backward(lengths, r, k, v, dw, da, gate, cols, y, t, u, s, lk, reads, dz):
    positions, part_width = r.shape
    rows_each = CHUNKS_BWD * CHUNK
    steps = positions // rows_each
    steps_per_seq = SEQ_LEN // rows_each
    pairs = part_width // PAIR
    wide = pl.BlockSpec((rows_each, part_width), lambda i: (steps - 1 - i, 0))
    shape = jax.ShapeDtypeStruct
    return pl.pallas_call(
        partial(mixer_backward, steps_per_seq),
        grid=(steps,),
        in_specs=[pl.BlockSpec(memory_space=pltpu.SMEM)]
        + [wide] * 6
        + [pl.BlockSpec((8, part_width), lambda i: (0, 0))]
        + [wide] * 3
        + [
            pl.BlockSpec((CHUNKS_BWD, pairs, PAIR, PAIR), lambda i: (steps - 1 - i, 0, 0, 0)),
            wide,
            pl.BlockSpec((rows_each, 2 * part_width), lambda i: (steps - 1 - i, 0)),
            wide,
        ],
        out_specs=[wide] * 6 + [pl.BlockSpec((8, 8, part_width), lambda i: (0, 0, 0))],
        out_shape=[shape((positions, part_width), jnp.bfloat16)] * 6
        + [shape((8, 8, part_width), jnp.float32)],
        scratch_shapes=[pltpu.VMEM((pairs, PAIR, PAIR), jnp.float32)],
        compiler_params=pltpu.CompilerParams(
            dimension_semantics=("arbitrary",), vmem_limit_bytes=40 * 1024 * 1024
        ),
        name="mixer_backward",
    )(lengths, r, k, v, dw, da, gate, cols, y, t, u, s, lk, reads, dz)


LINE = "mp"
END_LAG = 3
MID_LAG = 1


def link_cost(elements):
    return elements * 2 * 2 * 40


def line_barrier(size):
    me = lax.axis_index(LINE)
    barrier = pltpu.get_barrier_semaphore()

    @pl.when(me > 0)
    def _():
        pl.semaphore_signal(barrier, inc=1, device_id={LINE: me - 1}, device_id_type=pl.DeviceIdType.MESH)

    @pl.when(me < size - 1)
    def _():
        pl.semaphore_signal(barrier, inc=1, device_id={LINE: me + 1}, device_id_type=pl.DeviceIdType.MESH)

    ends = jnp.where((me == 0) | (me == size - 1), 1, 2)
    pl.semaphore_wait(barrier, ends)


class Flow:
    def __init__(self, size, side):
        self.size = size
        self.side = side
        self.me = lax.axis_index(LINE)
        self.step = 1 - 2 * side
        self.target = self.me + self.step
        source = self.me - self.step
        self.has_source = (source >= 0) & (source < size)
        self.has_target = (self.target >= 0) & (self.target < size)

    def copy(self, source, place, send_sem, recv_sem):
        return pltpu.make_async_remote_copy(
            src_ref=source,
            dst_ref=place,
            send_sem=send_sem,
            recv_sem=recv_sem,
            device_id={LINE: self.target},
            device_id_type=pl.DeviceIdType.MESH,
        )


def two_flows(size):
    me = lax.axis_index(LINE)
    near = jnp.where(me < size // 2, 0, 1)
    return Flow(size, near), Flow(size, 1 - near)


def line_sum_kernel(size, chunk_rows, x_ref, out_ref, got, sent, send_sem, recv_sem):
    line_barrier(size)
    me = lax.axis_index(LINE)
    flows = two_flows(size)
    chunks = x_ref.shape[0] // chunk_rows

    def copy_of(flow, chunk, source):
        rows = pl.ds(pl.multiple_of(chunk * chunk_rows, chunk_rows), chunk_rows)
        return flow.copy(
            source.at[rows], got.at[flow.side, rows], send_sem.at[flow.side, chunk], recv_sem.at[flow.side, chunk]
        )

    def pass_on(flow, chunk):
        rows = pl.ds(pl.multiple_of(chunk * chunk_rows, chunk_rows), chunk_rows)

        @pl.when(flow.has_source)
        def _():
            copy_of(flow, chunk, x_ref).wait_recv()

        @pl.when(flow.has_source & flow.has_target)
        def _():
            total = got[flow.side, rows].astype(jnp.float32) + x_ref[rows].astype(jnp.float32)
            sent[flow.side, rows] = total.astype(sent.dtype)
            copy_of(flow, chunk, sent.at[flow.side]).start()

        @pl.when(jnp.logical_not(flow.has_source))
        def _():
            copy_of(flow, chunk, x_ref).start()

    is_end = (me == 0) | (me == size - 1)
    lag = jnp.where(is_end, END_LAG, MID_LAG)

    def step(turn, carry):
        @pl.when(turn < chunks)
        def _():
            pass_on(flows[0], turn)

        chunk = turn - lag

        @pl.when((chunk >= 0) & (chunk < chunks))
        def _():
            pass_on(flows[1], chunk)
            rows = pl.ds(pl.multiple_of(chunk * chunk_rows, chunk_rows), chunk_rows)

            @pl.when(is_end)
            def _():
                other = got[flows[1].side, rows].astype(jnp.float32)
                out_ref[rows] = (other + x_ref[rows].astype(jnp.float32)).astype(out_ref.dtype)

            @pl.when(jnp.logical_not(is_end))
            def _():
                other = got[0, rows].astype(jnp.float32) + got[1, rows].astype(jnp.float32)
                out_ref[rows] = (other + x_ref[rows].astype(jnp.float32)).astype(out_ref.dtype)

        return carry

    lax.fori_loop(0, chunks + END_LAG, step, 0)

    def drain(chunk, carry):
        for flow in flows:

            @pl.when(flow.has_target)
            def _():
                copy_of(flow, chunk, x_ref).wait_send()

        return carry

    lax.fori_loop(0, chunks, drain, 0)


def line_sum(x, size, collective_id, chunk_rows=64):
    rows, cols = x.shape
    chunks = rows // chunk_rows
    return pl.pallas_call(
        partial(line_sum_kernel, size, chunk_rows),
        out_shape=jax.ShapeDtypeStruct(x.shape, x.dtype),
        in_specs=[pl.BlockSpec(memory_space=pltpu.VMEM)],
        out_specs=pl.BlockSpec(memory_space=pltpu.VMEM),
        scratch_shapes=[
            pltpu.VMEM((2, rows, cols), x.dtype),
            pltpu.VMEM((2, rows, cols), x.dtype),
            pltpu.SemaphoreType.DMA((2, chunks)),
            pltpu.SemaphoreType.DMA((2, chunks)),
        ],
        compiler_params=pltpu.CompilerParams(
            collective_id=collective_id, has_side_effects=True, vmem_limit_bytes=48 * 1024 * 1024
        ),
        cost_estimate=pl.CostEstimate(flops=0, bytes_accessed=link_cost(rows * cols), transcendentals=0),
        name="line_sum",
    )(x)


def line_gather_kernel(size, chunk_rows, x_ref, out_ref, send_sem, recv_sem):
    line_barrier(size)
    me = lax.axis_index(LINE)
    flows = two_flows(size)
    width = x_ref.shape[1]
    chunks = x_ref.shape[0] // chunk_rows

    def place(block, chunk):
        rows = pl.ds(pl.multiple_of(chunk * chunk_rows, chunk_rows), chunk_rows)
        return out_ref.at[rows, pl.ds(pl.multiple_of(block * width, width), width)]

    def copy_of(flow, block, chunk):
        return flow.copy(
            place(block, chunk), place(block, chunk), send_sem.at[flow.side, block, chunk], recv_sem.at[flow.side, block, chunk]
        )

    def step(chunk, carry):
        rows = pl.ds(pl.multiple_of(chunk * chunk_rows, chunk_rows), chunk_rows)
        out_ref[rows, pl.ds(pl.multiple_of(me * width, width), width)] = x_ref[rows]
        for flow in flows:

            @pl.when(flow.has_target)
            def _():
                copy_of(flow, me, chunk).start()

        return carry

    lax.fori_loop(0, chunks, step, 0)
    for hop in range(1, size):

        def forward(chunk, carry):
            for flow in flows:
                block = me - hop * flow.step
                exists = (block >= 0) & (block < size)

                @pl.when(exists)
                def _():
                    copy_of(flow, block, chunk).wait_recv()

                @pl.when(exists & flow.has_target)
                def _():
                    copy_of(flow, block, chunk).start()

            return carry

        lax.fori_loop(0, chunks, forward, 0)
    for hop in range(size):

        def drain(chunk, carry):
            for flow in flows:
                block = me - hop * flow.step
                exists = (block >= 0) & (block < size)

                @pl.when(exists & flow.has_target)
                def _():
                    copy_of(flow, block, chunk).wait_send()

            return carry

        lax.fori_loop(0, chunks, drain, 0)


def line_gather(x, size, collective_id, chunk_rows=256):
    rows, cols = x.shape
    chunks = rows // chunk_rows
    return pl.pallas_call(
        partial(line_gather_kernel, size, chunk_rows),
        out_shape=jax.ShapeDtypeStruct((rows, size * cols), x.dtype),
        in_specs=[pl.BlockSpec(memory_space=pltpu.VMEM)],
        out_specs=pl.BlockSpec(memory_space=pltpu.VMEM),
        scratch_shapes=[
            pltpu.SemaphoreType.DMA((2, size, chunks)),
            pltpu.SemaphoreType.DMA((2, size, chunks)),
        ],
        compiler_params=pltpu.CompilerParams(
            collective_id=collective_id, has_side_effects=True, vmem_limit_bytes=48 * 1024 * 1024
        ),
        cost_estimate=pl.CostEstimate(flops=0, bytes_accessed=link_cost(3 * rows * cols), transcendentals=0),
        name="line_gather",
    )(x)


def line_scatter_kernel(size, chunk_rows, x_ref, out_ref, got, sent, send_sem, recv_sem):
    line_barrier(size)
    me = lax.axis_index(LINE)
    flows = two_flows(size)
    width = out_ref.shape[1]
    chunks = x_ref.shape[0] // chunk_rows

    def rows_of(chunk):
        return pl.ds(pl.multiple_of(chunk * chunk_rows, chunk_rows), chunk_rows)

    def cols_of(block):
        return pl.ds(pl.multiple_of(block * width, width), width)

    def copy_of(flow, block, chunk, source):
        return flow.copy(
            source,
            got.at[flow.side, rows_of(chunk), cols_of(block)],
            send_sem.at[flow.side, block, chunk],
            recv_sem.at[flow.side, block, chunk],
        )

    def own(block, chunk):
        return x_ref[rows_of(chunk), cols_of(block)].astype(jnp.float32)

    for hop in range(size - 1):

        def forward(chunk, carry):
            for flow in flows:
                block = jnp.where(flow.side == 0, size - 1 - hop, hop)
                ahead = (block - me) * flow.step > 0

                @pl.when(ahead & flow.has_source)
                def _():
                    source = x_ref.at[rows_of(chunk), cols_of(block)]
                    copy_of(flow, block, chunk, source).wait_recv()
                    total = got[flow.side, rows_of(chunk), cols_of(block)].astype(jnp.float32) + own(block, chunk)
                    sent[flow.side, rows_of(chunk), cols_of(block)] = total.astype(sent.dtype)
                    copy_of(flow, block, chunk, sent.at[flow.side, rows_of(chunk), cols_of(block)]).start()

                @pl.when(ahead & jnp.logical_not(flow.has_source))
                def _():
                    copy_of(flow, block, chunk, x_ref.at[rows_of(chunk), cols_of(block)]).start()

            return carry

        lax.fori_loop(0, chunks, forward, 0)

    def finish(chunk, carry):
        rows = rows_of(chunk)
        for flow in flows:

            @pl.when(flow.has_source)
            def _():
                copy_of(flow, me, chunk, x_ref.at[rows, cols_of(me)]).wait_recv()

        @pl.when(me == 0)
        def _():
            out_ref[rows] = (got[1, rows, cols_of(me)].astype(jnp.float32) + own(me, chunk)).astype(out_ref.dtype)

        @pl.when(me == size - 1)
        def _():
            out_ref[rows] = (got[0, rows, cols_of(me)].astype(jnp.float32) + own(me, chunk)).astype(out_ref.dtype)

        @pl.when((me > 0) & (me < size - 1))
        def _():
            other = got[0, rows, cols_of(me)].astype(jnp.float32) + got[1, rows, cols_of(me)].astype(jnp.float32)
            out_ref[rows] = (other + own(me, chunk)).astype(out_ref.dtype)

        return carry

    lax.fori_loop(0, chunks, finish, 0)
    for hop in range(size - 1):

        def drain(chunk, carry):
            for flow in flows:
                block = jnp.where(flow.side == 0, size - 1 - hop, hop)
                ahead = (block - me) * flow.step > 0

                @pl.when(ahead)
                def _():
                    copy_of(flow, block, chunk, x_ref.at[rows_of(chunk), cols_of(block)]).wait_send()

            return carry

        lax.fori_loop(0, chunks, drain, 0)


def line_scatter(x, size, collective_id, out_dtype=jnp.float32, chunk_rows=256):
    rows, cols = x.shape
    chunks = rows // chunk_rows
    return pl.pallas_call(
        partial(line_scatter_kernel, size, chunk_rows),
        out_shape=jax.ShapeDtypeStruct((rows, cols // size), out_dtype),
        in_specs=[pl.BlockSpec(memory_space=pltpu.VMEM)],
        out_specs=pl.BlockSpec(memory_space=pltpu.VMEM),
        scratch_shapes=[
            pltpu.VMEM((2, rows, cols), x.dtype),
            pltpu.VMEM((2, rows, cols), x.dtype),
            pltpu.SemaphoreType.DMA((2, size, chunks)),
            pltpu.SemaphoreType.DMA((2, size, chunks)),
        ],
        compiler_params=pltpu.CompilerParams(
            collective_id=collective_id, has_side_effects=True, vmem_limit_bytes=48 * 1024 * 1024
        ),
        cost_estimate=pl.CostEstimate(flops=0, bytes_accessed=link_cost(3 * rows * cols // size), transcendentals=0),
        name="line_scatter",
    )(x)


def input_backward_kernel(
    seq_len, splits, whole_ref, dr_ref, dk_ref, dv_ref, dl_ref, three_ref, down_ref, params_ref, din_ref, gparams_ref, gdown_ref, carry, kept
):
    step = pl.program_id(0)
    tile = pl.num_programs(0) - 1 - step
    rows_each = dr_ref.shape[0]
    part = dr_ref.shape[1]
    width = whole_ref.shape[1]
    start = tile * rows_each
    at_start = lax.rem(start, seq_len) == 0
    at_end = lax.rem(start + rows_each, seq_len) == 0

    @pl.when(step == 0)
    def _():
        gparams_ref[...] = jnp.zeros_like(gparams_ref)
        gdown_ref[...] = jnp.zeros_like(gdown_ref)

    @pl.when(at_end)
    def _():
        carry[...] = jnp.zeros_like(carry)

    edge = 16
    rows = pl.ds(pl.multiple_of(start, rows_each), rows_each)
    edge_rows = pl.ds(pl.multiple_of(jnp.maximum(start - edge, 0), edge), edge)
    inverse_width = 1.0 / width

    def moments(place):
        values = whole_ref[place, :].astype(jnp.float32)
        centre = jnp.sum(values, axis=1, keepdims=True) * inverse_width
        values = values - centre
        spread = jnp.sum(values * values, axis=1, keepdims=True) * inverse_width
        return centre, lax.rsqrt(spread + norm_eps)

    centre, inv = moments(rows)
    edge_centre, edge_inv = moments(edge_rows)
    block_cols = 256
    row_index = iota((rows_each, block_cols), 0)
    dl = dl_ref[...]
    lane = iota(dl.shape, 1)
    zero = jnp.zeros_like(dl)
    first, second = splits
    dls = (
        jnp.where(lane < first, dl, zero),
        jnp.where((lane >= first) & (lane < second), dl, zero),
        jnp.where(lane >= second, dl, zero),
    )
    down_row = iota((dl.shape[1], block_cols), 0)
    sum_grad = jnp.zeros((rows_each, 1), jnp.float32)
    sum_prod = jnp.zeros((rows_each, 1), jnp.float32)

    def add_param(index, cols, values):
        total = values[0:8]
        for place in range(8, rows_each, 8):
            total = total + values[place : place + 8]
        gparams_ref[index, :, cols] += total

    for block in range(width // block_cols):
        cols = slice(block * block_cols, (block + 1) * block_cols)
        gain, bias = params_ref[0:1, cols], params_ref[1:2, cols]
        unit = (whole_ref[rows, cols].astype(jnp.float32) - centre) * inv
        normed = unit * gain + bias
        edge_unit = (whole_ref[edge_rows, cols].astype(jnp.float32) - edge_centre) * edge_inv
        edge_normed = (edge_unit * gain + bias)[edge - 1 : edge]
        edge_normed = jnp.where(at_start, 0.0, edge_normed)
        before = jnp.where(row_index == 0, edge_normed, pltpu.roll(normed, 1, 0))
        shift = before - normed
        down = down_ref[cols, :]
        weights = three_ref[cols, :]
        grads = (
            dot_nt(dr_ref[...], weights[:, :part]),
            dot_nt(dls[0], down),
            dot_nt(dk_ref[...], weights[:, part : 2 * part]),
            dot_nt(dv_ref[...], weights[:, 2 * part :]),
            dot_nt(dls[1], down),
            dot_nt(dls[2], down),
        )
        total = grads[0]
        for grad in grads[1:]:
            total = total + grad
        mixed = None
        for index, grad in enumerate(grads):
            rate = params_ref[2 + index : 3 + index, cols]
            mixed = grad * rate if mixed is None else mixed + grad * rate
            add_param(2 + index, cols, grad * shift)
        after = jnp.where(row_index == rows_each - 1, carry[0:1, cols], pltpu.roll(mixed, rows_each - 1, 0))
        carry[0:1, cols] = mixed[0:1]
        dnormed = total - mixed + after
        add_param(0, cols, dnormed * unit)
        add_param(1, cols, dnormed)
        dunit = dnormed * gain
        kept[:, cols] = dunit
        sum_grad = sum_grad + jnp.sum(dunit, axis=1, keepdims=True)
        sum_prod = sum_prod + jnp.sum(dunit * unit, axis=1, keepdims=True)
        outs = [
            dot_tn(dl, low(normed + shift * params_ref[index : index + 1, cols])) for index in (3, 6, 7)
        ]
        gdown_ref[:, cols] += jnp.where(
            down_row < first, outs[0], jnp.where(down_row < second, outs[1], outs[2])
        )
    sum_grad = sum_grad * inverse_width
    sum_prod = sum_prod * inverse_width
    for block in range(width // block_cols):
        cols = slice(block * block_cols, (block + 1) * block_cols)
        unit = (whole_ref[rows, cols].astype(jnp.float32) - centre) * inv
        din_ref[:, cols] = low(inv * (kept[:, cols] - sum_grad - unit * sum_prod))


def input_backward(whole, dr, dk, dv, dl, splits, three, down, params):
    positions, width = whole.shape
    part = dr.shape[1]
    rows_each = 256
    steps = positions // rows_each
    tile = lambda cols: pl.BlockSpec((rows_each, cols), lambda i: (steps - 1 - i, 0))
    full = pl.BlockSpec(memory_space=pltpu.VMEM)
    shape = jax.ShapeDtypeStruct
    return pl.pallas_call(
        partial(input_backward_kernel, SEQ_LEN, splits),
        grid=(steps,),
        in_specs=[full, tile(part), tile(part), tile(part), tile(dl.shape[1]), full, full, full],
        out_specs=[
            tile(width),
            pl.BlockSpec((8, 8, width), lambda i: (0, 0, 0)),
            pl.BlockSpec((dl.shape[1], width), lambda i: (0, 0)),
        ],
        out_shape=[
            shape((positions, width), jnp.bfloat16),
            shape((8, 8, width), jnp.float32),
            shape((dl.shape[1], width), jnp.float32),
        ],
        scratch_shapes=[pltpu.VMEM((8, width), jnp.float32), pltpu.VMEM((rows_each, width), jnp.float32)],
        compiler_params=pltpu.CompilerParams(
            dimension_semantics=("arbitrary",), vmem_limit_bytes=48 * 1024 * 1024
        ),
        name="input_backward",
    )(whole, dr, dk, dv, dl, three, down, params)


def weight_grads_kernel(left_refs, right_refs, out_ref):
    part = right_refs[0].shape[1]
    for index, (left_ref, right_ref) in enumerate(zip(left_refs, right_refs)):
        out_ref[:, index * part : (index + 1) * part] = low(dot_tn(left_ref[...], right_ref[...]))


def weight_grads(lefts, rights):
    positions, width = lefts[0].shape
    part = rights[0].shape[1]
    count = len(lefts)
    block = 512

    def kernel(*refs):
        weight_grads_kernel(refs[:count], refs[count : 2 * count], refs[2 * count])

    return pl.pallas_call(
        kernel,
        grid=(width // block,),
        in_specs=[pl.BlockSpec((positions, block), lambda i: (0, i))] * count
        + [pl.BlockSpec((positions, part), lambda i: (0, 0))] * count,
        out_specs=pl.BlockSpec((block, count * part), lambda i: (i, 0)),
        out_shape=jax.ShapeDtypeStruct((width, count * part), jnp.bfloat16),
        compiler_params=pltpu.CompilerParams(
            dimension_semantics=("arbitrary",), vmem_limit_bytes=40 * 1024 * 1024
        ),
        name="weight_grads",
    )(*lefts, *rights)


def line_error_kernel(
    size, chunk_rows, x_ref, base_ref, teacher_ref, weight_ref, state_ref, error_ref, got, sent, send_sem, recv_sem, out_send_sem, out_recv_sem
):
    line_barrier(size)
    me = lax.axis_index(LINE)
    flows = two_flows(size)
    width = base_ref.shape[1]
    chunks = x_ref.shape[0] // chunk_rows
    is_end = (me == 0) | (me == size - 1)
    lag = jnp.where(is_end, END_LAG, MID_LAG)

    def rows_of(chunk):
        return pl.ds(pl.multiple_of(chunk * chunk_rows, chunk_rows), chunk_rows)

    def cols_of(block):
        return pl.ds(pl.multiple_of(block * width, width), width)

    def part_copy(flow, block, chunk, source):
        place = (rows_of(chunk), cols_of(block))
        return flow.copy(
            source.at[place],
            got.at[(flow.side,) + place],
            send_sem.at[flow.side, block, chunk],
            recv_sem.at[flow.side, block, chunk],
        )

    def error_copy(flow, block, chunk):
        place = error_ref.at[rows_of(chunk), cols_of(block)]
        return flow.copy(
            place, place, out_send_sem.at[flow.side, block, chunk], out_recv_sem.at[flow.side, block, chunk]
        )

    def target_of(flow, hop):
        block = jnp.where(flow.side == 0, size - 1 - hop, hop)
        return block, (block - me) * flow.step > 0

    def reduce_part(flow, chunk):
        for hop in range(size - 1):
            block, ahead = target_of(flow, hop)

            @pl.when(ahead & flow.has_source)
            def _():
                part_copy(flow, block, chunk, x_ref).wait_recv()
                place = (rows_of(chunk), cols_of(block))
                total = got[(flow.side,) + place].astype(jnp.float32) + x_ref[place].astype(jnp.float32)
                sent[(flow.side,) + place] = total.astype(sent.dtype)
                part_copy(flow, block, chunk, sent.at[flow.side]).start()

            @pl.when(ahead & jnp.logical_not(flow.has_source))
            def _():
                part_copy(flow, block, chunk, x_ref).start()

    def finish(chunk):
        rows = rows_of(chunk)
        for flow in flows:

            @pl.when(flow.has_source)
            def _():
                part_copy(flow, me, chunk, x_ref).wait_recv()

        def write(others):
            result = base_ref[rows] + (others + x_ref[rows, cols_of(me)].astype(jnp.float32))
            state_ref[rows] = result.astype(state_ref.dtype)
            error = weight_ref[rows, 0:1] * (result - teacher_ref[rows].astype(jnp.float32))
            error_ref[rows, cols_of(me)] = error.astype(error_ref.dtype)

        @pl.when(is_end)
        def _():
            write(got[flows[1].side, rows, cols_of(me)].astype(jnp.float32))

        @pl.when(jnp.logical_not(is_end))
        def _():
            write(
                got[0, rows, cols_of(me)].astype(jnp.float32) + got[1, rows, cols_of(me)].astype(jnp.float32)
            )

        for flow in flows:

            @pl.when(flow.has_target)
            def _():
                error_copy(flow, me, chunk).start()

    def forward(hop, chunk):
        for flow in flows:
            block = me - hop * flow.step
            exists = (block >= 0) & (block < size)

            @pl.when(exists)
            def _():
                error_copy(flow, block, chunk).wait_recv()

            @pl.when(exists & flow.has_target)
            def _():
                error_copy(flow, block, chunk).start()

    def at(chunk, action):
        @pl.when((chunk >= 0) & (chunk < chunks))
        def _():
            action(chunk)

    def step(turn, carry):
        at(turn, lambda chunk: reduce_part(flows[0], chunk))
        at(turn - lag, lambda chunk: reduce_part(flows[1], chunk))
        at(turn - lag - 1, finish)
        for hop in range(1, size):
            at(turn - lag - 1 - 2 * hop, partial(forward, hop))
        return carry

    lax.fori_loop(0, chunks + END_LAG + 1 + 2 * (size - 1), step, 0)

    def drain(chunk, carry):
        for flow in flows:
            for hop in range(size - 1):
                block, ahead = target_of(flow, hop)

                @pl.when(ahead)
                def _():
                    part_copy(flow, block, chunk, x_ref).wait_send()

            for hop in range(size):
                source = me - hop * flow.step
                exists = (source >= 0) & (source < size)

                @pl.when(exists & flow.has_target)
                def _():
                    error_copy(flow, source, chunk).wait_send()

        return carry

    lax.fori_loop(0, chunks, drain, 0)


def line_error(x, base, teacher, weight, size, collective_id, chunk_rows=64):
    rows, cols = x.shape
    chunks = rows // chunk_rows
    sems = pltpu.SemaphoreType.DMA((2, size, chunks))
    return pl.pallas_call(
        partial(line_error_kernel, size, chunk_rows),
        out_shape=[
            jax.ShapeDtypeStruct(base.shape, jnp.bfloat16),
            jax.ShapeDtypeStruct(x.shape, jnp.bfloat16),
        ],
        in_specs=[pl.BlockSpec(memory_space=pltpu.VMEM)] * 4,
        out_specs=[pl.BlockSpec(memory_space=pltpu.VMEM)] * 2,
        scratch_shapes=[
            pltpu.VMEM((2, rows, cols), x.dtype),
            pltpu.VMEM((2, rows, cols), x.dtype),
            sems,
            sems,
            sems,
            sems,
        ],
        compiler_params=pltpu.CompilerParams(
            collective_id=collective_id, has_side_effects=True, vmem_limit_bytes=48 * 1024 * 1024
        ),
        cost_estimate=pl.CostEstimate(flops=0, bytes_accessed=link_cost(rows * cols), transcendentals=0),
        name="line_error",
    )(x, base, teacher, weight)


def output_backward_kernel(
    seq_len, whole_ref, delta_ref, dpre_ref, weight_ref, params_ref, dres_ref, gparams_ref, carry, kept
):
    step = pl.program_id(0)
    tile = pl.num_programs(0) - 1 - step
    rows_each = dpre_ref.shape[0]
    width = whole_ref.shape[1]
    start = tile * rows_each
    at_start = lax.rem(start, seq_len) == 0
    at_end = lax.rem(start + rows_each, seq_len) == 0

    @pl.when(step == 0)
    def _():
        gparams_ref[...] = jnp.zeros_like(gparams_ref)

    @pl.when(at_end)
    def _():
        carry[...] = jnp.zeros_like(carry)

    edge = 16
    rows = pl.ds(pl.multiple_of(start, rows_each), rows_each)
    edge_rows = pl.ds(pl.multiple_of(jnp.maximum(start - edge, 0), edge), edge)
    inverse_width = 1.0 / width

    def residual(place, cols):
        return whole_ref[place, cols].astype(jnp.float32) + delta_ref[place, cols].astype(jnp.float32)

    def moments(place):
        values = residual(place, slice(0, width))
        centre = jnp.sum(values, axis=1, keepdims=True) * inverse_width
        values = values - centre
        spread = jnp.sum(values * values, axis=1, keepdims=True) * inverse_width
        return centre, lax.rsqrt(spread + norm_eps)

    centre, inv = moments(rows)
    edge_centre, edge_inv = moments(edge_rows)
    block_cols = 256
    row_index = iota((rows_each, block_cols), 0)
    sum_grad = jnp.zeros((rows_each, 1), jnp.float32)
    sum_prod = jnp.zeros((rows_each, 1), jnp.float32)

    def add_param(index, cols, values):
        total = values[0:8]
        for place in range(8, rows_each, 8):
            total = total + values[place : place + 8]
        gparams_ref[index, :, cols] += total

    for block in range(width // block_cols):
        cols = slice(block * block_cols, (block + 1) * block_cols)
        gain, bias, rate = params_ref[0:1, cols], params_ref[1:2, cols], params_ref[2:3, cols]
        unit = (residual(rows, cols) - centre) * inv
        normed = unit * gain + bias
        edge_unit = (residual(edge_rows, cols) - edge_centre) * edge_inv
        edge_normed = (edge_unit * gain + bias)[edge - 1 : edge]
        edge_normed = jnp.where(at_start, 0.0, edge_normed)
        before = jnp.where(row_index == 0, edge_normed, pltpu.roll(normed, 1, 0))
        grad = dot_nt(dpre_ref[...], weight_ref[cols, :])
        add_param(2, cols, grad * (before - normed))
        mixed = grad * rate
        after = jnp.where(row_index == rows_each - 1, carry[0:1, cols], pltpu.roll(mixed, rows_each - 1, 0))
        carry[0:1, cols] = mixed[0:1]
        dnormed = grad - mixed + after
        add_param(0, cols, dnormed * unit)
        add_param(1, cols, dnormed)
        dunit = dnormed * gain
        kept[:, cols] = dunit
        sum_grad = sum_grad + jnp.sum(dunit, axis=1, keepdims=True)
        sum_prod = sum_prod + jnp.sum(dunit * unit, axis=1, keepdims=True)
    sum_grad = sum_grad * inverse_width
    sum_prod = sum_prod * inverse_width
    for block in range(width // block_cols):
        cols = slice(block * block_cols, (block + 1) * block_cols)
        unit = (residual(rows, cols) - centre) * inv
        dres_ref[:, cols] = low(inv * (kept[:, cols] - sum_grad - unit * sum_prod))


def output_backward(whole, delta, dpre, weight, params):
    positions, width = whole.shape
    rows_each = 256
    steps = positions // rows_each
    tile = lambda cols: pl.BlockSpec((rows_each, cols), lambda i: (steps - 1 - i, 0))
    full = pl.BlockSpec(memory_space=pltpu.VMEM)
    return pl.pallas_call(
        partial(output_backward_kernel, SEQ_LEN),
        grid=(steps,),
        in_specs=[full, full, tile(dpre.shape[1]), full, full],
        out_specs=[tile(width), pl.BlockSpec((8, 8, width), lambda i: (0, 0, 0))],
        out_shape=[
            jax.ShapeDtypeStruct((positions, width), jnp.bfloat16),
            jax.ShapeDtypeStruct((8, 8, width), jnp.float32),
        ],
        scratch_shapes=[pltpu.VMEM((8, width), jnp.float32), pltpu.VMEM((rows_each, width), jnp.float32)],
        compiler_params=pltpu.CompilerParams(
            dimension_semantics=("arbitrary",), vmem_limit_bytes=48 * 1024 * 1024
        ),
        name="output_backward",
    )(whole, delta, dpre, weight, params)


def input_forward_kernel(
    seq_len,
    tanh_end,
    plain_end,
    whole_ref,
    three_ref,
    down_ref,
    ups_ref,
    params_ref,
    r_ref,
    k_ref,
    v_ref,
    dw_ref,
    da_ref,
    gate_ref,
    mr_ref,
    mk_ref,
    mv_ref,
    inner_ref,
):
    tile = pl.program_id(0)
    rows_each = r_ref.shape[0]
    part = r_ref.shape[1]
    width = whole_ref.shape[1]
    start = tile * rows_each
    at_start = lax.rem(start, seq_len) == 0
    edge = 16
    rows = pl.ds(pl.multiple_of(start, rows_each), rows_each)
    edge_rows = pl.ds(pl.multiple_of(jnp.maximum(start - edge, 0), edge), edge)
    inverse_width = 1.0 / width

    def moments(place):
        values = whole_ref[place, :].astype(jnp.float32)
        centre = jnp.sum(values, axis=1, keepdims=True) * inverse_width
        values = values - centre
        spread = jnp.sum(values * values, axis=1, keepdims=True) * inverse_width
        return centre, lax.rsqrt(spread + norm_eps)

    centre, inv = moments(rows)
    edge_centre, edge_inv = moments(edge_rows)
    block_cols = 256
    row_index = iota((rows_each, block_cols), 0)
    lane = iota((rows_each, down_ref.shape[1]), 1)
    r = k = v = inner_w = inner_a = inner_g = 0.0
    for block in range(width // block_cols):
        cols = slice(block * block_cols, (block + 1) * block_cols)
        gain, bias = params_ref[0:1, cols], params_ref[1:2, cols]
        normed = (whole_ref[rows, cols].astype(jnp.float32) - centre) * inv * gain + bias
        edge_unit = (whole_ref[edge_rows, cols].astype(jnp.float32) - edge_centre) * edge_inv
        edge_normed = (edge_unit * gain + bias)[edge - 1 : edge]
        edge_normed = jnp.where(at_start, 0.0, edge_normed)
        before = jnp.where(row_index == 0, edge_normed, pltpu.roll(normed, 1, 0))
        shift = before - normed

        def mix(index):
            return low(normed + shift * params_ref[index : index + 1, cols])

        mix_r, mix_k, mix_v = mix(2), mix(4), mix(5)
        mr_ref[:, cols], mk_ref[:, cols], mv_ref[:, cols] = mix_r, mix_k, mix_v
        weights = three_ref[cols, :]
        r = r + dot_nn(mix_r, weights[:, :part])
        k = k + dot_nn(mix_k, weights[:, part : 2 * part])
        v = v + dot_nn(mix_v, weights[:, 2 * part :])
        down = down_ref[cols, :]
        inner_w = inner_w + dot_nn(mix(3), down)
        inner_a = inner_a + dot_nn(mix(6), down)
        inner_g = inner_g + dot_nn(mix(7), down)
    r_ref[...], k_ref[...], v_ref[...] = r, k, v
    inner = jnp.where(
        lane < tanh_end,
        jnp.tanh(inner_w),
        jnp.where(lane < plain_end, inner_a, jax.nn.sigmoid(inner_g)),
    )
    inner_ref[...] = inner
    inner_low = low(inner)
    zero = jnp.zeros_like(inner_low)
    ups = ups_ref[...]
    dw_ref[...] = dot_nn(jnp.where(lane < tanh_end, inner_low, zero), ups)
    da_ref[...] = dot_nn(jnp.where((lane >= tanh_end) & (lane < plain_end), inner_low, zero), ups)
    gate_ref[...] = dot_nn(jnp.where(lane >= plain_end, inner_low, zero), ups)


def input_forward(whole, three, down, ups, ends, params):
    positions, width = whole.shape
    part = ups.shape[1]
    rows_each = 256
    tile = lambda cols: pl.BlockSpec((rows_each, cols), lambda i: (i, 0))
    full = pl.BlockSpec(memory_space=pltpu.VMEM)
    shape = jax.ShapeDtypeStruct
    return pl.pallas_call(
        partial(input_forward_kernel, SEQ_LEN, *ends),
        grid=(positions // rows_each,),
        in_specs=[full] * 5,
        out_specs=[tile(part)] * 6 + [tile(width)] * 3 + [tile(down.shape[1])],
        out_shape=[shape((positions, part), jnp.float32)] * 6
        + [shape((positions, width), jnp.bfloat16)] * 3
        + [shape((positions, down.shape[1]), jnp.float32)],
        compiler_params=pltpu.CompilerParams(
            dimension_semantics=("arbitrary",), vmem_limit_bytes=52 * 1024 * 1024
        ),
        name="input_forward",
    )(whole, three, down, ups, params)


def matmul(left_op, right_op):
    return jnp.dot(left_op, right_op, preferred_element_type=jnp.float32)


def contract_rows(left_op, right_op):
    return jnp.einsum("tk,tn->kn", left_op, right_op, preferred_element_type=jnp.float32)


def against(grad_op, weight_op):
    return jnp.einsum("tn,kn->tk", grad_op, weight_op, preferred_element_type=jnp.float32)


def layer_norm(values, scale_in, offset):
    centre = jnp.mean(values, axis=-1, keepdims=True)
    centred = values - centre
    spread = jnp.mean(centred * centred, axis=-1, keepdims=True)
    return centred * lax.rsqrt(spread + norm_eps) * scale_in + offset


def shifted(values):
    grid_view = values.reshape(values.shape[0] // SEQ_LEN, SEQ_LEN, values.shape[1])
    earlier = jnp.concatenate([jnp.zeros_like(grid_view[:, :1]), grid_view[:, :-1]], axis=1)
    return earlier.reshape(values.shape)


def section_out(residual, scale_in, offset, mix_rate):
    standardized_source = layer_norm(residual, scale_in, offset)
    return standardized_source + (shifted(standardized_source) - standardized_source) * mix_rate


def body(
    hidden,
    teacher,
    lengths,
    feature_params,
    decay_down,
    rate_down,
    gate_down,
    decay_up,
    rate_up,
    gate_up,
    receptance,
    key_proj,
    value_proj,
    output_proj,
    ffn_key,
    ffn_value,
):
    position_count, part_width = hidden.shape
    seq_dev = position_count // SEQ_LEN
    mp_index = lax.axis_index("mp")
    col_start = mp_index * part_width
    groups = lax.axis_size("dp")
    own_lengths = lax.dynamic_slice_in_dim(lengths, lax.axis_index("dp") * seq_dev, seq_dev)
    places = jnp.arange(SEQ_LEN, dtype=jnp.int32)
    valid = (places[None, :] < own_lengths[:, None]).astype(jnp.float32).reshape(position_count)
    loss_scale = position_count * lax.axis_size("dp") / jnp.sum(lengths).astype(jnp.float32)
    line_size = lax.axis_size("mp")
    whole_low = line_gather(hidden, line_size, 1)
    low_rank = (decay_down.shape[1], rate_down.shape[1], gate_down.shape[1])
    narrow = jnp.concatenate([decay_down, rate_down, gate_down, feature_params], axis=1)
    narrow = jnp.pad(narrow, ((0, 0), (0, -narrow.shape[1] % 128)))
    narrow_w = lax.all_gather(narrow, "mp", axis=0, tiled=True)
    narrow_w = lax.all_gather(narrow_w, "dp", axis=0, tiled=True)
    decay_down_w = narrow_w[:, : low_rank[0]]
    rate_down_w = narrow_w[:, low_rank[0] : low_rank[0] + low_rank[1]]
    gate_down_w = narrow_w[:, low_rank[0] + low_rank[1] : sum(low_rank)]
    params_low = narrow_w[:, sum(low_rank) : sum(low_rank) + feature_params.shape[1]]
    three = lax.all_gather(
        jnp.concatenate([receptance, key_proj, value_proj], axis=1), "dp", axis=0, tiled=True
    )
    up_rows = (decay_up.shape[0], rate_up.shape[0], gate_up.shape[0])
    ups = lax.all_gather(jnp.concatenate([decay_up, rate_up, gate_up], axis=0), "dp", axis=0)
    decay_up_w = ups[:, : up_rows[0]].reshape(-1, part_width)
    rate_up_w = ups[:, up_rows[0] : up_rows[0] + up_rows[1]].reshape(-1, part_width)
    gate_up_w = ups[:, up_rows[0] + up_rows[1] :].reshape(-1, part_width)
    output_w = lax.all_gather(output_proj, "dp", axis=1, tiled=True)
    ffn_key_w = lax.all_gather(ffn_key, "dp", axis=0, tiled=True)
    ffn_value_w = lax.all_gather(ffn_value, "dp", axis=1, tiled=True)
    params = params_low.astype(jnp.float32)
    model_width = whole_low.shape[1]
    params_rows = jnp.pad(params.T, ((0, -params.shape[1] % 8), (0, 0)))
    up_all = jnp.concatenate([decay_up_w, rate_up_w, gate_up_w], axis=0)
    up_all = jnp.pad(up_all, ((0, narrow_w.shape[1] - up_all.shape[0]), (0, 0)))
    (
        acceptance_matrix,
        keys_in,
        payload_source,
        decay_in,
        rate_in,
        sigmoid_source,
        mix_r,
        mix_k,
        mix_v,
        inner_hid,
    ) = input_forward(
        whole_low, three, narrow_w, up_all, (low_rank[0], low_rank[0] + low_rank[1]), params_rows
    )
    inner_low = inner_hid.astype(jnp.bfloat16)
    decay_hid = inner_hid[:, : low_rank[0]]
    gate_hid = inner_hid[:, low_rank[0] + low_rank[1] : sum(low_rank)]
    decay_low = inner_low[:, : low_rank[0]]
    rate_low = inner_low[:, low_rank[0] : low_rank[0] + low_rank[1]]
    gate_low = inner_low[:, low_rank[0] + low_rank[1] : sum(low_rank)]
    columns = lax.dynamic_slice(params_rows, (8, col_start), (8, part_width))
    mixer_args = (
        own_lengths,
        acceptance_matrix,
        keys_in,
        payload_source,
        decay_in,
        rate_in,
        sigmoid_source,
        columns,
    )
    gated_low, *kept = run_mixer_forward(*mixer_args)
    delta_low = line_sum(matmul(gated_low, output_w).astype(jnp.bfloat16), line_size, 2)
    residual = whole_low.astype(jnp.float32) + delta_low.astype(jnp.float32)
    ffn_in = section_out(residual, params[:, 15], params[:, 16], params[:, 17])
    ffn_low = ffn_in.astype(jnp.bfloat16)
    pre_act = matmul(ffn_low, ffn_key_w)
    active = jnp.maximum(pre_act, 0.0)
    squared = (active * active).astype(jnp.bfloat16)
    ffn_part = matmul(squared, ffn_value_w).astype(jnp.bfloat16)
    own_residual = lax.dynamic_slice_in_dim(residual, col_start, part_width, 1)
    error_scale = jnp.broadcast_to((loss_scale * valid)[:, None], (position_count, 128))
    out_state, grad_low = line_error(ffn_part, own_residual, teacher, error_scale, line_size, 3)
    grad_ffn_value = contract_rows(squared, grad_low).astype(jnp.bfloat16)
    grad_low, grad_ffn_value = lax.optimization_barrier((grad_low, grad_ffn_value))
    grad_ffn_value = lax.psum_scatter(grad_ffn_value, "dp", scatter_dimension=1, tiled=True)
    grad_squared = against(grad_low, ffn_value_w)
    grad_pre = (grad_squared * 2.0 * active).astype(jnp.bfloat16)
    grad_ffn_key = contract_rows(ffn_low, grad_pre).astype(jnp.bfloat16)
    grad_pre, grad_ffn_key = lax.optimization_barrier((grad_pre, grad_ffn_key))
    grad_ffn_key = lax.psum_scatter(grad_ffn_key, "dp", scatter_dimension=0, tiled=True)
    d_resid_part, d_params_out = output_backward(
        whole_low, delta_low, grad_pre, ffn_key_w, params_rows[15:23]
    )
    d_residual = grad_low.astype(jnp.float32) + line_sum(d_resid_part, line_size, 5).astype(jnp.float32)
    d_low = d_residual.astype(jnp.bfloat16)
    grad_output_proj = contract_rows(gated_low, d_low).astype(jnp.bfloat16)
    d_low, grad_output_proj = lax.optimization_barrier((d_low, grad_output_proj))
    grad_output_proj = lax.psum_scatter(grad_output_proj, "dp", scatter_dimension=1, tiled=True)
    d_gated = against(d_low, output_w)
    d_gated, grad_ffn_value, grad_ffn_key = lax.optimization_barrier(
        (d_gated, grad_ffn_value, grad_ffn_key)
    )
    d_recept, d_keys, d_values, d_decay, d_rate, d_gate, d_columns = run_mixer_backward(
        *mixer_args, *kept, d_gated
    )
    d_columns = jnp.sum(d_columns, axis=1)[:7]
    grad_three = weight_grads((mix_r, mix_k, mix_v), (d_recept, d_keys, d_values))
    d_decay, d_rate, d_gate, grad_three = lax.optimization_barrier((d_decay, d_rate, d_gate, grad_three))
    grad_three = lax.psum_scatter(grad_three, "dp", scatter_dimension=0, tiled=True)
    shares = [rank // line_size for rank in low_rank]
    starts = (0, shares[0], shares[0] + shares[1])
    own_rank = sum(shares) + -sum(shares) % 128

    def spread_rows(weight, share, start):
        grouped = weight.reshape(line_size, share, part_width)
        grouped = jnp.pad(grouped, ((0, 0), (start, own_rank - start - share), (0, 0)))
        return grouped.reshape(line_size * own_rank, part_width)

    def own_columns(values, share):
        return lax.dynamic_slice_in_dim(values, mp_index * share, share, 1)

    def own_group(members):
        taken = jnp.concatenate(
            [own_columns(member, share) for member, share in zip(members, shares)], axis=1
        )
        return jnp.pad(taken, ((0, 0), (0, own_rank - sum(shares))))

    d_inner = (
        against(d_decay, spread_rows(decay_up_w, shares[0], starts[0]))
        + against(d_rate, spread_rows(rate_up_w, shares[1], starts[1]))
        + against(d_gate, spread_rows(gate_up_w, shares[2], starts[2]))
    ).astype(jnp.bfloat16)
    d_own = line_scatter(d_inner, line_size, 6)
    d_own, grad_output_proj = lax.optimization_barrier((d_own, grad_output_proj))
    slope = own_group(
        (
            1.0 - decay_hid * decay_hid,
            jnp.ones((position_count, low_rank[1]), jnp.float32),
            gate_hid * (1.0 - gate_hid),
        )
    )
    d_own_pre = (d_own * slope).astype(jnp.bfloat16)
    down_own = own_group((decay_down_w, rate_down_w, gate_down_w))
    d_in_part, d_params_in, d_down = input_backward(
        whole_low, d_recept, d_keys, d_values, d_own_pre, starts[1:], three, down_own, params_rows
    )
    up_grads = jnp.concatenate(
        [
            contract_rows(low_part, grad).reshape(groups, -1, part_width)
            for low_part, grad in ((decay_low, d_decay), (rate_low, d_rate), (gate_low, d_gate))
        ],
        axis=1,
    ).astype(jnp.bfloat16)
    d_in_part, grad_three, up_grads = lax.optimization_barrier((d_in_part, grad_three, up_grads))
    up_grads = lax.psum_scatter(up_grads, "dp", scatter_dimension=0, tiled=True)
    up_grads = up_grads.reshape(-1, part_width).astype(jnp.float32)
    core_grads = lax.dynamic_update_slice_in_dim(
        jnp.zeros((7, model_width), jnp.float32), d_columns, col_start, 1
    )
    param_rows = jnp.concatenate(
        [
            jnp.sum(d_params_in, axis=1),
            core_grads,
            jnp.sum(d_params_out, axis=1)[:3],
        ],
        axis=0,
    )
    param_count = param_rows.shape[0]
    narrow_grads = jnp.pad(
        jnp.concatenate([d_down, param_rows], axis=0), ((0, -(own_rank + param_count) % 8), (0, 0))
    )
    d_in_part, narrow_grads = lax.optimization_barrier((d_in_part, narrow_grads))
    narrow_grads = lax.psum_scatter(narrow_grads, "dp", scatter_dimension=1, tiled=True)
    grad_hidden = lax.dynamic_slice_in_dim(d_residual, col_start, part_width, 1) + line_scatter(
        d_in_part, line_size, 7
    )
    row_block = decay_down.shape[0]
    narrow_grads = jnp.pad(narrow_grads, ((0, 0), (0, -narrow_grads.shape[1] % 128)))
    narrow_rows = narrow_grads.shape[0]
    narrow_grads = line_gather(narrow_grads, line_size, 4, chunk_rows=narrow_rows)
    narrow_grads = narrow_grads.reshape(narrow_rows, line_size, -1)
    narrow_grads = lax.dynamic_slice_in_dim(narrow_grads, mp_index * row_block, row_block, 2)

    def down_grad(start, share):
        taken = narrow_grads[start : start + share].transpose(1, 0, 2)
        return taken.reshape(line_size * share, row_block).T

    grad_params = jnp.sum(narrow_grads[own_rank : own_rank + param_count], axis=1).T
    return (
        out_state,
        grad_hidden,
        grad_params,
        down_grad(starts[0], shares[0]),
        down_grad(starts[1], shares[1]),
        down_grad(starts[2], shares[2]),
        up_grads[: up_rows[0]],
        up_grads[up_rows[0] : up_rows[0] + up_rows[1]],
        up_grads[up_rows[0] + up_rows[1] :],
        grad_three[:, :part_width].astype(jnp.float32),
        grad_three[:, part_width : 2 * part_width].astype(jnp.float32),
        grad_three[:, 2 * part_width :].astype(jnp.float32),
        grad_output_proj.astype(jnp.float32),
        grad_ffn_key.astype(jnp.float32),
        grad_ffn_value.astype(jnp.float32),
    )


def solution(mesh):
    in_specs = (
        P("dp", "mp"),
        P("dp", "mp"),
        P(),
        P(("dp", "mp"), None),
        P(("dp", "mp"), None),
        P(("dp", "mp"), None),
        P(("dp", "mp"), None),
        P("dp", "mp"),
        P("dp", "mp"),
        P("dp", "mp"),
        P("dp", "mp"),
        P("dp", "mp"),
        P("dp", "mp"),
        P("mp", "dp"),
        P("dp", "mp"),
        P("mp", "dp"),
    )
    out_specs = (
        P("dp", "mp"),
        P("dp", "mp"),
        P(("dp", "mp"), None),
        P(("dp", "mp"), None),
        P(("dp", "mp"), None),
        P(("dp", "mp"), None),
        P("dp", "mp"),
        P("dp", "mp"),
        P("dp", "mp"),
        P("dp", "mp"),
        P("dp", "mp"),
        P("dp", "mp"),
        P("mp", "dp"),
        P("dp", "mp"),
        P("mp", "dp"),
    )
    return jax.shard_map(body, mesh=mesh, in_specs=in_specs, out_specs=out_specs, check_vma=False)
```

```python
from functools import partial
import math
from types import SimpleNamespace

import jax
import jax.numpy as jnp
from jax import lax
from jax.experimental import pallas as pl
from jax.experimental.pallas import tpu as pltpu
from jax.sharding import PartitionSpec as P

norm_eps = 1e-05
SUBSPACE_SIZE = 64
SEQ_LEN = 1024
group_eps = 0.00064
CHUNK = 64
PAIR = 2 * SUBSPACE_SIZE
CHUNKS_FWD = 4
CHUNKS_BWD = 2
DECAY_SCALE = math.exp(-0.5)


def dot_nn(left_op, right_op):
    return lax.dot_general(left_op, right_op, (((1,), (0,)), ((), ())), preferred_element_type=jnp.float32)


def dot_nt(left_op, right_op):
    return lax.dot_general(left_op, right_op, (((1,), (1,)), ((), ())), preferred_element_type=jnp.float32)


def dot_tn(left_op, right_op):
    return lax.dot_general(left_op, right_op, (((0,), (0,)), ((), ())), preferred_element_type=jnp.float32)


def low(values):
    return values.astype(jnp.bfloat16)


def split_dot(ones_op, values):
    top = low(values)
    rest = values - top.astype(jnp.float32)
    mid = low(rest)
    tail = low(rest - mid.astype(jnp.float32))
    return dot_nn(ones_op, top) + dot_nn(ones_op, mid) + dot_nn(ones_op, tail)


def halves(values):
    top = low(values)
    return top, low(values - top.astype(jnp.float32))


def iota(shape, axis):
    return lax.broadcasted_iota(jnp.int32, shape, axis)


def head_masks():
    lane = iota((CHUNK, PAIR), 1)
    return lane < SUBSPACE_SIZE


def stack_heads(values):
    first = iota(values.shape, 1) < SUBSPACE_SIZE
    zero = jnp.zeros_like(values)
    return jnp.concatenate(
        [jnp.where(first, values, zero), jnp.where(first, zero, values)], axis=0
    )


def fold_heads(values):
    first = iota((CHUNK, PAIR), 1) < SUBSPACE_SIZE
    return jnp.where(first, values[:CHUNK], values[CHUNK:])


def head_ones():
    return (
        iota((PAIR, PAIR), 0) // SUBSPACE_SIZE == iota((PAIR, PAIR), 1) // SUBSPACE_SIZE
    )


def head_sum(values, ones_op):
    top = low(values)
    rest = low(values - top.astype(jnp.float32))
    return dot_nn(top, ones_op) + dot_nn(rest, ones_op)


def lower_inverses(lower_parts):
    row = iota((CHUNK, PAIR), 0)
    col = iota((CHUNK, PAIR), 1) % CHUNK
    eye = jnp.where(row == col, 1.0, 0.0)

    def times(lefts, rights):
        return [
            dot_nn(low(left_op), stack_heads(low(right_op)))
            for left_op, right_op in zip(lefts, rights)
        ]

    def plus(*lists):
        return [sum(members[1:], members[0]) for members in zip(*lists)]

    near = row // 8 == col // 8
    base = [jnp.where(near, part, 0.0) for part in lower_parts]
    square = times(base, base)
    cube = times(base, square)
    fourth = times(square, square)
    accum = [eye + first + second + third for first, second, third in zip(base, square, cube)]
    accum = plus(accum, times(accum, fourth))
    width = 8
    while width < CHUNK:
        level = (row // (2 * width) == col // (2 * width)) & (row // width != col // width)
        off = [jnp.where(level, part, 0.0) for part in lower_parts]
        accum = plus(accum, times(times(accum, off), accum))
        width *= 2
    return accum


def prepare(r, k, dw, da, cols, live, tri_op, ones_op):
    sw = jax.nn.sigmoid(dw + cols[0:1])
    full_log = -DECAY_SCALE * sw
    log_decay = jnp.where(live, full_log, 0.0)
    rate = jax.nn.sigmoid(da + cols[1:2])
    scaled = k * cols[2:3]
    inv = lax.rsqrt(head_sum(scaled * scaled, ones_op) + 1e-06)
    unit = scaled * inv
    unit_live = jnp.where(live, unit, 0.0)
    lag_scale = 1.0 + (rate - 1.0) * cols[3:4]
    lagged = jnp.where(live, k * lag_scale, 0.0)
    running = split_dot(tri_op, log_decay)
    grown = jnp.exp(running)
    before = jnp.exp(running - log_decay)
    shrunk = jnp.exp(-running)
    last = running[CHUNK - 1 : CHUNK]
    til_end = jnp.exp(last - running)
    write = unit_live * rate
    return SimpleNamespace(
        sw=sw,
        full_log=full_log,
        rate=rate,
        inv=inv,
        unit=unit,
        unit_live=unit_live,
        lag_scale=lag_scale,
        lagged=lagged,
        grown=grown,
        before=before,
        shrunk=shrunk,
        til_end=til_end,
        final=jnp.exp(last),
        read_wide=r * grown,
        write_wide=write * shrunk,
        key_wide=lagged * shrunk,
        read_hat=low(r * grown),
        remove_hat=low(-unit_live * before),
        write_hat=low(write * shrunk),
        key_hat=low(lagged * shrunk),
        write_end=low(write * til_end),
        key_end=low(lagged * til_end),
    )


def tri_masks():
    row = iota((CHUNK, PAIR), 0)
    col = iota((CHUNK, PAIR), 1) % CHUNK
    return row > col, row >= col


def mixer_forward(
    steps_per_seq,
    length_ref,
    r_ref,
    k_ref,
    v_ref,
    dw_ref,
    da_ref,
    gate_ref,
    cols_ref,
    z_ref,
    y_ref,
    t_ref,
    u_ref,
    s_ref,
    lk_ref,
    reads_ref,
    state,
):
    step = pl.program_id(0)
    within_seq = lax.rem(step, steps_per_seq)
    length = length_ref[step // steps_per_seq]

    @pl.when(within_seq == 0)
    def _():
        state[...] = jnp.zeros_like(state)

    rows_each = r_ref.shape[0]
    chunks = rows_each // CHUNK
    pairs = r_ref.shape[1] // PAIR
    ones_mask = head_ones()
    ones_op = jnp.where(ones_mask, 1.0, 0.0).astype(jnp.bfloat16)
    tri_op = jnp.where(iota((CHUNK, CHUNK), 0) >= iota((CHUNK, CHUNK), 1), 1.0, 0.0).astype(jnp.bfloat16)
    strict, within = tri_masks()
    within_two = jnp.concatenate([within, within], axis=1)
    units = [(chunk, pair) for chunk in range(chunks) for pair in range(pairs)]

    def place_of(unit):
        chunk, pair = unit
        return slice(chunk * CHUNK, (chunk + 1) * CHUNK), slice(pair * PAIR, (pair + 1) * PAIR)

    prepared, scored, lower_parts = [], [], []
    for unit in units:
        rows, lanes = place_of(unit)
        live = within_seq * rows_each + unit[0] * CHUNK + iota((CHUNK, PAIR), 0) < length
        got = prepare(
            r_ref[rows, lanes],
            k_ref[rows, lanes],
            dw_ref[rows, lanes],
            da_ref[rows, lanes],
            cols_ref[:, lanes],
            live,
            tri_op,
            ones_op,
        )
        prepared.append(got)
    for unit, got in zip(units, prepared):
        got.both = jnp.concatenate([got.remove_hat, got.read_hat], axis=0)
        past = jnp.concatenate([stack_heads(got.write_hat), stack_heads(got.key_hat)], axis=0)
        scores = dot_nt(got.both, past)
        past_rest = jnp.concatenate(
            [stack_heads(halves(got.write_wide)[1]), stack_heads(halves(got.key_wide)[1])], axis=0
        )
        got.read_rest = halves(got.read_wide)[1]
        fine = scores[CHUNK:] + (dot_nt(got.read_rest, past) + dot_nt(got.read_hat, past_rest))
        lower_parts.append(jnp.where(strict, scores[:CHUNK, :PAIR], 0.0))
        lower_key = low(jnp.where(strict, scores[:CHUNK, PAIR:], 0.0))
        reads = low(jnp.where(within_two, fine, 0.0))
        scored.append((lower_key, reads))
    solves = [low(part) for part in lower_inverses(lower_parts)]
    for unit, solve in zip(units, solves):
        t_ref[place_of(unit)] = solve
    for chunk in range(chunks):
        group = [index for index, unit in enumerate(units) if unit[0] == chunk]
        lows = [low(v_ref[place_of(units[index])]) for index in group]
        stacks = [stack_heads(values) for values in lows]
        olds = [state[units[index][1]] for index in group]
        old_parts = [halves(old) for old in olds]
        from_state = [dot_nt(prepared[index].both, old[0]) for index, old in zip(group, old_parts)]
        read_state = [
            part[CHUNK:]
            + (dot_nt(prepared[index].read_rest, old[0]) + dot_nt(prepared[index].read_hat, old[1]))
            for index, part, old in zip(group, from_state, old_parts)
        ]
        right = [
            low(part[:CHUNK] + dot_nn(scored[index][0], stack))
            for index, part, stack in zip(group, from_state, stacks)
        ]
        removed = [low(dot_nn(solves[index], stack_heads(part))) for index, part in zip(group, right)]
        for slot, index in enumerate(group):
            pair = units[index][1]
            got = prepared[index]
            ends = jnp.concatenate([got.write_end, got.key_end], axis=0)
            adds = dot_tn(jnp.concatenate([removed[slot], lows[slot]], axis=0), ends)
            state[pair] = olds[slot] * got.final + jnp.where(ones_mask, adds, 0.0)
            u_ref[place_of(units[index])] = removed[slot]
            rows, lanes = place_of(units[index])
            lk_ref[rows, lanes], reads_ref[rows, slice(2 * lanes.start, 2 * lanes.stop)] = scored[index]
            s_ref[chunk, pair] = olds[slot]
        outs = [
            read_state[slot]
            + dot_nn(scored[index][1], jnp.concatenate([stack_heads(removed[slot]), stacks[slot]], axis=0))
            for slot, index in enumerate(group)
        ]
        centred = [y - head_sum(y, ones_op) * (1.0 / SUBSPACE_SIZE) for y in outs]
        spread = [head_sum(part * part, ones_op) * (1.0 / SUBSPACE_SIZE) for part in centred]
        for slot, index in enumerate(group):
            rows, lanes = place_of(units[index])
            cols = cols_ref[:, lanes]
            normed = centred[slot] * lax.rsqrt(spread[slot] + group_eps)
            bonus = head_sum(r_ref[rows, lanes] * prepared[index].lagged * cols[4:5], ones_op)
            mixed = normed * cols[5:6] + cols[6:7] + bonus * v_ref[rows, lanes]
            y_ref[rows, lanes] = outs[slot]
            z_ref[rows, lanes] = low(mixed * gate_ref[rows, lanes])


def mixer_backward(
    steps_per_seq,
    length_ref,
    r_ref,
    k_ref,
    v_ref,
    dw_ref,
    da_ref,
    gate_ref,
    cols_ref,
    y_ref,
    t_ref,
    u_ref,
    s_ref,
    lk_ref,
    reads_ref,
    dz_ref,
    dr_ref,
    dk_ref,
    dv_ref,
    ddw_ref,
    dda_ref,
    dgate_ref,
    dcols_ref,
    dstate,
):
    step = pl.num_programs(0) - 1 - pl.program_id(0)
    within_seq = lax.rem(step, steps_per_seq)
    length = length_ref[step // steps_per_seq]

    @pl.when(within_seq == steps_per_seq - 1)
    def _():
        dstate[...] = jnp.zeros_like(dstate)

    @pl.when(pl.program_id(0) == 0)
    def _():
        dcols_ref[...] = jnp.zeros_like(dcols_ref)

    rows_each = r_ref.shape[0]
    chunks = rows_each // CHUNK
    pairs = r_ref.shape[1] // PAIR
    ones_mask = head_ones()
    ones_op = jnp.where(ones_mask, 1.0, 0.0).astype(jnp.bfloat16)
    row = iota((CHUNK, CHUNK), 0)
    col = iota((CHUNK, CHUNK), 1)
    tri_op = jnp.where(row >= col, 1.0, 0.0).astype(jnp.bfloat16)
    suffix_op = jnp.where(row <= col, 1.0, 0.0).astype(jnp.bfloat16)
    prefix_op = jnp.where(row > col, 1.0, 0.0).astype(jnp.bfloat16)
    sums_op = jnp.concatenate([suffix_op, prefix_op], axis=1)
    strict, within = tri_masks()

    def add_col(index, lanes, values):
        part = values[0:8]
        for start in range(8, CHUNK, 8):
            part = part + values[start : start + 8]
        dcols_ref[index, :, lanes] += part

    strict_two = jnp.concatenate([strict, strict], axis=1)
    within_two = jnp.concatenate([within, within], axis=1)
    all_masks = jnp.concatenate([strict_two, within_two], axis=0)
    units = [(chunk, pair) for chunk in reversed(range(chunks)) for pair in range(pairs)]
    mean_of = 1.0 / SUBSPACE_SIZE
    known = []
    for chunk, pair in units:
        rows = slice(chunk * CHUNK, (chunk + 1) * CHUNK)
        lanes = slice(pair * PAIR, (pair + 1) * PAIR)
        live = within_seq * rows_each + chunk * CHUNK + iota((CHUNK, PAIR), 0) < length
        cols = cols_ref[:, lanes]
        got = prepare(
            r_ref[rows, lanes],
            k_ref[rows, lanes],
            dw_ref[rows, lanes],
            da_ref[rows, lanes],
            cols,
            live,
            tri_op,
            ones_op,
        )
        got.rows, got.lanes, got.live, got.cols = rows, lanes, live, cols
        got.pair, got.chunk = pair, chunk
        known.append(got)
    for got in known:
        y = y_ref[got.rows, got.lanes]
        got.centred = y - head_sum(y, ones_op) * mean_of
    for got in known:
        spread = head_sum(got.centred * got.centred, ones_op) * mean_of
        got.inv_y = lax.rsqrt(spread + group_eps)
    for got in known:
        rows, lanes, cols = got.rows, got.lanes, got.cols
        r, v, dz = r_ref[rows, lanes], v_ref[rows, lanes], dz_ref[rows, lanes]
        normed = got.centred * got.inv_y
        got.bonus = head_sum(r * got.lagged * cols[4:5], ones_op)
        mixed = normed * cols[5:6] + cols[6:7] + got.bonus * v
        dgate_ref[rows, lanes] = low(dz * mixed)
        dmix = dz * gate_ref[rows, lanes]
        add_col(5, lanes, dmix * normed)
        add_col(6, lanes, dmix)
        dnormed = dmix * cols[5:6]
        got.dbonus = head_sum(dmix * v, ones_op)
        mean_grad = head_sum(dnormed, ones_op) * mean_of
        mean_prod = head_sum(dnormed * normed, ones_op) * mean_of
        got.dy_low, got.dy_rest = halves(got.inv_y * (dnormed - mean_grad - normed * mean_prod))
        got.dv = got.bonus * dmix
    for got in known:
        rows, lanes = got.rows, got.lanes
        got.both = jnp.concatenate([got.remove_hat, got.read_hat], axis=0)
        got.past = jnp.concatenate(
            [stack_heads(got.write_hat), stack_heads(got.key_hat)], axis=0
        )
        got.lower_key = lk_ref[rows, lanes]
        reads = reads_ref[rows, slice(2 * lanes.start, 2 * lanes.stop)]
        got.from_y = dot_tn(reads, got.dy_low)
        v_low = low(v_ref[rows, lanes])
        removed = u_ref[rows, lanes]
        got.sent = jnp.concatenate([removed, v_low], axis=0)
        got.stacks = jnp.concatenate([stack_heads(removed), stack_heads(v_low)], axis=0)
    for chunk in reversed(range(chunks)):
        group = [got for got in known if got.chunk == chunk]
        for got in group:
            got.later = dstate[got.pair]
            got.later_low, got.later_rest = halves(got.later)
            ends = jnp.concatenate([got.write_end, got.key_end], axis=0)
            got.from_later = dot_nt(ends, got.later_low)
        for got in group:
            dremoved = low(got.from_later[:CHUNK] + fold_heads(got.from_y[:PAIR]))
            got.dright = low(fold_heads(dot_tn(t_ref[got.rows, got.lanes], dremoved)))
        for got in group:
            got.douts = jnp.concatenate([got.dright, got.dy_low], axis=0)
            adds = dot_tn(got.douts, got.both) + dot_tn(got.dy_rest, got.read_hat)
            adds = jnp.where(ones_mask, adds, 0.0)
            dstate[got.pair] = got.later * got.final + adds
    for got in known:
        dv = got.dv + got.from_later[CHUNK:] + fold_heads(got.from_y[PAIR:])
        dv = dv + fold_heads(dot_tn(got.lower_key, got.dright))
        dv_ref[got.rows, got.lanes] = low(dv)
        dscores = dot_nt(got.douts, got.stacks)
        fine = dscores[CHUNK:] + dot_nt(got.dy_rest, got.stacks)
        dscores = low(jnp.where(all_masks, jnp.concatenate([dscores[:CHUNK], fine], axis=0), 0.0))
        old_wide = s_ref[got.chunk, got.pair]
        old_low, old_rest = halves(old_wide)
        from_old = dot_nn(got.douts, old_low)
        fine = from_old[CHUNK:] + (dot_nn(got.dy_rest, old_low) + dot_nn(got.dy_low, old_rest))
        got.dboth = jnp.concatenate([from_old[:CHUNK], fine], axis=0) + dot_nn(dscores, got.past)
        dpast = dot_tn(dscores, got.both)
        got.dwrite_hat = fold_heads(dpast[:PAIR])
        got.dkey_hat = fold_heads(dpast[PAIR:])
        got.dends = dot_nn(got.sent, got.later_low) + dot_nn(got.sent, got.later_rest)
        got.dfinal = jnp.sum(got.later * old_wide, axis=0, keepdims=True)
    for got in known:
        rows, lanes, cols, live = got.rows, got.lanes, got.cols, got.live

        def wide(values):
            return values.astype(jnp.float32)

        r, k = r_ref[rows, lanes], k_ref[rows, lanes]
        dwrite_hat, dkey_hat = got.dwrite_hat, got.dkey_hat
        dwrite_end, dkey_end = got.dends[:CHUNK], got.dends[CHUNK:]
        dremove_hat, dread_hat = got.dboth[:CHUNK], got.dboth[CHUNK:]
        dbonus, lagged = got.dbonus, got.lagged
        bonus_lag = dbonus * lagged
        add_col(4, lanes, bonus_lag * r)
        dr_ref[rows, lanes] = low(bonus_lag * cols[4:5] + dread_hat * got.grown)
        minus = wide(got.remove_hat) * dremove_hat
        plus = wide(got.read_hat) * dread_hat + minus
        plus = plus - wide(got.write_hat) * dwrite_hat - wide(got.key_hat) * dkey_hat
        ending = wide(got.write_end) * dwrite_end + wide(got.key_end) * dkey_end
        sums = split_dot(sums_op, jnp.concatenate([plus, ending], axis=0))
        dlog = sums - minus + got.final * got.dfinal
        ddw = jnp.where(live, dlog * got.full_log * (1.0 - got.sw), 0.0)
        add_col(0, lanes, ddw)
        ddw_ref[rows, lanes] = low(ddw)
        dwrite = dwrite_hat * got.shrunk + dwrite_end * got.til_end
        dlag = dbonus * r * cols[4:5] + dkey_hat * got.shrunk + dkey_end * got.til_end
        dlag = jnp.where(live, dlag, 0.0)
        rate = got.rate
        dunit = jnp.where(live, dwrite * rate - dremove_hat * got.before, 0.0)
        lag_k = dlag * k
        drate = dwrite * got.unit_live + lag_k * cols[3:4]
        add_col(3, lanes, lag_k * (rate - 1.0))
        dscaled = got.inv * (dunit - got.unit * head_sum(dunit * got.unit, ones_op))
        add_col(2, lanes, dscaled * k)
        dk_ref[rows, lanes] = low(dlag * got.lag_scale + dscaled * cols[2:3])
        dda = drate * rate * (1.0 - rate)
        add_col(1, lanes, dda)
        dda_ref[rows, lanes] = low(dda)


def run_mixer_forward(lengths, r, k, v, dw, da, gate, cols):
    positions, part_width = r.shape
    rows_each = CHUNKS_FWD * CHUNK
    steps = positions // rows_each
    steps_per_seq = SEQ_LEN // rows_each
    pairs = part_width // PAIR
    wide = pl.BlockSpec((rows_each, part_width), lambda i: (i, 0))
    shape = jax.ShapeDtypeStruct
    return pl.pallas_call(
        partial(mixer_forward, steps_per_seq),
        grid=(steps,),
        in_specs=[pl.BlockSpec(memory_space=pltpu.SMEM)]
        + [wide] * 6
        + [pl.BlockSpec((8, part_width), lambda i: (0, 0))],
        out_specs=[wide] * 4
        + [
            pl.BlockSpec((CHUNKS_FWD, pairs, PAIR, PAIR), lambda i: (i, 0, 0, 0)),
            wide,
            pl.BlockSpec((rows_each, 2 * part_width), lambda i: (i, 0)),
        ],
        out_shape=[
            shape((positions, part_width), jnp.bfloat16),
            shape((positions, part_width), jnp.float32),
            shape((positions, part_width), jnp.bfloat16),
            shape((positions, part_width), jnp.bfloat16),
            shape((positions // CHUNK, pairs, PAIR, PAIR), jnp.float32),
            shape((positions, part_width), jnp.bfloat16),
            shape((positions, 2 * part_width), jnp.bfloat16),
        ],
        scratch_shapes=[pltpu.VMEM((pairs, PAIR, PAIR), jnp.float32)],
        compiler_params=pltpu.CompilerParams(
            dimension_semantics=("arbitrary",), vmem_limit_bytes=40 * 1024 * 1024
        ),
        name="mixer_forward",
    )(lengths, r, k, v, dw, da, gate, cols)


def run_mixer_backward(lengths, r, k, v, dw, da, gate, cols, y, t, u, s, lk, reads, dz):
    positions, part_width = r.shape
    rows_each = CHUNKS_BWD * CHUNK
    steps = positions // rows_each
    steps_per_seq = SEQ_LEN // rows_each
    pairs = part_width // PAIR
    wide = pl.BlockSpec((rows_each, part_width), lambda i: (steps - 1 - i, 0))
    shape = jax.ShapeDtypeStruct
    return pl.pallas_call(
        partial(mixer_backward, steps_per_seq),
        grid=(steps,),
        in_specs=[pl.BlockSpec(memory_space=pltpu.SMEM)]
        + [wide] * 6
        + [pl.BlockSpec((8, part_width), lambda i: (0, 0))]
        + [wide] * 3
        + [
            pl.BlockSpec((CHUNKS_BWD, pairs, PAIR, PAIR), lambda i: (steps - 1 - i, 0, 0, 0)),
            wide,
            pl.BlockSpec((rows_each, 2 * part_width), lambda i: (steps - 1 - i, 0)),
            wide,
        ],
        out_specs=[wide] * 6 + [pl.BlockSpec((8, 8, part_width), lambda i: (0, 0, 0))],
        out_shape=[shape((positions, part_width), jnp.bfloat16)] * 6
        + [shape((8, 8, part_width), jnp.float32)],
        scratch_shapes=[pltpu.VMEM((pairs, PAIR, PAIR), jnp.float32)],
        compiler_params=pltpu.CompilerParams(
            dimension_semantics=("arbitrary",), vmem_limit_bytes=40 * 1024 * 1024
        ),
        name="mixer_backward",
    )(lengths, r, k, v, dw, da, gate, cols, y, t, u, s, lk, reads, dz)


LINE = "mp"
GROUP = "dp"
END_LAG = 3
MID_LAG = 1


def link_cost(elements):
    return elements * 2 * 2 * 40


def line_barrier(size):
    me = lax.axis_index(LINE)
    barrier = pltpu.get_barrier_semaphore()

    @pl.when(me > 0)
    def _():
        pl.semaphore_signal(barrier, inc=1, device_id={LINE: me - 1}, device_id_type=pl.DeviceIdType.MESH)

    @pl.when(me < size - 1)
    def _():
        pl.semaphore_signal(barrier, inc=1, device_id={LINE: me + 1}, device_id_type=pl.DeviceIdType.MESH)

    ends = jnp.where((me == 0) | (me == size - 1), 1, 2)
    pl.semaphore_wait(barrier, ends)


class Flow:
    def __init__(self, size, side):
        self.size = size
        self.side = side
        self.me = lax.axis_index(LINE)
        self.step = 1 - 2 * side
        self.target = self.me + self.step
        source = self.me - self.step
        self.has_source = (source >= 0) & (source < size)
        self.has_target = (self.target >= 0) & (self.target < size)

    def copy(self, source, place, send_sem, recv_sem):
        return pltpu.make_async_remote_copy(
            src_ref=source,
            dst_ref=place,
            send_sem=send_sem,
            recv_sem=recv_sem,
            device_id={LINE: self.target},
            device_id_type=pl.DeviceIdType.MESH,
        )


def two_flows(size):
    me = lax.axis_index(LINE)
    near = jnp.where(me < size // 2, 0, 1)
    return Flow(size, near), Flow(size, 1 - near)


def line_sum_kernel(size, chunk_rows, x_ref, out_ref, got, sent, send_sem, recv_sem):
    line_barrier(size)
    me = lax.axis_index(LINE)
    flows = two_flows(size)
    chunks = x_ref.shape[0] // chunk_rows

    def copy_of(flow, chunk, source):
        rows = pl.ds(pl.multiple_of(chunk * chunk_rows, chunk_rows), chunk_rows)
        return flow.copy(
            source.at[rows], got.at[flow.side, rows], send_sem.at[flow.side, chunk], recv_sem.at[flow.side, chunk]
        )

    def pass_on(flow, chunk):
        rows = pl.ds(pl.multiple_of(chunk * chunk_rows, chunk_rows), chunk_rows)

        @pl.when(flow.has_source)
        def _():
            copy_of(flow, chunk, x_ref).wait_recv()

        @pl.when(flow.has_source & flow.has_target)
        def _():
            total = got[flow.side, rows].astype(jnp.float32) + x_ref[rows].astype(jnp.float32)
            sent[flow.side, rows] = total.astype(sent.dtype)
            copy_of(flow, chunk, sent.at[flow.side]).start()

        @pl.when(jnp.logical_not(flow.has_source))
        def _():
            copy_of(flow, chunk, x_ref).start()

    is_end = (me == 0) | (me == size - 1)
    lag = jnp.where(is_end, END_LAG, MID_LAG)

    def step(turn, carry):
        @pl.when(turn < chunks)
        def _():
            pass_on(flows[0], turn)

        chunk = turn - lag

        @pl.when((chunk >= 0) & (chunk < chunks))
        def _():
            pass_on(flows[1], chunk)
            rows = pl.ds(pl.multiple_of(chunk * chunk_rows, chunk_rows), chunk_rows)

            @pl.when(is_end)
            def _():
                other = got[flows[1].side, rows].astype(jnp.float32)
                out_ref[rows] = (other + x_ref[rows].astype(jnp.float32)).astype(out_ref.dtype)

            @pl.when(jnp.logical_not(is_end))
            def _():
                other = got[0, rows].astype(jnp.float32) + got[1, rows].astype(jnp.float32)
                out_ref[rows] = (other + x_ref[rows].astype(jnp.float32)).astype(out_ref.dtype)

        return carry

    lax.fori_loop(0, chunks + END_LAG, step, 0)

    def drain(chunk, carry):
        for flow in flows:

            @pl.when(flow.has_target)
            def _():
                copy_of(flow, chunk, x_ref).wait_send()

        return carry

    lax.fori_loop(0, chunks, drain, 0)


def line_sum(x, size, collective_id, chunk_rows=64):
    rows, cols = x.shape
    chunks = rows // chunk_rows
    return pl.pallas_call(
        partial(line_sum_kernel, size, chunk_rows),
        out_shape=jax.ShapeDtypeStruct(x.shape, x.dtype),
        in_specs=[pl.BlockSpec(memory_space=pltpu.VMEM)],
        out_specs=pl.BlockSpec(memory_space=pltpu.VMEM),
        scratch_shapes=[
            pltpu.VMEM((2, rows, cols), x.dtype),
            pltpu.VMEM((2, rows, cols), x.dtype),
            pltpu.SemaphoreType.DMA((2, chunks)),
            pltpu.SemaphoreType.DMA((2, chunks)),
        ],
        compiler_params=pltpu.CompilerParams(
            collective_id=collective_id, has_side_effects=True, vmem_limit_bytes=48 * 1024 * 1024
        ),
        cost_estimate=pl.CostEstimate(flops=0, bytes_accessed=link_cost(rows * cols), transcendentals=0),
        name="line_sum",
    )(x)


def line_gather_kernel(size, chunk_rows, x_ref, out_ref, send_sem, recv_sem):
    line_barrier(size)
    me = lax.axis_index(LINE)
    flows = two_flows(size)
    width = x_ref.shape[1]
    chunks = x_ref.shape[0] // chunk_rows

    def place(block, chunk):
        rows = pl.ds(pl.multiple_of(chunk * chunk_rows, chunk_rows), chunk_rows)
        return out_ref.at[rows, pl.ds(pl.multiple_of(block * width, width), width)]

    def copy_of(flow, block, chunk):
        return flow.copy(
            place(block, chunk), place(block, chunk), send_sem.at[flow.side, block, chunk], recv_sem.at[flow.side, block, chunk]
        )

    def step(chunk, carry):
        rows = pl.ds(pl.multiple_of(chunk * chunk_rows, chunk_rows), chunk_rows)
        out_ref[rows, pl.ds(pl.multiple_of(me * width, width), width)] = x_ref[rows]
        for flow in flows:

            @pl.when(flow.has_target)
            def _():
                copy_of(flow, me, chunk).start()

        return carry

    lax.fori_loop(0, chunks, step, 0)
    for hop in range(1, size):

        def forward(chunk, carry):
            for flow in flows:
                block = me - hop * flow.step
                exists = (block >= 0) & (block < size)

                @pl.when(exists)
                def _():
                    copy_of(flow, block, chunk).wait_recv()

                @pl.when(exists & flow.has_target)
                def _():
                    copy_of(flow, block, chunk).start()

            return carry

        lax.fori_loop(0, chunks, forward, 0)
    for hop in range(size):

        def drain(chunk, carry):
            for flow in flows:
                block = me - hop * flow.step
                exists = (block >= 0) & (block < size)

                @pl.when(exists & flow.has_target)
                def _():
                    copy_of(flow, block, chunk).wait_send()

            return carry

        lax.fori_loop(0, chunks, drain, 0)


def line_gather(x, size, collective_id, chunk_rows=256):
    rows, cols = x.shape
    chunks = rows // chunk_rows
    return pl.pallas_call(
        partial(line_gather_kernel, size, chunk_rows),
        out_shape=jax.ShapeDtypeStruct((rows, size * cols), x.dtype),
        in_specs=[pl.BlockSpec(memory_space=pltpu.VMEM)],
        out_specs=pl.BlockSpec(memory_space=pltpu.VMEM),
        scratch_shapes=[
            pltpu.SemaphoreType.DMA((2, size, chunks)),
            pltpu.SemaphoreType.DMA((2, size, chunks)),
        ],
        compiler_params=pltpu.CompilerParams(
            collective_id=collective_id, has_side_effects=True, vmem_limit_bytes=48 * 1024 * 1024
        ),
        cost_estimate=pl.CostEstimate(flops=0, bytes_accessed=link_cost(3 * rows * cols), transcendentals=0),
        name="line_gather",
    )(x)


def line_scatter_kernel(size, chunk_rows, x_ref, out_ref, got, sent, send_sem, recv_sem):
    line_barrier(size)
    me = lax.axis_index(LINE)
    flows = two_flows(size)
    width = out_ref.shape[1]
    chunks = x_ref.shape[0] // chunk_rows

    def rows_of(chunk):
        return pl.ds(pl.multiple_of(chunk * chunk_rows, chunk_rows), chunk_rows)

    def cols_of(block):
        return pl.ds(pl.multiple_of(block * width, width), width)

    def copy_of(flow, block, chunk, source):
        return flow.copy(
            source,
            got.at[flow.side, rows_of(chunk), cols_of(block)],
            send_sem.at[flow.side, block, chunk],
            recv_sem.at[flow.side, block, chunk],
        )

    def own(block, chunk):
        return x_ref[rows_of(chunk), cols_of(block)].astype(jnp.float32)

    for hop in range(size - 1):

        def forward(chunk, carry):
            for flow in flows:
                block = jnp.where(flow.side == 0, size - 1 - hop, hop)
                ahead = (block - me) * flow.step > 0

                @pl.when(ahead & flow.has_source)
                def _():
                    source = x_ref.at[rows_of(chunk), cols_of(block)]
                    copy_of(flow, block, chunk, source).wait_recv()
                    total = got[flow.side, rows_of(chunk), cols_of(block)].astype(jnp.float32) + own(block, chunk)
                    sent[flow.side, rows_of(chunk), cols_of(block)] = total.astype(sent.dtype)
                    copy_of(flow, block, chunk, sent.at[flow.side, rows_of(chunk), cols_of(block)]).start()

                @pl.when(ahead & jnp.logical_not(flow.has_source))
                def _():
                    copy_of(flow, block, chunk, x_ref.at[rows_of(chunk), cols_of(block)]).start()

            return carry

        lax.fori_loop(0, chunks, forward, 0)

    def finish(chunk, carry):
        rows = rows_of(chunk)
        for flow in flows:

            @pl.when(flow.has_source)
            def _():
                copy_of(flow, me, chunk, x_ref.at[rows, cols_of(me)]).wait_recv()

        @pl.when(me == 0)
        def _():
            out_ref[rows] = (got[1, rows, cols_of(me)].astype(jnp.float32) + own(me, chunk)).astype(out_ref.dtype)

        @pl.when(me == size - 1)
        def _():
            out_ref[rows] = (got[0, rows, cols_of(me)].astype(jnp.float32) + own(me, chunk)).astype(out_ref.dtype)

        @pl.when((me > 0) & (me < size - 1))
        def _():
            other = got[0, rows, cols_of(me)].astype(jnp.float32) + got[1, rows, cols_of(me)].astype(jnp.float32)
            out_ref[rows] = (other + own(me, chunk)).astype(out_ref.dtype)

        return carry

    lax.fori_loop(0, chunks, finish, 0)
    for hop in range(size - 1):

        def drain(chunk, carry):
            for flow in flows:
                block = jnp.where(flow.side == 0, size - 1 - hop, hop)
                ahead = (block - me) * flow.step > 0

                @pl.when(ahead)
                def _():
                    copy_of(flow, block, chunk, x_ref.at[rows_of(chunk), cols_of(block)]).wait_send()

            return carry

        lax.fori_loop(0, chunks, drain, 0)


def line_scatter(x, size, collective_id, out_dtype=jnp.float32, chunk_rows=256):
    rows, cols = x.shape
    chunks = rows // chunk_rows
    return pl.pallas_call(
        partial(line_scatter_kernel, size, chunk_rows),
        out_shape=jax.ShapeDtypeStruct((rows, cols // size), out_dtype),
        in_specs=[pl.BlockSpec(memory_space=pltpu.VMEM)],
        out_specs=pl.BlockSpec(memory_space=pltpu.VMEM),
        scratch_shapes=[
            pltpu.VMEM((2, rows, cols), x.dtype),
            pltpu.VMEM((2, rows, cols), x.dtype),
            pltpu.SemaphoreType.DMA((2, size, chunks)),
            pltpu.SemaphoreType.DMA((2, size, chunks)),
        ],
        compiler_params=pltpu.CompilerParams(
            collective_id=collective_id, has_side_effects=True, vmem_limit_bytes=48 * 1024 * 1024
        ),
        cost_estimate=pl.CostEstimate(flops=0, bytes_accessed=link_cost(3 * rows * cols // size), transcendentals=0),
        name="line_scatter",
    )(x)


def input_backward_kernel(
    seq_len, splits, whole_ref, dr_ref, dk_ref, dv_ref, dl_ref, three_ref, down_ref, params_ref, din_ref, gparams_ref, gdown_ref, carry, kept
):
    step = pl.program_id(0)
    tile = pl.num_programs(0) - 1 - step
    rows_each = dr_ref.shape[0]
    part = dr_ref.shape[1]
    width = whole_ref.shape[1]
    start = tile * rows_each
    at_start = lax.rem(start, seq_len) == 0
    at_end = lax.rem(start + rows_each, seq_len) == 0

    @pl.when(step == 0)
    def _():
        gparams_ref[...] = jnp.zeros_like(gparams_ref)
        gdown_ref[...] = jnp.zeros_like(gdown_ref)

    @pl.when(at_end)
    def _():
        carry[...] = jnp.zeros_like(carry)

    edge = 16
    rows = pl.ds(pl.multiple_of(start, rows_each), rows_each)
    edge_rows = pl.ds(pl.multiple_of(jnp.maximum(start - edge, 0), edge), edge)
    inverse_width = 1.0 / width

    def moments(place):
        values = whole_ref[place, :].astype(jnp.float32)
        centre = jnp.sum(values, axis=1, keepdims=True) * inverse_width
        values = values - centre
        spread = jnp.sum(values * values, axis=1, keepdims=True) * inverse_width
        return centre, lax.rsqrt(spread + norm_eps)

    centre, inv = moments(rows)
    edge_centre, edge_inv = moments(edge_rows)
    block_cols = 256
    row_index = iota((rows_each, block_cols), 0)
    dl = dl_ref[...]
    lane = iota(dl.shape, 1)
    zero = jnp.zeros_like(dl)
    first, second = splits
    dls = (
        jnp.where(lane < first, dl, zero),
        jnp.where((lane >= first) & (lane < second), dl, zero),
        jnp.where(lane >= second, dl, zero),
    )
    down_row = iota((dl.shape[1], block_cols), 0)
    sum_grad = jnp.zeros((rows_each, 1), jnp.float32)
    sum_prod = jnp.zeros((rows_each, 1), jnp.float32)

    def add_param(index, cols, values):
        total = values[0:8]
        for place in range(8, rows_each, 8):
            total = total + values[place : place + 8]
        gparams_ref[index, :, cols] += total

    for block in range(width // block_cols):
        cols = slice(block * block_cols, (block + 1) * block_cols)
        gain, bias = params_ref[0:1, cols], params_ref[1:2, cols]
        unit = (whole_ref[rows, cols].astype(jnp.float32) - centre) * inv
        normed = unit * gain + bias
        edge_unit = (whole_ref[edge_rows, cols].astype(jnp.float32) - edge_centre) * edge_inv
        edge_normed = (edge_unit * gain + bias)[edge - 1 : edge]
        edge_normed = jnp.where(at_start, 0.0, edge_normed)
        before = jnp.where(row_index == 0, edge_normed, pltpu.roll(normed, 1, 0))
        shift = before - normed
        down = down_ref[cols, :]
        weights = three_ref[cols, :]
        grads = (
            dot_nt(dr_ref[...], weights[:, :part]),
            dot_nt(dls[0], down),
            dot_nt(dk_ref[...], weights[:, part : 2 * part]),
            dot_nt(dv_ref[...], weights[:, 2 * part :]),
            dot_nt(dls[1], down),
            dot_nt(dls[2], down),
        )
        total = grads[0]
        for grad in grads[1:]:
            total = total + grad
        mixed = None
        for index, grad in enumerate(grads):
            rate = params_ref[2 + index : 3 + index, cols]
            mixed = grad * rate if mixed is None else mixed + grad * rate
            add_param(2 + index, cols, grad * shift)
        after = jnp.where(row_index == rows_each - 1, carry[0:1, cols], pltpu.roll(mixed, rows_each - 1, 0))
        carry[0:1, cols] = mixed[0:1]
        dnormed = total - mixed + after
        add_param(0, cols, dnormed * unit)
        add_param(1, cols, dnormed)
        dunit = dnormed * gain
        kept[:, cols] = dunit
        sum_grad = sum_grad + jnp.sum(dunit, axis=1, keepdims=True)
        sum_prod = sum_prod + jnp.sum(dunit * unit, axis=1, keepdims=True)
        outs = [
            dot_tn(dl, low(normed + shift * params_ref[index : index + 1, cols])) for index in (3, 6, 7)
        ]
        gdown_ref[:, cols] += jnp.where(
            down_row < first, outs[0], jnp.where(down_row < second, outs[1], outs[2])
        )
    sum_grad = sum_grad * inverse_width
    sum_prod = sum_prod * inverse_width
    for block in range(width // block_cols):
        cols = slice(block * block_cols, (block + 1) * block_cols)
        unit = (whole_ref[rows, cols].astype(jnp.float32) - centre) * inv
        din_ref[:, cols] = low(inv * (kept[:, cols] - sum_grad - unit * sum_prod))


def input_backward(whole, dr, dk, dv, dl, splits, three, down, params):
    positions, width = whole.shape
    part = dr.shape[1]
    rows_each = 256
    steps = positions // rows_each
    tile = lambda cols: pl.BlockSpec((rows_each, cols), lambda i: (steps - 1 - i, 0))
    full = pl.BlockSpec(memory_space=pltpu.VMEM)
    shape = jax.ShapeDtypeStruct
    return pl.pallas_call(
        partial(input_backward_kernel, SEQ_LEN, splits),
        grid=(steps,),
        in_specs=[full, tile(part), tile(part), tile(part), tile(dl.shape[1]), full, full, full],
        out_specs=[
            tile(width),
            pl.BlockSpec((8, 8, width), lambda i: (0, 0, 0)),
            pl.BlockSpec((dl.shape[1], width), lambda i: (0, 0)),
        ],
        out_shape=[
            shape((positions, width), jnp.bfloat16),
            shape((8, 8, width), jnp.float32),
            shape((dl.shape[1], width), jnp.float32),
        ],
        scratch_shapes=[pltpu.VMEM((8, width), jnp.float32), pltpu.VMEM((rows_each, width), jnp.float32)],
        compiler_params=pltpu.CompilerParams(
            dimension_semantics=("arbitrary",), vmem_limit_bytes=48 * 1024 * 1024
        ),
        name="input_backward",
    )(whole, dr, dk, dv, dl, three, down, params)


def weight_grads_kernel(left_refs, right_refs, out_ref):
    part = right_refs[0].shape[1]
    for index, (left_ref, right_ref) in enumerate(zip(left_refs, right_refs)):
        out_ref[:, index * part : (index + 1) * part] = low(dot_tn(left_ref[...], right_ref[...]))


def weight_grads(lefts, rights):
    positions, width = lefts[0].shape
    part = rights[0].shape[1]
    count = len(lefts)
    block = 512

    def kernel(*refs):
        weight_grads_kernel(refs[:count], refs[count : 2 * count], refs[2 * count])

    return pl.pallas_call(
        kernel,
        grid=(width // block,),
        in_specs=[pl.BlockSpec((positions, block), lambda i: (0, i))] * count
        + [pl.BlockSpec((positions, part), lambda i: (0, 0))] * count,
        out_specs=pl.BlockSpec((block, count * part), lambda i: (i, 0)),
        out_shape=jax.ShapeDtypeStruct((width, count * part), jnp.bfloat16),
        compiler_params=pltpu.CompilerParams(
            dimension_semantics=("arbitrary",), vmem_limit_bytes=40 * 1024 * 1024
        ),
        name="weight_grads",
    )(*lefts, *rights)


def line_error_kernel(
    size, chunk_rows, x_ref, base_ref, teacher_ref, weight_ref, state_ref, error_ref, got, sent, send_sem, recv_sem, out_send_sem, out_recv_sem
):
    line_barrier(size)
    me = lax.axis_index(LINE)
    flows = two_flows(size)
    width = base_ref.shape[1]
    chunks = x_ref.shape[0] // chunk_rows
    is_end = (me == 0) | (me == size - 1)
    lag = jnp.where(is_end, END_LAG, MID_LAG)

    def rows_of(chunk):
        return pl.ds(pl.multiple_of(chunk * chunk_rows, chunk_rows), chunk_rows)

    def cols_of(block):
        return pl.ds(pl.multiple_of(block * width, width), width)

    def part_copy(flow, block, chunk, source):
        place = (rows_of(chunk), cols_of(block))
        return flow.copy(
            source.at[place],
            got.at[(flow.side,) + place],
            send_sem.at[flow.side, block, chunk],
            recv_sem.at[flow.side, block, chunk],
        )

    def error_copy(flow, block, chunk):
        place = error_ref.at[rows_of(chunk), cols_of(block)]
        return flow.copy(
            place, place, out_send_sem.at[flow.side, block, chunk], out_recv_sem.at[flow.side, block, chunk]
        )

    def target_of(flow, hop):
        block = jnp.where(flow.side == 0, size - 1 - hop, hop)
        return block, (block - me) * flow.step > 0

    def reduce_part(flow, chunk):
        for hop in range(size - 1):
            block, ahead = target_of(flow, hop)

            @pl.when(ahead & flow.has_source)
            def _():
                part_copy(flow, block, chunk, x_ref).wait_recv()
                place = (rows_of(chunk), cols_of(block))
                total = got[(flow.side,) + place].astype(jnp.float32) + x_ref[place].astype(jnp.float32)
                sent[(flow.side,) + place] = total.astype(sent.dtype)
                part_copy(flow, block, chunk, sent.at[flow.side]).start()

            @pl.when(ahead & jnp.logical_not(flow.has_source))
            def _():
                part_copy(flow, block, chunk, x_ref).start()

    def finish(chunk):
        rows = rows_of(chunk)
        for flow in flows:

            @pl.when(flow.has_source)
            def _():
                part_copy(flow, me, chunk, x_ref).wait_recv()

        def write(others):
            result = base_ref[rows] + (others + x_ref[rows, cols_of(me)].astype(jnp.float32))
            state_ref[rows] = result.astype(state_ref.dtype)
            error = weight_ref[rows, 0:1] * (result - teacher_ref[rows].astype(jnp.float32))
            error_ref[rows, cols_of(me)] = error.astype(error_ref.dtype)

        @pl.when(is_end)
        def _():
            write(got[flows[1].side, rows, cols_of(me)].astype(jnp.float32))

        @pl.when(jnp.logical_not(is_end))
        def _():
            write(
                got[0, rows, cols_of(me)].astype(jnp.float32) + got[1, rows, cols_of(me)].astype(jnp.float32)
            )

        for flow in flows:

            @pl.when(flow.has_target)
            def _():
                error_copy(flow, me, chunk).start()

    def forward(hop, chunk):
        for flow in flows:
            block = me - hop * flow.step
            exists = (block >= 0) & (block < size)

            @pl.when(exists)
            def _():
                error_copy(flow, block, chunk).wait_recv()

            @pl.when(exists & flow.has_target)
            def _():
                error_copy(flow, block, chunk).start()

    def at(chunk, action):
        @pl.when((chunk >= 0) & (chunk < chunks))
        def _():
            action(chunk)

    def step(turn, carry):
        at(turn, lambda chunk: reduce_part(flows[0], chunk))
        at(turn - lag, lambda chunk: reduce_part(flows[1], chunk))
        at(turn - lag - 1, finish)
        for hop in range(1, size):
            at(turn - lag - 1 - 2 * hop, partial(forward, hop))
        return carry

    lax.fori_loop(0, chunks + END_LAG + 1 + 2 * (size - 1), step, 0)

    def drain(chunk, carry):
        for flow in flows:
            for hop in range(size - 1):
                block, ahead = target_of(flow, hop)

                @pl.when(ahead)
                def _():
                    part_copy(flow, block, chunk, x_ref).wait_send()

            for hop in range(size):
                source = me - hop * flow.step
                exists = (source >= 0) & (source < size)

                @pl.when(exists & flow.has_target)
                def _():
                    error_copy(flow, source, chunk).wait_send()

        return carry

    lax.fori_loop(0, chunks, drain, 0)


def line_error(x, base, teacher, weight, size, collective_id, chunk_rows=64):
    rows, cols = x.shape
    chunks = rows // chunk_rows
    sems = pltpu.SemaphoreType.DMA((2, size, chunks))
    return pl.pallas_call(
        partial(line_error_kernel, size, chunk_rows),
        out_shape=[
            jax.ShapeDtypeStruct(base.shape, jnp.bfloat16),
            jax.ShapeDtypeStruct(x.shape, jnp.bfloat16),
        ],
        in_specs=[pl.BlockSpec(memory_space=pltpu.VMEM)] * 4,
        out_specs=[pl.BlockSpec(memory_space=pltpu.VMEM)] * 2,
        scratch_shapes=[
            pltpu.VMEM((2, rows, cols), x.dtype),
            pltpu.VMEM((2, rows, cols), x.dtype),
            sems,
            sems,
            sems,
            sems,
        ],
        compiler_params=pltpu.CompilerParams(
            collective_id=collective_id, has_side_effects=True, vmem_limit_bytes=48 * 1024 * 1024
        ),
        cost_estimate=pl.CostEstimate(flops=0, bytes_accessed=link_cost(rows * cols), transcendentals=0),
        name="line_error",
    )(x, base, teacher, weight)


def output_backward_kernel(
    seq_len, whole_ref, delta_ref, dpre_ref, weight_ref, params_ref, dres_ref, gparams_ref, carry, kept
):
    step = pl.program_id(0)
    tile = pl.num_programs(0) - 1 - step
    rows_each = dpre_ref.shape[0]
    width = whole_ref.shape[1]
    start = tile * rows_each
    at_start = lax.rem(start, seq_len) == 0
    at_end = lax.rem(start + rows_each, seq_len) == 0

    @pl.when(step == 0)
    def _():
        gparams_ref[...] = jnp.zeros_like(gparams_ref)

    @pl.when(at_end)
    def _():
        carry[...] = jnp.zeros_like(carry)

    edge = 16
    rows = pl.ds(pl.multiple_of(start, rows_each), rows_each)
    edge_rows = pl.ds(pl.multiple_of(jnp.maximum(start - edge, 0), edge), edge)
    inverse_width = 1.0 / width

    def residual(place, cols):
        return whole_ref[place, cols].astype(jnp.float32) + delta_ref[place, cols].astype(jnp.float32)

    def moments(place):
        values = residual(place, slice(0, width))
        centre = jnp.sum(values, axis=1, keepdims=True) * inverse_width
        values = values - centre
        spread = jnp.sum(values * values, axis=1, keepdims=True) * inverse_width
        return centre, lax.rsqrt(spread + norm_eps)

    centre, inv = moments(rows)
    edge_centre, edge_inv = moments(edge_rows)
    block_cols = 256
    row_index = iota((rows_each, block_cols), 0)
    sum_grad = jnp.zeros((rows_each, 1), jnp.float32)
    sum_prod = jnp.zeros((rows_each, 1), jnp.float32)

    def add_param(index, cols, values):
        total = values[0:8]
        for place in range(8, rows_each, 8):
            total = total + values[place : place + 8]
        gparams_ref[index, :, cols] += total

    for block in range(width // block_cols):
        cols = slice(block * block_cols, (block + 1) * block_cols)
        gain, bias, rate = params_ref[0:1, cols], params_ref[1:2, cols], params_ref[2:3, cols]
        unit = (residual(rows, cols) - centre) * inv
        normed = unit * gain + bias
        edge_unit = (residual(edge_rows, cols) - edge_centre) * edge_inv
        edge_normed = (edge_unit * gain + bias)[edge - 1 : edge]
        edge_normed = jnp.where(at_start, 0.0, edge_normed)
        before = jnp.where(row_index == 0, edge_normed, pltpu.roll(normed, 1, 0))
        grad = dot_nt(dpre_ref[...], weight_ref[cols, :])
        add_param(2, cols, grad * (before - normed))
        mixed = grad * rate
        after = jnp.where(row_index == rows_each - 1, carry[0:1, cols], pltpu.roll(mixed, rows_each - 1, 0))
        carry[0:1, cols] = mixed[0:1]
        dnormed = grad - mixed + after
        add_param(0, cols, dnormed * unit)
        add_param(1, cols, dnormed)
        dunit = dnormed * gain
        kept[:, cols] = dunit
        sum_grad = sum_grad + jnp.sum(dunit, axis=1, keepdims=True)
        sum_prod = sum_prod + jnp.sum(dunit * unit, axis=1, keepdims=True)
    sum_grad = sum_grad * inverse_width
    sum_prod = sum_prod * inverse_width
    for block in range(width // block_cols):
        cols = slice(block * block_cols, (block + 1) * block_cols)
        unit = (residual(rows, cols) - centre) * inv
        dres_ref[:, cols] = low(inv * (kept[:, cols] - sum_grad - unit * sum_prod))


def output_backward(whole, delta, dpre, weight, params):
    positions, width = whole.shape
    rows_each = 256
    steps = positions // rows_each
    tile = lambda cols: pl.BlockSpec((rows_each, cols), lambda i: (steps - 1 - i, 0))
    full = pl.BlockSpec(memory_space=pltpu.VMEM)
    return pl.pallas_call(
        partial(output_backward_kernel, SEQ_LEN),
        grid=(steps,),
        in_specs=[full, full, tile(dpre.shape[1]), full, full],
        out_specs=[tile(width), pl.BlockSpec((8, 8, width), lambda i: (0, 0, 0))],
        out_shape=[
            jax.ShapeDtypeStruct((positions, width), jnp.bfloat16),
            jax.ShapeDtypeStruct((8, 8, width), jnp.float32),
        ],
        scratch_shapes=[pltpu.VMEM((8, width), jnp.float32), pltpu.VMEM((rows_each, width), jnp.float32)],
        compiler_params=pltpu.CompilerParams(
            dimension_semantics=("arbitrary",), vmem_limit_bytes=48 * 1024 * 1024
        ),
        name="output_backward",
    )(whole, delta, dpre, weight, params)


def input_forward_kernel(
    seq_len,
    tanh_end,
    plain_end,
    whole_ref,
    three_ref,
    down_ref,
    ups_ref,
    params_ref,
    r_ref,
    k_ref,
    v_ref,
    dw_ref,
    da_ref,
    gate_ref,
    mr_ref,
    mk_ref,
    mv_ref,
    inner_ref,
):
    tile = pl.program_id(0)
    rows_each = r_ref.shape[0]
    part = r_ref.shape[1]
    width = whole_ref.shape[1]
    start = tile * rows_each
    at_start = lax.rem(start, seq_len) == 0
    edge = 16
    rows = pl.ds(pl.multiple_of(start, rows_each), rows_each)
    edge_rows = pl.ds(pl.multiple_of(jnp.maximum(start - edge, 0), edge), edge)
    inverse_width = 1.0 / width

    def moments(place):
        values = whole_ref[place, :].astype(jnp.float32)
        centre = jnp.sum(values, axis=1, keepdims=True) * inverse_width
        values = values - centre
        spread = jnp.sum(values * values, axis=1, keepdims=True) * inverse_width
        return centre, lax.rsqrt(spread + norm_eps)

    centre, inv = moments(rows)
    edge_centre, edge_inv = moments(edge_rows)
    block_cols = 256
    row_index = iota((rows_each, block_cols), 0)
    lane = iota((rows_each, down_ref.shape[1]), 1)
    r = k = v = inner_w = inner_a = inner_g = 0.0
    for block in range(width // block_cols):
        cols = slice(block * block_cols, (block + 1) * block_cols)
        gain, bias = params_ref[0:1, cols], params_ref[1:2, cols]
        normed = (whole_ref[rows, cols].astype(jnp.float32) - centre) * inv * gain + bias
        edge_unit = (whole_ref[edge_rows, cols].astype(jnp.float32) - edge_centre) * edge_inv
        edge_normed = (edge_unit * gain + bias)[edge - 1 : edge]
        edge_normed = jnp.where(at_start, 0.0, edge_normed)
        before = jnp.where(row_index == 0, edge_normed, pltpu.roll(normed, 1, 0))
        shift = before - normed

        def mix(index):
            return low(normed + shift * params_ref[index : index + 1, cols])

        mix_r, mix_k, mix_v = mix(2), mix(4), mix(5)
        mr_ref[:, cols], mk_ref[:, cols], mv_ref[:, cols] = mix_r, mix_k, mix_v
        weights = three_ref[cols, :]
        r = r + dot_nn(mix_r, weights[:, :part])
        k = k + dot_nn(mix_k, weights[:, part : 2 * part])
        v = v + dot_nn(mix_v, weights[:, 2 * part :])
        down = down_ref[cols, :]
        inner_w = inner_w + dot_nn(mix(3), down)
        inner_a = inner_a + dot_nn(mix(6), down)
        inner_g = inner_g + dot_nn(mix(7), down)
    r_ref[...], k_ref[...], v_ref[...] = r, k, v
    inner = jnp.where(
        lane < tanh_end,
        jnp.tanh(inner_w),
        jnp.where(lane < plain_end, inner_a, jax.nn.sigmoid(inner_g)),
    )
    inner_ref[...] = inner
    inner_low = low(inner)
    zero = jnp.zeros_like(inner_low)
    ups = ups_ref[...]
    dw_ref[...] = dot_nn(jnp.where(lane < tanh_end, inner_low, zero), ups)
    da_ref[...] = dot_nn(jnp.where((lane >= tanh_end) & (lane < plain_end), inner_low, zero), ups)
    gate_ref[...] = dot_nn(jnp.where(lane >= plain_end, inner_low, zero), ups)


def input_forward(whole, three, down, ups, ends, params):
    positions, width = whole.shape
    part = ups.shape[1]
    rows_each = 256
    tile = lambda cols: pl.BlockSpec((rows_each, cols), lambda i: (i, 0))
    full = pl.BlockSpec(memory_space=pltpu.VMEM)
    shape = jax.ShapeDtypeStruct
    return pl.pallas_call(
        partial(input_forward_kernel, SEQ_LEN, *ends),
        grid=(positions // rows_each,),
        in_specs=[full] * 5,
        out_specs=[tile(part)] * 6 + [tile(width)] * 3 + [tile(down.shape[1])],
        out_shape=[shape((positions, part), jnp.float32)] * 6
        + [shape((positions, width), jnp.bfloat16)] * 3
        + [shape((positions, down.shape[1]), jnp.float32)],
        compiler_params=pltpu.CompilerParams(
            dimension_semantics=("arbitrary",), vmem_limit_bytes=52 * 1024 * 1024
        ),
        name="input_forward",
    )(whole, three, down, ups, params)


def start_gather_kernel(
    size,
    groups,
    chunk_rows,
    x_ref,
    narrow_ref,
    ups_ref,
    out_ref,
    narrow_out,
    ups_out,
    send_sem,
    recv_sem,
    line_send,
    line_recv,
    group_send,
    group_recv,
):
    me = lax.axis_index(LINE)
    mine = lax.axis_index(GROUP)
    barrier = pltpu.get_barrier_semaphore()
    for offset in range(1, groups):
        peer = lax.rem(mine + offset, groups)
        pl.semaphore_signal(barrier, inc=1, device_id={GROUP: peer}, device_id_type=pl.DeviceIdType.MESH)

    @pl.when(me > 0)
    def _():
        pl.semaphore_signal(barrier, inc=1, device_id={LINE: me - 1}, device_id_type=pl.DeviceIdType.MESH)

    @pl.when(me < size - 1)
    def _():
        pl.semaphore_signal(barrier, inc=1, device_id={LINE: me + 1}, device_id_type=pl.DeviceIdType.MESH)

    ends = jnp.where((me == 0) | (me == size - 1), 1, 2)
    pl.semaphore_wait(barrier, ends + groups - 1)
    flows = two_flows(size)
    width = x_ref.shape[1]
    chunks = x_ref.shape[0] // chunk_rows

    def place(block, chunk):
        rows = pl.ds(pl.multiple_of(chunk * chunk_rows, chunk_rows), chunk_rows)
        return out_ref.at[rows, pl.ds(pl.multiple_of(block * width, width), width)]

    def copy_of(flow, block, chunk):
        return flow.copy(
            place(block, chunk), place(block, chunk), send_sem.at[flow.side, block, chunk], recv_sem.at[flow.side, block, chunk]
        )

    def narrow_copy(flow, block):
        spot = narrow_out.at[mine, block]
        return flow.copy(spot, spot, line_send.at[flow.side, block], line_recv.at[flow.side, block])

    def group_copy(kind, out, peer, slot):
        return pltpu.make_async_remote_copy(
            src_ref=out.at[slot],
            dst_ref=out.at[slot],
            send_sem=group_send.at[kind, peer],
            recv_sem=group_recv.at[kind, slot],
            device_id={GROUP: peer},
            device_id_type=pl.DeviceIdType.MESH,
        )

    narrow_out[mine, me] = narrow_ref[...]
    for flow in flows:

        @pl.when(flow.has_target)
        def _():
            narrow_copy(flow, me).start()

    def first(chunk, carry):
        rows = pl.ds(pl.multiple_of(chunk * chunk_rows, chunk_rows), chunk_rows)
        out_ref[rows, pl.ds(pl.multiple_of(me * width, width), width)] = x_ref[rows]
        for flow in flows:

            @pl.when(flow.has_target)
            def _():
                copy_of(flow, me, chunk).start()

        return carry

    lax.fori_loop(0, chunks, first, 0)
    ups_out[mine] = ups_ref[...]
    for offset in range(1, groups):
        group_copy(0, ups_out, lax.rem(mine + offset, groups), mine).start()
    for hop in range(1, size):
        for flow in flows:
            block = me - hop * flow.step
            exists = (block >= 0) & (block < size)

            @pl.when(exists)
            def _():
                narrow_copy(flow, block).wait_recv()

            @pl.when(exists & flow.has_target)
            def _():
                narrow_copy(flow, block).start()

        if hop == size - 1:
            for offset in range(1, groups):
                group_copy(1, narrow_out, lax.rem(mine + offset, groups), mine).start()

        def forward(chunk, carry):
            for flow in flows:
                block = me - hop * flow.step
                exists = (block >= 0) & (block < size)

                @pl.when(exists)
                def _():
                    copy_of(flow, block, chunk).wait_recv()

                @pl.when(exists & flow.has_target)
                def _():
                    copy_of(flow, block, chunk).start()

            return carry

        lax.fori_loop(0, chunks, forward, 0)
    for offset in range(1, groups):
        peer = lax.rem(mine + offset, groups)
        for kind, out in ((0, ups_out), (1, narrow_out)):
            group_copy(kind, out, peer, peer).wait_recv()
            group_copy(kind, out, peer, mine).wait_send()
    for hop in range(size):

        def drain(chunk, carry):
            for flow in flows:
                block = me - hop * flow.step
                exists = (block >= 0) & (block < size)

                @pl.when(exists & flow.has_target)
                def _():
                    copy_of(flow, block, chunk).wait_send()

            return carry

        lax.fori_loop(0, chunks, drain, 0)
        for flow in flows:
            block = me - hop * flow.step
            exists = (block >= 0) & (block < size)

            @pl.when(exists & flow.has_target)
            def _():
                narrow_copy(flow, block).wait_send()


def start_gather(x, narrow, ups, size, groups, collective_id, chunk_rows=256):
    rows, cols = x.shape
    chunks = rows // chunk_rows
    shape = jax.ShapeDtypeStruct
    dma = pltpu.SemaphoreType.DMA
    return pl.pallas_call(
        partial(start_gather_kernel, size, groups, chunk_rows),
        out_shape=[
            shape((rows, size * cols), x.dtype),
            shape((groups, size) + narrow.shape, x.dtype),
            shape((groups,) + ups.shape, x.dtype),
        ],
        in_specs=[pl.BlockSpec(memory_space=pltpu.VMEM)] * 3,
        out_specs=[pl.BlockSpec(memory_space=pltpu.VMEM)] * 3,
        scratch_shapes=[
            dma((2, size, chunks)),
            dma((2, size, chunks)),
            dma((2, size)),
            dma((2, size)),
            dma((2, groups)),
            dma((2, groups)),
        ],
        compiler_params=pltpu.CompilerParams(
            collective_id=collective_id, has_side_effects=True, vmem_limit_bytes=48 * 1024 * 1024
        ),
        cost_estimate=pl.CostEstimate(flops=0, bytes_accessed=link_cost(3 * rows * cols), transcendentals=0),
        name="start_gather",
    )(x, narrow, ups)


def channel_forward_kernel(
    seq_len,
    whole_ref,
    delta_ref,
    key_ref,
    value_ref,
    params_ref,
    mixed_ref,
    active_ref,
    squared_ref,
    part_ref,
    own_ref,
):
    tile = pl.program_id(0)
    rows_each = mixed_ref.shape[0]
    width = whole_ref.shape[1]
    own_width = own_ref.shape[1]
    start = tile * rows_each
    at_start = lax.rem(start, seq_len) == 0
    edge = 16
    rows = pl.ds(pl.multiple_of(start, rows_each), rows_each)
    edge_rows = pl.ds(pl.multiple_of(jnp.maximum(start - edge, 0), edge), edge)
    inverse_width = 1.0 / width

    def residual(place, cols):
        return whole_ref[place, cols].astype(jnp.float32) + delta_ref[place, cols].astype(jnp.float32)

    def moments(place):
        values = residual(place, slice(0, width))
        centre = jnp.sum(values, axis=1, keepdims=True) * inverse_width
        values = values - centre
        spread = jnp.sum(values * values, axis=1, keepdims=True) * inverse_width
        return centre, lax.rsqrt(spread + norm_eps)

    centre, inv = moments(rows)
    edge_centre, edge_inv = moments(edge_rows)
    own_start = pl.multiple_of(lax.axis_index(LINE) * own_width, own_width)
    own_ref[...] = residual(rows, pl.ds(own_start, own_width))
    block_cols = 256
    row_index = iota((rows_each, block_cols), 0)
    for block in range(width // block_cols):
        cols = slice(block * block_cols, (block + 1) * block_cols)
        gain, bias, rate = params_ref[0:1, cols], params_ref[1:2, cols], params_ref[2:3, cols]
        normed = (residual(rows, cols) - centre) * inv * gain + bias
        edge_unit = (residual(edge_rows, cols) - edge_centre) * edge_inv
        edge_normed = (edge_unit * gain + bias)[edge - 1 : edge]
        edge_normed = jnp.where(at_start, 0.0, edge_normed)
        before = jnp.where(row_index == 0, edge_normed, pltpu.roll(normed, 1, 0))
        mixed_ref[:, cols] = low(normed + (before - normed) * rate)
    hidden_cols = 512
    for block in range(key_ref.shape[1] // hidden_cols):
        cols = slice(block * hidden_cols, (block + 1) * hidden_cols)
        active = jnp.maximum(dot_nn(mixed_ref[...], key_ref[:, cols]), 0.0)
        active_ref[:, cols] = active
        squared_ref[:, cols] = low(active * active)
    for block in range(width // hidden_cols):
        cols = slice(block * hidden_cols, (block + 1) * hidden_cols)
        part_ref[:, cols] = low(dot_nn(squared_ref[...], value_ref[:, cols]))


def channel_forward(whole, delta, key_w, value_w, params, own_width):
    positions, width = whole.shape
    units = key_w.shape[1]
    rows_each = 256
    tile = lambda cols: pl.BlockSpec((rows_each, cols), lambda i: (i, 0))
    full = pl.BlockSpec(memory_space=pltpu.VMEM)
    shape = jax.ShapeDtypeStruct
    return pl.pallas_call(
        partial(channel_forward_kernel, SEQ_LEN),
        grid=(positions // rows_each,),
        in_specs=[full] * 5,
        out_specs=[tile(width), tile(units), tile(units), tile(width), tile(own_width)],
        out_shape=[
            shape((positions, width), jnp.bfloat16),
            shape((positions, units), jnp.float32),
            shape((positions, units), jnp.bfloat16),
            shape((positions, width), jnp.bfloat16),
            shape((positions, own_width), jnp.float32),
        ],
        compiler_params=pltpu.CompilerParams(
            dimension_semantics=("arbitrary",), vmem_limit_bytes=56 * 1024 * 1024
        ),
        name="channel_forward",
    )(whole, delta, key_w, value_w, params)


def matmul(left_op, right_op):
    return jnp.dot(left_op, right_op, preferred_element_type=jnp.float32)


def contract_rows(left_op, right_op):
    return jnp.einsum("tk,tn->kn", left_op, right_op, preferred_element_type=jnp.float32)


def against(grad_op, weight_op):
    return jnp.einsum("tn,kn->tk", grad_op, weight_op, preferred_element_type=jnp.float32)


def body(
    hidden,
    teacher,
    lengths,
    feature_params,
    decay_down,
    rate_down,
    gate_down,
    decay_up,
    rate_up,
    gate_up,
    receptance,
    key_proj,
    value_proj,
    output_proj,
    ffn_key,
    ffn_value,
):
    position_count, part_width = hidden.shape
    seq_dev = position_count // SEQ_LEN
    mp_index = lax.axis_index("mp")
    col_start = mp_index * part_width
    groups = lax.axis_size("dp")
    own_lengths = lax.dynamic_slice_in_dim(lengths, lax.axis_index("dp") * seq_dev, seq_dev)
    places = jnp.arange(SEQ_LEN, dtype=jnp.int32)
    valid = (places[None, :] < own_lengths[:, None]).astype(jnp.float32).reshape(position_count)
    loss_scale = position_count * lax.axis_size("dp") / jnp.sum(lengths).astype(jnp.float32)
    line_size = lax.axis_size("mp")
    low_rank = (decay_down.shape[1], rate_down.shape[1], gate_down.shape[1])
    narrow = jnp.concatenate([decay_down, rate_down, gate_down, feature_params], axis=1)
    narrow = jnp.pad(narrow, ((0, 0), (0, -narrow.shape[1] % 128)))
    ups = jnp.concatenate([decay_up, rate_up, gate_up], axis=0)
    ups = jnp.pad(ups, ((0, -ups.shape[0] % 16), (0, 0)))
    whole_low, narrow_w, ups = start_gather(hidden, narrow, ups, line_size, groups, 1)
    narrow_w = narrow_w.reshape(-1, narrow.shape[1])
    decay_down_w = narrow_w[:, : low_rank[0]]
    rate_down_w = narrow_w[:, low_rank[0] : low_rank[0] + low_rank[1]]
    gate_down_w = narrow_w[:, low_rank[0] + low_rank[1] : sum(low_rank)]
    params_low = narrow_w[:, sum(low_rank) : sum(low_rank) + feature_params.shape[1]]
    three = lax.all_gather(
        jnp.concatenate([receptance, key_proj, value_proj], axis=1), "dp", axis=0, tiled=True
    )
    up_rows = (decay_up.shape[0], rate_up.shape[0], gate_up.shape[0])
    decay_up_w = ups[:, : up_rows[0]].reshape(-1, part_width)
    rate_up_w = ups[:, up_rows[0] : up_rows[0] + up_rows[1]].reshape(-1, part_width)
    gate_up_w = ups[:, up_rows[0] + up_rows[1] : sum(up_rows)].reshape(-1, part_width)
    output_w = lax.all_gather(output_proj, "dp", axis=1, tiled=True)
    ffn_key_w = lax.all_gather(ffn_key, "dp", axis=0, tiled=True)
    ffn_value_w = lax.all_gather(ffn_value, "dp", axis=1, tiled=True)
    params = params_low.astype(jnp.float32)
    model_width = whole_low.shape[1]
    params_rows = jnp.pad(params.T, ((0, -params.shape[1] % 8), (0, 0)))
    up_all = jnp.concatenate([decay_up_w, rate_up_w, gate_up_w], axis=0)
    up_all = jnp.pad(up_all, ((0, narrow_w.shape[1] - up_all.shape[0]), (0, 0)))
    (
        acceptance_matrix,
        keys_in,
        payload_source,
        decay_in,
        rate_in,
        sigmoid_source,
        mix_r,
        mix_k,
        mix_v,
        inner_hid,
    ) = input_forward(
        whole_low, three, narrow_w, up_all, (low_rank[0], low_rank[0] + low_rank[1]), params_rows
    )
    inner_low = inner_hid.astype(jnp.bfloat16)
    decay_hid = inner_hid[:, : low_rank[0]]
    gate_hid = inner_hid[:, low_rank[0] + low_rank[1] : sum(low_rank)]
    decay_low = inner_low[:, : low_rank[0]]
    rate_low = inner_low[:, low_rank[0] : low_rank[0] + low_rank[1]]
    gate_low = inner_low[:, low_rank[0] + low_rank[1] : sum(low_rank)]
    columns = lax.dynamic_slice(params_rows, (8, col_start), (8, part_width))
    mixer_args = (
        own_lengths,
        acceptance_matrix,
        keys_in,
        payload_source,
        decay_in,
        rate_in,
        sigmoid_source,
        columns,
    )
    gated_low, *kept = run_mixer_forward(*mixer_args)
    delta_low = line_sum(matmul(gated_low, output_w).astype(jnp.bfloat16), line_size, 2)
    ffn_low, active, squared, ffn_part, own_residual = channel_forward(
        whole_low, delta_low, ffn_key_w, ffn_value_w, params_rows[15:23], part_width
    )
    error_scale = jnp.broadcast_to((loss_scale * valid)[:, None], (position_count, 128))
    out_state, grad_low = line_error(ffn_part, own_residual, teacher, error_scale, line_size, 3)
    grad_ffn_value = contract_rows(squared, grad_low).astype(jnp.bfloat16)
    grad_low, grad_ffn_value = lax.optimization_barrier((grad_low, grad_ffn_value))
    grad_ffn_value = lax.psum_scatter(grad_ffn_value, "dp", scatter_dimension=1, tiled=True)
    grad_squared = against(grad_low, ffn_value_w)
    grad_pre = (grad_squared * 2.0 * active).astype(jnp.bfloat16)
    grad_ffn_key = contract_rows(ffn_low, grad_pre).astype(jnp.bfloat16)
    grad_pre, grad_ffn_key = lax.optimization_barrier((grad_pre, grad_ffn_key))
    grad_ffn_key = lax.psum_scatter(grad_ffn_key, "dp", scatter_dimension=0, tiled=True)
    d_resid_part, d_params_out = output_backward(
        whole_low, delta_low, grad_pre, ffn_key_w, params_rows[15:23]
    )
    d_delta = line_sum(d_resid_part, line_size, 5)
    d_low = (grad_low.astype(jnp.float32) + d_delta.astype(jnp.float32)).astype(jnp.bfloat16)
    grad_output_proj = contract_rows(gated_low, d_low).astype(jnp.bfloat16)
    d_low, grad_output_proj = lax.optimization_barrier((d_low, grad_output_proj))
    grad_output_proj = lax.psum_scatter(grad_output_proj, "dp", scatter_dimension=1, tiled=True)
    d_gated = against(d_low, output_w)
    d_gated, grad_ffn_value, grad_ffn_key = lax.optimization_barrier(
        (d_gated, grad_ffn_value, grad_ffn_key)
    )
    d_recept, d_keys, d_values, d_decay, d_rate, d_gate, d_columns = run_mixer_backward(
        *mixer_args, *kept, d_gated
    )
    d_columns = jnp.sum(d_columns, axis=1)[:7]
    grad_three = weight_grads((mix_r, mix_k, mix_v), (d_recept, d_keys, d_values))
    d_decay, d_rate, d_gate, grad_three = lax.optimization_barrier((d_decay, d_rate, d_gate, grad_three))
    grad_three = lax.psum_scatter(grad_three, "dp", scatter_dimension=0, tiled=True)
    shares = [rank // line_size for rank in low_rank]
    starts = (0, shares[0], shares[0] + shares[1])
    own_rank = sum(shares) + -sum(shares) % 128

    def spread_rows(weight, share, start):
        grouped = weight.reshape(line_size, share, part_width)
        grouped = jnp.pad(grouped, ((0, 0), (start, own_rank - start - share), (0, 0)))
        return grouped.reshape(line_size * own_rank, part_width)

    def own_columns(values, share):
        return lax.dynamic_slice_in_dim(values, mp_index * share, share, 1)

    def own_group(members):
        taken = jnp.concatenate(
            [own_columns(member, share) for member, share in zip(members, shares)], axis=1
        )
        return jnp.pad(taken, ((0, 0), (0, own_rank - sum(shares))))

    d_inner = (
        against(d_decay, spread_rows(decay_up_w, shares[0], starts[0]))
        + against(d_rate, spread_rows(rate_up_w, shares[1], starts[1]))
        + against(d_gate, spread_rows(gate_up_w, shares[2], starts[2]))
    ).astype(jnp.bfloat16)
    d_own = line_scatter(d_inner, line_size, 6)
    d_own, grad_output_proj = lax.optimization_barrier((d_own, grad_output_proj))
    slope = own_group(
        (
            1.0 - decay_hid * decay_hid,
            jnp.ones((position_count, low_rank[1]), jnp.float32),
            gate_hid * (1.0 - gate_hid),
        )
    )
    d_own_pre = (d_own * slope).astype(jnp.bfloat16)
    down_own = own_group((decay_down_w, rate_down_w, gate_down_w))
    d_in_part, d_params_in, d_down = input_backward(
        whole_low, d_recept, d_keys, d_values, d_own_pre, starts[1:], three, down_own, params_rows
    )
    up_grads = jnp.concatenate(
        [
            contract_rows(low_part, grad).reshape(groups, -1, part_width)
            for low_part, grad in ((decay_low, d_decay), (rate_low, d_rate), (gate_low, d_gate))
        ],
        axis=1,
    ).astype(jnp.bfloat16)
    d_in_part, grad_three = lax.optimization_barrier((d_in_part, grad_three))
    core_grads = lax.dynamic_update_slice_in_dim(
        jnp.zeros((7, model_width), jnp.float32), d_columns, col_start, 1
    )
    param_rows = jnp.concatenate(
        [
            jnp.sum(d_params_in, axis=1),
            core_grads,
            jnp.sum(d_params_out, axis=1)[:3],
        ],
        axis=0,
    )
    param_count = param_rows.shape[0]
    narrow_grads = jnp.pad(
        jnp.concatenate([d_down, param_rows], axis=0), ((0, -(own_rank + param_count) % 32), (0, 0))
    )
    d_in_part, narrow_grads = lax.optimization_barrier((d_in_part, narrow_grads))
    narrow_grads = lax.psum_scatter(narrow_grads, "dp", scatter_dimension=1, tiled=True)
    up_grads = lax.psum_scatter(up_grads, "dp", scatter_dimension=0, tiled=True)
    up_grads = up_grads.reshape(-1, part_width).astype(jnp.float32)
    grad_hidden = line_scatter(d_in_part, line_size, 7) + (
        lax.dynamic_slice_in_dim(grad_low, col_start, part_width, 1).astype(jnp.float32)
        + lax.dynamic_slice_in_dim(d_delta, col_start, part_width, 1).astype(jnp.float32)
    )
    row_block = decay_down.shape[0]
    narrow_grads = jnp.pad(narrow_grads, ((0, 0), (0, -narrow_grads.shape[1] % 128)))
    narrow_rows = narrow_grads.shape[0]
    narrow_grads = line_gather(narrow_grads, line_size, 4, chunk_rows=narrow_rows // 4)
    narrow_grads = narrow_grads.reshape(narrow_rows, line_size, -1)
    narrow_grads = lax.dynamic_slice_in_dim(narrow_grads, mp_index * row_block, row_block, 2)

    def down_grad(start, share):
        taken = narrow_grads[start : start + share].transpose(1, 0, 2)
        return taken.reshape(line_size * share, row_block).T

    grad_params = jnp.sum(narrow_grads[own_rank : own_rank + param_count], axis=1).T
    return (
        out_state,
        grad_hidden,
        grad_params,
        down_grad(starts[0], shares[0]),
        down_grad(starts[1], shares[1]),
        down_grad(starts[2], shares[2]),
        up_grads[: up_rows[0]],
        up_grads[up_rows[0] : up_rows[0] + up_rows[1]],
        up_grads[up_rows[0] + up_rows[1] :],
        grad_three[:, :part_width].astype(jnp.float32),
        grad_three[:, part_width : 2 * part_width].astype(jnp.float32),
        grad_three[:, 2 * part_width :].astype(jnp.float32),
        grad_output_proj.astype(jnp.float32),
        grad_ffn_key.astype(jnp.float32),
        grad_ffn_value.astype(jnp.float32),
    )


def solution(mesh):
    in_specs = (
        P("dp", "mp"),
        P("dp", "mp"),
        P(),
        P(("dp", "mp"), None),
        P(("dp", "mp"), None),
        P(("dp", "mp"), None),
        P(("dp", "mp"), None),
        P("dp", "mp"),
        P("dp", "mp"),
        P("dp", "mp"),
        P("dp", "mp"),
        P("dp", "mp"),
        P("dp", "mp"),
        P("mp", "dp"),
        P("dp", "mp"),
        P("mp", "dp"),
    )
    out_specs = (
        P("dp", "mp"),
        P("dp", "mp"),
        P(("dp", "mp"), None),
        P(("dp", "mp"), None),
        P(("dp", "mp"), None),
        P(("dp", "mp"), None),
        P("dp", "mp"),
        P("dp", "mp"),
        P("dp", "mp"),
        P("dp", "mp"),
        P("dp", "mp"),
        P("dp", "mp"),
        P("mp", "dp"),
        P("dp", "mp"),
        P("mp", "dp"),
    )
    return jax.shard_map(body, mesh=mesh, in_specs=in_specs, out_specs=out_specs, check_vma=False)
```

```python
from functools import partial
import math
from types import SimpleNamespace

import jax
import jax.numpy as jnp
from jax import lax
from jax.experimental import pallas as pl
from jax.experimental.pallas import tpu as pltpu
from jax.sharding import PartitionSpec as P

norm_eps = 1e-05
SUBSPACE_SIZE = 64
SEQ_LEN = 1024
group_eps = 0.00064
CHUNK = 64
PAIR = 2 * SUBSPACE_SIZE
CHUNKS_FWD = 4
CHUNKS_BWD = 2
DECAY_SCALE = math.exp(-0.5)


def dot_nn(left_op, right_op):
    return lax.dot_general(left_op, right_op, (((1,), (0,)), ((), ())), preferred_element_type=jnp.float32)


def dot_nt(left_op, right_op):
    return lax.dot_general(left_op, right_op, (((1,), (1,)), ((), ())), preferred_element_type=jnp.float32)


def dot_tn(left_op, right_op):
    return lax.dot_general(left_op, right_op, (((0,), (0,)), ((), ())), preferred_element_type=jnp.float32)


def low(values):
    return values.astype(jnp.bfloat16)


def split_dot(ones_op, values):
    top = low(values)
    rest = values - top.astype(jnp.float32)
    mid = low(rest)
    tail = low(rest - mid.astype(jnp.float32))
    return dot_nn(ones_op, top) + dot_nn(ones_op, mid) + dot_nn(ones_op, tail)


def halves(values):
    top = low(values)
    return top, low(values - top.astype(jnp.float32))


def iota(shape, axis):
    return lax.broadcasted_iota(jnp.int32, shape, axis)


def head_masks():
    lane = iota((CHUNK, PAIR), 1)
    return lane < SUBSPACE_SIZE


def stack_heads(values):
    first = iota(values.shape, 1) < SUBSPACE_SIZE
    zero = jnp.zeros_like(values)
    return jnp.concatenate(
        [jnp.where(first, values, zero), jnp.where(first, zero, values)], axis=0
    )


def fold_heads(values):
    first = iota((CHUNK, PAIR), 1) < SUBSPACE_SIZE
    return jnp.where(first, values[:CHUNK], values[CHUNK:])


def head_ones():
    return (
        iota((PAIR, PAIR), 0) // SUBSPACE_SIZE == iota((PAIR, PAIR), 1) // SUBSPACE_SIZE
    )


def head_sum(values, ones_op):
    top = low(values)
    rest = low(values - top.astype(jnp.float32))
    return dot_nn(top, ones_op) + dot_nn(rest, ones_op)


def lower_inverses(lower_parts):
    row = iota((CHUNK, PAIR), 0)
    col = iota((CHUNK, PAIR), 1) % CHUNK
    eye = jnp.where(row == col, 1.0, 0.0)

    def times(lefts, rights):
        return [
            dot_nn(low(left_op), stack_heads(low(right_op)))
            for left_op, right_op in zip(lefts, rights)
        ]

    def plus(*lists):
        return [sum(members[1:], members[0]) for members in zip(*lists)]

    near = row // 8 == col // 8
    base = [jnp.where(near, part, 0.0) for part in lower_parts]
    square = times(base, base)
    cube = times(base, square)
    fourth = times(square, square)
    accum = [eye + first + second + third for first, second, third in zip(base, square, cube)]
    accum = plus(accum, times(accum, fourth))
    width = 8
    while width < CHUNK:
        level = (row // (2 * width) == col // (2 * width)) & (row // width != col // width)
        off = [jnp.where(level, part, 0.0) for part in lower_parts]
        accum = plus(accum, times(times(accum, off), accum))
        width *= 2
    return accum


def prepare(r, k, dw, da, cols, live, tri_op, ones_op):
    sw = jax.nn.sigmoid(dw + cols[0:1])
    full_log = -DECAY_SCALE * sw
    log_decay = jnp.where(live, full_log, 0.0)
    rate = jax.nn.sigmoid(da + cols[1:2])
    scaled = k * cols[2:3]
    inv = lax.rsqrt(head_sum(scaled * scaled, ones_op) + 1e-06)
    unit = scaled * inv
    unit_live = jnp.where(live, unit, 0.0)
    lag_scale = 1.0 + (rate - 1.0) * cols[3:4]
    lagged = jnp.where(live, k * lag_scale, 0.0)
    running = split_dot(tri_op, log_decay)
    grown = jnp.exp(running)
    before = jnp.exp(running - log_decay)
    shrunk = jnp.exp(-running)
    last = running[CHUNK - 1 : CHUNK]
    til_end = jnp.exp(last - running)
    write = unit_live * rate
    return SimpleNamespace(
        sw=sw,
        full_log=full_log,
        rate=rate,
        inv=inv,
        unit=unit,
        unit_live=unit_live,
        lag_scale=lag_scale,
        lagged=lagged,
        grown=grown,
        before=before,
        shrunk=shrunk,
        til_end=til_end,
        final=jnp.exp(last),
        read_wide=r * grown,
        write_wide=write * shrunk,
        key_wide=lagged * shrunk,
        read_hat=low(r * grown),
        remove_hat=low(-unit_live * before),
        write_hat=low(write * shrunk),
        key_hat=low(lagged * shrunk),
        write_end=low(write * til_end),
        key_end=low(lagged * til_end),
    )


def tri_masks():
    row = iota((CHUNK, PAIR), 0)
    col = iota((CHUNK, PAIR), 1) % CHUNK
    return row > col, row >= col


def mixer_forward(
    steps_per_seq,
    length_ref,
    r_ref,
    k_ref,
    v_ref,
    dw_ref,
    da_ref,
    gate_ref,
    cols_ref,
    z_ref,
    y_ref,
    t_ref,
    u_ref,
    s_ref,
    lk_ref,
    reads_ref,
    state,
):
    step = pl.program_id(0)
    within_seq = lax.rem(step, steps_per_seq)
    length = length_ref[step // steps_per_seq]

    @pl.when(within_seq == 0)
    def _():
        state[...] = jnp.zeros_like(state)

    rows_each = r_ref.shape[0]
    chunks = rows_each // CHUNK
    pairs = r_ref.shape[1] // PAIR
    ones_mask = head_ones()
    ones_op = jnp.where(ones_mask, 1.0, 0.0).astype(jnp.bfloat16)
    tri_op = jnp.where(iota((CHUNK, CHUNK), 0) >= iota((CHUNK, CHUNK), 1), 1.0, 0.0).astype(jnp.bfloat16)
    strict, within = tri_masks()
    within_two = jnp.concatenate([within, within], axis=1)
    units = [(chunk, pair) for chunk in range(chunks) for pair in range(pairs)]

    def place_of(unit):
        chunk, pair = unit
        return slice(chunk * CHUNK, (chunk + 1) * CHUNK), slice(pair * PAIR, (pair + 1) * PAIR)

    prepared, scored, lower_parts = [], [], []
    for unit in units:
        rows, lanes = place_of(unit)
        live = within_seq * rows_each + unit[0] * CHUNK + iota((CHUNK, PAIR), 0) < length
        got = prepare(
            r_ref[rows, lanes],
            k_ref[rows, lanes],
            dw_ref[rows, lanes],
            da_ref[rows, lanes],
            cols_ref[:, lanes],
            live,
            tri_op,
            ones_op,
        )
        prepared.append(got)
    for unit, got in zip(units, prepared):
        got.both = jnp.concatenate([got.remove_hat, got.read_hat], axis=0)
        past = jnp.concatenate([stack_heads(got.write_hat), stack_heads(got.key_hat)], axis=0)
        scores = dot_nt(got.both, past)
        past_rest = jnp.concatenate(
            [stack_heads(halves(got.write_wide)[1]), stack_heads(halves(got.key_wide)[1])], axis=0
        )
        got.read_rest = halves(got.read_wide)[1]
        fine = scores[CHUNK:] + (dot_nt(got.read_rest, past) + dot_nt(got.read_hat, past_rest))
        lower_parts.append(jnp.where(strict, scores[:CHUNK, :PAIR], 0.0))
        lower_key = low(jnp.where(strict, scores[:CHUNK, PAIR:], 0.0))
        reads = low(jnp.where(within_two, fine, 0.0))
        scored.append((lower_key, reads))
    solves = [low(part) for part in lower_inverses(lower_parts)]
    for unit, solve in zip(units, solves):
        t_ref[place_of(unit)] = solve
    for chunk in range(chunks):
        group = [index for index, unit in enumerate(units) if unit[0] == chunk]
        lows = [low(v_ref[place_of(units[index])]) for index in group]
        stacks = [stack_heads(values) for values in lows]
        olds = [state[units[index][1]] for index in group]
        old_parts = [halves(old) for old in olds]
        from_state = [dot_nt(prepared[index].both, old[0]) for index, old in zip(group, old_parts)]
        read_state = [
            part[CHUNK:]
            + (dot_nt(prepared[index].read_rest, old[0]) + dot_nt(prepared[index].read_hat, old[1]))
            for index, part, old in zip(group, from_state, old_parts)
        ]
        right = [
            low(part[:CHUNK] + dot_nn(scored[index][0], stack))
            for index, part, stack in zip(group, from_state, stacks)
        ]
        removed = [low(dot_nn(solves[index], stack_heads(part))) for index, part in zip(group, right)]
        for slot, index in enumerate(group):
            pair = units[index][1]
            got = prepared[index]
            ends = jnp.concatenate([got.write_end, got.key_end], axis=0)
            adds = dot_tn(jnp.concatenate([removed[slot], lows[slot]], axis=0), ends)
            state[pair] = olds[slot] * got.final + jnp.where(ones_mask, adds, 0.0)
            u_ref[place_of(units[index])] = removed[slot]
            rows, lanes = place_of(units[index])
            lk_ref[rows, lanes], reads_ref[rows, slice(2 * lanes.start, 2 * lanes.stop)] = scored[index]
            s_ref[chunk, pair] = olds[slot]
        outs = [
            read_state[slot]
            + dot_nn(scored[index][1], jnp.concatenate([stack_heads(removed[slot]), stacks[slot]], axis=0))
            for slot, index in enumerate(group)
        ]
        centred = [y - head_sum(y, ones_op) * (1.0 / SUBSPACE_SIZE) for y in outs]
        spread = [head_sum(part * part, ones_op) * (1.0 / SUBSPACE_SIZE) for part in centred]
        for slot, index in enumerate(group):
            rows, lanes = place_of(units[index])
            cols = cols_ref[:, lanes]
            normed = centred[slot] * lax.rsqrt(spread[slot] + group_eps)
            bonus = head_sum(r_ref[rows, lanes] * prepared[index].lagged * cols[4:5], ones_op)
            mixed = normed * cols[5:6] + cols[6:7] + bonus * v_ref[rows, lanes]
            y_ref[rows, lanes] = outs[slot]
            z_ref[rows, lanes] = low(mixed * gate_ref[rows, lanes])


def mixer_backward(
    steps_per_seq,
    length_ref,
    r_ref,
    k_ref,
    v_ref,
    dw_ref,
    da_ref,
    gate_ref,
    cols_ref,
    y_ref,
    t_ref,
    u_ref,
    s_ref,
    lk_ref,
    reads_ref,
    dz_ref,
    dr_ref,
    dk_ref,
    dv_ref,
    ddw_ref,
    dda_ref,
    dgate_ref,
    dcols_ref,
    dstate,
):
    step = pl.num_programs(0) - 1 - pl.program_id(0)
    within_seq = lax.rem(step, steps_per_seq)
    length = length_ref[step // steps_per_seq]

    @pl.when(within_seq == steps_per_seq - 1)
    def _():
        dstate[...] = jnp.zeros_like(dstate)

    @pl.when(pl.program_id(0) == 0)
    def _():
        dcols_ref[...] = jnp.zeros_like(dcols_ref)

    rows_each = r_ref.shape[0]
    chunks = rows_each // CHUNK
    pairs = r_ref.shape[1] // PAIR
    ones_mask = head_ones()
    ones_op = jnp.where(ones_mask, 1.0, 0.0).astype(jnp.bfloat16)
    row = iota((CHUNK, CHUNK), 0)
    col = iota((CHUNK, CHUNK), 1)
    tri_op = jnp.where(row >= col, 1.0, 0.0).astype(jnp.bfloat16)
    suffix_op = jnp.where(row <= col, 1.0, 0.0).astype(jnp.bfloat16)
    prefix_op = jnp.where(row > col, 1.0, 0.0).astype(jnp.bfloat16)
    sums_op = jnp.concatenate([suffix_op, prefix_op], axis=1)
    strict, within = tri_masks()

    def add_col(index, lanes, values):
        part = values[0:8]
        for start in range(8, CHUNK, 8):
            part = part + values[start : start + 8]
        dcols_ref[index, :, lanes] += part

    strict_two = jnp.concatenate([strict, strict], axis=1)
    within_two = jnp.concatenate([within, within], axis=1)
    all_masks = jnp.concatenate([strict_two, within_two], axis=0)
    units = [(chunk, pair) for chunk in reversed(range(chunks)) for pair in range(pairs)]
    mean_of = 1.0 / SUBSPACE_SIZE
    known = []
    for chunk, pair in units:
        rows = slice(chunk * CHUNK, (chunk + 1) * CHUNK)
        lanes = slice(pair * PAIR, (pair + 1) * PAIR)
        live = within_seq * rows_each + chunk * CHUNK + iota((CHUNK, PAIR), 0) < length
        cols = cols_ref[:, lanes]
        got = prepare(
            r_ref[rows, lanes],
            k_ref[rows, lanes],
            dw_ref[rows, lanes],
            da_ref[rows, lanes],
            cols,
            live,
            tri_op,
            ones_op,
        )
        got.rows, got.lanes, got.live, got.cols = rows, lanes, live, cols
        got.pair, got.chunk = pair, chunk
        known.append(got)
    for got in known:
        y = y_ref[got.rows, got.lanes]
        got.centred = y - head_sum(y, ones_op) * mean_of
    for got in known:
        spread = head_sum(got.centred * got.centred, ones_op) * mean_of
        got.inv_y = lax.rsqrt(spread + group_eps)
    for got in known:
        rows, lanes, cols = got.rows, got.lanes, got.cols
        r, v, dz = r_ref[rows, lanes], v_ref[rows, lanes], dz_ref[rows, lanes]
        normed = got.centred * got.inv_y
        got.bonus = head_sum(r * got.lagged * cols[4:5], ones_op)
        mixed = normed * cols[5:6] + cols[6:7] + got.bonus * v
        dgate_ref[rows, lanes] = low(dz * mixed)
        dmix = dz * gate_ref[rows, lanes]
        add_col(5, lanes, dmix * normed)
        add_col(6, lanes, dmix)
        dnormed = dmix * cols[5:6]
        got.dbonus = head_sum(dmix * v, ones_op)
        mean_grad = head_sum(dnormed, ones_op) * mean_of
        mean_prod = head_sum(dnormed * normed, ones_op) * mean_of
        got.dy_low, got.dy_rest = halves(got.inv_y * (dnormed - mean_grad - normed * mean_prod))
        got.dv = got.bonus * dmix
    for got in known:
        rows, lanes = got.rows, got.lanes
        got.both = jnp.concatenate([got.remove_hat, got.read_hat], axis=0)
        got.past = jnp.concatenate(
            [stack_heads(got.write_hat), stack_heads(got.key_hat)], axis=0
        )
        got.lower_key = lk_ref[rows, lanes]
        reads = reads_ref[rows, slice(2 * lanes.start, 2 * lanes.stop)]
        got.from_y = dot_tn(reads, got.dy_low)
        v_low = low(v_ref[rows, lanes])
        removed = u_ref[rows, lanes]
        got.sent = jnp.concatenate([removed, v_low], axis=0)
        got.stacks = jnp.concatenate([stack_heads(removed), stack_heads(v_low)], axis=0)
    for chunk in reversed(range(chunks)):
        group = [got for got in known if got.chunk == chunk]
        for got in group:
            got.later = dstate[got.pair]
            got.later_low, got.later_rest = halves(got.later)
            ends = jnp.concatenate([got.write_end, got.key_end], axis=0)
            got.from_later = dot_nt(ends, got.later_low)
        for got in group:
            dremoved = low(got.from_later[:CHUNK] + fold_heads(got.from_y[:PAIR]))
            got.dright = low(fold_heads(dot_tn(t_ref[got.rows, got.lanes], dremoved)))
        for got in group:
            got.douts = jnp.concatenate([got.dright, got.dy_low], axis=0)
            adds = dot_tn(got.douts, got.both) + dot_tn(got.dy_rest, got.read_hat)
            adds = jnp.where(ones_mask, adds, 0.0)
            dstate[got.pair] = got.later * got.final + adds
    for got in known:
        dv = got.dv + got.from_later[CHUNK:] + fold_heads(got.from_y[PAIR:])
        dv = dv + fold_heads(dot_tn(got.lower_key, got.dright))
        dv_ref[got.rows, got.lanes] = low(dv)
        dscores = dot_nt(got.douts, got.stacks)
        fine = dscores[CHUNK:] + dot_nt(got.dy_rest, got.stacks)
        dscores = low(jnp.where(all_masks, jnp.concatenate([dscores[:CHUNK], fine], axis=0), 0.0))
        old_wide = s_ref[got.chunk, got.pair]
        old_low, old_rest = halves(old_wide)
        from_old = dot_nn(got.douts, old_low)
        fine = from_old[CHUNK:] + (dot_nn(got.dy_rest, old_low) + dot_nn(got.dy_low, old_rest))
        got.dboth = jnp.concatenate([from_old[:CHUNK], fine], axis=0) + dot_nn(dscores, got.past)
        dpast = dot_tn(dscores, got.both)
        got.dwrite_hat = fold_heads(dpast[:PAIR])
        got.dkey_hat = fold_heads(dpast[PAIR:])
        got.dends = dot_nn(got.sent, got.later_low) + dot_nn(got.sent, got.later_rest)
        got.dfinal = jnp.sum(got.later * old_wide, axis=0, keepdims=True)
    for got in known:
        rows, lanes, cols, live = got.rows, got.lanes, got.cols, got.live

        def wide(values):
            return values.astype(jnp.float32)

        r, k = r_ref[rows, lanes], k_ref[rows, lanes]
        dwrite_hat, dkey_hat = got.dwrite_hat, got.dkey_hat
        dwrite_end, dkey_end = got.dends[:CHUNK], got.dends[CHUNK:]
        dremove_hat, dread_hat = got.dboth[:CHUNK], got.dboth[CHUNK:]
        dbonus, lagged = got.dbonus, got.lagged
        bonus_lag = dbonus * lagged
        add_col(4, lanes, bonus_lag * r)
        dr_ref[rows, lanes] = low(bonus_lag * cols[4:5] + dread_hat * got.grown)
        minus = wide(got.remove_hat) * dremove_hat
        plus = wide(got.read_hat) * dread_hat + minus
        plus = plus - wide(got.write_hat) * dwrite_hat - wide(got.key_hat) * dkey_hat
        ending = wide(got.write_end) * dwrite_end + wide(got.key_end) * dkey_end
        sums = split_dot(sums_op, jnp.concatenate([plus, ending], axis=0))
        dlog = sums - minus + got.final * got.dfinal
        ddw = jnp.where(live, dlog * got.full_log * (1.0 - got.sw), 0.0)
        add_col(0, lanes, ddw)
        ddw_ref[rows, lanes] = low(ddw)
        dwrite = dwrite_hat * got.shrunk + dwrite_end * got.til_end
        dlag = dbonus * r * cols[4:5] + dkey_hat * got.shrunk + dkey_end * got.til_end
        dlag = jnp.where(live, dlag, 0.0)
        rate = got.rate
        dunit = jnp.where(live, dwrite * rate - dremove_hat * got.before, 0.0)
        lag_k = dlag * k
        drate = dwrite * got.unit_live + lag_k * cols[3:4]
        add_col(3, lanes, lag_k * (rate - 1.0))
        dscaled = got.inv * (dunit - got.unit * head_sum(dunit * got.unit, ones_op))
        add_col(2, lanes, dscaled * k)
        dk_ref[rows, lanes] = low(dlag * got.lag_scale + dscaled * cols[2:3])
        dda = drate * rate * (1.0 - rate)
        add_col(1, lanes, dda)
        dda_ref[rows, lanes] = low(dda)


def run_mixer_forward(lengths, r, k, v, dw, da, gate, cols):
    positions, part_width = r.shape
    rows_each = CHUNKS_FWD * CHUNK
    steps = positions // rows_each
    steps_per_seq = SEQ_LEN // rows_each
    pairs = part_width // PAIR
    wide = pl.BlockSpec((rows_each, part_width), lambda i: (i, 0))
    shape = jax.ShapeDtypeStruct
    return pl.pallas_call(
        partial(mixer_forward, steps_per_seq),
        grid=(steps,),
        in_specs=[pl.BlockSpec(memory_space=pltpu.SMEM)]
        + [wide] * 6
        + [pl.BlockSpec((8, part_width), lambda i: (0, 0))],
        out_specs=[wide] * 4
        + [
            pl.BlockSpec((CHUNKS_FWD, pairs, PAIR, PAIR), lambda i: (i, 0, 0, 0)),
            wide,
            pl.BlockSpec((rows_each, 2 * part_width), lambda i: (i, 0)),
        ],
        out_shape=[
            shape((positions, part_width), jnp.bfloat16),
            shape((positions, part_width), jnp.float32),
            shape((positions, part_width), jnp.bfloat16),
            shape((positions, part_width), jnp.bfloat16),
            shape((positions // CHUNK, pairs, PAIR, PAIR), jnp.float32),
            shape((positions, part_width), jnp.bfloat16),
            shape((positions, 2 * part_width), jnp.bfloat16),
        ],
        scratch_shapes=[pltpu.VMEM((pairs, PAIR, PAIR), jnp.float32)],
        compiler_params=pltpu.CompilerParams(
            dimension_semantics=("arbitrary",), vmem_limit_bytes=60 * 1024 * 1024
        ),
        name="mixer_forward",
    )(lengths, r, k, v, dw, da, gate, cols)


def run_mixer_backward(lengths, r, k, v, dw, da, gate, cols, y, t, u, s, lk, reads, dz):
    positions, part_width = r.shape
    rows_each = CHUNKS_BWD * CHUNK
    steps = positions // rows_each
    steps_per_seq = SEQ_LEN // rows_each
    pairs = part_width // PAIR
    wide = pl.BlockSpec((rows_each, part_width), lambda i: (steps - 1 - i, 0))
    shape = jax.ShapeDtypeStruct
    return pl.pallas_call(
        partial(mixer_backward, steps_per_seq),
        grid=(steps,),
        in_specs=[pl.BlockSpec(memory_space=pltpu.SMEM)]
        + [wide] * 6
        + [pl.BlockSpec((8, part_width), lambda i: (0, 0))]
        + [wide] * 3
        + [
            pl.BlockSpec((CHUNKS_BWD, pairs, PAIR, PAIR), lambda i: (steps - 1 - i, 0, 0, 0)),
            wide,
            pl.BlockSpec((rows_each, 2 * part_width), lambda i: (steps - 1 - i, 0)),
            wide,
        ],
        out_specs=[wide] * 6 + [pl.BlockSpec((8, 8, part_width), lambda i: (0, 0, 0))],
        out_shape=[shape((positions, part_width), jnp.bfloat16)] * 6
        + [shape((8, 8, part_width), jnp.float32)],
        scratch_shapes=[pltpu.VMEM((pairs, PAIR, PAIR), jnp.float32)],
        compiler_params=pltpu.CompilerParams(
            dimension_semantics=("arbitrary",), vmem_limit_bytes=60 * 1024 * 1024
        ),
        name="mixer_backward",
    )(lengths, r, k, v, dw, da, gate, cols, y, t, u, s, lk, reads, dz)


LINE = "mp"
GROUP = "dp"
END_LAG = 3
MID_LAG = 1


def link_cost(elements):
    return elements * 2 * 2 * 40


def line_barrier(size):
    me = lax.axis_index(LINE)
    barrier = pltpu.get_barrier_semaphore()

    @pl.when(me > 0)
    def _():
        pl.semaphore_signal(barrier, inc=1, device_id={LINE: me - 1}, device_id_type=pl.DeviceIdType.MESH)

    @pl.when(me < size - 1)
    def _():
        pl.semaphore_signal(barrier, inc=1, device_id={LINE: me + 1}, device_id_type=pl.DeviceIdType.MESH)

    ends = jnp.where((me == 0) | (me == size - 1), 1, 2)
    pl.semaphore_wait(barrier, ends)


class Flow:
    def __init__(self, size, side):
        self.size = size
        self.side = side
        self.me = lax.axis_index(LINE)
        self.step = 1 - 2 * side
        self.target = self.me + self.step
        source = self.me - self.step
        self.has_source = (source >= 0) & (source < size)
        self.has_target = (self.target >= 0) & (self.target < size)

    def copy(self, source, place, send_sem, recv_sem):
        return pltpu.make_async_remote_copy(
            src_ref=source,
            dst_ref=place,
            send_sem=send_sem,
            recv_sem=recv_sem,
            device_id={LINE: self.target},
            device_id_type=pl.DeviceIdType.MESH,
        )


def two_flows(size):
    me = lax.axis_index(LINE)
    near = jnp.where(me < size // 2, 0, 1)
    return Flow(size, near), Flow(size, 1 - near)


def line_sum_kernel(size, chunk_rows, x_ref, out_ref, got, sent, send_sem, recv_sem):
    line_barrier(size)
    me = lax.axis_index(LINE)
    flows = two_flows(size)
    chunks = x_ref.shape[0] // chunk_rows

    def copy_of(flow, chunk, source):
        rows = pl.ds(pl.multiple_of(chunk * chunk_rows, chunk_rows), chunk_rows)
        return flow.copy(
            source.at[rows], got.at[flow.side, rows], send_sem.at[flow.side, chunk], recv_sem.at[flow.side, chunk]
        )

    def pass_on(flow, chunk):
        rows = pl.ds(pl.multiple_of(chunk * chunk_rows, chunk_rows), chunk_rows)

        @pl.when(flow.has_source)
        def _():
            copy_of(flow, chunk, x_ref).wait_recv()

        @pl.when(flow.has_source & flow.has_target)
        def _():
            total = got[flow.side, rows].astype(jnp.float32) + x_ref[rows].astype(jnp.float32)
            sent[flow.side, rows] = total.astype(sent.dtype)
            copy_of(flow, chunk, sent.at[flow.side]).start()

        @pl.when(jnp.logical_not(flow.has_source))
        def _():
            copy_of(flow, chunk, x_ref).start()

    is_end = (me == 0) | (me == size - 1)
    lag = jnp.where(is_end, END_LAG, MID_LAG)

    def step(turn, carry):
        @pl.when(turn < chunks)
        def _():
            pass_on(flows[0], turn)

        chunk = turn - lag

        @pl.when((chunk >= 0) & (chunk < chunks))
        def _():
            pass_on(flows[1], chunk)
            rows = pl.ds(pl.multiple_of(chunk * chunk_rows, chunk_rows), chunk_rows)

            @pl.when(is_end)
            def _():
                other = got[flows[1].side, rows].astype(jnp.float32)
                out_ref[rows] = (other + x_ref[rows].astype(jnp.float32)).astype(out_ref.dtype)

            @pl.when(jnp.logical_not(is_end))
            def _():
                other = got[0, rows].astype(jnp.float32) + got[1, rows].astype(jnp.float32)
                out_ref[rows] = (other + x_ref[rows].astype(jnp.float32)).astype(out_ref.dtype)

        return carry

    lax.fori_loop(0, chunks + END_LAG, step, 0)

    def drain(chunk, carry):
        for flow in flows:

            @pl.when(flow.has_target)
            def _():
                copy_of(flow, chunk, x_ref).wait_send()

        return carry

    lax.fori_loop(0, chunks, drain, 0)


def line_sum(x, size, collective_id, chunk_rows=64):
    rows, cols = x.shape
    chunks = rows // chunk_rows
    return pl.pallas_call(
        partial(line_sum_kernel, size, chunk_rows),
        out_shape=jax.ShapeDtypeStruct(x.shape, x.dtype),
        in_specs=[pl.BlockSpec(memory_space=pltpu.VMEM)],
        out_specs=pl.BlockSpec(memory_space=pltpu.VMEM),
        scratch_shapes=[
            pltpu.VMEM((2, rows, cols), x.dtype),
            pltpu.VMEM((2, rows, cols), x.dtype),
            pltpu.SemaphoreType.DMA((2, chunks)),
            pltpu.SemaphoreType.DMA((2, chunks)),
        ],
        compiler_params=pltpu.CompilerParams(
            collective_id=collective_id, has_side_effects=True, vmem_limit_bytes=48 * 1024 * 1024
        ),
        cost_estimate=pl.CostEstimate(flops=0, bytes_accessed=link_cost(rows * cols), transcendentals=0),
        name="line_sum",
    )(x)


def line_gather_kernel(size, chunk_rows, x_ref, out_ref, send_sem, recv_sem):
    line_barrier(size)
    me = lax.axis_index(LINE)
    flows = two_flows(size)
    width = x_ref.shape[1]
    chunks = x_ref.shape[0] // chunk_rows

    def place(block, chunk):
        rows = pl.ds(pl.multiple_of(chunk * chunk_rows, chunk_rows), chunk_rows)
        return out_ref.at[rows, pl.ds(pl.multiple_of(block * width, width), width)]

    def copy_of(flow, block, chunk):
        return flow.copy(
            place(block, chunk), place(block, chunk), send_sem.at[flow.side, block, chunk], recv_sem.at[flow.side, block, chunk]
        )

    def step(chunk, carry):
        rows = pl.ds(pl.multiple_of(chunk * chunk_rows, chunk_rows), chunk_rows)
        out_ref[rows, pl.ds(pl.multiple_of(me * width, width), width)] = x_ref[rows]
        for flow in flows:

            @pl.when(flow.has_target)
            def _():
                copy_of(flow, me, chunk).start()

        return carry

    lax.fori_loop(0, chunks, step, 0)
    for hop in range(1, size):

        def forward(chunk, carry):
            for flow in flows:
                block = me - hop * flow.step
                exists = (block >= 0) & (block < size)

                @pl.when(exists)
                def _():
                    copy_of(flow, block, chunk).wait_recv()

                @pl.when(exists & flow.has_target)
                def _():
                    copy_of(flow, block, chunk).start()

            return carry

        lax.fori_loop(0, chunks, forward, 0)
    for hop in range(size):

        def drain(chunk, carry):
            for flow in flows:
                block = me - hop * flow.step
                exists = (block >= 0) & (block < size)

                @pl.when(exists & flow.has_target)
                def _():
                    copy_of(flow, block, chunk).wait_send()

            return carry

        lax.fori_loop(0, chunks, drain, 0)


def line_gather(x, size, collective_id, chunk_rows=256):
    rows, cols = x.shape
    chunks = rows // chunk_rows
    return pl.pallas_call(
        partial(line_gather_kernel, size, chunk_rows),
        out_shape=jax.ShapeDtypeStruct((rows, size * cols), x.dtype),
        in_specs=[pl.BlockSpec(memory_space=pltpu.VMEM)],
        out_specs=pl.BlockSpec(memory_space=pltpu.VMEM),
        scratch_shapes=[
            pltpu.SemaphoreType.DMA((2, size, chunks)),
            pltpu.SemaphoreType.DMA((2, size, chunks)),
        ],
        compiler_params=pltpu.CompilerParams(
            collective_id=collective_id, has_side_effects=True, vmem_limit_bytes=48 * 1024 * 1024
        ),
        cost_estimate=pl.CostEstimate(flops=0, bytes_accessed=link_cost(3 * rows * cols), transcendentals=0),
        name="line_gather",
    )(x)


def line_scatter_kernel(size, chunk_rows, x_ref, out_ref, got, sent, send_sem, recv_sem):
    line_barrier(size)
    me = lax.axis_index(LINE)
    flows = two_flows(size)
    width = out_ref.shape[1]
    chunks = x_ref.shape[0] // chunk_rows

    def rows_of(chunk):
        return pl.ds(pl.multiple_of(chunk * chunk_rows, chunk_rows), chunk_rows)

    def cols_of(block):
        return pl.ds(pl.multiple_of(block * width, width), width)

    def copy_of(flow, block, chunk, source):
        return flow.copy(
            source,
            got.at[flow.side, rows_of(chunk), cols_of(block)],
            send_sem.at[flow.side, block, chunk],
            recv_sem.at[flow.side, block, chunk],
        )

    def own(block, chunk):
        return x_ref[rows_of(chunk), cols_of(block)].astype(jnp.float32)

    for hop in range(size - 1):

        def forward(chunk, carry):
            for flow in flows:
                block = jnp.where(flow.side == 0, size - 1 - hop, hop)
                ahead = (block - me) * flow.step > 0

                @pl.when(ahead & flow.has_source)
                def _():
                    source = x_ref.at[rows_of(chunk), cols_of(block)]
                    copy_of(flow, block, chunk, source).wait_recv()
                    total = got[flow.side, rows_of(chunk), cols_of(block)].astype(jnp.float32) + own(block, chunk)
                    sent[flow.side, rows_of(chunk), cols_of(block)] = total.astype(sent.dtype)
                    copy_of(flow, block, chunk, sent.at[flow.side, rows_of(chunk), cols_of(block)]).start()

                @pl.when(ahead & jnp.logical_not(flow.has_source))
                def _():
                    copy_of(flow, block, chunk, x_ref.at[rows_of(chunk), cols_of(block)]).start()

            return carry

        lax.fori_loop(0, chunks, forward, 0)

    def finish(chunk, carry):
        rows = rows_of(chunk)
        for flow in flows:

            @pl.when(flow.has_source)
            def _():
                copy_of(flow, me, chunk, x_ref.at[rows, cols_of(me)]).wait_recv()

        @pl.when(me == 0)
        def _():
            out_ref[rows] = (got[1, rows, cols_of(me)].astype(jnp.float32) + own(me, chunk)).astype(out_ref.dtype)

        @pl.when(me == size - 1)
        def _():
            out_ref[rows] = (got[0, rows, cols_of(me)].astype(jnp.float32) + own(me, chunk)).astype(out_ref.dtype)

        @pl.when((me > 0) & (me < size - 1))
        def _():
            other = got[0, rows, cols_of(me)].astype(jnp.float32) + got[1, rows, cols_of(me)].astype(jnp.float32)
            out_ref[rows] = (other + own(me, chunk)).astype(out_ref.dtype)

        return carry

    lax.fori_loop(0, chunks, finish, 0)
    for hop in range(size - 1):

        def drain(chunk, carry):
            for flow in flows:
                block = jnp.where(flow.side == 0, size - 1 - hop, hop)
                ahead = (block - me) * flow.step > 0

                @pl.when(ahead)
                def _():
                    copy_of(flow, block, chunk, x_ref.at[rows_of(chunk), cols_of(block)]).wait_send()

            return carry

        lax.fori_loop(0, chunks, drain, 0)


def line_scatter(x, size, collective_id, out_dtype=jnp.float32, chunk_rows=256):
    rows, cols = x.shape
    chunks = rows // chunk_rows
    return pl.pallas_call(
        partial(line_scatter_kernel, size, chunk_rows),
        out_shape=jax.ShapeDtypeStruct((rows, cols // size), out_dtype),
        in_specs=[pl.BlockSpec(memory_space=pltpu.VMEM)],
        out_specs=pl.BlockSpec(memory_space=pltpu.VMEM),
        scratch_shapes=[
            pltpu.VMEM((2, rows, cols), x.dtype),
            pltpu.VMEM((2, rows, cols), x.dtype),
            pltpu.SemaphoreType.DMA((2, size, chunks)),
            pltpu.SemaphoreType.DMA((2, size, chunks)),
        ],
        compiler_params=pltpu.CompilerParams(
            collective_id=collective_id, has_side_effects=True, vmem_limit_bytes=48 * 1024 * 1024
        ),
        cost_estimate=pl.CostEstimate(flops=0, bytes_accessed=link_cost(3 * rows * cols // size), transcendentals=0),
        name="line_scatter",
    )(x)


def input_backward_kernel(
    seq_len, splits, whole_ref, dr_ref, dk_ref, dv_ref, dl_ref, three_ref, down_ref, params_ref, din_ref, gparams_ref, gdown_ref, carry, kept
):
    step = pl.program_id(0)
    tile = pl.num_programs(0) - 1 - step
    rows_each = dr_ref.shape[0]
    part = dr_ref.shape[1]
    width = whole_ref.shape[1]
    start = tile * rows_each
    at_start = lax.rem(start, seq_len) == 0
    at_end = lax.rem(start + rows_each, seq_len) == 0

    @pl.when(step == 0)
    def _():
        gparams_ref[...] = jnp.zeros_like(gparams_ref)
        gdown_ref[...] = jnp.zeros_like(gdown_ref)

    @pl.when(at_end)
    def _():
        carry[...] = jnp.zeros_like(carry)

    edge = 16
    rows = pl.ds(pl.multiple_of(start, rows_each), rows_each)
    edge_rows = pl.ds(pl.multiple_of(jnp.maximum(start - edge, 0), edge), edge)
    inverse_width = 1.0 / width

    def moments(place):
        values = whole_ref[place, :].astype(jnp.float32)
        centre = jnp.sum(values, axis=1, keepdims=True) * inverse_width
        values = values - centre
        spread = jnp.sum(values * values, axis=1, keepdims=True) * inverse_width
        return centre, lax.rsqrt(spread + norm_eps)

    centre, inv = moments(rows)
    edge_centre, edge_inv = moments(edge_rows)
    block_cols = 256
    row_index = iota((rows_each, block_cols), 0)
    dl = dl_ref[...]
    lane = iota(dl.shape, 1)
    zero = jnp.zeros_like(dl)
    first, second = splits
    dls = (
        jnp.where(lane < first, dl, zero),
        jnp.where((lane >= first) & (lane < second), dl, zero),
        jnp.where(lane >= second, dl, zero),
    )
    down_row = iota((dl.shape[1], block_cols), 0)
    sum_grad = jnp.zeros((rows_each, 1), jnp.float32)
    sum_prod = jnp.zeros((rows_each, 1), jnp.float32)

    def add_param(index, cols, values):
        total = values[0:8]
        for place in range(8, rows_each, 8):
            total = total + values[place : place + 8]
        gparams_ref[index, :, cols] += total

    for block in range(width // block_cols):
        cols = slice(block * block_cols, (block + 1) * block_cols)
        gain, bias = params_ref[0:1, cols], params_ref[1:2, cols]
        unit = (whole_ref[rows, cols].astype(jnp.float32) - centre) * inv
        normed = unit * gain + bias
        edge_unit = (whole_ref[edge_rows, cols].astype(jnp.float32) - edge_centre) * edge_inv
        edge_normed = (edge_unit * gain + bias)[edge - 1 : edge]
        edge_normed = jnp.where(at_start, 0.0, edge_normed)
        before = jnp.where(row_index == 0, edge_normed, pltpu.roll(normed, 1, 0))
        shift = before - normed
        down = down_ref[cols, :]
        weights = three_ref[cols, :]
        grads = (
            dot_nt(dr_ref[...], weights[:, :part]),
            dot_nt(dls[0], down),
            dot_nt(dk_ref[...], weights[:, part : 2 * part]),
            dot_nt(dv_ref[...], weights[:, 2 * part :]),
            dot_nt(dls[1], down),
            dot_nt(dls[2], down),
        )
        total = grads[0]
        for grad in grads[1:]:
            total = total + grad
        mixed = None
        for index, grad in enumerate(grads):
            rate = params_ref[2 + index : 3 + index, cols]
            mixed = grad * rate if mixed is None else mixed + grad * rate
            add_param(2 + index, cols, grad * shift)
        after = jnp.where(row_index == rows_each - 1, carry[0:1, cols], pltpu.roll(mixed, rows_each - 1, 0))
        carry[0:1, cols] = mixed[0:1]
        dnormed = total - mixed + after
        add_param(0, cols, dnormed * unit)
        add_param(1, cols, dnormed)
        dunit = dnormed * gain
        kept[:, cols] = dunit
        sum_grad = sum_grad + jnp.sum(dunit, axis=1, keepdims=True)
        sum_prod = sum_prod + jnp.sum(dunit * unit, axis=1, keepdims=True)
        outs = [
            dot_tn(dl, low(normed + shift * params_ref[index : index + 1, cols])) for index in (3, 6, 7)
        ]
        gdown_ref[:, cols] += jnp.where(
            down_row < first, outs[0], jnp.where(down_row < second, outs[1], outs[2])
        )
    sum_grad = sum_grad * inverse_width
    sum_prod = sum_prod * inverse_width
    for block in range(width // block_cols):
        cols = slice(block * block_cols, (block + 1) * block_cols)
        unit = (whole_ref[rows, cols].astype(jnp.float32) - centre) * inv
        din_ref[:, cols] = low(inv * (kept[:, cols] - sum_grad - unit * sum_prod))


def input_backward(whole, dr, dk, dv, dl, splits, three, down, params):
    positions, width = whole.shape
    part = dr.shape[1]
    rows_each = 256
    steps = positions // rows_each
    tile = lambda cols: pl.BlockSpec((rows_each, cols), lambda i: (steps - 1 - i, 0))
    full = pl.BlockSpec(memory_space=pltpu.VMEM)
    shape = jax.ShapeDtypeStruct
    return pl.pallas_call(
        partial(input_backward_kernel, SEQ_LEN, splits),
        grid=(steps,),
        in_specs=[full, tile(part), tile(part), tile(part), tile(dl.shape[1]), full, full, full],
        out_specs=[
            tile(width),
            pl.BlockSpec((8, 8, width), lambda i: (0, 0, 0)),
            pl.BlockSpec((dl.shape[1], width), lambda i: (0, 0)),
        ],
        out_shape=[
            shape((positions, width), jnp.bfloat16),
            shape((8, 8, width), jnp.float32),
            shape((dl.shape[1], width), jnp.float32),
        ],
        scratch_shapes=[pltpu.VMEM((8, width), jnp.float32), pltpu.VMEM((rows_each, width), jnp.float32)],
        compiler_params=pltpu.CompilerParams(
            dimension_semantics=("arbitrary",), vmem_limit_bytes=48 * 1024 * 1024
        ),
        name="input_backward",
    )(whole, dr, dk, dv, dl, three, down, params)


def weight_grads_kernel(left_refs, right_refs, out_ref):
    part = right_refs[0].shape[1]
    for index, (left_ref, right_ref) in enumerate(zip(left_refs, right_refs)):
        out_ref[:, index * part : (index + 1) * part] = low(dot_tn(left_ref[...], right_ref[...]))


def weight_grads(lefts, rights):
    positions, width = lefts[0].shape
    part = rights[0].shape[1]
    count = len(lefts)
    block = 512

    def kernel(*refs):
        weight_grads_kernel(refs[:count], refs[count : 2 * count], refs[2 * count])

    return pl.pallas_call(
        kernel,
        grid=(width // block,),
        in_specs=[pl.BlockSpec((positions, block), lambda i: (0, i))] * count
        + [pl.BlockSpec((positions, part), lambda i: (0, 0))] * count,
        out_specs=pl.BlockSpec((block, count * part), lambda i: (i, 0)),
        out_shape=jax.ShapeDtypeStruct((width, count * part), jnp.bfloat16),
        compiler_params=pltpu.CompilerParams(
            dimension_semantics=("arbitrary",), vmem_limit_bytes=60 * 1024 * 1024
        ),
        name="weight_grads",
    )(*lefts, *rights)


def line_error_kernel(
    size, chunk_rows, x_ref, base_ref, teacher_ref, weight_ref, state_ref, error_ref, got, sent, send_sem, recv_sem, out_send_sem, out_recv_sem
):
    line_barrier(size)
    me = lax.axis_index(LINE)
    flows = two_flows(size)
    width = base_ref.shape[1]
    chunks = x_ref.shape[0] // chunk_rows
    is_end = (me == 0) | (me == size - 1)
    lag = jnp.where(is_end, END_LAG, MID_LAG)

    def rows_of(chunk):
        return pl.ds(pl.multiple_of(chunk * chunk_rows, chunk_rows), chunk_rows)

    def cols_of(block):
        return pl.ds(pl.multiple_of(block * width, width), width)

    def part_copy(flow, block, chunk, source):
        place = (rows_of(chunk), cols_of(block))
        return flow.copy(
            source.at[place],
            got.at[(flow.side,) + place],
            send_sem.at[flow.side, block, chunk],
            recv_sem.at[flow.side, block, chunk],
        )

    def error_copy(flow, block, chunk):
        place = error_ref.at[rows_of(chunk), cols_of(block)]
        return flow.copy(
            place, place, out_send_sem.at[flow.side, block, chunk], out_recv_sem.at[flow.side, block, chunk]
        )

    def target_of(flow, hop):
        block = jnp.where(flow.side == 0, size - 1 - hop, hop)
        return block, (block - me) * flow.step > 0

    def reduce_part(flow, chunk):
        for hop in range(size - 1):
            block, ahead = target_of(flow, hop)

            @pl.when(ahead & flow.has_source)
            def _():
                part_copy(flow, block, chunk, x_ref).wait_recv()
                place = (rows_of(chunk), cols_of(block))
                total = got[(flow.side,) + place].astype(jnp.float32) + x_ref[place].astype(jnp.float32)
                sent[(flow.side,) + place] = total.astype(sent.dtype)
                part_copy(flow, block, chunk, sent.at[flow.side]).start()

            @pl.when(ahead & jnp.logical_not(flow.has_source))
            def _():
                part_copy(flow, block, chunk, x_ref).start()

    def finish(chunk):
        rows = rows_of(chunk)
        for flow in flows:

            @pl.when(flow.has_source)
            def _():
                part_copy(flow, me, chunk, x_ref).wait_recv()

        def write(others):
            result = base_ref[rows] + (others + x_ref[rows, cols_of(me)].astype(jnp.float32))
            state_ref[rows] = result.astype(state_ref.dtype)
            error = weight_ref[rows, 0:1] * (result - teacher_ref[rows].astype(jnp.float32))
            error_ref[rows, cols_of(me)] = error.astype(error_ref.dtype)

        @pl.when(is_end)
        def _():
            write(got[flows[1].side, rows, cols_of(me)].astype(jnp.float32))

        @pl.when(jnp.logical_not(is_end))
        def _():
            write(
                got[0, rows, cols_of(me)].astype(jnp.float32) + got[1, rows, cols_of(me)].astype(jnp.float32)
            )

        for flow in flows:

            @pl.when(flow.has_target)
            def _():
                error_copy(flow, me, chunk).start()

    def forward(hop, chunk):
        for flow in flows:
            block = me - hop * flow.step
            exists = (block >= 0) & (block < size)

            @pl.when(exists)
            def _():
                error_copy(flow, block, chunk).wait_recv()

            @pl.when(exists & flow.has_target)
            def _():
                error_copy(flow, block, chunk).start()

    def at(chunk, action):
        @pl.when((chunk >= 0) & (chunk < chunks))
        def _():
            action(chunk)

    def step(turn, carry):
        at(turn, lambda chunk: reduce_part(flows[0], chunk))
        at(turn - lag, lambda chunk: reduce_part(flows[1], chunk))
        at(turn - lag - 1, finish)
        for hop in range(1, size):
            at(turn - lag - 1 - 2 * hop, partial(forward, hop))
        return carry

    lax.fori_loop(0, chunks + END_LAG + 1 + 2 * (size - 1), step, 0)

    def drain(chunk, carry):
        for flow in flows:
            for hop in range(size - 1):
                block, ahead = target_of(flow, hop)

                @pl.when(ahead)
                def _():
                    part_copy(flow, block, chunk, x_ref).wait_send()

            for hop in range(size):
                source = me - hop * flow.step
                exists = (source >= 0) & (source < size)

                @pl.when(exists & flow.has_target)
                def _():
                    error_copy(flow, source, chunk).wait_send()

        return carry

    lax.fori_loop(0, chunks, drain, 0)


def line_error(x, base, teacher, weight, size, collective_id, chunk_rows=64):
    rows, cols = x.shape
    chunks = rows // chunk_rows
    sems = pltpu.SemaphoreType.DMA((2, size, chunks))
    return pl.pallas_call(
        partial(line_error_kernel, size, chunk_rows),
        out_shape=[
            jax.ShapeDtypeStruct(base.shape, jnp.bfloat16),
            jax.ShapeDtypeStruct(x.shape, jnp.bfloat16),
        ],
        in_specs=[pl.BlockSpec(memory_space=pltpu.VMEM)] * 4,
        out_specs=[pl.BlockSpec(memory_space=pltpu.VMEM)] * 2,
        scratch_shapes=[
            pltpu.VMEM((2, rows, cols), x.dtype),
            pltpu.VMEM((2, rows, cols), x.dtype),
            sems,
            sems,
            sems,
            sems,
        ],
        compiler_params=pltpu.CompilerParams(
            collective_id=collective_id, has_side_effects=True, vmem_limit_bytes=48 * 1024 * 1024
        ),
        cost_estimate=pl.CostEstimate(flops=0, bytes_accessed=link_cost(rows * cols), transcendentals=0),
        name="line_error",
    )(x, base, teacher, weight)


def output_backward_kernel(
    seq_len, whole_ref, delta_ref, dpre_ref, weight_ref, params_ref, dres_ref, gparams_ref, carry, kept
):
    step = pl.program_id(0)
    tile = pl.num_programs(0) - 1 - step
    rows_each = dpre_ref.shape[0]
    width = whole_ref.shape[1]
    start = tile * rows_each
    at_start = lax.rem(start, seq_len) == 0
    at_end = lax.rem(start + rows_each, seq_len) == 0

    @pl.when(step == 0)
    def _():
        gparams_ref[...] = jnp.zeros_like(gparams_ref)

    @pl.when(at_end)
    def _():
        carry[...] = jnp.zeros_like(carry)

    edge = 16
    rows = pl.ds(pl.multiple_of(start, rows_each), rows_each)
    edge_rows = pl.ds(pl.multiple_of(jnp.maximum(start - edge, 0), edge), edge)
    inverse_width = 1.0 / width

    def residual(place, cols):
        return whole_ref[place, cols].astype(jnp.float32) + delta_ref[place, cols].astype(jnp.float32)

    def moments(place):
        values = residual(place, slice(0, width))
        centre = jnp.sum(values, axis=1, keepdims=True) * inverse_width
        values = values - centre
        spread = jnp.sum(values * values, axis=1, keepdims=True) * inverse_width
        return centre, lax.rsqrt(spread + norm_eps)

    centre, inv = moments(rows)
    edge_centre, edge_inv = moments(edge_rows)
    block_cols = 256
    row_index = iota((rows_each, block_cols), 0)
    sum_grad = jnp.zeros((rows_each, 1), jnp.float32)
    sum_prod = jnp.zeros((rows_each, 1), jnp.float32)

    def add_param(index, cols, values):
        total = values[0:8]
        for place in range(8, rows_each, 8):
            total = total + values[place : place + 8]
        gparams_ref[index, :, cols] += total

    for block in range(width // block_cols):
        cols = slice(block * block_cols, (block + 1) * block_cols)
        gain, bias, rate = params_ref[0:1, cols], params_ref[1:2, cols], params_ref[2:3, cols]
        unit = (residual(rows, cols) - centre) * inv
        normed = unit * gain + bias
        edge_unit = (residual(edge_rows, cols) - edge_centre) * edge_inv
        edge_normed = (edge_unit * gain + bias)[edge - 1 : edge]
        edge_normed = jnp.where(at_start, 0.0, edge_normed)
        before = jnp.where(row_index == 0, edge_normed, pltpu.roll(normed, 1, 0))
        grad = dot_nt(dpre_ref[...], weight_ref[cols, :])
        add_param(2, cols, grad * (before - normed))
        mixed = grad * rate
        after = jnp.where(row_index == rows_each - 1, carry[0:1, cols], pltpu.roll(mixed, rows_each - 1, 0))
        carry[0:1, cols] = mixed[0:1]
        dnormed = grad - mixed + after
        add_param(0, cols, dnormed * unit)
        add_param(1, cols, dnormed)
        dunit = dnormed * gain
        kept[:, cols] = dunit
        sum_grad = sum_grad + jnp.sum(dunit, axis=1, keepdims=True)
        sum_prod = sum_prod + jnp.sum(dunit * unit, axis=1, keepdims=True)
    sum_grad = sum_grad * inverse_width
    sum_prod = sum_prod * inverse_width
    for block in range(width // block_cols):
        cols = slice(block * block_cols, (block + 1) * block_cols)
        unit = (residual(rows, cols) - centre) * inv
        dres_ref[:, cols] = low(inv * (kept[:, cols] - sum_grad - unit * sum_prod))


def output_backward(whole, delta, dpre, weight, params):
    positions, width = whole.shape
    rows_each = 256
    steps = positions // rows_each
    tile = lambda cols: pl.BlockSpec((rows_each, cols), lambda i: (steps - 1 - i, 0))
    full = pl.BlockSpec(memory_space=pltpu.VMEM)
    return pl.pallas_call(
        partial(output_backward_kernel, SEQ_LEN),
        grid=(steps,),
        in_specs=[full, full, tile(dpre.shape[1]), full, full],
        out_specs=[tile(width), pl.BlockSpec((8, 8, width), lambda i: (0, 0, 0))],
        out_shape=[
            jax.ShapeDtypeStruct((positions, width), jnp.bfloat16),
            jax.ShapeDtypeStruct((8, 8, width), jnp.float32),
        ],
        scratch_shapes=[pltpu.VMEM((8, width), jnp.float32), pltpu.VMEM((rows_each, width), jnp.float32)],
        compiler_params=pltpu.CompilerParams(
            dimension_semantics=("arbitrary",), vmem_limit_bytes=48 * 1024 * 1024
        ),
        name="output_backward",
    )(whole, delta, dpre, weight, params)


def input_forward_kernel(
    seq_len,
    tanh_end,
    plain_end,
    whole_ref,
    three_ref,
    down_ref,
    ups_ref,
    params_ref,
    r_ref,
    k_ref,
    v_ref,
    dw_ref,
    da_ref,
    gate_ref,
    mr_ref,
    mk_ref,
    mv_ref,
    inner_ref,
):
    tile = pl.program_id(0)
    rows_each = r_ref.shape[0]
    part = r_ref.shape[1]
    width = whole_ref.shape[1]
    start = tile * rows_each
    at_start = lax.rem(start, seq_len) == 0
    edge = 16
    rows = pl.ds(pl.multiple_of(start, rows_each), rows_each)
    edge_rows = pl.ds(pl.multiple_of(jnp.maximum(start - edge, 0), edge), edge)
    inverse_width = 1.0 / width

    def moments(place):
        values = whole_ref[place, :].astype(jnp.float32)
        centre = jnp.sum(values, axis=1, keepdims=True) * inverse_width
        values = values - centre
        spread = jnp.sum(values * values, axis=1, keepdims=True) * inverse_width
        return centre, lax.rsqrt(spread + norm_eps)

    centre, inv = moments(rows)
    edge_centre, edge_inv = moments(edge_rows)
    block_cols = 256
    row_index = iota((rows_each, block_cols), 0)
    lane = iota((rows_each, down_ref.shape[1]), 1)
    r = k = v = inner_w = inner_a = inner_g = 0.0
    for block in range(width // block_cols):
        cols = slice(block * block_cols, (block + 1) * block_cols)
        gain, bias = params_ref[0:1, cols], params_ref[1:2, cols]
        normed = (whole_ref[rows, cols].astype(jnp.float32) - centre) * inv * gain + bias
        edge_unit = (whole_ref[edge_rows, cols].astype(jnp.float32) - edge_centre) * edge_inv
        edge_normed = (edge_unit * gain + bias)[edge - 1 : edge]
        edge_normed = jnp.where(at_start, 0.0, edge_normed)
        before = jnp.where(row_index == 0, edge_normed, pltpu.roll(normed, 1, 0))
        shift = before - normed

        def mix(index):
            return low(normed + shift * params_ref[index : index + 1, cols])

        mix_r, mix_k, mix_v = mix(2), mix(4), mix(5)
        mr_ref[:, cols], mk_ref[:, cols], mv_ref[:, cols] = mix_r, mix_k, mix_v
        weights = three_ref[cols, :]
        r = r + dot_nn(mix_r, weights[:, :part])
        k = k + dot_nn(mix_k, weights[:, part : 2 * part])
        v = v + dot_nn(mix_v, weights[:, 2 * part :])
        down = down_ref[cols, :]
        inner_w = inner_w + dot_nn(mix(3), down)
        inner_a = inner_a + dot_nn(mix(6), down)
        inner_g = inner_g + dot_nn(mix(7), down)
    r_ref[...], k_ref[...], v_ref[...] = r, k, v
    inner = jnp.where(
        lane < tanh_end,
        jnp.tanh(inner_w),
        jnp.where(lane < plain_end, inner_a, jax.nn.sigmoid(inner_g)),
    )
    inner_ref[...] = inner
    inner_low = low(inner)
    zero = jnp.zeros_like(inner_low)
    ups = ups_ref[...]
    dw_ref[...] = dot_nn(jnp.where(lane < tanh_end, inner_low, zero), ups)
    da_ref[...] = dot_nn(jnp.where((lane >= tanh_end) & (lane < plain_end), inner_low, zero), ups)
    gate_ref[...] = dot_nn(jnp.where(lane >= plain_end, inner_low, zero), ups)


def input_forward(whole, three, down, ups, ends, params):
    positions, width = whole.shape
    part = ups.shape[1]
    rows_each = 256
    tile = lambda cols: pl.BlockSpec((rows_each, cols), lambda i: (i, 0))
    full = pl.BlockSpec(memory_space=pltpu.VMEM)
    shape = jax.ShapeDtypeStruct
    return pl.pallas_call(
        partial(input_forward_kernel, SEQ_LEN, *ends),
        grid=(positions // rows_each,),
        in_specs=[full] * 5,
        out_specs=[tile(part)] * 6 + [tile(width)] * 3 + [tile(down.shape[1])],
        out_shape=[shape((positions, part), jnp.float32)] * 6
        + [shape((positions, width), jnp.bfloat16)] * 3
        + [shape((positions, down.shape[1]), jnp.float32)],
        compiler_params=pltpu.CompilerParams(
            dimension_semantics=("arbitrary",), vmem_limit_bytes=52 * 1024 * 1024
        ),
        name="input_forward",
    )(whole, three, down, ups, params)


def start_gather_kernel(
    size,
    groups,
    chunk_rows,
    x_ref,
    narrow_ref,
    ups_ref,
    out_ref,
    narrow_out,
    ups_out,
    send_sem,
    recv_sem,
    line_send,
    line_recv,
    group_send,
    group_recv,
):
    me = lax.axis_index(LINE)
    mine = lax.axis_index(GROUP)
    barrier = pltpu.get_barrier_semaphore()
    for offset in range(1, groups):
        peer = lax.rem(mine + offset, groups)
        pl.semaphore_signal(barrier, inc=1, device_id={GROUP: peer}, device_id_type=pl.DeviceIdType.MESH)

    @pl.when(me > 0)
    def _():
        pl.semaphore_signal(barrier, inc=1, device_id={LINE: me - 1}, device_id_type=pl.DeviceIdType.MESH)

    @pl.when(me < size - 1)
    def _():
        pl.semaphore_signal(barrier, inc=1, device_id={LINE: me + 1}, device_id_type=pl.DeviceIdType.MESH)

    ends = jnp.where((me == 0) | (me == size - 1), 1, 2)
    pl.semaphore_wait(barrier, ends + groups - 1)
    flows = two_flows(size)
    width = x_ref.shape[1]
    chunks = x_ref.shape[0] // chunk_rows

    def place(block, chunk):
        rows = pl.ds(pl.multiple_of(chunk * chunk_rows, chunk_rows), chunk_rows)
        return out_ref.at[rows, pl.ds(pl.multiple_of(block * width, width), width)]

    def copy_of(flow, block, chunk):
        return flow.copy(
            place(block, chunk), place(block, chunk), send_sem.at[flow.side, block, chunk], recv_sem.at[flow.side, block, chunk]
        )

    def narrow_copy(flow, block):
        spot = narrow_out.at[mine, block]
        return flow.copy(spot, spot, line_send.at[flow.side, block], line_recv.at[flow.side, block])

    def group_copy(kind, out, peer, slot):
        return pltpu.make_async_remote_copy(
            src_ref=out.at[slot],
            dst_ref=out.at[slot],
            send_sem=group_send.at[kind, peer],
            recv_sem=group_recv.at[kind, slot],
            device_id={GROUP: peer},
            device_id_type=pl.DeviceIdType.MESH,
        )

    narrow_out[mine, me] = narrow_ref[...]
    for flow in flows:

        @pl.when(flow.has_target)
        def _():
            narrow_copy(flow, me).start()

    def first(chunk, carry):
        rows = pl.ds(pl.multiple_of(chunk * chunk_rows, chunk_rows), chunk_rows)
        out_ref[rows, pl.ds(pl.multiple_of(me * width, width), width)] = x_ref[rows]
        for flow in flows:

            @pl.when(flow.has_target)
            def _():
                copy_of(flow, me, chunk).start()

        return carry

    lax.fori_loop(0, chunks, first, 0)
    ups_out[mine] = ups_ref[...]
    for offset in range(1, groups):
        group_copy(0, ups_out, lax.rem(mine + offset, groups), mine).start()
    for hop in range(1, size):
        for flow in flows:
            block = me - hop * flow.step
            exists = (block >= 0) & (block < size)

            @pl.when(exists)
            def _():
                narrow_copy(flow, block).wait_recv()

            @pl.when(exists & flow.has_target)
            def _():
                narrow_copy(flow, block).start()

        if hop == size - 1:
            for offset in range(1, groups):
                group_copy(1, narrow_out, lax.rem(mine + offset, groups), mine).start()

        def forward(chunk, carry):
            for flow in flows:
                block = me - hop * flow.step
                exists = (block >= 0) & (block < size)

                @pl.when(exists)
                def _():
                    copy_of(flow, block, chunk).wait_recv()

                @pl.when(exists & flow.has_target)
                def _():
                    copy_of(flow, block, chunk).start()

            return carry

        lax.fori_loop(0, chunks, forward, 0)
    for offset in range(1, groups):
        peer = lax.rem(mine + offset, groups)
        for kind, out in ((0, ups_out), (1, narrow_out)):
            group_copy(kind, out, peer, peer).wait_recv()
            group_copy(kind, out, peer, mine).wait_send()
    for hop in range(size):

        def drain(chunk, carry):
            for flow in flows:
                block = me - hop * flow.step
                exists = (block >= 0) & (block < size)

                @pl.when(exists & flow.has_target)
                def _():
                    copy_of(flow, block, chunk).wait_send()

            return carry

        lax.fori_loop(0, chunks, drain, 0)
        for flow in flows:
            block = me - hop * flow.step
            exists = (block >= 0) & (block < size)

            @pl.when(exists & flow.has_target)
            def _():
                narrow_copy(flow, block).wait_send()


def start_gather(x, narrow, ups, size, groups, collective_id, chunk_rows=256):
    rows, cols = x.shape
    chunks = rows // chunk_rows
    shape = jax.ShapeDtypeStruct
    dma = pltpu.SemaphoreType.DMA
    return pl.pallas_call(
        partial(start_gather_kernel, size, groups, chunk_rows),
        out_shape=[
            shape((rows, size * cols), x.dtype),
            shape((groups, size) + narrow.shape, x.dtype),
            shape((groups,) + ups.shape, x.dtype),
        ],
        in_specs=[pl.BlockSpec(memory_space=pltpu.VMEM)] * 3,
        out_specs=[pl.BlockSpec(memory_space=pltpu.VMEM)] * 3,
        scratch_shapes=[
            dma((2, size, chunks)),
            dma((2, size, chunks)),
            dma((2, size)),
            dma((2, size)),
            dma((2, groups)),
            dma((2, groups)),
        ],
        compiler_params=pltpu.CompilerParams(
            collective_id=collective_id, has_side_effects=True, vmem_limit_bytes=48 * 1024 * 1024
        ),
        cost_estimate=pl.CostEstimate(flops=0, bytes_accessed=link_cost(3 * rows * cols), transcendentals=0),
        name="start_gather",
    )(x, narrow, ups)


def channel_forward_kernel(
    seq_len,
    whole_ref,
    delta_ref,
    key_ref,
    value_ref,
    params_ref,
    mixed_ref,
    active_ref,
    squared_ref,
    part_ref,
    own_ref,
):
    tile = pl.program_id(0)
    rows_each = mixed_ref.shape[0]
    width = whole_ref.shape[1]
    own_width = own_ref.shape[1]
    start = tile * rows_each
    at_start = lax.rem(start, seq_len) == 0
    edge = 16
    rows = pl.ds(pl.multiple_of(start, rows_each), rows_each)
    edge_rows = pl.ds(pl.multiple_of(jnp.maximum(start - edge, 0), edge), edge)
    inverse_width = 1.0 / width

    def residual(place, cols):
        return whole_ref[place, cols].astype(jnp.float32) + delta_ref[place, cols].astype(jnp.float32)

    def moments(place):
        values = residual(place, slice(0, width))
        centre = jnp.sum(values, axis=1, keepdims=True) * inverse_width
        values = values - centre
        spread = jnp.sum(values * values, axis=1, keepdims=True) * inverse_width
        return centre, lax.rsqrt(spread + norm_eps)

    centre, inv = moments(rows)
    edge_centre, edge_inv = moments(edge_rows)
    own_start = pl.multiple_of(lax.axis_index(LINE) * own_width, own_width)
    own_ref[...] = residual(rows, pl.ds(own_start, own_width))
    block_cols = 256
    row_index = iota((rows_each, block_cols), 0)
    for block in range(width // block_cols):
        cols = slice(block * block_cols, (block + 1) * block_cols)
        gain, bias, rate = params_ref[0:1, cols], params_ref[1:2, cols], params_ref[2:3, cols]
        normed = (residual(rows, cols) - centre) * inv * gain + bias
        edge_unit = (residual(edge_rows, cols) - edge_centre) * edge_inv
        edge_normed = (edge_unit * gain + bias)[edge - 1 : edge]
        edge_normed = jnp.where(at_start, 0.0, edge_normed)
        before = jnp.where(row_index == 0, edge_normed, pltpu.roll(normed, 1, 0))
        mixed_ref[:, cols] = low(normed + (before - normed) * rate)
    hidden_cols = 512
    for block in range(key_ref.shape[1] // hidden_cols):
        cols = slice(block * hidden_cols, (block + 1) * hidden_cols)
        active = jnp.maximum(dot_nn(mixed_ref[...], key_ref[:, cols]), 0.0)
        active_ref[:, cols] = active
        squared_ref[:, cols] = low(active * active)
    for block in range(width // hidden_cols):
        cols = slice(block * hidden_cols, (block + 1) * hidden_cols)
        part_ref[:, cols] = low(dot_nn(squared_ref[...], value_ref[:, cols]))


def channel_forward(whole, delta, key_w, value_w, params, own_width):
    positions, width = whole.shape
    units = key_w.shape[1]
    rows_each = 256
    tile = lambda cols: pl.BlockSpec((rows_each, cols), lambda i: (i, 0))
    full = pl.BlockSpec(memory_space=pltpu.VMEM)
    shape = jax.ShapeDtypeStruct
    return pl.pallas_call(
        partial(channel_forward_kernel, SEQ_LEN),
        grid=(positions // rows_each,),
        in_specs=[full] * 5,
        out_specs=[tile(width), tile(units), tile(units), tile(width), tile(own_width)],
        out_shape=[
            shape((positions, width), jnp.bfloat16),
            shape((positions, units), jnp.float32),
            shape((positions, units), jnp.bfloat16),
            shape((positions, width), jnp.bfloat16),
            shape((positions, own_width), jnp.float32),
        ],
        compiler_params=pltpu.CompilerParams(
            dimension_semantics=("arbitrary",), vmem_limit_bytes=56 * 1024 * 1024
        ),
        name="channel_forward",
    )(whole, delta, key_w, value_w, params)


def matmul(left_op, right_op):
    return jnp.dot(left_op, right_op, preferred_element_type=jnp.float32)


def contract_rows(left_op, right_op):
    return jnp.einsum("tk,tn->kn", left_op, right_op, preferred_element_type=jnp.float32)


def against(grad_op, weight_op):
    return jnp.einsum("tn,kn->tk", grad_op, weight_op, preferred_element_type=jnp.float32)


def body(
    hidden,
    teacher,
    lengths,
    feature_params,
    decay_down,
    rate_down,
    gate_down,
    decay_up,
    rate_up,
    gate_up,
    receptance,
    key_proj,
    value_proj,
    output_proj,
    ffn_key,
    ffn_value,
):
    position_count, part_width = hidden.shape
    seq_dev = position_count // SEQ_LEN
    mp_index = lax.axis_index("mp")
    col_start = mp_index * part_width
    groups = lax.axis_size("dp")
    own_lengths = lax.dynamic_slice_in_dim(lengths, lax.axis_index("dp") * seq_dev, seq_dev)
    places = jnp.arange(SEQ_LEN, dtype=jnp.int32)
    valid = (places[None, :] < own_lengths[:, None]).astype(jnp.float32).reshape(position_count)
    loss_scale = position_count * lax.axis_size("dp") / jnp.sum(lengths).astype(jnp.float32)
    line_size = lax.axis_size("mp")
    low_rank = (decay_down.shape[1], rate_down.shape[1], gate_down.shape[1])
    narrow = jnp.concatenate([decay_down, rate_down, gate_down, feature_params], axis=1)
    narrow = jnp.pad(narrow, ((0, 0), (0, -narrow.shape[1] % 128)))
    ups = jnp.concatenate([decay_up, rate_up, gate_up], axis=0)
    ups = jnp.pad(ups, ((0, -ups.shape[0] % 16), (0, 0)))
    whole_low, narrow_w, ups = start_gather(hidden, narrow, ups, line_size, groups, 1)
    narrow_w = narrow_w.reshape(-1, narrow.shape[1])
    decay_down_w = narrow_w[:, : low_rank[0]]
    rate_down_w = narrow_w[:, low_rank[0] : low_rank[0] + low_rank[1]]
    gate_down_w = narrow_w[:, low_rank[0] + low_rank[1] : sum(low_rank)]
    params_low = narrow_w[:, sum(low_rank) : sum(low_rank) + feature_params.shape[1]]
    three = lax.all_gather(
        jnp.concatenate([receptance, key_proj, value_proj], axis=1), "dp", axis=0, tiled=True
    )
    up_rows = (decay_up.shape[0], rate_up.shape[0], gate_up.shape[0])
    decay_up_w = ups[:, : up_rows[0]].reshape(-1, part_width)
    rate_up_w = ups[:, up_rows[0] : up_rows[0] + up_rows[1]].reshape(-1, part_width)
    gate_up_w = ups[:, up_rows[0] + up_rows[1] : sum(up_rows)].reshape(-1, part_width)
    output_w = lax.all_gather(output_proj, "dp", axis=1, tiled=True)
    ffn_key_w = lax.all_gather(ffn_key, "dp", axis=0, tiled=True)
    ffn_value_w = lax.all_gather(ffn_value, "dp", axis=1, tiled=True)
    params = params_low.astype(jnp.float32)
    model_width = whole_low.shape[1]
    params_rows = jnp.pad(params.T, ((0, -params.shape[1] % 8), (0, 0)))
    up_all = jnp.concatenate([decay_up_w, rate_up_w, gate_up_w], axis=0)
    up_all = jnp.pad(up_all, ((0, narrow_w.shape[1] - up_all.shape[0]), (0, 0)))
    (
        acceptance_matrix,
        keys_in,
        payload_source,
        decay_in,
        rate_in,
        sigmoid_source,
        mix_r,
        mix_k,
        mix_v,
        inner_hid,
    ) = input_forward(
        whole_low, three, narrow_w, up_all, (low_rank[0], low_rank[0] + low_rank[1]), params_rows
    )
    inner_low = inner_hid.astype(jnp.bfloat16)
    decay_hid = inner_hid[:, : low_rank[0]]
    gate_hid = inner_hid[:, low_rank[0] + low_rank[1] : sum(low_rank)]
    decay_low = inner_low[:, : low_rank[0]]
    rate_low = inner_low[:, low_rank[0] : low_rank[0] + low_rank[1]]
    gate_low = inner_low[:, low_rank[0] + low_rank[1] : sum(low_rank)]
    columns = lax.dynamic_slice(params_rows, (8, col_start), (8, part_width))
    mixer_args = (
        own_lengths,
        acceptance_matrix,
        keys_in,
        payload_source,
        decay_in,
        rate_in,
        sigmoid_source,
        columns,
    )
    gated_low, *kept = run_mixer_forward(*mixer_args)
    delta_low = line_sum(matmul(gated_low, output_w).astype(jnp.bfloat16), line_size, 2)
    ffn_low, active, squared, ffn_part, own_residual = channel_forward(
        whole_low, delta_low, ffn_key_w, ffn_value_w, params_rows[15:23], part_width
    )
    error_scale = jnp.broadcast_to((loss_scale * valid)[:, None], (position_count, 128))
    out_state, grad_low = line_error(ffn_part, own_residual, teacher, error_scale, line_size, 3)
    grad_ffn_value = contract_rows(squared, grad_low).astype(jnp.bfloat16)
    grad_low, grad_ffn_value = lax.optimization_barrier((grad_low, grad_ffn_value))
    grad_ffn_value = lax.psum_scatter(grad_ffn_value, "dp", scatter_dimension=1, tiled=True)
    grad_squared = against(grad_low, ffn_value_w)
    grad_pre = (grad_squared * 2.0 * active).astype(jnp.bfloat16)
    grad_ffn_key = contract_rows(ffn_low, grad_pre).astype(jnp.bfloat16)
    grad_pre, grad_ffn_key = lax.optimization_barrier((grad_pre, grad_ffn_key))
    grad_ffn_key = lax.psum_scatter(grad_ffn_key, "dp", scatter_dimension=0, tiled=True)
    d_resid_part, d_params_out = output_backward(
        whole_low, delta_low, grad_pre, ffn_key_w, params_rows[15:23]
    )
    d_delta = line_sum(d_resid_part, line_size, 5)
    d_low = (grad_low.astype(jnp.float32) + d_delta.astype(jnp.float32)).astype(jnp.bfloat16)
    grad_output_proj = contract_rows(gated_low, d_low).astype(jnp.bfloat16)
    d_low, grad_output_proj = lax.optimization_barrier((d_low, grad_output_proj))
    grad_output_proj = lax.psum_scatter(grad_output_proj, "dp", scatter_dimension=1, tiled=True)
    d_gated = against(d_low, output_w)
    d_gated, grad_ffn_value, grad_ffn_key = lax.optimization_barrier(
        (d_gated, grad_ffn_value, grad_ffn_key)
    )
    d_recept, d_keys, d_values, d_decay, d_rate, d_gate, d_columns = run_mixer_backward(
        *mixer_args, *kept, d_gated
    )
    d_columns = jnp.sum(d_columns, axis=1)[:7]
    grad_three = weight_grads((mix_r, mix_k, mix_v), (d_recept, d_keys, d_values))
    d_decay, d_rate, d_gate, grad_three = lax.optimization_barrier((d_decay, d_rate, d_gate, grad_three))
    grad_three = lax.psum_scatter(grad_three, "dp", scatter_dimension=0, tiled=True)
    shares = [rank // line_size for rank in low_rank]
    starts = (0, shares[0], shares[0] + shares[1])
    own_rank = sum(shares) + -sum(shares) % 128

    def spread_rows(weight, share, start):
        grouped = weight.reshape(line_size, share, part_width)
        grouped = jnp.pad(grouped, ((0, 0), (start, own_rank - start - share), (0, 0)))
        return grouped.reshape(line_size * own_rank, part_width)

    def own_columns(values, share):
        return lax.dynamic_slice_in_dim(values, mp_index * share, share, 1)

    def own_group(members):
        taken = jnp.concatenate(
            [own_columns(member, share) for member, share in zip(members, shares)], axis=1
        )
        return jnp.pad(taken, ((0, 0), (0, own_rank - sum(shares))))

    d_inner = (
        against(d_decay, spread_rows(decay_up_w, shares[0], starts[0]))
        + against(d_rate, spread_rows(rate_up_w, shares[1], starts[1]))
        + against(d_gate, spread_rows(gate_up_w, shares[2], starts[2]))
    ).astype(jnp.bfloat16)
    d_own = line_scatter(d_inner, line_size, 6)
    d_own, grad_output_proj = lax.optimization_barrier((d_own, grad_output_proj))
    slope = own_group(
        (
            1.0 - decay_hid * decay_hid,
            jnp.ones((position_count, low_rank[1]), jnp.float32),
            gate_hid * (1.0 - gate_hid),
        )
    )
    d_own_pre = (d_own * slope).astype(jnp.bfloat16)
    down_own = own_group((decay_down_w, rate_down_w, gate_down_w))
    d_in_part, d_params_in, d_down = input_backward(
        whole_low, d_recept, d_keys, d_values, d_own_pre, starts[1:], three, down_own, params_rows
    )
    up_grads = jnp.concatenate(
        [
            contract_rows(low_part, grad).reshape(groups, -1, part_width)
            for low_part, grad in ((decay_low, d_decay), (rate_low, d_rate), (gate_low, d_gate))
        ],
        axis=1,
    ).astype(jnp.bfloat16)
    d_in_part, grad_three = lax.optimization_barrier((d_in_part, grad_three))
    core_grads = lax.dynamic_update_slice_in_dim(
        jnp.zeros((7, model_width), jnp.float32), d_columns, col_start, 1
    )
    param_rows = jnp.concatenate(
        [
            jnp.sum(d_params_in, axis=1),
            core_grads,
            jnp.sum(d_params_out, axis=1)[:3],
        ],
        axis=0,
    )
    param_count = param_rows.shape[0]
    narrow_grads = jnp.pad(
        jnp.concatenate([d_down, param_rows], axis=0), ((0, -(own_rank + param_count) % 32), (0, 0))
    )
    d_in_part, narrow_grads, up_grads = lax.optimization_barrier((d_in_part, narrow_grads, up_grads))
    narrow_grads = lax.psum_scatter(narrow_grads, "dp", scatter_dimension=1, tiled=True)
    up_grads = lax.psum_scatter(up_grads, "dp", scatter_dimension=0, tiled=True)
    up_grads = up_grads.reshape(-1, part_width).astype(jnp.float32)
    grad_hidden = line_scatter(d_in_part, line_size, 7) + (
        lax.dynamic_slice_in_dim(grad_low, col_start, part_width, 1).astype(jnp.float32)
        + lax.dynamic_slice_in_dim(d_delta, col_start, part_width, 1).astype(jnp.float32)
    )
    row_block = decay_down.shape[0]
    narrow_grads = jnp.pad(narrow_grads, ((0, 0), (0, -narrow_grads.shape[1] % 128)))
    narrow_rows = narrow_grads.shape[0]
    narrow_grads = line_gather(narrow_grads, line_size, 4, chunk_rows=narrow_rows // 4)
    narrow_grads = narrow_grads.reshape(narrow_rows, line_size, -1)
    narrow_grads = lax.dynamic_slice_in_dim(narrow_grads, mp_index * row_block, row_block, 2)

    def down_grad(start, share):
        taken = narrow_grads[start : start + share].transpose(1, 0, 2)
        return taken.reshape(line_size * share, row_block).T

    grad_params = jnp.sum(narrow_grads[own_rank : own_rank + param_count], axis=1).T
    return (
        out_state,
        grad_hidden,
        grad_params,
        down_grad(starts[0], shares[0]),
        down_grad(starts[1], shares[1]),
        down_grad(starts[2], shares[2]),
        up_grads[: up_rows[0]],
        up_grads[up_rows[0] : up_rows[0] + up_rows[1]],
        up_grads[up_rows[0] + up_rows[1] :],
        grad_three[:, :part_width].astype(jnp.float32),
        grad_three[:, part_width : 2 * part_width].astype(jnp.float32),
        grad_three[:, 2 * part_width :].astype(jnp.float32),
        grad_output_proj.astype(jnp.float32),
        grad_ffn_key.astype(jnp.float32),
        grad_ffn_value.astype(jnp.float32),
    )


def solution(mesh):
    in_specs = (
        P("dp", "mp"),
        P("dp", "mp"),
        P(),
        P(("dp", "mp"), None),
        P(("dp", "mp"), None),
        P(("dp", "mp"), None),
        P(("dp", "mp"), None),
        P("dp", "mp"),
        P("dp", "mp"),
        P("dp", "mp"),
        P("dp", "mp"),
        P("dp", "mp"),
        P("dp", "mp"),
        P("mp", "dp"),
        P("dp", "mp"),
        P("mp", "dp"),
    )
    out_specs = (
        P("dp", "mp"),
        P("dp", "mp"),
        P(("dp", "mp"), None),
        P(("dp", "mp"), None),
        P(("dp", "mp"), None),
        P(("dp", "mp"), None),
        P("dp", "mp"),
        P("dp", "mp"),
        P("dp", "mp"),
        P("dp", "mp"),
        P("dp", "mp"),
        P("dp", "mp"),
        P("mp", "dp"),
        P("dp", "mp"),
        P("mp", "dp"),
    )
    return jax.shard_map(body, mesh=mesh, in_specs=in_specs, out_specs=out_specs, check_vma=False)
```

```python
from functools import partial
import math
from types import SimpleNamespace

import jax
import jax.numpy as jnp
from jax import lax
from jax.experimental import pallas as pl
from jax.experimental.pallas import tpu as pltpu
from jax.sharding import PartitionSpec as P

norm_eps = 1e-05
SUBSPACE_SIZE = 64
SEQ_LEN = 1024
group_eps = 0.00064
CHUNK = 64
PAIR = 2 * SUBSPACE_SIZE
CHUNKS_FWD = 4
CHUNKS_BWD = 2
DECAY_SCALE = math.exp(-0.5)


def dot_nn(left_op, right_op):
    return lax.dot_general(left_op, right_op, (((1,), (0,)), ((), ())), preferred_element_type=jnp.float32)


def dot_nt(left_op, right_op):
    return lax.dot_general(left_op, right_op, (((1,), (1,)), ((), ())), preferred_element_type=jnp.float32)


def dot_tn(left_op, right_op):
    return lax.dot_general(left_op, right_op, (((0,), (0,)), ((), ())), preferred_element_type=jnp.float32)


def low(values):
    return values.astype(jnp.bfloat16)


def split_dot(ones_op, values):
    top = low(values)
    rest = values - top.astype(jnp.float32)
    mid = low(rest)
    tail = low(rest - mid.astype(jnp.float32))
    return dot_nn(ones_op, top) + dot_nn(ones_op, mid) + dot_nn(ones_op, tail)


def halves(values):
    top = low(values)
    return top, low(values - top.astype(jnp.float32))


def iota(shape, axis):
    return lax.broadcasted_iota(jnp.int32, shape, axis)


def head_masks():
    lane = iota((CHUNK, PAIR), 1)
    return lane < SUBSPACE_SIZE


def stack_heads(values):
    first = iota(values.shape, 1) < SUBSPACE_SIZE
    zero = jnp.zeros_like(values)
    return jnp.concatenate(
        [jnp.where(first, values, zero), jnp.where(first, zero, values)], axis=0
    )


def fold_heads(values):
    first = iota((CHUNK, PAIR), 1) < SUBSPACE_SIZE
    return jnp.where(first, values[:CHUNK], values[CHUNK:])


def head_ones():
    return (
        iota((PAIR, PAIR), 0) // SUBSPACE_SIZE == iota((PAIR, PAIR), 1) // SUBSPACE_SIZE
    )


def head_sum(values, ones_op):
    top = low(values)
    rest = low(values - top.astype(jnp.float32))
    return dot_nn(top, ones_op) + dot_nn(rest, ones_op)


def lower_inverses(lower_parts):
    row = iota((CHUNK, PAIR), 0)
    col = iota((CHUNK, PAIR), 1) % CHUNK
    eye = jnp.where(row == col, 1.0, 0.0)

    def times(lefts, rights):
        return [
            dot_nn(low(left_op), stack_heads(low(right_op)))
            for left_op, right_op in zip(lefts, rights)
        ]

    def plus(*lists):
        return [sum(members[1:], members[0]) for members in zip(*lists)]

    near = row // 8 == col // 8
    base = [jnp.where(near, part, 0.0) for part in lower_parts]
    square = times(base, base)
    cube = times(base, square)
    fourth = times(square, square)
    accum = [eye + first + second + third for first, second, third in zip(base, square, cube)]
    accum = plus(accum, times(accum, fourth))
    width = 8
    while width < CHUNK:
        level = (row // (2 * width) == col // (2 * width)) & (row // width != col // width)
        off = [jnp.where(level, part, 0.0) for part in lower_parts]
        accum = plus(accum, times(times(accum, off), accum))
        width *= 2
    return accum


def prepare(r, k, dw, da, cols, live, tri_op, ones_op):
    sw = jax.nn.sigmoid(dw + cols[0:1])
    full_log = -DECAY_SCALE * sw
    log_decay = jnp.where(live, full_log, 0.0)
    rate = jax.nn.sigmoid(da + cols[1:2])
    scaled = k * cols[2:3]
    inv = lax.rsqrt(head_sum(scaled * scaled, ones_op) + 1e-06)
    unit = scaled * inv
    unit_live = jnp.where(live, unit, 0.0)
    lag_scale = 1.0 + (rate - 1.0) * cols[3:4]
    lagged = jnp.where(live, k * lag_scale, 0.0)
    running = split_dot(tri_op, log_decay)
    grown = jnp.exp(running)
    before = jnp.exp(running - log_decay)
    shrunk = jnp.exp(-running)
    last = running[CHUNK - 1 : CHUNK]
    til_end = jnp.exp(last - running)
    write = unit_live * rate
    return SimpleNamespace(
        sw=sw,
        full_log=full_log,
        rate=rate,
        inv=inv,
        unit=unit,
        unit_live=unit_live,
        lag_scale=lag_scale,
        lagged=lagged,
        grown=grown,
        before=before,
        shrunk=shrunk,
        til_end=til_end,
        final=jnp.exp(last),
        read_wide=r * grown,
        write_wide=write * shrunk,
        key_wide=lagged * shrunk,
        read_hat=low(r * grown),
        remove_hat=low(-unit_live * before),
        write_hat=low(write * shrunk),
        key_hat=low(lagged * shrunk),
        write_end=low(write * til_end),
        key_end=low(lagged * til_end),
    )


def tri_masks():
    row = iota((CHUNK, PAIR), 0)
    col = iota((CHUNK, PAIR), 1) % CHUNK
    return row > col, row >= col


def mixer_forward(
    steps_per_seq,
    length_ref,
    r_ref,
    k_ref,
    v_ref,
    dw_ref,
    da_ref,
    gate_ref,
    cols_ref,
    z_ref,
    y_ref,
    t_ref,
    u_ref,
    s_ref,
    lk_ref,
    reads_ref,
    state,
):
    step = pl.program_id(0)
    within_seq = lax.rem(step, steps_per_seq)
    length = length_ref[step // steps_per_seq]

    @pl.when(within_seq == 0)
    def _():
        state[...] = jnp.zeros_like(state)

    rows_each = r_ref.shape[0]
    chunks = rows_each // CHUNK
    pairs = r_ref.shape[1] // PAIR
    ones_mask = head_ones()
    ones_op = jnp.where(ones_mask, 1.0, 0.0).astype(jnp.bfloat16)
    tri_op = jnp.where(iota((CHUNK, CHUNK), 0) >= iota((CHUNK, CHUNK), 1), 1.0, 0.0).astype(jnp.bfloat16)
    strict, within = tri_masks()
    within_two = jnp.concatenate([within, within], axis=1)
    units = [(chunk, pair) for chunk in range(chunks) for pair in range(pairs)]

    def place_of(unit):
        chunk, pair = unit
        return slice(chunk * CHUNK, (chunk + 1) * CHUNK), slice(pair * PAIR, (pair + 1) * PAIR)

    prepared, scored, lower_parts = [], [], []
    for unit in units:
        rows, lanes = place_of(unit)
        live = within_seq * rows_each + unit[0] * CHUNK + iota((CHUNK, PAIR), 0) < length
        got = prepare(
            r_ref[rows, lanes],
            k_ref[rows, lanes],
            dw_ref[rows, lanes],
            da_ref[rows, lanes],
            cols_ref[:, lanes],
            live,
            tri_op,
            ones_op,
        )
        prepared.append(got)
    for unit, got in zip(units, prepared):
        got.both = jnp.concatenate([got.remove_hat, got.read_hat], axis=0)
        past = jnp.concatenate([stack_heads(got.write_hat), stack_heads(got.key_hat)], axis=0)
        scores = dot_nt(got.both, past)
        past_rest = jnp.concatenate(
            [stack_heads(halves(got.write_wide)[1]), stack_heads(halves(got.key_wide)[1])], axis=0
        )
        got.read_rest = halves(got.read_wide)[1]
        fine = scores[CHUNK:] + (dot_nt(got.read_rest, past) + dot_nt(got.read_hat, past_rest))
        lower_parts.append(jnp.where(strict, scores[:CHUNK, :PAIR], 0.0))
        lower_key = low(jnp.where(strict, scores[:CHUNK, PAIR:], 0.0))
        reads = low(jnp.where(within_two, fine, 0.0))
        scored.append((lower_key, reads))
    solves = [low(part) for part in lower_inverses(lower_parts)]
    for unit, solve in zip(units, solves):
        t_ref[place_of(unit)] = solve
    for chunk in range(chunks):
        group = [index for index, unit in enumerate(units) if unit[0] == chunk]
        lows = [low(v_ref[place_of(units[index])]) for index in group]
        stacks = [stack_heads(values) for values in lows]
        olds = [state[units[index][1]] for index in group]
        old_parts = [halves(old) for old in olds]
        from_state = [dot_nt(prepared[index].both, old[0]) for index, old in zip(group, old_parts)]
        read_state = [
            part[CHUNK:]
            + (dot_nt(prepared[index].read_rest, old[0]) + dot_nt(prepared[index].read_hat, old[1]))
            for index, part, old in zip(group, from_state, old_parts)
        ]
        right = [
            low(part[:CHUNK] + dot_nn(scored[index][0], stack))
            for index, part, stack in zip(group, from_state, stacks)
        ]
        removed = [low(dot_nn(solves[index], stack_heads(part))) for index, part in zip(group, right)]
        for slot, index in enumerate(group):
            pair = units[index][1]
            got = prepared[index]
            ends = jnp.concatenate([got.write_end, got.key_end], axis=0)
            adds = dot_tn(jnp.concatenate([removed[slot], lows[slot]], axis=0), ends)
            state[pair] = olds[slot] * got.final + jnp.where(ones_mask, adds, 0.0)
            u_ref[place_of(units[index])] = removed[slot]
            rows, lanes = place_of(units[index])
            lk_ref[rows, lanes], reads_ref[rows, slice(2 * lanes.start, 2 * lanes.stop)] = scored[index]
            s_ref[chunk, pair] = olds[slot]
        outs = [
            read_state[slot]
            + dot_nn(scored[index][1], jnp.concatenate([stack_heads(removed[slot]), stacks[slot]], axis=0))
            for slot, index in enumerate(group)
        ]
        centred = [y - head_sum(y, ones_op) * (1.0 / SUBSPACE_SIZE) for y in outs]
        spread = [head_sum(part * part, ones_op) * (1.0 / SUBSPACE_SIZE) for part in centred]
        for slot, index in enumerate(group):
            rows, lanes = place_of(units[index])
            cols = cols_ref[:, lanes]
            normed = centred[slot] * lax.rsqrt(spread[slot] + group_eps)
            bonus = head_sum(r_ref[rows, lanes] * prepared[index].lagged * cols[4:5], ones_op)
            mixed = normed * cols[5:6] + cols[6:7] + bonus * v_ref[rows, lanes]
            y_ref[rows, lanes] = outs[slot]
            z_ref[rows, lanes] = low(mixed * gate_ref[rows, lanes])


def mixer_backward(
    steps_per_seq,
    length_ref,
    r_ref,
    k_ref,
    v_ref,
    dw_ref,
    da_ref,
    gate_ref,
    cols_ref,
    y_ref,
    t_ref,
    u_ref,
    s_ref,
    lk_ref,
    reads_ref,
    dz_ref,
    dr_ref,
    dk_ref,
    dv_ref,
    ddw_ref,
    dda_ref,
    dgate_ref,
    dcols_ref,
    dstate,
):
    step = pl.num_programs(0) - 1 - pl.program_id(0)
    within_seq = lax.rem(step, steps_per_seq)
    length = length_ref[step // steps_per_seq]

    @pl.when(within_seq == steps_per_seq - 1)
    def _():
        dstate[...] = jnp.zeros_like(dstate)

    @pl.when(pl.program_id(0) == 0)
    def _():
        dcols_ref[...] = jnp.zeros_like(dcols_ref)

    rows_each = r_ref.shape[0]
    chunks = rows_each // CHUNK
    pairs = r_ref.shape[1] // PAIR
    ones_mask = head_ones()
    ones_op = jnp.where(ones_mask, 1.0, 0.0).astype(jnp.bfloat16)
    row = iota((CHUNK, CHUNK), 0)
    col = iota((CHUNK, CHUNK), 1)
    tri_op = jnp.where(row >= col, 1.0, 0.0).astype(jnp.bfloat16)
    suffix_op = jnp.where(row <= col, 1.0, 0.0).astype(jnp.bfloat16)
    prefix_op = jnp.where(row > col, 1.0, 0.0).astype(jnp.bfloat16)
    sums_op = jnp.concatenate([suffix_op, prefix_op], axis=1)
    strict, within = tri_masks()

    def add_col(index, lanes, values):
        part = values[0:8]
        for start in range(8, CHUNK, 8):
            part = part + values[start : start + 8]
        dcols_ref[index, :, lanes] += part

    strict_two = jnp.concatenate([strict, strict], axis=1)
    within_two = jnp.concatenate([within, within], axis=1)
    all_masks = jnp.concatenate([strict_two, within_two], axis=0)
    units = [(chunk, pair) for chunk in reversed(range(chunks)) for pair in range(pairs)]
    mean_of = 1.0 / SUBSPACE_SIZE
    known = []
    for chunk, pair in units:
        rows = slice(chunk * CHUNK, (chunk + 1) * CHUNK)
        lanes = slice(pair * PAIR, (pair + 1) * PAIR)
        live = within_seq * rows_each + chunk * CHUNK + iota((CHUNK, PAIR), 0) < length
        cols = cols_ref[:, lanes]
        got = prepare(
            r_ref[rows, lanes],
            k_ref[rows, lanes],
            dw_ref[rows, lanes],
            da_ref[rows, lanes],
            cols,
            live,
            tri_op,
            ones_op,
        )
        got.rows, got.lanes, got.live, got.cols = rows, lanes, live, cols
        got.pair, got.chunk = pair, chunk
        known.append(got)
    for got in known:
        y = y_ref[got.rows, got.lanes]
        got.centred = y - head_sum(y, ones_op) * mean_of
    for got in known:
        spread = head_sum(got.centred * got.centred, ones_op) * mean_of
        got.inv_y = lax.rsqrt(spread + group_eps)
    for got in known:
        rows, lanes, cols = got.rows, got.lanes, got.cols
        r, v, dz = r_ref[rows, lanes], v_ref[rows, lanes], dz_ref[rows, lanes]
        normed = got.centred * got.inv_y
        got.bonus = head_sum(r * got.lagged * cols[4:5], ones_op)
        mixed = normed * cols[5:6] + cols[6:7] + got.bonus * v
        dgate_ref[rows, lanes] = low(dz * mixed)
        dmix = dz * gate_ref[rows, lanes]
        add_col(5, lanes, dmix * normed)
        add_col(6, lanes, dmix)
        dnormed = dmix * cols[5:6]
        got.dbonus = head_sum(dmix * v, ones_op)
        mean_grad = head_sum(dnormed, ones_op) * mean_of
        mean_prod = head_sum(dnormed * normed, ones_op) * mean_of
        got.dy_low, got.dy_rest = halves(got.inv_y * (dnormed - mean_grad - normed * mean_prod))
        got.dv = got.bonus * dmix
    for got in known:
        rows, lanes = got.rows, got.lanes
        got.both = jnp.concatenate([got.remove_hat, got.read_hat], axis=0)
        got.past = jnp.concatenate(
            [stack_heads(got.write_hat), stack_heads(got.key_hat)], axis=0
        )
        got.lower_key = lk_ref[rows, lanes]
        reads = reads_ref[rows, slice(2 * lanes.start, 2 * lanes.stop)]
        got.from_y = dot_tn(reads, got.dy_low)
        v_low = low(v_ref[rows, lanes])
        removed = u_ref[rows, lanes]
        got.sent = jnp.concatenate([removed, v_low], axis=0)
        got.stacks = jnp.concatenate([stack_heads(removed), stack_heads(v_low)], axis=0)
    for chunk in reversed(range(chunks)):
        group = [got for got in known if got.chunk == chunk]
        for got in group:
            got.later = dstate[got.pair]
            got.later_low, got.later_rest = halves(got.later)
            ends = jnp.concatenate([got.write_end, got.key_end], axis=0)
            got.from_later = dot_nt(ends, got.later_low)
        for got in group:
            dremoved = low(got.from_later[:CHUNK] + fold_heads(got.from_y[:PAIR]))
            got.dright = low(fold_heads(dot_tn(t_ref[got.rows, got.lanes], dremoved)))
        for got in group:
            got.douts = jnp.concatenate([got.dright, got.dy_low], axis=0)
            adds = dot_tn(got.douts, got.both) + dot_tn(got.dy_rest, got.read_hat)
            adds = jnp.where(ones_mask, adds, 0.0)
            dstate[got.pair] = got.later * got.final + adds
    for got in known:
        dv = got.dv + got.from_later[CHUNK:] + fold_heads(got.from_y[PAIR:])
        dv = dv + fold_heads(dot_tn(got.lower_key, got.dright))
        dv_ref[got.rows, got.lanes] = low(dv)
        dscores = dot_nt(got.douts, got.stacks)
        fine = dscores[CHUNK:] + dot_nt(got.dy_rest, got.stacks)
        dscores = low(jnp.where(all_masks, jnp.concatenate([dscores[:CHUNK], fine], axis=0), 0.0))
        old_wide = s_ref[got.chunk, got.pair]
        old_low, old_rest = halves(old_wide)
        from_old = dot_nn(got.douts, old_low)
        fine = from_old[CHUNK:] + (dot_nn(got.dy_rest, old_low) + dot_nn(got.dy_low, old_rest))
        got.dboth = jnp.concatenate([from_old[:CHUNK], fine], axis=0) + dot_nn(dscores, got.past)
        dpast = dot_tn(dscores, got.both)
        got.dwrite_hat = fold_heads(dpast[:PAIR])
        got.dkey_hat = fold_heads(dpast[PAIR:])
        got.dends = dot_nn(got.sent, got.later_low) + dot_nn(got.sent, got.later_rest)
        got.dfinal = jnp.sum(got.later * old_wide, axis=0, keepdims=True)
    for got in known:
        rows, lanes, cols, live = got.rows, got.lanes, got.cols, got.live

        def wide(values):
            return values.astype(jnp.float32)

        r, k = r_ref[rows, lanes], k_ref[rows, lanes]
        dwrite_hat, dkey_hat = got.dwrite_hat, got.dkey_hat
        dwrite_end, dkey_end = got.dends[:CHUNK], got.dends[CHUNK:]
        dremove_hat, dread_hat = got.dboth[:CHUNK], got.dboth[CHUNK:]
        dbonus, lagged = got.dbonus, got.lagged
        bonus_lag = dbonus * lagged
        add_col(4, lanes, bonus_lag * r)
        dr_ref[rows, lanes] = low(bonus_lag * cols[4:5] + dread_hat * got.grown)
        minus = wide(got.remove_hat) * dremove_hat
        plus = wide(got.read_hat) * dread_hat + minus
        plus = plus - wide(got.write_hat) * dwrite_hat - wide(got.key_hat) * dkey_hat
        ending = wide(got.write_end) * dwrite_end + wide(got.key_end) * dkey_end
        sums = split_dot(sums_op, jnp.concatenate([plus, ending], axis=0))
        dlog = sums - minus + got.final * got.dfinal
        ddw = jnp.where(live, dlog * got.full_log * (1.0 - got.sw), 0.0)
        add_col(0, lanes, ddw)
        ddw_ref[rows, lanes] = low(ddw)
        dwrite = dwrite_hat * got.shrunk + dwrite_end * got.til_end
        dlag = dbonus * r * cols[4:5] + dkey_hat * got.shrunk + dkey_end * got.til_end
        dlag = jnp.where(live, dlag, 0.0)
        rate = got.rate
        dunit = jnp.where(live, dwrite * rate - dremove_hat * got.before, 0.0)
        lag_k = dlag * k
        drate = dwrite * got.unit_live + lag_k * cols[3:4]
        add_col(3, lanes, lag_k * (rate - 1.0))
        dscaled = got.inv * (dunit - got.unit * head_sum(dunit * got.unit, ones_op))
        add_col(2, lanes, dscaled * k)
        dk_ref[rows, lanes] = low(dlag * got.lag_scale + dscaled * cols[2:3])
        dda = drate * rate * (1.0 - rate)
        add_col(1, lanes, dda)
        dda_ref[rows, lanes] = low(dda)


def run_mixer_forward(lengths, r, k, v, dw, da, gate, cols):
    positions, part_width = r.shape
    rows_each = CHUNKS_FWD * CHUNK
    steps = positions // rows_each
    steps_per_seq = SEQ_LEN // rows_each
    pairs = part_width // PAIR
    wide = pl.BlockSpec((rows_each, part_width), lambda i: (i, 0))
    shape = jax.ShapeDtypeStruct
    return pl.pallas_call(
        partial(mixer_forward, steps_per_seq),
        grid=(steps,),
        in_specs=[pl.BlockSpec(memory_space=pltpu.SMEM)]
        + [wide] * 6
        + [pl.BlockSpec((8, part_width), lambda i: (0, 0))],
        out_specs=[wide] * 4
        + [
            pl.BlockSpec((CHUNKS_FWD, pairs, PAIR, PAIR), lambda i: (i, 0, 0, 0)),
            wide,
            pl.BlockSpec((rows_each, 2 * part_width), lambda i: (i, 0)),
        ],
        out_shape=[
            shape((positions, part_width), jnp.bfloat16),
            shape((positions, part_width), jnp.float32),
            shape((positions, part_width), jnp.bfloat16),
            shape((positions, part_width), jnp.bfloat16),
            shape((positions // CHUNK, pairs, PAIR, PAIR), jnp.float32),
            shape((positions, part_width), jnp.bfloat16),
            shape((positions, 2 * part_width), jnp.bfloat16),
        ],
        scratch_shapes=[pltpu.VMEM((pairs, PAIR, PAIR), jnp.float32)],
        compiler_params=pltpu.CompilerParams(
            dimension_semantics=("arbitrary",), vmem_limit_bytes=60 * 1024 * 1024
        ),
        name="mixer_forward",
    )(lengths, r, k, v, dw, da, gate, cols)


def run_mixer_backward(lengths, r, k, v, dw, da, gate, cols, y, t, u, s, lk, reads, dz):
    positions, part_width = r.shape
    rows_each = CHUNKS_BWD * CHUNK
    steps = positions // rows_each
    steps_per_seq = SEQ_LEN // rows_each
    pairs = part_width // PAIR
    wide = pl.BlockSpec((rows_each, part_width), lambda i: (steps - 1 - i, 0))
    shape = jax.ShapeDtypeStruct
    return pl.pallas_call(
        partial(mixer_backward, steps_per_seq),
        grid=(steps,),
        in_specs=[pl.BlockSpec(memory_space=pltpu.SMEM)]
        + [wide] * 6
        + [pl.BlockSpec((8, part_width), lambda i: (0, 0))]
        + [wide] * 3
        + [
            pl.BlockSpec((CHUNKS_BWD, pairs, PAIR, PAIR), lambda i: (steps - 1 - i, 0, 0, 0)),
            wide,
            pl.BlockSpec((rows_each, 2 * part_width), lambda i: (steps - 1 - i, 0)),
            wide,
        ],
        out_specs=[wide] * 6 + [pl.BlockSpec((8, 8, part_width), lambda i: (0, 0, 0))],
        out_shape=[shape((positions, part_width), jnp.bfloat16)] * 6
        + [shape((8, 8, part_width), jnp.float32)],
        scratch_shapes=[pltpu.VMEM((pairs, PAIR, PAIR), jnp.float32)],
        compiler_params=pltpu.CompilerParams(
            dimension_semantics=("arbitrary",), vmem_limit_bytes=60 * 1024 * 1024
        ),
        name="mixer_backward",
    )(lengths, r, k, v, dw, da, gate, cols, y, t, u, s, lk, reads, dz)


LINE = "mp"
GROUP = "dp"
END_LAG = 3
MID_LAG = 1


def link_cost(elements):
    return elements * 2 * 2 * 40


def line_barrier(size):
    me = lax.axis_index(LINE)
    barrier = pltpu.get_barrier_semaphore()

    @pl.when(me > 0)
    def _():
        pl.semaphore_signal(barrier, inc=1, device_id={LINE: me - 1}, device_id_type=pl.DeviceIdType.MESH)

    @pl.when(me < size - 1)
    def _():
        pl.semaphore_signal(barrier, inc=1, device_id={LINE: me + 1}, device_id_type=pl.DeviceIdType.MESH)

    ends = jnp.where((me == 0) | (me == size - 1), 1, 2)
    pl.semaphore_wait(barrier, ends)


class Flow:
    def __init__(self, size, side):
        self.size = size
        self.side = side
        self.me = lax.axis_index(LINE)
        self.step = 1 - 2 * side
        self.target = self.me + self.step
        source = self.me - self.step
        self.has_source = (source >= 0) & (source < size)
        self.has_target = (self.target >= 0) & (self.target < size)

    def copy(self, source, place, send_sem, recv_sem):
        return pltpu.make_async_remote_copy(
            src_ref=source,
            dst_ref=place,
            send_sem=send_sem,
            recv_sem=recv_sem,
            device_id={LINE: self.target},
            device_id_type=pl.DeviceIdType.MESH,
        )


def two_flows(size):
    me = lax.axis_index(LINE)
    near = jnp.where(me < size // 2, 0, 1)
    return Flow(size, near), Flow(size, 1 - near)


def line_sum_kernel(size, chunk_rows, x_ref, out_ref, got, sent, send_sem, recv_sem):
    line_barrier(size)
    me = lax.axis_index(LINE)
    flows = two_flows(size)
    chunks = x_ref.shape[0] // chunk_rows

    def copy_of(flow, chunk, source):
        rows = pl.ds(pl.multiple_of(chunk * chunk_rows, chunk_rows), chunk_rows)
        return flow.copy(
            source.at[rows], got.at[flow.side, rows], send_sem.at[flow.side, chunk], recv_sem.at[flow.side, chunk]
        )

    def pass_on(flow, chunk):
        rows = pl.ds(pl.multiple_of(chunk * chunk_rows, chunk_rows), chunk_rows)

        @pl.when(flow.has_source)
        def _():
            copy_of(flow, chunk, x_ref).wait_recv()

        @pl.when(flow.has_source & flow.has_target)
        def _():
            total = got[flow.side, rows].astype(jnp.float32) + x_ref[rows].astype(jnp.float32)
            sent[flow.side, rows] = total.astype(sent.dtype)
            copy_of(flow, chunk, sent.at[flow.side]).start()

        @pl.when(jnp.logical_not(flow.has_source))
        def _():
            copy_of(flow, chunk, x_ref).start()

    is_end = (me == 0) | (me == size - 1)
    lag = jnp.where(is_end, END_LAG, MID_LAG)

    def step(turn, carry):
        @pl.when(turn < chunks)
        def _():
            pass_on(flows[0], turn)

        chunk = turn - lag

        @pl.when((chunk >= 0) & (chunk < chunks))
        def _():
            pass_on(flows[1], chunk)
            rows = pl.ds(pl.multiple_of(chunk * chunk_rows, chunk_rows), chunk_rows)

            @pl.when(is_end)
            def _():
                other = got[flows[1].side, rows].astype(jnp.float32)
                out_ref[rows] = (other + x_ref[rows].astype(jnp.float32)).astype(out_ref.dtype)

            @pl.when(jnp.logical_not(is_end))
            def _():
                other = got[0, rows].astype(jnp.float32) + got[1, rows].astype(jnp.float32)
                out_ref[rows] = (other + x_ref[rows].astype(jnp.float32)).astype(out_ref.dtype)

        return carry

    lax.fori_loop(0, chunks + END_LAG, step, 0)

    def drain(chunk, carry):
        for flow in flows:

            @pl.when(flow.has_target)
            def _():
                copy_of(flow, chunk, x_ref).wait_send()

        return carry

    lax.fori_loop(0, chunks, drain, 0)


def line_sum(x, size, collective_id, chunk_rows=64):
    rows, cols = x.shape
    chunks = rows // chunk_rows
    return pl.pallas_call(
        partial(line_sum_kernel, size, chunk_rows),
        out_shape=jax.ShapeDtypeStruct(x.shape, x.dtype),
        in_specs=[pl.BlockSpec(memory_space=pltpu.VMEM)],
        out_specs=pl.BlockSpec(memory_space=pltpu.VMEM),
        scratch_shapes=[
            pltpu.VMEM((2, rows, cols), x.dtype),
            pltpu.VMEM((2, rows, cols), x.dtype),
            pltpu.SemaphoreType.DMA((2, chunks)),
            pltpu.SemaphoreType.DMA((2, chunks)),
        ],
        compiler_params=pltpu.CompilerParams(
            collective_id=collective_id, has_side_effects=True, vmem_limit_bytes=48 * 1024 * 1024
        ),
        cost_estimate=pl.CostEstimate(flops=0, bytes_accessed=link_cost(rows * cols), transcendentals=0),
        name="line_sum",
    )(x)


def line_gather_kernel(size, chunk_rows, x_ref, out_ref, send_sem, recv_sem):
    line_barrier(size)
    me = lax.axis_index(LINE)
    flows = two_flows(size)
    width = x_ref.shape[1]
    chunks = x_ref.shape[0] // chunk_rows

    def place(block, chunk):
        rows = pl.ds(pl.multiple_of(chunk * chunk_rows, chunk_rows), chunk_rows)
        return out_ref.at[rows, pl.ds(pl.multiple_of(block * width, width), width)]

    def copy_of(flow, block, chunk):
        return flow.copy(
            place(block, chunk), place(block, chunk), send_sem.at[flow.side, block, chunk], recv_sem.at[flow.side, block, chunk]
        )

    def step(chunk, carry):
        rows = pl.ds(pl.multiple_of(chunk * chunk_rows, chunk_rows), chunk_rows)
        out_ref[rows, pl.ds(pl.multiple_of(me * width, width), width)] = x_ref[rows]
        for flow in flows:

            @pl.when(flow.has_target)
            def _():
                copy_of(flow, me, chunk).start()

        return carry

    lax.fori_loop(0, chunks, step, 0)
    for hop in range(1, size):

        def forward(chunk, carry):
            for flow in flows:
                block = me - hop * flow.step
                exists = (block >= 0) & (block < size)

                @pl.when(exists)
                def _():
                    copy_of(flow, block, chunk).wait_recv()

                @pl.when(exists & flow.has_target)
                def _():
                    copy_of(flow, block, chunk).start()

            return carry

        lax.fori_loop(0, chunks, forward, 0)
    for hop in range(size):

        def drain(chunk, carry):
            for flow in flows:
                block = me - hop * flow.step
                exists = (block >= 0) & (block < size)

                @pl.when(exists & flow.has_target)
                def _():
                    copy_of(flow, block, chunk).wait_send()

            return carry

        lax.fori_loop(0, chunks, drain, 0)


def line_gather(x, size, collective_id, chunk_rows=256):
    rows, cols = x.shape
    chunks = rows // chunk_rows
    return pl.pallas_call(
        partial(line_gather_kernel, size, chunk_rows),
        out_shape=jax.ShapeDtypeStruct((rows, size * cols), x.dtype),
        in_specs=[pl.BlockSpec(memory_space=pltpu.VMEM)],
        out_specs=pl.BlockSpec(memory_space=pltpu.VMEM),
        scratch_shapes=[
            pltpu.SemaphoreType.DMA((2, size, chunks)),
            pltpu.SemaphoreType.DMA((2, size, chunks)),
        ],
        compiler_params=pltpu.CompilerParams(
            collective_id=collective_id, has_side_effects=True, vmem_limit_bytes=48 * 1024 * 1024
        ),
        cost_estimate=pl.CostEstimate(flops=0, bytes_accessed=link_cost(3 * rows * cols), transcendentals=0),
        name="line_gather",
    )(x)


def line_scatter_kernel(size, chunk_rows, x_ref, out_ref, got, sent, send_sem, recv_sem):
    line_barrier(size)
    me = lax.axis_index(LINE)
    flows = two_flows(size)
    width = out_ref.shape[1]
    chunks = x_ref.shape[0] // chunk_rows

    def rows_of(chunk):
        return pl.ds(pl.multiple_of(chunk * chunk_rows, chunk_rows), chunk_rows)

    def cols_of(block):
        return pl.ds(pl.multiple_of(block * width, width), width)

    def copy_of(flow, block, chunk, source):
        return flow.copy(
            source,
            got.at[flow.side, rows_of(chunk), cols_of(block)],
            send_sem.at[flow.side, block, chunk],
            recv_sem.at[flow.side, block, chunk],
        )

    def own(block, chunk):
        return x_ref[rows_of(chunk), cols_of(block)].astype(jnp.float32)

    for hop in range(size - 1):

        def forward(chunk, carry):
            for flow in flows:
                block = jnp.where(flow.side == 0, size - 1 - hop, hop)
                ahead = (block - me) * flow.step > 0

                @pl.when(ahead & flow.has_source)
                def _():
                    source = x_ref.at[rows_of(chunk), cols_of(block)]
                    copy_of(flow, block, chunk, source).wait_recv()
                    total = got[flow.side, rows_of(chunk), cols_of(block)].astype(jnp.float32) + own(block, chunk)
                    sent[flow.side, rows_of(chunk), cols_of(block)] = total.astype(sent.dtype)
                    copy_of(flow, block, chunk, sent.at[flow.side, rows_of(chunk), cols_of(block)]).start()

                @pl.when(ahead & jnp.logical_not(flow.has_source))
                def _():
                    copy_of(flow, block, chunk, x_ref.at[rows_of(chunk), cols_of(block)]).start()

            return carry

        lax.fori_loop(0, chunks, forward, 0)

    def finish(chunk, carry):
        rows = rows_of(chunk)
        for flow in flows:

            @pl.when(flow.has_source)
            def _():
                copy_of(flow, me, chunk, x_ref.at[rows, cols_of(me)]).wait_recv()

        @pl.when(me == 0)
        def _():
            out_ref[rows] = (got[1, rows, cols_of(me)].astype(jnp.float32) + own(me, chunk)).astype(out_ref.dtype)

        @pl.when(me == size - 1)
        def _():
            out_ref[rows] = (got[0, rows, cols_of(me)].astype(jnp.float32) + own(me, chunk)).astype(out_ref.dtype)

        @pl.when((me > 0) & (me < size - 1))
        def _():
            other = got[0, rows, cols_of(me)].astype(jnp.float32) + got[1, rows, cols_of(me)].astype(jnp.float32)
            out_ref[rows] = (other + own(me, chunk)).astype(out_ref.dtype)

        return carry

    lax.fori_loop(0, chunks, finish, 0)
    for hop in range(size - 1):

        def drain(chunk, carry):
            for flow in flows:
                block = jnp.where(flow.side == 0, size - 1 - hop, hop)
                ahead = (block - me) * flow.step > 0

                @pl.when(ahead)
                def _():
                    copy_of(flow, block, chunk, x_ref.at[rows_of(chunk), cols_of(block)]).wait_send()

            return carry

        lax.fori_loop(0, chunks, drain, 0)


def line_scatter(x, size, collective_id, out_dtype=jnp.float32, chunk_rows=256):
    rows, cols = x.shape
    chunks = rows // chunk_rows
    return pl.pallas_call(
        partial(line_scatter_kernel, size, chunk_rows),
        out_shape=jax.ShapeDtypeStruct((rows, cols // size), out_dtype),
        in_specs=[pl.BlockSpec(memory_space=pltpu.VMEM)],
        out_specs=pl.BlockSpec(memory_space=pltpu.VMEM),
        scratch_shapes=[
            pltpu.VMEM((2, rows, cols), x.dtype),
            pltpu.VMEM((2, rows, cols), x.dtype),
            pltpu.SemaphoreType.DMA((2, size, chunks)),
            pltpu.SemaphoreType.DMA((2, size, chunks)),
        ],
        compiler_params=pltpu.CompilerParams(
            collective_id=collective_id, has_side_effects=True, vmem_limit_bytes=48 * 1024 * 1024
        ),
        cost_estimate=pl.CostEstimate(flops=0, bytes_accessed=link_cost(3 * rows * cols // size), transcendentals=0),
        name="line_scatter",
    )(x)


def input_backward_kernel(
    seq_len, splits, whole_ref, dr_ref, dk_ref, dv_ref, dl_ref, three_ref, down_ref, params_ref, din_ref, gparams_ref, gdown_ref, carry, kept
):
    step = pl.program_id(0)
    tile = pl.num_programs(0) - 1 - step
    rows_each = dr_ref.shape[0]
    part = dr_ref.shape[1]
    width = whole_ref.shape[1]
    start = tile * rows_each
    at_start = lax.rem(start, seq_len) == 0
    at_end = lax.rem(start + rows_each, seq_len) == 0

    @pl.when(step == 0)
    def _():
        gparams_ref[...] = jnp.zeros_like(gparams_ref)
        gdown_ref[...] = jnp.zeros_like(gdown_ref)

    @pl.when(at_end)
    def _():
        carry[...] = jnp.zeros_like(carry)

    edge = 16
    rows = pl.ds(pl.multiple_of(start, rows_each), rows_each)
    edge_rows = pl.ds(pl.multiple_of(jnp.maximum(start - edge, 0), edge), edge)
    inverse_width = 1.0 / width

    def moments(place):
        values = whole_ref[place, :].astype(jnp.float32)
        centre = jnp.sum(values, axis=1, keepdims=True) * inverse_width
        values = values - centre
        spread = jnp.sum(values * values, axis=1, keepdims=True) * inverse_width
        return centre, lax.rsqrt(spread + norm_eps)

    centre, inv = moments(rows)
    edge_centre, edge_inv = moments(edge_rows)
    block_cols = 256
    row_index = iota((rows_each, block_cols), 0)
    dl = dl_ref[...]
    lane = iota(dl.shape, 1)
    zero = jnp.zeros_like(dl)
    first, second = splits
    dls = (
        jnp.where(lane < first, dl, zero),
        jnp.where((lane >= first) & (lane < second), dl, zero),
        jnp.where(lane >= second, dl, zero),
    )
    down_row = iota((dl.shape[1], block_cols), 0)
    sum_grad = jnp.zeros((rows_each, 1), jnp.float32)
    sum_prod = jnp.zeros((rows_each, 1), jnp.float32)

    def add_param(index, cols, values):
        total = values[0:8]
        for place in range(8, rows_each, 8):
            total = total + values[place : place + 8]
        gparams_ref[index, :, cols] += total

    for block in range(width // block_cols):
        cols = slice(block * block_cols, (block + 1) * block_cols)
        gain, bias = params_ref[0:1, cols], params_ref[1:2, cols]
        unit = (whole_ref[rows, cols].astype(jnp.float32) - centre) * inv
        normed = unit * gain + bias
        edge_unit = (whole_ref[edge_rows, cols].astype(jnp.float32) - edge_centre) * edge_inv
        edge_normed = (edge_unit * gain + bias)[edge - 1 : edge]
        edge_normed = jnp.where(at_start, 0.0, edge_normed)
        before = jnp.where(row_index == 0, edge_normed, pltpu.roll(normed, 1, 0))
        shift = before - normed
        down = down_ref[cols, :]
        weights = three_ref[cols, :]
        grads = (
            dot_nt(dr_ref[...], weights[:, :part]),
            dot_nt(dls[0], down),
            dot_nt(dk_ref[...], weights[:, part : 2 * part]),
            dot_nt(dv_ref[...], weights[:, 2 * part :]),
            dot_nt(dls[1], down),
            dot_nt(dls[2], down),
        )
        total = grads[0]
        for grad in grads[1:]:
            total = total + grad
        mixed = None
        for index, grad in enumerate(grads):
            rate = params_ref[2 + index : 3 + index, cols]
            mixed = grad * rate if mixed is None else mixed + grad * rate
            add_param(2 + index, cols, grad * shift)
        after = jnp.where(row_index == rows_each - 1, carry[0:1, cols], pltpu.roll(mixed, rows_each - 1, 0))
        carry[0:1, cols] = mixed[0:1]
        dnormed = total - mixed + after
        add_param(0, cols, dnormed * unit)
        add_param(1, cols, dnormed)
        dunit = dnormed * gain
        kept[:, cols] = dunit
        sum_grad = sum_grad + jnp.sum(dunit, axis=1, keepdims=True)
        sum_prod = sum_prod + jnp.sum(dunit * unit, axis=1, keepdims=True)
        outs = [
            dot_tn(dl, low(normed + shift * params_ref[index : index + 1, cols])) for index in (3, 6, 7)
        ]
        gdown_ref[:, cols] += jnp.where(
            down_row < first, outs[0], jnp.where(down_row < second, outs[1], outs[2])
        )
    sum_grad = sum_grad * inverse_width
    sum_prod = sum_prod * inverse_width
    for block in range(width // block_cols):
        cols = slice(block * block_cols, (block + 1) * block_cols)
        unit = (whole_ref[rows, cols].astype(jnp.float32) - centre) * inv
        din_ref[:, cols] = low(inv * (kept[:, cols] - sum_grad - unit * sum_prod))


def input_backward(whole, dr, dk, dv, dl, splits, three, down, params):
    positions, width = whole.shape
    part = dr.shape[1]
    rows_each = 256
    steps = positions // rows_each
    tile = lambda cols: pl.BlockSpec((rows_each, cols), lambda i: (steps - 1 - i, 0))
    full = pl.BlockSpec(memory_space=pltpu.VMEM)
    shape = jax.ShapeDtypeStruct
    return pl.pallas_call(
        partial(input_backward_kernel, SEQ_LEN, splits),
        grid=(steps,),
        in_specs=[full, tile(part), tile(part), tile(part), tile(dl.shape[1]), full, full, full],
        out_specs=[
            tile(width),
            pl.BlockSpec((8, 8, width), lambda i: (0, 0, 0)),
            pl.BlockSpec((dl.shape[1], width), lambda i: (0, 0)),
        ],
        out_shape=[
            shape((positions, width), jnp.bfloat16),
            shape((8, 8, width), jnp.float32),
            shape((dl.shape[1], width), jnp.float32),
        ],
        scratch_shapes=[pltpu.VMEM((8, width), jnp.float32), pltpu.VMEM((rows_each, width), jnp.float32)],
        compiler_params=pltpu.CompilerParams(
            dimension_semantics=("arbitrary",), vmem_limit_bytes=60 * 1024 * 1024
        ),
        name="input_backward",
    )(whole, dr, dk, dv, dl, three, down, params)


def weight_grads_kernel(left_refs, right_refs, out_ref):
    part = right_refs[0].shape[1]
    for index, (left_ref, right_ref) in enumerate(zip(left_refs, right_refs)):
        out_ref[:, index * part : (index + 1) * part] = low(dot_tn(left_ref[...], right_ref[...]))


def weight_grads(lefts, rights):
    positions, width = lefts[0].shape
    part = rights[0].shape[1]
    count = len(lefts)
    block = 512

    def kernel(*refs):
        weight_grads_kernel(refs[:count], refs[count : 2 * count], refs[2 * count])

    return pl.pallas_call(
        kernel,
        grid=(width // block,),
        in_specs=[pl.BlockSpec((positions, block), lambda i: (0, i))] * count
        + [pl.BlockSpec((positions, part), lambda i: (0, 0))] * count,
        out_specs=pl.BlockSpec((block, count * part), lambda i: (i, 0)),
        out_shape=jax.ShapeDtypeStruct((width, count * part), jnp.bfloat16),
        compiler_params=pltpu.CompilerParams(
            dimension_semantics=("arbitrary",), vmem_limit_bytes=60 * 1024 * 1024
        ),
        name="weight_grads",
    )(*lefts, *rights)


def line_error_kernel(
    size, chunk_rows, x_ref, base_ref, teacher_ref, weight_ref, state_ref, error_ref, got, sent, send_sem, recv_sem, out_send_sem, out_recv_sem
):
    line_barrier(size)
    me = lax.axis_index(LINE)
    flows = two_flows(size)
    width = base_ref.shape[1]
    chunks = x_ref.shape[0] // chunk_rows
    is_end = (me == 0) | (me == size - 1)
    lag = jnp.where(is_end, END_LAG, MID_LAG)

    def rows_of(chunk):
        return pl.ds(pl.multiple_of(chunk * chunk_rows, chunk_rows), chunk_rows)

    def cols_of(block):
        return pl.ds(pl.multiple_of(block * width, width), width)

    def part_copy(flow, block, chunk, source):
        place = (rows_of(chunk), cols_of(block))
        return flow.copy(
            source.at[place],
            got.at[(flow.side,) + place],
            send_sem.at[flow.side, block, chunk],
            recv_sem.at[flow.side, block, chunk],
        )

    def error_copy(flow, block, chunk):
        place = error_ref.at[rows_of(chunk), cols_of(block)]
        return flow.copy(
            place, place, out_send_sem.at[flow.side, block, chunk], out_recv_sem.at[flow.side, block, chunk]
        )

    def target_of(flow, hop):
        block = jnp.where(flow.side == 0, size - 1 - hop, hop)
        return block, (block - me) * flow.step > 0

    def reduce_part(flow, chunk):
        for hop in range(size - 1):
            block, ahead = target_of(flow, hop)

            @pl.when(ahead & flow.has_source)
            def _():
                part_copy(flow, block, chunk, x_ref).wait_recv()
                place = (rows_of(chunk), cols_of(block))
                total = got[(flow.side,) + place].astype(jnp.float32) + x_ref[place].astype(jnp.float32)
                sent[(flow.side,) + place] = total.astype(sent.dtype)
                part_copy(flow, block, chunk, sent.at[flow.side]).start()

            @pl.when(ahead & jnp.logical_not(flow.has_source))
            def _():
                part_copy(flow, block, chunk, x_ref).start()

    def finish(chunk):
        rows = rows_of(chunk)
        for flow in flows:

            @pl.when(flow.has_source)
            def _():
                part_copy(flow, me, chunk, x_ref).wait_recv()

        def write(others):
            result = base_ref[rows] + (others + x_ref[rows, cols_of(me)].astype(jnp.float32))
            state_ref[rows] = result.astype(state_ref.dtype)
            error = weight_ref[rows, 0:1] * (result - teacher_ref[rows].astype(jnp.float32))
            error_ref[rows, cols_of(me)] = error.astype(error_ref.dtype)

        @pl.when(is_end)
        def _():
            write(got[flows[1].side, rows, cols_of(me)].astype(jnp.float32))

        @pl.when(jnp.logical_not(is_end))
        def _():
            write(
                got[0, rows, cols_of(me)].astype(jnp.float32) + got[1, rows, cols_of(me)].astype(jnp.float32)
            )

        for flow in flows:

            @pl.when(flow.has_target)
            def _():
                error_copy(flow, me, chunk).start()

    def forward(hop, chunk):
        for flow in flows:
            block = me - hop * flow.step
            exists = (block >= 0) & (block < size)

            @pl.when(exists)
            def _():
                error_copy(flow, block, chunk).wait_recv()

            @pl.when(exists & flow.has_target)
            def _():
                error_copy(flow, block, chunk).start()

    def at(chunk, action):
        @pl.when((chunk >= 0) & (chunk < chunks))
        def _():
            action(chunk)

    def step(turn, carry):
        at(turn, lambda chunk: reduce_part(flows[0], chunk))
        at(turn - lag, lambda chunk: reduce_part(flows[1], chunk))
        at(turn - lag - 1, finish)
        for hop in range(1, size):
            at(turn - lag - 1 - 2 * hop, partial(forward, hop))
        return carry

    lax.fori_loop(0, chunks + END_LAG + 1 + 2 * (size - 1), step, 0)

    def drain(chunk, carry):
        for flow in flows:
            for hop in range(size - 1):
                block, ahead = target_of(flow, hop)

                @pl.when(ahead)
                def _():
                    part_copy(flow, block, chunk, x_ref).wait_send()

            for hop in range(size):
                source = me - hop * flow.step
                exists = (source >= 0) & (source < size)

                @pl.when(exists & flow.has_target)
                def _():
                    error_copy(flow, source, chunk).wait_send()

        return carry

    lax.fori_loop(0, chunks, drain, 0)


def line_error(x, base, teacher, weight, size, collective_id, chunk_rows=64):
    rows, cols = x.shape
    chunks = rows // chunk_rows
    sems = pltpu.SemaphoreType.DMA((2, size, chunks))
    return pl.pallas_call(
        partial(line_error_kernel, size, chunk_rows),
        out_shape=[
            jax.ShapeDtypeStruct(base.shape, jnp.bfloat16),
            jax.ShapeDtypeStruct(x.shape, jnp.bfloat16),
        ],
        in_specs=[pl.BlockSpec(memory_space=pltpu.VMEM)] * 4,
        out_specs=[pl.BlockSpec(memory_space=pltpu.VMEM)] * 2,
        scratch_shapes=[
            pltpu.VMEM((2, rows, cols), x.dtype),
            pltpu.VMEM((2, rows, cols), x.dtype),
            sems,
            sems,
            sems,
            sems,
        ],
        compiler_params=pltpu.CompilerParams(
            collective_id=collective_id, has_side_effects=True, vmem_limit_bytes=48 * 1024 * 1024
        ),
        cost_estimate=pl.CostEstimate(flops=0, bytes_accessed=link_cost(rows * cols), transcendentals=0),
        name="line_error",
    )(x, base, teacher, weight)


def output_backward_kernel(
    seq_len, whole_ref, delta_ref, dpre_ref, weight_ref, params_ref, dres_ref, gparams_ref, carry, kept
):
    step = pl.program_id(0)
    tile = pl.num_programs(0) - 1 - step
    rows_each = dpre_ref.shape[0]
    width = whole_ref.shape[1]
    start = tile * rows_each
    at_start = lax.rem(start, seq_len) == 0
    at_end = lax.rem(start + rows_each, seq_len) == 0

    @pl.when(step == 0)
    def _():
        gparams_ref[...] = jnp.zeros_like(gparams_ref)

    @pl.when(at_end)
    def _():
        carry[...] = jnp.zeros_like(carry)

    edge = 16
    rows = pl.ds(pl.multiple_of(start, rows_each), rows_each)
    edge_rows = pl.ds(pl.multiple_of(jnp.maximum(start - edge, 0), edge), edge)
    inverse_width = 1.0 / width

    def residual(place, cols):
        return whole_ref[place, cols].astype(jnp.float32) + delta_ref[place, cols].astype(jnp.float32)

    def moments(place):
        values = residual(place, slice(0, width))
        centre = jnp.sum(values, axis=1, keepdims=True) * inverse_width
        values = values - centre
        spread = jnp.sum(values * values, axis=1, keepdims=True) * inverse_width
        return centre, lax.rsqrt(spread + norm_eps)

    centre, inv = moments(rows)
    edge_centre, edge_inv = moments(edge_rows)
    block_cols = 256
    row_index = iota((rows_each, block_cols), 0)
    sum_grad = jnp.zeros((rows_each, 1), jnp.float32)
    sum_prod = jnp.zeros((rows_each, 1), jnp.float32)

    def add_param(index, cols, values):
        total = values[0:8]
        for place in range(8, rows_each, 8):
            total = total + values[place : place + 8]
        gparams_ref[index, :, cols] += total

    for block in range(width // block_cols):
        cols = slice(block * block_cols, (block + 1) * block_cols)
        gain, bias, rate = params_ref[0:1, cols], params_ref[1:2, cols], params_ref[2:3, cols]
        unit = (residual(rows, cols) - centre) * inv
        normed = unit * gain + bias
        edge_unit = (residual(edge_rows, cols) - edge_centre) * edge_inv
        edge_normed = (edge_unit * gain + bias)[edge - 1 : edge]
        edge_normed = jnp.where(at_start, 0.0, edge_normed)
        before = jnp.where(row_index == 0, edge_normed, pltpu.roll(normed, 1, 0))
        grad = dot_nt(dpre_ref[...], weight_ref[cols, :])
        add_param(2, cols, grad * (before - normed))
        mixed = grad * rate
        after = jnp.where(row_index == rows_each - 1, carry[0:1, cols], pltpu.roll(mixed, rows_each - 1, 0))
        carry[0:1, cols] = mixed[0:1]
        dnormed = grad - mixed + after
        add_param(0, cols, dnormed * unit)
        add_param(1, cols, dnormed)
        dunit = dnormed * gain
        kept[:, cols] = dunit
        sum_grad = sum_grad + jnp.sum(dunit, axis=1, keepdims=True)
        sum_prod = sum_prod + jnp.sum(dunit * unit, axis=1, keepdims=True)
    sum_grad = sum_grad * inverse_width
    sum_prod = sum_prod * inverse_width
    for block in range(width // block_cols):
        cols = slice(block * block_cols, (block + 1) * block_cols)
        unit = (residual(rows, cols) - centre) * inv
        dres_ref[:, cols] = low(inv * (kept[:, cols] - sum_grad - unit * sum_prod))


def output_backward(whole, delta, dpre, weight, params):
    positions, width = whole.shape
    rows_each = 256
    steps = positions // rows_each
    tile = lambda cols: pl.BlockSpec((rows_each, cols), lambda i: (steps - 1 - i, 0))
    full = pl.BlockSpec(memory_space=pltpu.VMEM)
    return pl.pallas_call(
        partial(output_backward_kernel, SEQ_LEN),
        grid=(steps,),
        in_specs=[full, full, tile(dpre.shape[1]), full, full],
        out_specs=[tile(width), pl.BlockSpec((8, 8, width), lambda i: (0, 0, 0))],
        out_shape=[
            jax.ShapeDtypeStruct((positions, width), jnp.bfloat16),
            jax.ShapeDtypeStruct((8, 8, width), jnp.float32),
        ],
        scratch_shapes=[pltpu.VMEM((8, width), jnp.float32), pltpu.VMEM((rows_each, width), jnp.float32)],
        compiler_params=pltpu.CompilerParams(
            dimension_semantics=("arbitrary",), vmem_limit_bytes=60 * 1024 * 1024
        ),
        name="output_backward",
    )(whole, delta, dpre, weight, params)


def input_forward_kernel(
    seq_len,
    tanh_end,
    plain_end,
    whole_ref,
    three_ref,
    down_ref,
    ups_ref,
    params_ref,
    r_ref,
    k_ref,
    v_ref,
    dw_ref,
    da_ref,
    gate_ref,
    mr_ref,
    mk_ref,
    mv_ref,
    inner_ref,
):
    tile = pl.program_id(0)
    rows_each = r_ref.shape[0]
    part = r_ref.shape[1]
    width = whole_ref.shape[1]
    start = tile * rows_each
    at_start = lax.rem(start, seq_len) == 0
    edge = 16
    rows = pl.ds(pl.multiple_of(start, rows_each), rows_each)
    edge_rows = pl.ds(pl.multiple_of(jnp.maximum(start - edge, 0), edge), edge)
    inverse_width = 1.0 / width

    def moments(place):
        values = whole_ref[place, :].astype(jnp.float32)
        centre = jnp.sum(values, axis=1, keepdims=True) * inverse_width
        values = values - centre
        spread = jnp.sum(values * values, axis=1, keepdims=True) * inverse_width
        return centre, lax.rsqrt(spread + norm_eps)

    centre, inv = moments(rows)
    edge_centre, edge_inv = moments(edge_rows)
    block_cols = 256
    row_index = iota((rows_each, block_cols), 0)
    lane = iota((rows_each, down_ref.shape[1]), 1)
    r = k = v = inner_w = inner_a = inner_g = 0.0
    for block in range(width // block_cols):
        cols = slice(block * block_cols, (block + 1) * block_cols)
        gain, bias = params_ref[0:1, cols], params_ref[1:2, cols]
        normed = (whole_ref[rows, cols].astype(jnp.float32) - centre) * inv * gain + bias
        edge_unit = (whole_ref[edge_rows, cols].astype(jnp.float32) - edge_centre) * edge_inv
        edge_normed = (edge_unit * gain + bias)[edge - 1 : edge]
        edge_normed = jnp.where(at_start, 0.0, edge_normed)
        before = jnp.where(row_index == 0, edge_normed, pltpu.roll(normed, 1, 0))
        shift = before - normed

        def mix(index):
            return low(normed + shift * params_ref[index : index + 1, cols])

        mix_r, mix_k, mix_v = mix(2), mix(4), mix(5)
        mr_ref[:, cols], mk_ref[:, cols], mv_ref[:, cols] = mix_r, mix_k, mix_v
        weights = three_ref[cols, :]
        r = r + dot_nn(mix_r, weights[:, :part])
        k = k + dot_nn(mix_k, weights[:, part : 2 * part])
        v = v + dot_nn(mix_v, weights[:, 2 * part :])
        down = down_ref[cols, :]
        inner_w = inner_w + dot_nn(mix(3), down)
        inner_a = inner_a + dot_nn(mix(6), down)
        inner_g = inner_g + dot_nn(mix(7), down)
    r_ref[...], k_ref[...], v_ref[...] = r, k, v
    inner = jnp.where(
        lane < tanh_end,
        jnp.tanh(inner_w),
        jnp.where(lane < plain_end, inner_a, jax.nn.sigmoid(inner_g)),
    )
    inner_ref[...] = inner
    inner_low = low(inner)
    zero = jnp.zeros_like(inner_low)
    ups = ups_ref[...]
    dw_ref[...] = dot_nn(jnp.where(lane < tanh_end, inner_low, zero), ups)
    da_ref[...] = dot_nn(jnp.where((lane >= tanh_end) & (lane < plain_end), inner_low, zero), ups)
    gate_ref[...] = dot_nn(jnp.where(lane >= plain_end, inner_low, zero), ups)


def input_forward(whole, three, down, ups, ends, params):
    positions, width = whole.shape
    part = ups.shape[1]
    rows_each = 256
    tile = lambda cols: pl.BlockSpec((rows_each, cols), lambda i: (i, 0))
    full = pl.BlockSpec(memory_space=pltpu.VMEM)
    shape = jax.ShapeDtypeStruct
    return pl.pallas_call(
        partial(input_forward_kernel, SEQ_LEN, *ends),
        grid=(positions // rows_each,),
        in_specs=[full] * 5,
        out_specs=[tile(part)] * 6 + [tile(width)] * 3 + [tile(down.shape[1])],
        out_shape=[shape((positions, part), jnp.float32)] * 6
        + [shape((positions, width), jnp.bfloat16)] * 3
        + [shape((positions, down.shape[1]), jnp.float32)],
        compiler_params=pltpu.CompilerParams(
            dimension_semantics=("arbitrary",), vmem_limit_bytes=60 * 1024 * 1024
        ),
        name="input_forward",
    )(whole, three, down, ups, params)


def start_gather_kernel(
    size,
    groups,
    chunk_rows,
    x_ref,
    narrow_ref,
    ups_ref,
    out_ref,
    narrow_out,
    ups_out,
    send_sem,
    recv_sem,
    line_send,
    line_recv,
    group_send,
    group_recv,
):
    me = lax.axis_index(LINE)
    mine = lax.axis_index(GROUP)
    barrier = pltpu.get_barrier_semaphore()
    for offset in range(1, groups):
        peer = lax.rem(mine + offset, groups)
        pl.semaphore_signal(barrier, inc=1, device_id={GROUP: peer}, device_id_type=pl.DeviceIdType.MESH)

    @pl.when(me > 0)
    def _():
        pl.semaphore_signal(barrier, inc=1, device_id={LINE: me - 1}, device_id_type=pl.DeviceIdType.MESH)

    @pl.when(me < size - 1)
    def _():
        pl.semaphore_signal(barrier, inc=1, device_id={LINE: me + 1}, device_id_type=pl.DeviceIdType.MESH)

    ends = jnp.where((me == 0) | (me == size - 1), 1, 2)
    pl.semaphore_wait(barrier, ends + groups - 1)
    flows = two_flows(size)
    width = x_ref.shape[1]
    chunks = x_ref.shape[0] // chunk_rows

    def place(block, chunk):
        rows = pl.ds(pl.multiple_of(chunk * chunk_rows, chunk_rows), chunk_rows)
        return out_ref.at[rows, pl.ds(pl.multiple_of(block * width, width), width)]

    def copy_of(flow, block, chunk):
        return flow.copy(
            place(block, chunk), place(block, chunk), send_sem.at[flow.side, block, chunk], recv_sem.at[flow.side, block, chunk]
        )

    def narrow_copy(flow, block):
        spot = narrow_out.at[mine, block]
        return flow.copy(spot, spot, line_send.at[flow.side, block], line_recv.at[flow.side, block])

    def group_copy(kind, out, peer, slot):
        return pltpu.make_async_remote_copy(
            src_ref=out.at[slot],
            dst_ref=out.at[slot],
            send_sem=group_send.at[kind, peer],
            recv_sem=group_recv.at[kind, slot],
            device_id={GROUP: peer},
            device_id_type=pl.DeviceIdType.MESH,
        )

    narrow_out[mine, me] = narrow_ref[...]
    for flow in flows:

        @pl.when(flow.has_target)
        def _():
            narrow_copy(flow, me).start()

    def first(chunk, carry):
        rows = pl.ds(pl.multiple_of(chunk * chunk_rows, chunk_rows), chunk_rows)
        out_ref[rows, pl.ds(pl.multiple_of(me * width, width), width)] = x_ref[rows]
        for flow in flows:

            @pl.when(flow.has_target)
            def _():
                copy_of(flow, me, chunk).start()

        return carry

    lax.fori_loop(0, chunks, first, 0)
    ups_out[mine] = ups_ref[...]
    for offset in range(1, groups):
        group_copy(0, ups_out, lax.rem(mine + offset, groups), mine).start()
    for hop in range(1, size):
        for flow in flows:
            block = me - hop * flow.step
            exists = (block >= 0) & (block < size)

            @pl.when(exists)
            def _():
                narrow_copy(flow, block).wait_recv()

            @pl.when(exists & flow.has_target)
            def _():
                narrow_copy(flow, block).start()

        if hop == size - 1:
            for offset in range(1, groups):
                group_copy(1, narrow_out, lax.rem(mine + offset, groups), mine).start()

        def forward(chunk, carry):
            for flow in flows:
                block = me - hop * flow.step
                exists = (block >= 0) & (block < size)

                @pl.when(exists)
                def _():
                    copy_of(flow, block, chunk).wait_recv()

                @pl.when(exists & flow.has_target)
                def _():
                    copy_of(flow, block, chunk).start()

            return carry

        lax.fori_loop(0, chunks, forward, 0)
    for offset in range(1, groups):
        peer = lax.rem(mine + offset, groups)
        for kind, out in ((0, ups_out), (1, narrow_out)):
            group_copy(kind, out, peer, peer).wait_recv()
            group_copy(kind, out, peer, mine).wait_send()
    for hop in range(size):

        def drain(chunk, carry):
            for flow in flows:
                block = me - hop * flow.step
                exists = (block >= 0) & (block < size)

                @pl.when(exists & flow.has_target)
                def _():
                    copy_of(flow, block, chunk).wait_send()

            return carry

        lax.fori_loop(0, chunks, drain, 0)
        for flow in flows:
            block = me - hop * flow.step
            exists = (block >= 0) & (block < size)

            @pl.when(exists & flow.has_target)
            def _():
                narrow_copy(flow, block).wait_send()


def start_gather(x, narrow, ups, size, groups, collective_id, chunk_rows=256):
    rows, cols = x.shape
    chunks = rows // chunk_rows
    shape = jax.ShapeDtypeStruct
    dma = pltpu.SemaphoreType.DMA
    return pl.pallas_call(
        partial(start_gather_kernel, size, groups, chunk_rows),
        out_shape=[
            shape((rows, size * cols), x.dtype),
            shape((groups, size) + narrow.shape, x.dtype),
            shape((groups,) + ups.shape, x.dtype),
        ],
        in_specs=[pl.BlockSpec(memory_space=pltpu.VMEM)] * 3,
        out_specs=[pl.BlockSpec(memory_space=pltpu.VMEM)] * 3,
        scratch_shapes=[
            dma((2, size, chunks)),
            dma((2, size, chunks)),
            dma((2, size)),
            dma((2, size)),
            dma((2, groups)),
            dma((2, groups)),
        ],
        compiler_params=pltpu.CompilerParams(
            collective_id=collective_id, has_side_effects=True, vmem_limit_bytes=48 * 1024 * 1024
        ),
        cost_estimate=pl.CostEstimate(flops=0, bytes_accessed=link_cost(3 * rows * cols), transcendentals=0),
        name="start_gather",
    )(x, narrow, ups)


def channel_forward_kernel(
    seq_len,
    whole_ref,
    delta_ref,
    key_ref,
    value_ref,
    params_ref,
    mixed_ref,
    active_ref,
    squared_ref,
    part_ref,
    own_ref,
):
    tile = pl.program_id(0)
    rows_each = mixed_ref.shape[0]
    width = whole_ref.shape[1]
    own_width = own_ref.shape[1]
    start = tile * rows_each
    at_start = lax.rem(start, seq_len) == 0
    edge = 16
    rows = pl.ds(pl.multiple_of(start, rows_each), rows_each)
    edge_rows = pl.ds(pl.multiple_of(jnp.maximum(start - edge, 0), edge), edge)
    inverse_width = 1.0 / width

    def residual(place, cols):
        return whole_ref[place, cols].astype(jnp.float32) + delta_ref[place, cols].astype(jnp.float32)

    def moments(place):
        values = residual(place, slice(0, width))
        centre = jnp.sum(values, axis=1, keepdims=True) * inverse_width
        values = values - centre
        spread = jnp.sum(values * values, axis=1, keepdims=True) * inverse_width
        return centre, lax.rsqrt(spread + norm_eps)

    centre, inv = moments(rows)
    edge_centre, edge_inv = moments(edge_rows)
    own_start = pl.multiple_of(lax.axis_index(LINE) * own_width, own_width)
    own_ref[...] = residual(rows, pl.ds(own_start, own_width))
    block_cols = 256
    row_index = iota((rows_each, block_cols), 0)
    for block in range(width // block_cols):
        cols = slice(block * block_cols, (block + 1) * block_cols)
        gain, bias, rate = params_ref[0:1, cols], params_ref[1:2, cols], params_ref[2:3, cols]
        normed = (residual(rows, cols) - centre) * inv * gain + bias
        edge_unit = (residual(edge_rows, cols) - edge_centre) * edge_inv
        edge_normed = (edge_unit * gain + bias)[edge - 1 : edge]
        edge_normed = jnp.where(at_start, 0.0, edge_normed)
        before = jnp.where(row_index == 0, edge_normed, pltpu.roll(normed, 1, 0))
        mixed_ref[:, cols] = low(normed + (before - normed) * rate)
    hidden_cols = 512
    for block in range(key_ref.shape[1] // hidden_cols):
        cols = slice(block * hidden_cols, (block + 1) * hidden_cols)
        active = jnp.maximum(dot_nn(mixed_ref[...], key_ref[:, cols]), 0.0)
        active_ref[:, cols] = active
        squared_ref[:, cols] = low(active * active)
    for block in range(width // hidden_cols):
        cols = slice(block * hidden_cols, (block + 1) * hidden_cols)
        part_ref[:, cols] = low(dot_nn(squared_ref[...], value_ref[:, cols]))


def channel_forward(whole, delta, key_w, value_w, params, own_width):
    positions, width = whole.shape
    units = key_w.shape[1]
    rows_each = 256
    tile = lambda cols: pl.BlockSpec((rows_each, cols), lambda i: (i, 0))
    full = pl.BlockSpec(memory_space=pltpu.VMEM)
    shape = jax.ShapeDtypeStruct
    return pl.pallas_call(
        partial(channel_forward_kernel, SEQ_LEN),
        grid=(positions // rows_each,),
        in_specs=[full] * 5,
        out_specs=[tile(width), tile(units), tile(units), tile(width), tile(own_width)],
        out_shape=[
            shape((positions, width), jnp.bfloat16),
            shape((positions, units), jnp.float32),
            shape((positions, units), jnp.bfloat16),
            shape((positions, width), jnp.bfloat16),
            shape((positions, own_width), jnp.float32),
        ],
        compiler_params=pltpu.CompilerParams(
            dimension_semantics=("arbitrary",), vmem_limit_bytes=60 * 1024 * 1024
        ),
        name="channel_forward",
    )(whole, delta, key_w, value_w, params)


def matmul(left_op, right_op):
    return jnp.dot(left_op, right_op, preferred_element_type=jnp.float32)


def contract_rows(left_op, right_op):
    return jnp.einsum("tk,tn->kn", left_op, right_op, preferred_element_type=jnp.float32)


def against(grad_op, weight_op):
    return jnp.einsum("tn,kn->tk", grad_op, weight_op, preferred_element_type=jnp.float32)


def body(
    hidden,
    teacher,
    lengths,
    feature_params,
    decay_down,
    rate_down,
    gate_down,
    decay_up,
    rate_up,
    gate_up,
    receptance,
    key_proj,
    value_proj,
    output_proj,
    ffn_key,
    ffn_value,
):
    position_count, part_width = hidden.shape
    seq_dev = position_count // SEQ_LEN
    mp_index = lax.axis_index("mp")
    col_start = mp_index * part_width
    groups = lax.axis_size("dp")
    own_lengths = lax.dynamic_slice_in_dim(lengths, lax.axis_index("dp") * seq_dev, seq_dev)
    places = jnp.arange(SEQ_LEN, dtype=jnp.int32)
    valid = (places[None, :] < own_lengths[:, None]).astype(jnp.float32).reshape(position_count)
    loss_scale = position_count * lax.axis_size("dp") / jnp.sum(lengths).astype(jnp.float32)
    line_size = lax.axis_size("mp")
    low_rank = (decay_down.shape[1], rate_down.shape[1], gate_down.shape[1])
    narrow = jnp.concatenate([decay_down, rate_down, gate_down, feature_params], axis=1)
    narrow = jnp.pad(narrow, ((0, 0), (0, -narrow.shape[1] % 128)))
    ups = jnp.concatenate([decay_up, rate_up, gate_up], axis=0)
    ups = jnp.pad(ups, ((0, -ups.shape[0] % 16), (0, 0)))
    whole_low, narrow_w, ups = start_gather(hidden, narrow, ups, line_size, groups, 1)
    narrow_w = narrow_w.reshape(-1, narrow.shape[1])
    decay_down_w = narrow_w[:, : low_rank[0]]
    rate_down_w = narrow_w[:, low_rank[0] : low_rank[0] + low_rank[1]]
    gate_down_w = narrow_w[:, low_rank[0] + low_rank[1] : sum(low_rank)]
    params_low = narrow_w[:, sum(low_rank) : sum(low_rank) + feature_params.shape[1]]
    three = lax.all_gather(
        jnp.concatenate([receptance, key_proj, value_proj], axis=1), "dp", axis=0, tiled=True
    )
    up_rows = (decay_up.shape[0], rate_up.shape[0], gate_up.shape[0])
    decay_up_w = ups[:, : up_rows[0]].reshape(-1, part_width)
    rate_up_w = ups[:, up_rows[0] : up_rows[0] + up_rows[1]].reshape(-1, part_width)
    gate_up_w = ups[:, up_rows[0] + up_rows[1] : sum(up_rows)].reshape(-1, part_width)
    output_w = lax.all_gather(output_proj, "dp", axis=1, tiled=True)
    ffn_key_w = lax.all_gather(ffn_key, "dp", axis=0, tiled=True)
    ffn_value_w = lax.all_gather(ffn_value, "dp", axis=1, tiled=True)
    params = params_low.astype(jnp.float32)
    model_width = whole_low.shape[1]
    params_rows = jnp.pad(params.T, ((0, -params.shape[1] % 8), (0, 0)))
    up_all = jnp.concatenate([decay_up_w, rate_up_w, gate_up_w], axis=0)
    up_all = jnp.pad(up_all, ((0, narrow_w.shape[1] - up_all.shape[0]), (0, 0)))
    (
        acceptance_matrix,
        keys_in,
        payload_source,
        decay_in,
        rate_in,
        sigmoid_source,
        mix_r,
        mix_k,
        mix_v,
        inner_hid,
    ) = input_forward(
        whole_low, three, narrow_w, up_all, (low_rank[0], low_rank[0] + low_rank[1]), params_rows
    )
    inner_low = inner_hid.astype(jnp.bfloat16)
    decay_hid = inner_hid[:, : low_rank[0]]
    gate_hid = inner_hid[:, low_rank[0] + low_rank[1] : sum(low_rank)]
    decay_low = inner_low[:, : low_rank[0]]
    rate_low = inner_low[:, low_rank[0] : low_rank[0] + low_rank[1]]
    gate_low = inner_low[:, low_rank[0] + low_rank[1] : sum(low_rank)]
    columns = lax.dynamic_slice(params_rows, (8, col_start), (8, part_width))
    mixer_args = (
        own_lengths,
        acceptance_matrix,
        keys_in,
        payload_source,
        decay_in,
        rate_in,
        sigmoid_source,
        columns,
    )
    gated_low, *kept = run_mixer_forward(*mixer_args)
    delta_low = line_sum(matmul(gated_low, output_w).astype(jnp.bfloat16), line_size, 2)
    ffn_low, active, squared, ffn_part, own_residual = channel_forward(
        whole_low, delta_low, ffn_key_w, ffn_value_w, params_rows[15:23], part_width
    )
    error_scale = jnp.broadcast_to((loss_scale * valid)[:, None], (position_count, 128))
    out_state, grad_low = line_error(ffn_part, own_residual, teacher, error_scale, line_size, 3)
    grad_ffn_value = contract_rows(squared, grad_low).astype(jnp.bfloat16)
    grad_low, grad_ffn_value = lax.optimization_barrier((grad_low, grad_ffn_value))
    grad_ffn_value = lax.psum_scatter(grad_ffn_value, "dp", scatter_dimension=1, tiled=True)
    grad_squared = against(grad_low, ffn_value_w)
    grad_pre = (grad_squared * 2.0 * active).astype(jnp.bfloat16)
    grad_ffn_key = contract_rows(ffn_low, grad_pre).astype(jnp.bfloat16)
    grad_pre, grad_ffn_key = lax.optimization_barrier((grad_pre, grad_ffn_key))
    grad_ffn_key = lax.psum_scatter(grad_ffn_key, "dp", scatter_dimension=0, tiled=True)
    d_resid_part, d_params_out = output_backward(
        whole_low, delta_low, grad_pre, ffn_key_w, params_rows[15:23]
    )
    d_delta = line_sum(d_resid_part, line_size, 5)
    d_low = (grad_low.astype(jnp.float32) + d_delta.astype(jnp.float32)).astype(jnp.bfloat16)
    grad_output_proj = contract_rows(gated_low, d_low).astype(jnp.bfloat16)
    d_low, grad_output_proj = lax.optimization_barrier((d_low, grad_output_proj))
    grad_output_proj = lax.psum_scatter(grad_output_proj, "dp", scatter_dimension=1, tiled=True)
    d_gated = against(d_low, output_w)
    d_gated, grad_ffn_value, grad_ffn_key = lax.optimization_barrier(
        (d_gated, grad_ffn_value, grad_ffn_key)
    )
    d_recept, d_keys, d_values, d_decay, d_rate, d_gate, d_columns = run_mixer_backward(
        *mixer_args, *kept, d_gated
    )
    d_columns = jnp.sum(d_columns, axis=1)[:7]
    grad_three = weight_grads((mix_r, mix_k, mix_v), (d_recept, d_keys, d_values))
    d_decay, d_rate, d_gate, grad_three = lax.optimization_barrier((d_decay, d_rate, d_gate, grad_three))
    grad_three = lax.psum_scatter(grad_three, "dp", scatter_dimension=0, tiled=True)
    shares = [rank // line_size for rank in low_rank]
    starts = (0, shares[0], shares[0] + shares[1])
    own_rank = sum(shares) + -sum(shares) % 128

    def spread_rows(weight, share, start):
        grouped = weight.reshape(line_size, share, part_width)
        grouped = jnp.pad(grouped, ((0, 0), (start, own_rank - start - share), (0, 0)))
        return grouped.reshape(line_size * own_rank, part_width)

    def own_columns(values, share):
        return lax.dynamic_slice_in_dim(values, mp_index * share, share, 1)

    def own_group(members):
        taken = jnp.concatenate(
            [own_columns(member, share) for member, share in zip(members, shares)], axis=1
        )
        return jnp.pad(taken, ((0, 0), (0, own_rank - sum(shares))))

    d_inner = (
        against(d_decay, spread_rows(decay_up_w, shares[0], starts[0]))
        + against(d_rate, spread_rows(rate_up_w, shares[1], starts[1]))
        + against(d_gate, spread_rows(gate_up_w, shares[2], starts[2]))
    ).astype(jnp.bfloat16)
    d_own = line_scatter(d_inner, line_size, 6)
    d_own, grad_output_proj = lax.optimization_barrier((d_own, grad_output_proj))
    slope = own_group(
        (
            1.0 - decay_hid * decay_hid,
            jnp.ones((position_count, low_rank[1]), jnp.float32),
            gate_hid * (1.0 - gate_hid),
        )
    )
    d_own_pre = (d_own * slope).astype(jnp.bfloat16)
    down_own = own_group((decay_down_w, rate_down_w, gate_down_w))
    d_in_part, d_params_in, d_down = input_backward(
        whole_low, d_recept, d_keys, d_values, d_own_pre, starts[1:], three, down_own, params_rows
    )
    up_grads = jnp.concatenate(
        [
            contract_rows(low_part, grad).reshape(groups, -1, part_width)
            for low_part, grad in ((decay_low, d_decay), (rate_low, d_rate), (gate_low, d_gate))
        ],
        axis=1,
    ).astype(jnp.bfloat16)
    d_in_part, grad_three = lax.optimization_barrier((d_in_part, grad_three))
    core_grads = lax.dynamic_update_slice_in_dim(
        jnp.zeros((7, model_width), jnp.float32), d_columns, col_start, 1
    )
    param_rows = jnp.concatenate(
        [
            jnp.sum(d_params_in, axis=1),
            core_grads,
            jnp.sum(d_params_out, axis=1)[:3],
        ],
        axis=0,
    )
    param_count = param_rows.shape[0]
    narrow_grads = jnp.pad(
        jnp.concatenate([d_down, param_rows], axis=0), ((0, -(own_rank + param_count) % 32), (0, 0))
    )
    d_in_part, narrow_grads, up_grads = lax.optimization_barrier((d_in_part, narrow_grads, up_grads))
    narrow_grads = lax.psum_scatter(narrow_grads, "dp", scatter_dimension=1, tiled=True)
    up_grads = lax.psum_scatter(up_grads, "dp", scatter_dimension=0, tiled=True)
    up_grads = up_grads.reshape(-1, part_width).astype(jnp.float32)
    grad_hidden = line_scatter(d_in_part, line_size, 7) + (
        lax.dynamic_slice_in_dim(grad_low, col_start, part_width, 1).astype(jnp.float32)
        + lax.dynamic_slice_in_dim(d_delta, col_start, part_width, 1).astype(jnp.float32)
    )
    row_block = decay_down.shape[0]
    narrow_grads = narrow_grads.T.reshape(line_size, row_block, -1)
    narrow_grads = lax.all_to_all(narrow_grads, "mp", 0, 0, tiled=True)

    def down_grad(start, share):
        taken = narrow_grads[:, :, start : start + share].transpose(1, 0, 2)
        return taken.reshape(row_block, line_size * share)

    grad_params = jnp.sum(narrow_grads[:, :, own_rank : own_rank + param_count], axis=0)
    return (
        out_state,
        grad_hidden,
        grad_params,
        down_grad(starts[0], shares[0]),
        down_grad(starts[1], shares[1]),
        down_grad(starts[2], shares[2]),
        up_grads[: up_rows[0]],
        up_grads[up_rows[0] : up_rows[0] + up_rows[1]],
        up_grads[up_rows[0] + up_rows[1] :],
        grad_three[:, :part_width].astype(jnp.float32),
        grad_three[:, part_width : 2 * part_width].astype(jnp.float32),
        grad_three[:, 2 * part_width :].astype(jnp.float32),
        grad_output_proj.astype(jnp.float32),
        grad_ffn_key.astype(jnp.float32),
        grad_ffn_value.astype(jnp.float32),
    )


def solution(mesh):
    in_specs = (
        P("dp", "mp"),
        P("dp", "mp"),
        P(),
        P(("dp", "mp"), None),
        P(("dp", "mp"), None),
        P(("dp", "mp"), None),
        P(("dp", "mp"), None),
        P("dp", "mp"),
        P("dp", "mp"),
        P("dp", "mp"),
        P("dp", "mp"),
        P("dp", "mp"),
        P("dp", "mp"),
        P("mp", "dp"),
        P("dp", "mp"),
        P("mp", "dp"),
    )
    out_specs = (
        P("dp", "mp"),
        P("dp", "mp"),
        P(("dp", "mp"), None),
        P(("dp", "mp"), None),
        P(("dp", "mp"), None),
        P(("dp", "mp"), None),
        P("dp", "mp"),
        P("dp", "mp"),
        P("dp", "mp"),
        P("dp", "mp"),
        P("dp", "mp"),
        P("dp", "mp"),
        P("mp", "dp"),
        P("dp", "mp"),
        P("mp", "dp"),
    )
    return jax.shard_map(body, mesh=mesh, in_specs=in_specs, out_specs=out_specs, check_vma=False)
```
